32 devices in a mesh: row: 4 (over z), seq: 2 (over y), head: 4 (over x, core).
Axes of the slice: x: 2, y: 2, z: 4, core: 2. Of those that a mesh axis runs over, the one named last changes fastest.
Arguments:
- hidden_in: bfloat16 [8, 2048, 2048], P('row', ('seq', 'head')), may hold values from -6 to 6
- grad_out: bfloat16 [8, 2048, 2048], P('row', ('seq', 'head')), may hold values from -6 to 6
- live_rows: int32 [4], P('row'), may hold values from 1 to 2, as said below
- doc_starts: int32 [8, 2048], P('row'), may hold values from 0 to 1, as said below
- norm_attn: bfloat16 [2048], replicated, may hold values from 0.5 to 1.5
- norm_ffn: bfloat16 [2048], replicated, may hold values from 0.5 to 1.5
- query_weight: bfloat16 [2048, 2048], P(('row', 'seq'), 'head'), may hold values from -0.125 to 0.125
- key_weight: bfloat16 [2048, 512], P(('row', 'seq'), 'head'), may hold values from -0.125 to 0.125
- value_weight: bfloat16 [2048, 512], P(('row', 'seq'), 'head'), may hold values from -0.125 to 0.125
- out_weight: bfloat16 [2048, 2048], P('head', ('row', 'seq')), may hold values from -0.5 to 0.5
- gate_weight: bfloat16 [2048, 8192], P(('row', 'seq'), 'head'), may hold values from -0.125 to 0.125
- up_weight: bfloat16 [2048, 8192], P(('row', 'seq'), 'head'), may hold values from -0.125 to 0.125
- down_weight: bfloat16 [8192, 2048], P('head', ('row', 'seq')), may hold values from -0.0625 to 0.0625
- query_adapt_in: bfloat16 [2048, 8], replicated, may hold values from -0.125 to 0.125
- query_adapt_out: bfloat16 [8, 2048], P(None, 'head'), may hold values from -0.59765625 to 0.59765625
- key_adapt_in: bfloat16 [2048, 8], replicated, may hold values from -0.125 to 0.125
- key_adapt_out: bfloat16 [8, 512], P(None, 'head'), may hold values from -0.59765625 to 0.59765625
- value_adapt_in: bfloat16 [2048, 8], replicated, may hold values from -0.125 to 0.125
- value_adapt_out: bfloat16 [8, 512], P(None, 'head'), may hold values from -0.59765625 to 0.59765625
- outproj_adapt_in: bfloat16 [2048, 8], P('head'), may hold values from -0.5 to 0.5
- projection_adapter_second: bfloat16 [8, 2048], replicated, may hold values from -0.59765625 to 0.59765625
- query_feature: bfloat16 [32, 64, 64], P('head'), may hold values from -0.75 to 0.75
- key_feature: bfloat16 [8, 64, 64], P('head'), may hold values from -0.75 to 0.75
Outputs:
- block_out: bfloat16 [8, 2048, 2048], P('row', ('seq', 'head'))
- grad_hidden: bfloat16 [8, 2048, 2048], P('row', ('seq', 'head'))
- grad_query_in: float32 [2048, 8], P(('row', 'seq', 'head'))
- grad_query_out: float32 [8, 2048], P(None, 'head')
- grad_key_in: float32 [2048, 8], P(('row', 'seq', 'head'))
- grad_key_out: float32 [8, 512], P(None, 'head')
- grad_value_in: float32 [2048, 8], P(('row', 'seq', 'head'))
- grad_value_out: float32 [8, 512], P(None, 'head')
- grad_outproj_in: float32 [2048, 8], P('head')
- grad_outproj_out: float32 [8, 2048], P(None, ('row', 'seq', 'head'))
- grad_query_feature: float32 [32, 64, 64], P('head')
- grad_key_feature: float32 [8, 64, 64], P('head')
The draws below stay inside these ranges and needn't reach their ends.
Inputs may be any that keep to these rules, and one draw needn't show every extreme that they name: Row slots 0 to live_rows[g] - 1 of the 2 slots of row group g are live, the others add nothing to any gradient; some group is full and some other group has a single live slot. `doc_starts`: 1 marks the first token of a document in a packed row; each row group has a row without marks.
All inputs are finite; a program needn't handle non-finite values.
Results may differ from the reference program's by a relative error of at most 0.028.
Values may be sent and summed in bfloat16 or wider, within the bound.
A program may use at most 224 MiB of HBM per device.

```python
import jax
import jax.numpy as jnp
from jax import lax

D = 2048
HEADS = 32
KVH = 8
HD = 64
FF = 8192
RANK = 8
WIN = 64
LEN = 2048
SLOTS = 2
GROUPS = 4
ROWS = 8


def draw_live_rows(key, part):
    key = jax.random.fold_in(key, 11)
    key_count, key_full, key_single = jax.random.split(key, 3)
    counts = jax.random.randint(key_count, (GROUPS,), 1, SLOTS + 1)
    full_group = jax.random.randint(key_full, (), 0, GROUPS)
    single_group = (full_group + 1 + jax.random.randint(key_single, (), 0, GROUPS - 1)) % GROUPS
    group_pos = jnp.arange(GROUPS)
    counts = jnp.where(group_pos == single_group, 1, counts)
    return jnp.where(group_pos == full_group, SLOTS, counts).astype(jnp.int32)


def draw_doc_starts(key, part):
    key = jax.random.fold_in(key, 23)
    key_marks, key_whole = jax.random.split(key)
    mark_pos = jax.random.randint(key_marks, (ROWS, 3), 1, LEN)
    chosen = jax.random.randint(key_whole, (GROUPS,), 0, SLOTS)
    whole_row = jnp.arange(GROUPS) * SLOTS + chosen
    keep_marks = jnp.all(jnp.arange(ROWS)[:, None] != whole_row[None, :], axis=1)
    mark_hits = jnp.any(jnp.arange(LEN)[None, None, :] == mark_pos[:, :, None], axis=1)
    return (mark_hits & keep_marks[:, None]).astype(jnp.int32)


def with_spikes(entries, key, source, target, shards_of, factor):
    def block_of(axis_at):
        return (jnp.arange(entries.shape[axis_at]) // (entries.shape[axis_at] // shards_of)).reshape((-1,) + (1,) * (entries.ndim - 1 - axis_at))

    one_side = jax.random.permutation(key, shards_of)[block_of(target)]
    other_side = (block_of(target) + shards_of // 2) % shards_of
    return jnp.where((block_of(source) == one_side) | (block_of(source) == other_side), factor * entries, entries)


def level_of(stream_key, dims, cuts, low, top_value):
    level = 1.0
    for position, shards_of in cuts:
        draws = jax.random.uniform(jax.random.fold_in(jax.random.fold_in(stream_key, 6), position), (shards_of,), jnp.float32, low / len(cuts), top_value / len(cuts))
        level = level * jnp.repeat(jnp.exp(draws), dims[position] // shards_of).reshape((-1,) + (1,) * (len(dims) - 1 - position))
    return level


def normal_values(rng, shape, deviation, reach, cuts=(), dtype=jnp.bfloat16):
    drawn = deviation * jax.random.normal(rng, shape, jnp.float32)
    if cuts:
        drawn = drawn * level_of(rng, shape, cuts, -0.22, 0.18)
    return jnp.clip(drawn, -reach, reach).astype(dtype)


def gaussian_with(rng, extent, width, bound, cuts, heavy, kind=jnp.bfloat16):
    drawn = width * jax.random.normal(rng, extent, jnp.float32)
    if cuts:
        drawn = drawn * level_of(rng, extent, cuts, -0.22, 0.18)
    return jnp.clip(with_spikes(drawn, jax.random.fold_in(rng, 3), *heavy), -bound, bound).astype(kind)


def setup_inputs(seed: int = 0) -> dict:
    streams_of = jax.random.split(jax.random.key(seed), 24)
    return {
        "hidden_in": normal_values(streams_of[0], (ROWS, LEN, D), 1.0, 6.0, ((0, 4), (1, 8))),
        "grad_out": gaussian_with(streams_of[1], (ROWS, LEN, D), 1.0, 6.0, ((0, 4), (1, 8)), (1, 2, 8, 2.0)),
        "live_rows": draw_live_rows(jax.random.fold_in(streams_of[23], 71), 0),
        "doc_starts": draw_doc_starts(jax.random.fold_in(streams_of[23], 71), 0),
        "norm_attn": jnp.clip(1.0 + 0.1 * jax.random.normal(streams_of[4], (D,), jnp.float32), 0.5, 1.5).astype(jnp.bfloat16),
        "norm_ffn": jnp.clip(1.0 + 0.1 * jax.random.normal(streams_of[5], (D,), jnp.float32), 0.5, 1.5).astype(jnp.bfloat16),
        "query_weight": normal_values(streams_of[6], (D, HEADS * HD), D ** -0.5, 0.125, ((0, 8), (1, 4))),
        "key_weight": normal_values(streams_of[7], (D, KVH * HD), D ** -0.5, 0.125, ((0, 8), (1, 4))),
        "value_weight": normal_values(streams_of[8], (D, KVH * HD), D ** -0.5, 0.125, ((0, 8), (1, 4))),
        "out_weight": normal_values(streams_of[9], (HEADS * HD, D), (HEADS * HD // 16) ** -0.5, 0.5, ((0, 4), (1, 8))),
        "gate_weight": normal_values(streams_of[10], (D, FF), D ** -0.5, 0.125, ((0, 8), (1, 4))),
        "up_weight": normal_values(streams_of[11], (D, FF), D ** -0.5, 0.125, ((0, 8), (1, 4))),
        "down_weight": normal_values(streams_of[12], (FF, D), FF ** -0.5, 0.0625, ((0, 4), (1, 8))),
        "query_adapt_in": normal_values(streams_of[13], (D, RANK), D ** -0.5, 0.125),
        "query_adapt_out": normal_values(streams_of[14], (RANK, HEADS * HD), 0.1, 0.59765625, ((1, 4),)),
        "key_adapt_in": normal_values(streams_of[15], (D, RANK), D ** -0.5, 0.125),
        "key_adapt_out": normal_values(streams_of[16], (RANK, KVH * HD), 0.1, 0.59765625, ((1, 4),)),
        "value_adapt_in": normal_values(streams_of[17], (D, RANK), D ** -0.5, 0.125),
        "value_adapt_out": normal_values(streams_of[18], (RANK, KVH * HD), 0.1, 0.59765625, ((1, 4),)),
        "outproj_adapt_in": normal_values(streams_of[19], (HEADS * HD, RANK), (HEADS * HD // 16) ** -0.5, 0.5, ((0, 4),)),
        "projection_adapter_second": normal_values(streams_of[20], (RANK, D), 0.1, 0.59765625),
        "query_feature": normal_values(streams_of[21], (HEADS, HD, HD), HD ** -0.5, 0.75, ((0, 4),)),
        "key_feature": normal_values(streams_of[22], (KVH, HD, HD), HD ** -0.5, 0.75, ((0, 4),)),
    }


NORM_EPS = 1e-05
ADAPTER_SCALE = 2.0
HIGHEST = lax.Precision.HIGHEST

@jax.custom_vjp
def low(v):
    return lax.optimization_barrier(v.astype(jnp.bfloat16)).astype(jnp.float32)

@jax.custom_vjp
def low_back(v):
    return v

def low_keep(v):
    return (low(v), None)

def low_pass(kept, grad):
    return (grad,)

def back_keep(v):
    return (v, None)

def back_low(kept, grad):
    return (low(grad),)
low.defvjp(low_keep, low_pass)
low_back.defvjp(back_keep, back_low)

def hedgehog(values):
    return jnp.concatenate([jax.nn.softmax(values, axis=-1), jax.nn.softmax(-values, axis=-1)], axis=-1)

def matrix_product(left_op, right_op):
    return jnp.dot(left_op, right_op, precision=HIGHEST)

def rms_scaled(values, gain_vec):
    return values * lax.rsqrt(lax.optimization_barrier(jnp.mean(values * values, axis=-1, keepdims=True)) + NORM_EPS) * gain_vec

def paired(blocks):
    return jnp.concatenate([blocks[:-1], blocks[1:]], axis=1)

def attend(query_low, key_low, value_low, query_feature, key_feature, doc_ids):
    blocks = LEN // WIN
    per_group = HEADS // KVH
    query_blk = query_low.reshape(blocks, WIN, KVH, per_group, HD)
    edge_pad = jnp.zeros((WIN, KVH * HD), jnp.float32)
    key_blk = jnp.concatenate([edge_pad, key_low], 0).reshape(blocks + 1, WIN, KVH, HD)
    value_blk = jnp.concatenate([edge_pad, value_low], 0).reshape(blocks + 1, WIN, KVH, HD)
    padded_docs = jnp.concatenate([jnp.full((WIN + 1,), -1, jnp.int32), doc_ids.astype(jnp.int32)])
    end_docs = padded_docs[::WIN][:blocks]
    key_docs = padded_docs[1:]
    query_docs = doc_ids.reshape(blocks, WIN)
    pair_docs = paired(key_docs.reshape(blocks + 1, WIN))
    same_doc = query_docs[:, :, None] == pair_docs[:, None, :]
    row_pos = jnp.arange(WIN)[:, None]
    col_pos = jnp.arange(2 * WIN)[None, :]
    window_mask = (same_doc & (col_pos > row_pos) & (col_pos <= row_pos + WIN)).astype(jnp.float32)
    linear_mask = (same_doc & (col_pos <= row_pos)).astype(jnp.float32)
    state_mask = ((jnp.arange(LEN + WIN)[None, :] < WIN * jnp.arange(blocks)[:, None]) & (key_docs[None, :] == end_docs[:, None])).astype(jnp.float32)
    state_valid = (query_docs == end_docs[:, None]).astype(jnp.float32)[:, :, None, None]
    query_logit = low_back(jnp.einsum('bigqd,gqde->bigqe', query_blk, query_feature.reshape(KVH, per_group, HD, HD), precision=HIGHEST))
    phi_query = low(hedgehog(query_logit))
    key_logit = low_back(jnp.einsum('bigd,gde->bige', key_blk, key_feature, precision=HIGHEST))
    phi_key = low(hedgehog(key_logit))
    key_pair = paired(key_blk)
    value_pair = paired(value_blk)
    phi_pair = paired(phi_key)
    scores = low_back(jnp.einsum('bigqd,bjgd->gqbij', query_blk, key_pair, precision=HIGHEST) * HD ** (-0.5))
    lin_score = low_back(jnp.einsum('bigqf,bjgf->gqbij', phi_query, phi_pair, precision=HIGHEST))
    weights = low(jnp.exp(scores) * window_mask + lin_score * linear_mask)
    phi_flat = phi_key.reshape(LEN + WIN, KVH, 2 * HD)
    value_flat = value_blk.reshape(LEN + WIN, KVH, HD)

    def head_state(pieces):
        phi_head, value_head = pieces
        masked_phi = state_mask[:, :, None] * phi_head[None]
        return (jnp.einsum('bef,ed->bfd', masked_phi, value_head, precision=HIGHEST), lax.optimization_barrier(jnp.sum(masked_phi, axis=1)))
    block_state, block_norm = lax.map(head_state, (phi_flat.transpose(1, 0, 2), value_flat.transpose(1, 0, 2)))
    block_state = low(block_state)
    block_norm = low(block_norm)
    numer_sum = jnp.einsum('gqbij,bjgd->bigqd', weights, value_pair, precision=HIGHEST) + state_valid[..., None] * jnp.einsum('bigqf,gbfd->bigqd', phi_query, block_state, precision=HIGHEST)
    denominator = lax.optimization_barrier(jnp.sum(weights, axis=-1)).transpose(2, 3, 0, 1) + state_valid * jnp.einsum('bigqf,gbf->bigq', phi_query, block_norm, precision=HIGHEST)
    numer_sum = low_back(numer_sum)
    denominator = low_back(denominator)
    return (numer_sum / denominator[..., None]).reshape(LEN, HEADS * HD)

def layer(rows_in, doc_ids, params, frozen):
    query_in, query_out, key_in, key_out, value_in, value_out, outproj_in, projection_output, query_feature, key_feature = params
    gain_attn, gain_ffn, query_mat, key_mat, value_mat, output_matrix, gate_mat, up_mat, down_mat = frozen
    normalized_rows = low(rms_scaled(rows_in, gain_attn))

    def project(weight_matrix, adapt_in, adapter_output):
        adapter_rank = low(low_back(matrix_product(normalized_rows, adapt_in)))
        return low(low_back(matrix_product(normalized_rows, weight_matrix) + ADAPTER_SCALE * matrix_product(adapter_rank, adapter_output)))
    query_low = project(query_mat, query_in, query_out)
    key_low = project(key_mat, key_in, key_out)
    value_low = project(value_mat, value_in, value_out)
    attention_lowrank = low(low_back(attend(query_low, key_low, value_low, query_feature, key_feature, doc_ids)))
    lowrank_mixed = low(low_back(matrix_product(attention_lowrank, outproj_in)))
    adapter_branch = low_back(matrix_product(attention_lowrank, output_matrix) + ADAPTER_SCALE * matrix_product(lowrank_mixed, projection_output))
    mid_rows = rows_in + adapter_branch
    normed_mid = low(rms_scaled(mid_rows, gain_ffn))
    gate_pre = low_back(matrix_product(normed_mid, gate_mat))
    up_pre = low_back(matrix_product(normed_mid, up_mat))
    mixed_act = low(jax.nn.silu(gate_pre) * up_pre)
    return mid_rows + low_back(matrix_product(mixed_act, down_mat))

def reference(hidden_in, grad_out, live_rows, doc_starts, norm_attn, norm_ffn, query_weight, key_weight, value_weight, out_weight, gate_weight, up_weight, down_weight, query_adapt_in, query_adapt_out, key_adapt_in, key_adapt_out, value_adapt_in, value_adapt_out, outproj_adapt_in, projection_adapter_second, query_feature, key_feature):
    frozen = jax.tree.map(lambda values: values.astype(jnp.float32), (norm_attn, norm_ffn, query_weight, key_weight, value_weight, out_weight, gate_weight, up_weight, down_weight))
    params = jax.tree.map(lambda values: values.astype(jnp.float32), (query_adapt_in, query_adapt_out, key_adapt_in, key_adapt_out, value_adapt_in, value_adapt_out, outproj_adapt_in, projection_adapter_second, query_feature, key_feature))
    doc_ids = jnp.cumsum(doc_starts, axis=1).astype(jnp.int32)
    slot_pos = (jnp.arange(ROWS) % SLOTS).astype(jnp.int32)
    live_mask = (slot_pos < jnp.repeat(live_rows, SLOTS)).astype(jnp.float32)

    def forward(rows_all, train_params):

        def one_row(pieces):
            return layer(pieces[0], pieces[1], train_params, frozen)
        return lax.map(jax.checkpoint(one_row), (rows_all, doc_ids))
    outputs, pull = jax.vjp(forward, hidden_in.astype(jnp.float32), params)
    grad_rows, grads = pull(grad_out.astype(jnp.float32) * live_mask[:, None, None])
    g_query_in, g_query_out, g_key_in, g_key_out, g_value_in, g_value_out, g_outproj_in, g_outproj_out, g_query_feat, g_key_feat = grads
    return (outputs.astype(jnp.bfloat16), grad_rows.astype(jnp.bfloat16), g_query_in, g_query_out, g_key_in, g_key_out, g_value_in, g_value_out, g_outproj_in, g_outproj_out, g_query_feat, g_key_feat)
```

```python
import functools

import jax
import jax.numpy as jnp
from jax import lax
from jax.experimental import pallas as pl
from jax.experimental.pallas import tpu as pltpu
from jax.sharding import PartitionSpec as P

HD = 64
RANK = 8
WIN = 64
FF_CHUNKS = 4

NORM_EPS = 1e-05
ADAPTER_SCALE = 2.0
F32 = jnp.float32
BF16 = jnp.bfloat16
HIGHEST = lax.Precision.HIGHEST


def shift(block, axis, distance):
    size = lax.axis_size(axis)
    return lax.ppermute(block, axis, [(i, (i + distance) % size) for i in range(size)])


def flip_core(block):
    return lax.ppermute(block, "head", [(i, i ^ 1) for i in range(lax.axis_size("head"))])


def flip_x(block):
    return lax.ppermute(block, "head", [(i, i ^ 2) for i in range(lax.axis_size("head"))])


def dot(a, b, dims=((1,), (0,))):
    return lax.dot_general(a, b, (dims, ((), ())), preferred_element_type=F32)


def rms_scaled(values, gain_vec):
    return (
        values * lax.rsqrt(jnp.mean(values * values, axis=-1, keepdims=True) + NORM_EPS) * gain_vec
    )


def rms_back(values, gain_vec, grad_in):
    factor = lax.rsqrt(jnp.mean(values * values, axis=-1, keepdims=True) + NORM_EPS)
    scaled = gain_vec * grad_in
    return factor * scaled - values * factor**3 * jnp.mean(values * scaled, axis=-1, keepdims=True)


def hedgehog(values):
    return jnp.concatenate(
        [jax.nn.softmax(values, axis=-1), jax.nn.softmax(-values, axis=-1)], axis=-1
    )


def paired(blocks):
    return jnp.concatenate([blocks[:, :-1], blocks[:, 1:]], axis=2)


def unpaired(grad_pair):
    half_width = grad_pair.shape[2] // 2
    rest_pad = ((0, 0),) * (grad_pair.ndim - 2)
    lower_half = jnp.pad(grad_pair[:, :, :half_width], ((0, 0), (0, 1)) + rest_pad)
    upper_half = jnp.pad(grad_pair[:, :, half_width:], ((0, 0), (1, 0)) + rest_pad)
    return lower_half + upper_half


def gather_zy(shard):
    rows, seqs = lax.axis_size("row"), lax.axis_size("seq")
    held = {(0, 0): shard}
    for k in range(1, rows):
        held[k, 0] = shift(held[k - 1, 0], "row", 1)
    for k in range(rows):
        for l in range(1, seqs):
            held[k, l] = shift(held[k, l - 1], "seq", 1)
    return held


def assemble(*held_sets):
    rows, seqs = lax.axis_size("row"), lax.axis_size("seq")
    row, seq = lax.axis_index("row"), lax.axis_index("seq")
    x_place = lax.axis_index("head") // 2
    depth, width = held_sets[0][0, 0].shape
    whole = jnp.zeros((rows * seqs * depth, len(held_sets) * width), held_sets[0][0, 0].dtype)
    for d, held in enumerate(held_sets):
        column = lax.rem(x_place + d, 2) * width if d or len(held_sets) > 1 else 0
        for (k, l), block in held.items():
            place = lax.rem(row - k + rows, rows) * seqs + lax.rem(seq - l + seqs, seqs)
            whole = lax.dynamic_update_slice(whole, block, (place * depth, column))
    return whole


def gather_x(held):
    return {k: flip_x(v) for k, v in held.items()}


def scatter_sum(parts, axis):
    size, place = lax.axis_size(axis), lax.axis_index(axis)
    total = lax.dynamic_index_in_dim(parts, place, 0, keepdims=False)
    for k in range(1, size):
        away = lax.dynamic_index_in_dim(parts, lax.rem(place + k, size), 0, keepdims=False)
        total = total + shift(away, axis, k)
    return total


def full_sum(part, axis):
    size = lax.axis_size(axis)
    step = 1
    while step < size:
        sent = part.astype(BF16)
        got = lax.ppermute(sent, axis, [(i, i ^ step) for i in range(size)])
        part = sent.astype(F32) + got.astype(F32)
        step *= 2
    return part


def ffn_pre_kernel(x_ref, cot_ref, w_ref, mixed_ref, gg_ref, gu_ref):
    width = mixed_ref.shape[1]
    x, cot = x_ref[...], cot_ref[...]
    gate = dot(x, w_ref[:, :width])
    up = dot(x, w_ref[:, width : 2 * width])
    gm = dot(cot, w_ref[:, 2 * width :])
    sig = jax.nn.sigmoid(gate)
    silu = gate * sig
    mixed_ref[...] = (silu * up).astype(BF16)
    gg_ref[...] = (gm * up * (sig + silu * (1.0 - sig))).astype(BF16)
    gu_ref[...] = (gm * silu).astype(BF16)


def ffn_pre(x, cot, w):
    tokens, depth = x.shape
    width = w.shape[1] // 3
    tile = min(256, tokens)
    out = jax.ShapeDtypeStruct((tokens, width), BF16)
    return pl.pallas_call(
        ffn_pre_kernel,
        grid=(tokens // tile,),
        in_specs=[
            pl.BlockSpec((tile, depth), lambda i: (i, 0)),
            pl.BlockSpec((tile, depth), lambda i: (i, 0)),
            pl.BlockSpec((depth, 3 * width), lambda i: (0, 0)),
        ],
        out_specs=[pl.BlockSpec((tile, width), lambda i: (i, 0))] * 3,
        out_shape=[out, out, out],
        compiler_params=pltpu.CompilerParams(vmem_limit_bytes=48 * 2**20),
        cost_estimate=pl.CostEstimate(
            flops=6 * tokens * depth * width,
            bytes_accessed=4 * tokens * depth + 6 * depth * width + 6 * tokens * width,
            transcendentals=tokens * width,
        ),
        name="ffn_pre",
    )(x, cot, w)


def ffn_post_kernel(chunks, *refs):
    lhs = refs[: 3 * chunks]
    weights = refs[3 * chunks : 4 * chunks]
    gn_ref, y_ref = refs[4 * chunks :]
    nt = ((1,), (1,))
    width = lhs[0].shape[1]
    gn = None
    y = None
    for j in range(chunks):
        mixed, gg, gu = (r[...] for r in lhs[3 * j : 3 * j + 3])
        w = weights[j]
        part = dot(gg, w[:, :width], nt) + dot(gu, w[:, width : 2 * width], nt)
        gn = part if gn is None else gn + part
        part = dot(mixed, w[:, 2 * width :], nt)
        y = part if y is None else y + part
    gn_ref[...] = gn.astype(BF16)
    y_ref[...] = y.astype(BF16)


def ffn_post(acts, weights):
    chunks = len(weights)
    tokens, width = acts[0][0].shape
    depth = weights[0].shape[0]
    tile = min(256, tokens)
    cols = min(512, depth)
    out = jax.ShapeDtypeStruct((tokens, depth), BF16)
    return pl.pallas_call(
        functools.partial(ffn_post_kernel, chunks),
        grid=(depth // cols, tokens // tile),
        in_specs=[pl.BlockSpec((tile, width), lambda d, i: (i, 0))] * (3 * chunks)
        + [pl.BlockSpec((cols, 3 * width), lambda d, i: (d, 0))] * chunks,
        out_specs=[pl.BlockSpec((tile, cols), lambda d, i: (i, d))] * 2,
        out_shape=[out, out],
        compiler_params=pltpu.CompilerParams(vmem_limit_bytes=48 * 2**20),
        cost_estimate=pl.CostEstimate(
            flops=6 * tokens * depth * width * chunks,
            bytes_accessed=(6 * depth * width + 6 * tokens * width) * chunks + 4 * tokens * depth,
            transcendentals=0,
        ),
        name="ffn_post",
    )(*[a for trio in acts for a in trio], *weights)


def local(
    hidden_in,
    grad_out,
    live_rows,
    doc_starts,
    norm_attn,
    norm_ffn,
    query_weight,
    key_weight,
    value_weight,
    out_weight,
    gate_weight,
    up_weight,
    down_weight,
    query_adapt_in,
    query_adapt_out,
    key_adapt_in,
    key_adapt_out,
    value_adapt_in,
    value_adapt_out,
    outproj_adapt_in,
    projection_adapter_second,
    query_feature,
    key_feature,
):
    rows, seqs, heads = lax.axis_size("row"), lax.axis_size("seq"), lax.axis_size("head")
    head = lax.axis_index("head")
    core = lax.rem(head, 2)
    x_count = heads // 2
    x_place = head // 2
    slots, share_len, model_dim = hidden_in.shape
    piece_len = 2 * share_len
    pieces = seqs * x_count
    piece = lax.axis_index("seq") * x_count + x_place
    blocks = piece_len // WIN
    ext_len = piece_len + WIN
    feat_dim = 2 * HD
    score_scale = HD ** (-0.5)
    q_cols, k_cols = query_weight.shape[1], key_weight.shape[1]
    ff_cols = gate_weight.shape[1]

    def in_order(own, other):
        first = jnp.where(core == 0, own, other)
        second = jnp.where(core == 0, other, own)
        return jnp.concatenate([first, second], axis=1)

    def own_half(both):
        return lax.dynamic_slice_in_dim(both, core * share_len, share_len, 1)

    def other_half(both):
        return lax.dynamic_slice_in_dim(both, (1 - core) * share_len, share_len, 1)

    qkv_shard = jnp.concatenate([query_weight, key_weight, value_weight], axis=1)
    out_shard = out_weight.T
    down_shard = down_weight.T
    chunk = ff_cols // FF_CHUNKS
    ffn_shards = [
        jnp.concatenate(
            [w[:, j * chunk : (j + 1) * chunk] for w in (gate_weight, up_weight, down_shard)], axis=1
        )
        for j in range(FF_CHUNKS)
    ]
    qkv_held = gather_zy(qkv_shard)
    qkv_mat = assemble(qkv_held, gather_x(qkv_held))
    out_held = gather_zy(out_shard)
    out_mat = assemble(out_held, gather_x(out_held))
    ffn_mats = [assemble(gather_zy(s)) for s in ffn_shards]

    def both(own, axis):
        other = flip_x(own)
        return jnp.concatenate(
            [jnp.where(x_place == 0, own, other), jnp.where(x_place == 0, other, own)], axis=axis
        )

    q_out, k_out, v_out = (both(v, 1) for v in (query_adapt_out, key_adapt_out, value_adapt_out))
    o_in = both(outproj_adapt_in, 0)
    query_feat_all = both(query_feature, 0)
    key_feat = both(key_feature, 0)
    groups = key_feat.shape[0]
    per_group = query_feat_all.shape[0] // groups
    query_feat = query_feat_all.reshape(groups, per_group, HD, HD)

    doc_ids = jnp.cumsum(doc_starts, axis=1)
    padded_docs = jnp.concatenate(
        [jnp.full((slots, WIN + 1), -1, jnp.int32), doc_ids], axis=1
    )
    piece_docs = padded_docs[:, ::piece_len][:, : pieces + 1]
    near_docs = lax.dynamic_slice_in_dim(padded_docs, piece * piece_len, ext_len + 1, 1)
    end_docs = near_docs[:, ::WIN][:, : blocks + 1]
    carry_doc = end_docs[:, 0]
    next_doc = end_docs[:, blocks]
    key_docs = near_docs[:, 1:]
    query_docs = near_docs[:, WIN + 1 :].reshape(slots, blocks, WIN)
    ext_pos = jnp.arange(ext_len)
    block_pos = jnp.arange(blocks + 1)
    row_pos = jnp.arange(WIN)[:, None]
    col_pos = jnp.arange(2 * WIN)[None, :]
    state_mask = (
        (ext_pos[None, None, :] < WIN * block_pos[None, :, None])
        & (key_docs[:, None, :] == end_docs[:, :, None])
    ).astype(F32)
    carry_in = (end_docs == carry_doc[:, None]).astype(F32)
    state_valid = (query_docs == end_docs[:, :blocks, None]).astype(F32)[:, :, :, None, None, None]
    pair_docs = paired(key_docs.reshape(slots, blocks + 1, WIN))
    same_doc = query_docs[:, :, :, None] == pair_docs[:, :, None, :]
    window_mask = (same_doc & (col_pos > row_pos) & (col_pos <= row_pos + WIN)).astype(F32)[
        :, None, None
    ]
    linear_mask = (same_doc & (col_pos <= row_pos)).astype(F32)[:, None, None]

    def from_pieces(block):
        held = []
        for d, start in enumerate((block, flip_x(block))):
            for l in range(seqs):
                if l:
                    start = shift(start, "seq", 1)
                source = (
                    lax.rem(lax.axis_index("seq") - l + seqs, seqs) * x_count
                    + lax.rem(x_place + d, x_count)
                )
                held.append((source, start))
        return held[1:]

    gain_attn = norm_attn.astype(F32)
    gain_ffn = norm_ffn.astype(F32)
    slot_live = (jnp.arange(slots) < live_rows[0])[:, None, None]
    grad_low = jnp.where(slot_live, grad_out, jnp.zeros_like(grad_out))
    grad_share = grad_low.astype(F32)
    rows_float = hidden_in.astype(F32)
    normed_share = rms_scaled(rows_float, gain_attn).astype(BF16)
    normed = in_order(normed_share, flip_core(normed_share))
    cot_x = flip_x(grad_low)

    flat = normed.reshape(slots * piece_len, model_dim)

    full = dot(flat, qkv_mat)
    set_cols = q_cols + 2 * k_cols

    def of_sets(v, start, count):
        return jnp.concatenate(
            [v[:, d * set_cols + start : d * set_cols + start + count] for d in range(2)], axis=1
        )

    def project(start, count, adapt_in, adapter_output):
        small = dot(flat, adapt_in).astype(BF16)
        low = (of_sets(full, start, count) + ADAPTER_SCALE * dot(small, adapter_output)).astype(BF16)
        return small, low.reshape(slots, piece_len, -1)

    small_query, query_low = project(0, q_cols, query_adapt_in, q_out)
    small_key, key_low = project(q_cols, k_cols, key_adapt_in, k_out)
    small_value, value_low = project(q_cols + k_cols, k_cols, value_adapt_in, v_out)

    def along_pieces(block, distance):
        route = []
        for p in range(pieces):
            to = p + distance
            if 0 <= to < pieces:
                for c in range(2):
                    route.append((2 * p + c, 2 * to + c))
        return lax.ppermute(block, ("seq", "head"), route)

    key_edge, value_edge = (along_pieces(v[:, -WIN:], 1) for v in (key_low, value_low))
    key_blk = jnp.concatenate([key_edge, key_low], axis=1).reshape(
        slots, blocks + 1, WIN, groups, HD
    )
    value_blk = jnp.concatenate([value_edge, value_low], axis=1).reshape(
        slots, blocks + 1, WIN, groups, HD
    )
    query_blk = query_low.reshape(slots, blocks, WIN, groups, per_group, HD)
    query_logit = jnp.einsum(
        "rbigqd,gqde->rbigqe", query_blk, query_feat, preferred_element_type=F32
    )
    phi_query = hedgehog(query_logit).astype(BF16)
    key_logit = jnp.einsum("rbigd,gde->rbige", key_blk, key_feat, preferred_element_type=F32)
    phi_key = hedgehog(key_logit).astype(BF16)
    key_pair = paired(key_blk)
    value_pair = paired(value_blk)
    phi_pair = paired(phi_key)
    scores = (
        jnp.einsum("rbigqd,rbjgd->rgqbij", query_blk, key_pair, preferred_element_type=F32)
        * score_scale
    )
    lin_score = jnp.einsum("rbigqf,rbjgf->rgqbij", phi_query, phi_pair, preferred_element_type=F32)
    exp_score = jnp.exp(scores)
    weights = (exp_score * window_mask + lin_score * linear_mask).astype(BF16)
    phi_flat = phi_key.reshape(slots, ext_len, groups, feat_dim).astype(F32)
    value_flat = value_blk.reshape(slots, ext_len, groups, HD).astype(F32)
    masked_phi = state_mask[:, :, :, None, None] * phi_flat[:, None]
    local_state = jnp.einsum("rbegf,regd->rbgfd", masked_phi, value_flat, precision=HIGHEST)
    local_norm = jnp.sum(masked_phi, axis=2)

    def with_norm(state, norm):
        return jnp.concatenate([state, norm[..., None]], axis=-1)

    carry = jnp.zeros((slots, groups, feat_dim, HD + 1), F32)
    for source, part in from_pieces(
        with_norm(local_state[:, blocks], local_norm[:, blocks]).astype(BF16)
    ):
        after = lax.dynamic_index_in_dim(piece_docs, source + 1, 1, keepdims=False)
        keep = (source < piece) & (after == carry_doc)
        carry = carry + jnp.where(keep[:, None, None, None], part.astype(F32), 0.0)
    carry_state, carry_norm = carry[..., :HD], carry[..., HD]
    block_state = (
        local_state[:, :blocks] + carry_in[:, :blocks, None, None, None] * carry_state[:, None]
    ).astype(BF16)
    block_norm = (
        local_norm[:, :blocks] + carry_in[:, :blocks, None, None] * carry_norm[:, None]
    ).astype(BF16)
    numer_sum = jnp.einsum(
        "rgqbij,rbjgd->rbigqd", weights, value_pair, preferred_element_type=F32
    ) + state_valid * jnp.einsum(
        "rbigqf,rbgfd->rbigqd", phi_query, block_state, preferred_element_type=F32
    )
    denominator = jnp.sum(weights, axis=-1, dtype=F32).transpose(0, 3, 4, 1, 2) + state_valid[
        ..., 0
    ] * jnp.einsum("rbigqf,rbgf->rbigq", phi_query, block_norm, preferred_element_type=F32)
    attn_float = numer_sum / denominator[..., None]
    attn = attn_float.reshape(slots * piece_len, -1).astype(BF16)

    proj_part = dot(attn, out_mat, ((1,), (1,))).reshape(slots, piece_len, model_dim)
    low_part = dot(attn, o_in).reshape(slots, piece_len, RANK)
    proj_sum = own_half(proj_part) + flip_core(other_half(proj_part).astype(BF16)).astype(F32)
    low_mix = (own_half(low_part) + flip_core(other_half(low_part))).astype(BF16)
    mid_rows = (
        rows_float
        + proj_sum
        + ADAPTER_SCALE
        * dot(low_mix.reshape(-1, RANK), projection_adapter_second).reshape(rows_float.shape)
    )

    nmid = rms_scaled(mid_rows, gain_ffn).astype(BF16)
    nmid_x = flip_x(nmid)

    def chip_tokens(own):
        return jnp.concatenate([own, flip_core(own)], axis=0).reshape(-1, model_dim)

    tokens = [(chip_tokens(nmid), chip_tokens(grad_low)), (chip_tokens(nmid_x), chip_tokens(cot_x))]
    acts = [[ffn_pre(x, c, w) for w in ffn_mats] for x, c in tokens]

    def to_own(mine, away):
        mine, away = (v.reshape(2, slots, share_len, model_dim) for v in (mine, away))
        there = (away[0].astype(F32) + flip_core(away[1]).astype(F32)).astype(BF16)
        back = flip_x(there)
        return mine[0].astype(F32) + flip_core(mine[1]).astype(F32) + back.astype(F32)

    gn_away, y_away = ffn_post(acts[1], ffn_mats)
    gn_mine, y_mine = ffn_post(acts[0], ffn_mats)
    grad_nmid = to_own(gn_mine, gn_away)
    block_out = (mid_rows + to_own(y_mine, y_away)).astype(BF16)
    grad_mid = grad_share + rms_back(mid_rows, gain_ffn, grad_nmid)

    branch_share = grad_mid.astype(BF16)
    branch = in_order(branch_share, flip_core(branch_share)).reshape(-1, model_dim)
    grad_low_mix = (
        ADAPTER_SCALE * dot(branch, projection_adapter_second, ((1,), (1,)))
    ).astype(BF16)
    sum_o_in = dot(attn, grad_low_mix, ((0,), (0,)))
    sum_o_out = ADAPTER_SCALE * dot(
        low_mix.reshape(-1, RANK), branch_share.reshape(-1, model_dim), ((0,), (0,))
    )
    grad_attn = (dot(branch, out_mat) + dot(grad_low_mix, o_in, ((1,), (1,)))).astype(BF16)

    grad_blk = grad_attn.reshape(slots, blocks, WIN, groups, per_group, HD).astype(F32)
    grad_numer = (grad_blk / denominator[..., None]).astype(BF16)
    grad_denom = (-jnp.sum(grad_blk * attn_float, axis=-1) / denominator).astype(BF16)
    grad_weight = (
        jnp.einsum("rbigqd,rbjgd->rgqbij", grad_numer, value_pair, preferred_element_type=F32)
        + grad_denom.transpose(0, 3, 4, 1, 2).astype(F32)[..., None]
    )
    grad_score = (exp_score * window_mask * grad_weight).astype(BF16)
    grad_lin = (linear_mask * grad_weight).astype(BF16)
    grad_query = (
        jnp.einsum("rgqbij,rbjgd->rbigqd", grad_score, key_pair, preferred_element_type=F32)
        * score_scale
    )
    grad_key_pair = (
        jnp.einsum("rgqbij,rbigqd->rbjgd", grad_score, query_blk, preferred_element_type=F32)
        * score_scale
    )
    grad_value_pair = jnp.einsum(
        "rgqbij,rbigqd->rbjgd", weights, grad_numer, preferred_element_type=F32
    )
    grad_phi_query = jnp.einsum(
        "rgqbij,rbjgf->rbigqf", grad_lin, phi_pair, preferred_element_type=F32
    ) + state_valid * (
        jnp.einsum("rbigqd,rbgfd->rbigqf", grad_numer, block_state, preferred_element_type=F32)
        + grad_denom.astype(F32)[..., None] * block_norm.astype(F32)[:, :, None, :, None, :]
    )
    grad_phi_pair = jnp.einsum(
        "rgqbij,rbigqf->rbjgf", grad_lin, phi_query, preferred_element_type=F32
    )
    phi_valid = phi_query * state_valid.astype(BF16)
    grad_state = jnp.einsum(
        "rbigqf,rbigqd->rbgfd", phi_valid, grad_numer, preferred_element_type=F32
    )
    grad_norm = jnp.einsum("rbigqf,rbigq->rbgf", phi_valid, grad_denom, preferred_element_type=F32)
    grad_carry = jnp.sum(carry_in[:, :blocks, None, None, None] * grad_state, axis=1)
    grad_carry_norm = jnp.sum(carry_in[:, :blocks, None, None] * grad_norm, axis=1)
    later = jnp.zeros((slots, groups, feat_dim, HD + 1), F32)
    for source, part in from_pieces(with_norm(grad_carry, grad_carry_norm).astype(BF16)):
        start = lax.dynamic_index_in_dim(piece_docs, source, 1, keepdims=False)
        keep = (source > piece) & (start == next_doc)
        later = later + jnp.where(keep[:, None, None, None], part.astype(F32), 0.0)
    state_all = jnp.concatenate([grad_state, later[:, None, :, :, :HD]], axis=1)
    norm_all = jnp.concatenate([grad_norm, later[:, None, :, :, HD]], axis=1)
    via_phi = jnp.einsum("rbgfd,regd->rbegf", state_all, value_flat, precision=HIGHEST)
    state_phi = jnp.einsum("rbe,rbegf->regf", state_mask, via_phi, precision=HIGHEST) + jnp.einsum(
        "rbe,rbgf->regf", state_mask, norm_all, precision=HIGHEST
    )
    grad_phi_key = unpaired(grad_phi_pair) + state_phi.reshape(
        slots, blocks + 1, WIN, groups, feat_dim
    )
    via_value = jnp.einsum("rbgfd,regf->rbegd", state_all, phi_flat, precision=HIGHEST)
    state_value = jnp.einsum("rbe,rbegd->regd", state_mask, via_value, precision=HIGHEST)
    grad_value_blk = unpaired(grad_value_pair) + state_value.reshape(
        slots, blocks + 1, WIN, groups, HD
    )
    _, pull_key = jax.vjp(hedgehog, key_logit)
    grad_key_logit = pull_key(grad_phi_key)[0].astype(BF16)
    grad_key_blk = unpaired(grad_key_pair) + jnp.einsum(
        "rbige,gde->rbigd", grad_key_logit, key_feat, preferred_element_type=F32
    )
    sum_k_feat = jnp.einsum(
        "rbigd,rbige->gde", key_blk, grad_key_logit, preferred_element_type=F32
    )
    _, pull_query = jax.vjp(hedgehog, query_logit)
    grad_query_logit = pull_query(grad_phi_query)[0].astype(BF16)
    grad_query = grad_query + jnp.einsum(
        "rbigqe,gqde->rbigqd", grad_query_logit, query_feat, preferred_element_type=F32
    )
    sum_q_feat = jnp.einsum(
        "rbigqd,rbigqe->gqde", query_blk, grad_query_logit, preferred_element_type=F32
    )
    grad_key_ext = grad_key_blk.reshape(slots, ext_len, groups * HD)
    grad_value_ext = grad_value_blk.reshape(slots, ext_len, groups * HD)
    tail_pad = ((0, 0), (piece_len - WIN, 0), (0, 0))

    def fold_back(ext):
        back = along_pieces(ext[:, :WIN].astype(BF16), -1).astype(F32)
        return (ext[:, WIN:] + jnp.pad(back, tail_pad)).astype(BF16)

    grad_key_low = fold_back(grad_key_ext).reshape(slots * piece_len, -1)
    grad_value_low = fold_back(grad_value_ext).reshape(slots * piece_len, -1)
    grad_query_low = grad_query.reshape(slots * piece_len, -1).astype(BF16)

    nt = ((1,), (1,))
    half = lambda v, d: v[:, d * (v.shape[1] // 2) : (d + 1) * (v.shape[1] // 2)]
    stacked = jnp.concatenate(
        [half(v, d) for d in range(2) for v in (grad_query_low, grad_key_low, grad_value_low)], axis=1
    )
    grad_normed_part = dot(stacked, qkv_mat, nt)
    small_part = jnp.concatenate(
        [
            ADAPTER_SCALE * dot(g, b, nt)
            for g, b in ((grad_query_low, q_out), (grad_key_low, k_out), (grad_value_low, v_out))
        ],
        axis=1,
    )
    outs = [
        ADAPTER_SCALE * dot(s, g, ((0,), (0,)))
        for s, g in (
            (small_query, grad_query_low),
            (small_key, grad_key_low),
            (small_value, grad_value_low),
        )
    ]
    grad_normed_part = grad_normed_part.reshape(slots, piece_len, model_dim)
    small_part = small_part.reshape(slots, piece_len, 3 * RANK)
    grad_normed = own_half(grad_normed_part) + flip_core(
        other_half(grad_normed_part).astype(BF16)
    ).astype(F32)
    small_low = (own_half(small_part) + flip_core(other_half(small_part))).astype(BF16)
    small_low = small_low.reshape(-1, 3 * RANK)
    adapt_in_all = jnp.concatenate([query_adapt_in, key_adapt_in, value_adapt_in], axis=1)
    grad_normed = grad_normed + dot(small_low, adapt_in_all, nt).reshape(rows_float.shape)
    sum_in = dot(small_low, normed_share.reshape(-1, model_dim), ((0,), (0,)))
    grad_hidden = (grad_mid + rms_back(rows_float, gain_attn, grad_normed)).astype(BF16)

    by_rows = jnp.concatenate([sum_in, sum_o_out], axis=0)
    width = model_dim // (rows * seqs * heads)
    by_rows = by_rows.reshape(4 * RANK, rows, seqs, heads, width).transpose(3, 2, 1, 0, 4)
    for axis in ("head", "seq", "row"):
        by_rows = scatter_sum(by_rows, axis)
    in_parts = by_rows.reshape(4, RANK, width)

    def to_heads(pair, axis):
        size = pair.shape[axis] // 2
        mine = lax.dynamic_slice_in_dim(pair, x_place * size, size, axis)
        away = lax.dynamic_slice_in_dim(pair, (1 - x_place) * size, size, axis)
        return mine + flip_x(away.astype(BF16)).astype(F32)

    cols = [
        to_heads(outs[0], 1),
        to_heads(outs[1], 1),
        to_heads(outs[2], 1),
        to_heads(sum_o_in, 0),
        to_heads(sum_q_feat.reshape(groups * per_group, HD, HD), 0),
        to_heads(sum_k_feat, 0),
    ]
    for axis in ("seq", "row"):
        cols = [full_sum(c, axis) for c in cols]
    return (
        block_out,
        grad_hidden,
        in_parts[0].T,
        cols[0],
        in_parts[1].T,
        cols[1],
        in_parts[2].T,
        cols[2],
        cols[3],
        in_parts[3],
        cols[4],
        cols[5],
    )


def solution(mesh):
    return jax.shard_map(
        local,
        mesh=mesh,
        in_specs=(
            P("row", ("seq", "head"), None),
            P("row", ("seq", "head"), None),
            P("row"),
            P("row", None),
            P(),
            P(),
            P(("row", "seq"), "head"),
            P(("row", "seq"), "head"),
            P(("row", "seq"), "head"),
            P("head", ("row", "seq")),
            P(("row", "seq"), "head"),
            P(("row", "seq"), "head"),
            P("head", ("row", "seq")),
            P(),
            P(None, "head"),
            P(),
            P(None, "head"),
            P(),
            P(None, "head"),
            P("head", None),
            P(),
            P("head", None, None),
            P("head", None, None),
        ),
        out_specs=(
            P("row", ("seq", "head"), None),
            P("row", ("seq", "head"), None),
            P(("row", "seq", "head"), None),
            P(None, "head"),
            P(("row", "seq", "head"), None),
            P(None, "head"),
            P(("row", "seq", "head"), None),
            P(None, "head"),
            P("head", None),
            P(None, ("row", "seq", "head")),
            P("head", None, None),
            P("head", None, None),
        ),
        check_vma=False,
    )
```

```python
import functools

import jax
import jax.numpy as jnp
from jax import lax
from jax.experimental import pallas as pl
from jax.experimental.pallas import tpu as pltpu
from jax.sharding import PartitionSpec as P

HD = 64
RANK = 8
WIN = 64
FF_CHUNKS = 4

NORM_EPS = 1e-05
ADAPTER_SCALE = 2.0
F32 = jnp.float32
NT = ((1,), (1,))
TN = ((0,), (0,))
BF16 = jnp.bfloat16


def shift(block, axis, distance):
    size = lax.axis_size(axis)
    return lax.ppermute(block, axis, [(i, (i + distance) % size) for i in range(size)])


def flip_core(block):
    return lax.ppermute(block, "head", [(i, i ^ 1) for i in range(lax.axis_size("head"))])


def flip_x(block):
    return lax.ppermute(block, "head", [(i, i ^ 2) for i in range(lax.axis_size("head"))])


def kernel_call(
    kernel, args, after, *, grid, in_specs, out_specs, out_shape, name, prefetch=0, scratch=(), cost=None
):
    count = len(args)

    def body(*refs):
        kernel(*refs[:count], *refs[count + len(after) :])

    return pl.pallas_call(
        body,
        grid_spec=pltpu.PrefetchScalarGridSpec(
            num_scalar_prefetch=prefetch,
            grid=grid,
            in_specs=list(in_specs) + [pl.BlockSpec(memory_space=pl.ANY)] * len(after),
            out_specs=out_specs,
            scratch_shapes=list(scratch),
        ),
        out_shape=out_shape,
        compiler_params=pltpu.CompilerParams(vmem_limit_bytes=60 * 2**20),
        cost_estimate=cost,
        name=name,
    )(*args, *after)


def copy_kernel(src_ref, dst_ref):
    dst_ref[...] = src_ref[...]


def hold(value, after):
    flat = value.reshape(-1, value.shape[-1])
    tile = min(256, flat.shape[0])
    block = pl.BlockSpec((tile, flat.shape[1]), lambda i: (i, 0))
    held = kernel_call(
        copy_kernel, [flat], after, grid=(flat.shape[0] // tile,), in_specs=[block], out_specs=block,
        out_shape=jax.ShapeDtypeStruct(flat.shape, flat.dtype), name="hold",
    )
    return held.reshape(value.shape)


def dot(a, b, dims=((1,), (0,))):
    return lax.dot_general(a, b, (dims, ((), ())), preferred_element_type=F32)


def tie(value, *after):
    return lax.optimization_barrier((value,) + after)[0]


def rms_scaled(values, gain_vec):
    return (
        values * lax.rsqrt(jnp.mean(values * values, axis=-1, keepdims=True) + NORM_EPS) * gain_vec
    )


def rms_back(values, gain_vec, grad_in):
    factor = lax.rsqrt(jnp.mean(values * values, axis=-1, keepdims=True) + NORM_EPS)
    scaled = gain_vec * grad_in
    return factor * scaled - values * factor**3 * jnp.mean(values * scaled, axis=-1, keepdims=True)


def scatter_sum(parts, axis):
    size, place = lax.axis_size(axis), lax.axis_index(axis)
    total = lax.dynamic_index_in_dim(parts, place, 0, keepdims=False)
    for k in range(1, size):
        away = lax.dynamic_index_in_dim(parts, lax.rem(place + k, size), 0, keepdims=False)
        total = total + shift(away, axis, k)
    return total


def full_sum(part, axis):
    size = lax.axis_size(axis)
    step = 1
    while step < size:
        sent = part.astype(BF16)
        got = lax.ppermute(sent, axis, [(i, i ^ step) for i in range(size)])
        part = sent.astype(F32) + got.astype(F32)
        step *= 2
    return part


def gather_plan(rows, seqs, weights):
    free = {"row": 0.0, "seq": 0.0, "x": 0.0}
    running = []
    plan = []

    def begin(now, starts):
        for t in starts:
            w, link = t[0], t[1]
            end = max(now, free[link]) + weights[w][0]
            free[link] = end
            running.append((end, len(plan), len(running), t))
        return starts

    def spread(w, k, l):
        starts = []
        row_first = weights[w][2]
        if (l == 0 or not row_first) and k + 1 < rows:
            starts.append((w, "row", k + 1, l))
        if (k == 0 or row_first) and l + 1 < seqs:
            starts.append((w, "seq", k, l + 1))
        if weights[w][1]:
            starts.append((w, "x", k, l))
        return starts

    first = [t for w in range(len(weights)) if weights[w][3] == 0 for t in spread(w, 0, 0)]
    plan.append((None, begin(0.0, first)))
    done = 0
    while running:
        event = min(running)
        running.remove(event)
        now, t = event[0], event[3]
        done += 1
        starts = [] if t[1] == "x" else spread(t[0], t[2], t[3])
        for w in range(len(weights)):
            if weights[w][3] == done:
                starts = starts + spread(w, 0, 0)
        plan.append((t, begin(now, starts)))
    return plan


def gather_kernel(plan, rows, seqs, parts, over_x, small_count, *refs):
    count = len(over_x)
    inputs, refs = refs[: count + small_count + 2], refs[count + small_count + 2 :]
    shards, smalls = inputs[:count], inputs[count : count + small_count]
    hidden, cot = inputs[count + small_count :]
    wholes, refs = refs[:count], refs[count:]
    small_outs, refs = refs[:small_count], refs[small_count:]
    hidden_out, cot_mine, cot_away = refs[:3]
    send_sem, recv_sem, copy_sem, more_send, more_recv = refs[3:]
    row, seq, head = lax.axis_index("row"), lax.axis_index("seq"), lax.axis_index("head")
    x_place = head // 2
    across = {"head": lax.rem(head + 2, 4)}
    partner = {"head": head + 1 - 2 * lax.rem(head, 2)}
    away = {
        "row": {"row": lax.rem(row + 1, rows)},
        "seq": {"seq": lax.rem(seq + 1, seqs)},
        "x": across,
    }
    barrier = pltpu.get_barrier_semaphore()
    sources = (
        {"row": lax.rem(row + rows - 1, rows)},
        {"seq": lax.rem(seq + seqs - 1, seqs)},
        across,
        partner,
    )
    for source in sources:
        pl.semaphore_signal(
            barrier, inc=1, device_id=source, device_id_type=pl.DeviceIdType.MESH
        )
    pl.semaphore_wait(barrier, len(sources))

    def slot(p, k, l):
        w, columns = parts[p][0], pl.ds(*parts[p][1])
        depth = shards[w].shape[0]
        place = lax.rem(row - k + rows, rows) * seqs + lax.rem(seq - l + seqs, seqs)
        at = pl.ds(pl.multiple_of(place * depth, depth), depth)
        return wholes[w].at[x_place, at, columns] if over_x[w] else wholes[w].at[at, columns]

    number = {}
    last_x = 0
    for i, (event, starts) in enumerate(plan):
        for t in starts:
            number[t] = len(number)
            if t[1] == "x":
                last_x = i

    def remote(src, dst, send, recv, device):
        return pltpu.make_async_remote_copy(
            src_ref=src, dst_ref=dst, send_sem=send, recv_sem=recv, device_id=device,
            device_id_type=pl.DeviceIdType.MESH,
        )

    def transfer(t):
        w, link, k, l = t
        source = {"row": (k - 1, l), "seq": (k, l - 1), "x": (k, l)}[link]
        dst = slot(w, *source)
        n = number[t]
        src = shards[parts[w][0]].at[:, pl.ds(*parts[w][1])] if source == (0, 0) else dst
        return remote(src, dst, send_sem.at[n], recv_sem.at[n], away[link])

    def more(i, src, dst, device):
        return remote(src, dst, more_send.at[i], more_recv.at[i], device)

    early = [more(i, a, b, across) for i, (a, b) in enumerate(zip(smalls, small_outs))]
    early.append(more(small_count, hidden, hidden_out, partner))
    early.append(more(small_count + 1, cot, cot_mine.at[1], partner))
    cot_x = more(small_count + 2, cot, cot_away.at[0], across)
    cot_last = more(small_count + 3, cot_away.at[0], cot_away.at[1], partner)
    own = [
        pltpu.make_async_copy(
            shards[w].at[:, pl.ds(*columns)], slot(p, 0, 0), copy_sem.at[p]
        )
        for p, (w, columns) in enumerate(parts)
    ] + [pltpu.make_async_copy(cot, cot_mine.at[0], copy_sem.at[len(parts)])]
    for i, (event, starts) in enumerate(plan):
        if event is not None:
            transfer(event).wait_recv()
        for t in starts:
            transfer(t).start()
        if event is None:
            for copy in early + own:
                copy.start()
        if i == last_x:
            cot_x.start()
    cot_x.wait()
    cot_last.start()
    for t in number:
        transfer(t).wait_send()
    for copy in early + own + [cot_last]:
        copy.wait()


def gather(shards, over_x, pieces, smalls, hidden, cot):
    rows, seqs = lax.axis_size("row"), lax.axis_size("seq")
    plan = gather_plan(
        rows,
        seqs,
        [(float(shards[w].shape[0] * c[1]), over_x[w], first, later) for w, c, first, later in pieces],
    )
    parts = [(w, c) for w, c, _, _ in pieces]
    total = sum(len(starts) for _, starts in plan)
    shapes = []
    for shard, x in zip(shards, over_x):
        depth, width = shard.shape
        whole = (rows * seqs * depth, width)
        shapes.append(jax.ShapeDtypeStruct(((2,) + whole) if x else whole, shard.dtype))
    same = lambda v: jax.ShapeDtypeStruct(v.shape, v.dtype)
    twice = jax.ShapeDtypeStruct((2,) + cot.shape, cot.dtype)
    shapes += [same(v) for v in smalls] + [same(hidden), twice, twice]
    more = len(smalls) + 4
    place = pl.BlockSpec(memory_space=pl.ANY)
    outs = pl.pallas_call(
        functools.partial(gather_kernel, plan, rows, seqs, parts, over_x, len(smalls)),
        out_shape=shapes,
        in_specs=[place] * (len(shards) + len(smalls) + 2),
        out_specs=[place] * len(shapes),
        scratch_shapes=[
            pltpu.SemaphoreType.DMA((total,)),
            pltpu.SemaphoreType.DMA((total,)),
            pltpu.SemaphoreType.DMA((len(parts) + 1,)),
            pltpu.SemaphoreType.DMA((more,)),
            pltpu.SemaphoreType.DMA((more,)),
        ],
        compiler_params=pltpu.CompilerParams(collective_id=0, has_side_effects=True),
        name="gather",
    )(*shards, *smalls, hidden, cot)
    n = len(shards)
    return outs[:n], outs[n : n + len(smalls)], outs[-3:]


def ffn_pre_kernel(
    share_len, slots, live_ref, x_ref, more_ref, cot_ref, w_ref, mixed_ref, gg_ref, gu_ref
):
    tile, width = mixed_ref.shape
    first = pl.program_id(0) < pl.num_programs(0) // 2
    slot = lax.rem(pl.program_id(0) * tile // share_len, slots)
    live = (slot < live_ref[0]).astype(F32)
    x, cot = jnp.where(first, x_ref[...], more_ref[...]), cot_ref[...]
    gate = dot(x, w_ref[:, :width])
    up = dot(x, w_ref[:, width : 2 * width])
    gm = dot(cot, w_ref[:, 2 * width :]) * live
    sig = jax.nn.sigmoid(gate)
    silu = gate * sig
    mixed_ref[...] = (silu * up).astype(BF16)
    gg_ref[...] = (gm * up * (sig + silu * (1.0 - sig))).astype(BF16)
    gu_ref[...] = (gm * silu).astype(BF16)


def ffn_pre(x, cot, w, live_rows, share_len, slots, after=()):
    tokens, depth = cot.shape
    width = w.shape[1] // 3
    tile = min(256, share_len)
    half = tokens // tile // 2
    out = jax.ShapeDtypeStruct((tokens, width), BF16)
    return kernel_call(
        functools.partial(ffn_pre_kernel, share_len, slots),
        [live_rows, x[0], x[1], cot, w],
        after,
        prefetch=1,
        grid=(tokens // tile,),
        in_specs=[
            pl.BlockSpec((tile, depth), lambda i, *_: (jnp.minimum(i, half - 1), 0)),
            pl.BlockSpec((tile, depth), lambda i, *_: (jnp.maximum(i - half, 0), 0)),
            pl.BlockSpec((tile, depth), lambda i, *_: (i, 0)),
            pl.BlockSpec((depth, 3 * width), lambda i, *_: (0, 0)),
        ],
        out_specs=[pl.BlockSpec((tile, width), lambda i, *_: (i, 0))] * 3,
        out_shape=[out, out, out],
        cost=pl.CostEstimate(
            flops=6 * tokens * depth * width,
            bytes_accessed=4 * tokens * depth + 6 * depth * width + 6 * tokens * width,
            transcendentals=tokens * width,
        ),
        name="ffn_pre",
    )


def ffn_post_kernel(chunks, start, lhs_count, *refs):
    out_ref = refs[-1]
    weights = refs[lhs_count * chunks : -1]
    width = refs[0].shape[1]
    total = None
    for j in range(chunks):
        for i in range(lhs_count):
            at = (start + i) * width
            part = dot(refs[lhs_count * j + i][...], weights[j][:, at : at + width], ((1,), (1,)))
            total = part if total is None else total + part
    out_ref[...] = total.astype(BF16)


def ffn_post(acts, weights, start, name, after=()):
    chunks, lhs_count = len(weights), len(acts[0])
    tokens, width = acts[0][0].shape
    depth = weights[0].shape[0]
    tile = min(512, tokens)
    cols = min(512, depth)
    return kernel_call(
        functools.partial(ffn_post_kernel, chunks, start, lhs_count),
        [*[a for group in acts for a in group], *weights],
        after,
        grid=(depth // cols, tokens // tile),
        in_specs=[pl.BlockSpec((tile, width), lambda d, i: (i, 0))] * (lhs_count * chunks)
        + [pl.BlockSpec((cols, 3 * width), lambda d, i: (d, 0))] * chunks,
        out_specs=pl.BlockSpec((tile, cols), lambda d, i: (i, d)),
        out_shape=jax.ShapeDtypeStruct((tokens, depth), BF16),
        cost=pl.CostEstimate(
            flops=2 * lhs_count * tokens * depth * width * chunks,
            bytes_accessed=(6 * depth * width + 2 * lhs_count * tokens * width) * chunks
            + 2 * tokens * depth,
            transcendentals=0,
        ),
        name=name,
    )


def lower_lanes(like):
    return lax.broadcasted_iota(jnp.int32, like.shape, 1) < HD


def half_ones():
    r = lax.broadcasted_iota(jnp.int32, (2 * HD, 2 * HD), 0) // HD
    c = lax.broadcasted_iota(jnp.int32, (2 * HD, 2 * HD), 1) // HD
    return (r == c).astype(F32).astype(BF16)


def swap(v):
    return pltpu.roll(v, HD, 1)


def features(x, feat):
    logit = dot(x, feat)
    low = lower_lanes(logit)
    top = jnp.max(jnp.where(low, logit, -jnp.inf), axis=1, keepdims=True)
    bottom = jnp.max(jnp.where(low, -jnp.inf, logit), axis=1, keepdims=True)
    e = jnp.exp(logit - jnp.where(low, top, bottom))
    return e / dot(e.astype(BF16), half_ones())


def features_back(phi, grad):
    p = phi.astype(F32)
    prod = p * grad
    low = lower_lanes(prod)
    first = jnp.sum(jnp.where(low, prod, 0.0), axis=1, keepdims=True)
    second = jnp.sum(jnp.where(low, 0.0, prod), axis=1, keepdims=True)
    g = prod - p * jnp.where(low, first, second)
    return (g - swap(g)).astype(BF16)[:, :HD]


def values_ones(kv):
    kv = kv.astype(F32)
    return jnp.where(lower_lanes(kv), swap(kv), 1.0).astype(BF16)


def key_state_kernel(ends_ref, kv_ref, feat_ref, kdoc_ref, phi_ref, state_ref):
    r = pl.program_id(0)
    kv = kv_ref[0, 0]
    body = kv.shape[0] - WIN
    phi = features(kv[:, :HD], feat_ref[0]).astype(BF16)
    phi_ref[0, 0] = phi
    last = ends_ref[r, body // WIN]
    held = jnp.where(kdoc_ref[0, :body] == last, phi[:body].astype(F32), 0.0).astype(BF16)
    state_ref[0, 0] = dot(held, values_ones(kv[:body]), TN).astype(BF16)


def key_state(ends, kv, feat, kdoc, after=()):
    slots, groups, ext, _ = kv.shape
    block = lambda r, g, *_: (r, g, 0, 0)
    return kernel_call(
        key_state_kernel,
        [ends, kv, feat, kdoc],
        after,
        prefetch=1,
        grid=(slots, groups),
        in_specs=[
            pl.BlockSpec((1, 1, ext, 2 * HD), block),
            pl.BlockSpec((1, HD, 2 * HD), lambda r, g, *_: (g, 0, 0)),
            pl.BlockSpec((1, ext, 2 * HD), lambda r, g, *_: (r, 0, 0)),
        ],
        out_specs=[
            pl.BlockSpec((1, 1, ext, 2 * HD), block),
            pl.BlockSpec((1, 1, 2 * HD, 2 * HD), block),
        ],
        out_shape=[
            jax.ShapeDtypeStruct((slots, groups, ext, 2 * HD), BF16),
            jax.ShapeDtypeStruct((slots, groups, 2 * HD, 2 * HD), BF16),
        ],
        name="key_state",
    )


def block_masks(b, qdoc_ref, pdoc_ref):
    rows = slice(WIN * b, WIN * b + WIN)
    same = qdoc_ref[0, rows] == pdoc_ref[0, b : b + 1]
    row = lax.broadcasted_iota(jnp.int32, (WIN, 2 * WIN), 0)
    col = lax.broadcasted_iota(jnp.int32, (WIN, 2 * WIN), 1)
    linear = same & (col <= row)
    window = same & (col > row) & (col <= row + WIN)
    return window, linear


def next_state(b, ends_ref, r, state, phi_ref, vx_ref, kdoc_ref):
    rows = slice(WIN * (b - 1), WIN * b)
    keep = (ends_ref[r, b] == ends_ref[r, b - 1]).astype(F32)
    held = jnp.where(
        kdoc_ref[0, rows] == ends_ref[r, b], phi_ref[0, 0, rows].astype(F32), 0.0
    ).astype(BF16)
    return state * keep + dot(held, vx_ref[rows], TN)


def block_forward(b, ends_ref, r, q_ref, kv_ref, phi_ref, phiq_ref, vx_ref, state_low, qdoc_ref, pdoc_ref):
    heads = q_ref.shape[1]
    rows, pair = slice(WIN * b, WIN * b + WIN), slice(WIN * b, WIN * b + 2 * WIN)
    window, linear = block_masks(b, qdoc_ref, pdoc_ref)
    valid = qdoc_ref[0, rows] == ends_ref[r, b]
    query = jnp.concatenate([q_ref[0, h, rows] for h in range(heads)], axis=0)
    phi_query = jnp.concatenate([phiq_ref[0, h, rows] for h in range(heads)], axis=0)
    key = kv_ref[0, 0, pair, :HD]
    phi_key = phi_ref[0, 0, pair]
    score = dot(query, key, NT) * (HD**-0.5)
    lin = dot(phi_query, phi_key, NT)
    part = lambda v, h: v[WIN * h : WIN * h + WIN]
    exps = [jnp.where(window, jnp.exp(part(score, h)), 0.0) for h in range(heads)]
    weight = jnp.concatenate(
        [jnp.where(linear, part(lin, h), exps[h]).astype(BF16) for h in range(heads)], axis=0
    )
    phi_valid = jnp.concatenate(
        [jnp.where(valid, part(phi_query, h).astype(F32), 0.0).astype(BF16) for h in range(heads)],
        axis=0,
    )
    both = dot(weight, vx_ref[pair]) + dot(phi_valid, state_low)
    denominator = jnp.where(lower_lanes(both), swap(both), both)
    return (query, phi_query, phi_valid, key, phi_key, exps, weight, both / denominator, denominator,
            window, linear, valid)


def attend_kernel(
    ends_ref, q_ref, kv_ref, phi_ref, feat_ref, carry_ref, qdoc_ref, kdoc_ref, pdoc_ref,
    attn_ref, phiq_ref, vx_ref,
):
    r = pl.program_id(0)
    heads, length = q_ref.shape[1], q_ref.shape[2]
    vx_ref[...] = values_ones(kv_ref[0, 0])
    for h in range(heads):
        phiq_ref[0, h] = features(q_ref[0, h], feat_ref[h]).astype(BF16)
    state = carry_ref[0, 0]
    for b in range(length // WIN):
        if b:
            state = next_state(b, ends_ref, r, state, phi_ref, vx_ref, kdoc_ref)
        out = block_forward(
            b, ends_ref, r, q_ref, kv_ref, phi_ref, phiq_ref, vx_ref, state.astype(BF16), qdoc_ref,
            pdoc_ref,
        )
        attn = out[7]
        low = lower_lanes(attn[:WIN])
        for h in range(0, heads, 2):
            first, second = attn[WIN * h : WIN * h + WIN], attn[WIN * h + WIN : WIN * h + 2 * WIN]
            attn_ref[0, WIN * b : WIN * b + WIN, HD * h : HD * h + 2 * HD] = jnp.where(
                low, first, swap(second)
            ).astype(BF16)


def attention_specs(slots, groups, heads, length):
    ext = length + WIN
    four = lambda r, g, *_: (r, g, 0, 0)
    docs = lambda r, g, *_: (r, 0, 0)
    return dict(
        q=pl.BlockSpec((1, heads, length, HD), four),
        kv=pl.BlockSpec((1, 1, ext, 2 * HD), four),
        phiq=pl.BlockSpec((1, heads, length, 2 * HD), four),
        feat=pl.BlockSpec((heads, HD, 2 * HD), lambda r, g, *_: (g, 0, 0)),
        state=pl.BlockSpec((1, 1, 2 * HD, 2 * HD), four),
        qdoc=pl.BlockSpec((1, length, 2 * HD), docs),
        kdoc=pl.BlockSpec((1, ext, 2 * HD), docs),
        pdoc=pl.BlockSpec((1, length // WIN, 2 * HD), docs),
        tokens=pl.BlockSpec((1, length, heads * HD), lambda r, g, *_: (r, 0, g)),
        fgrad=pl.BlockSpec((1, heads // 2, HD, 2 * HD), four),
    )


def attend(ends, q, kv, phi, feat, carry, qdoc, kdoc, pdoc, after=()):
    slots, all_heads, length, _ = q.shape
    groups = kv.shape[1]
    heads = all_heads // groups
    sp = attention_specs(slots, groups, heads, length)
    return kernel_call(
        attend_kernel,
        [ends, q, kv, phi, feat, carry, qdoc, kdoc, pdoc],
        after,
        prefetch=1,
        grid=(slots, groups),
        in_specs=[sp[n] for n in ("q", "kv", "kv", "feat", "state", "qdoc", "kdoc", "pdoc")],
        out_specs=[sp["tokens"], sp["phiq"]],
        scratch=[pltpu.VMEM((length + WIN, 2 * HD), BF16)],
        out_shape=[
            jax.ShapeDtypeStruct((slots, length, all_heads * HD), BF16),
            jax.ShapeDtypeStruct((slots, all_heads, length, 2 * HD), BF16),
        ],
        name="attend",
    )


def attend_back_kernel(
    ends_ref, q_ref, kv_ref, phi_ref, phiq_ref, feat_ref, carry_ref, qdoc_ref, kdoc_ref, pdoc_ref,
    g_ref, gq_ref, gfeat_ref, gphi_ref, gkv_ref, gcarry_ref, vx_ref, gstate_ref, gphiq_ref, gk_ref,
    gv_ref,
):
    r = pl.program_id(0)
    heads, length = q_ref.shape[1], q_ref.shape[2]
    blocks = length // WIN
    vx_ref[...] = values_ones(kv_ref[0, 0])
    gphi_ref[...] = jnp.zeros_like(gphi_ref)
    gk_ref[...] = jnp.zeros_like(gk_ref)
    gv_ref[...] = jnp.zeros_like(gv_ref)
    scale = HD**-0.5
    state = carry_ref[0, 0]
    for b in range(blocks):
        rows, pair = slice(WIN * b, WIN * b + WIN), slice(WIN * b, WIN * b + 2 * WIN)
        if b:
            state = next_state(b, ends_ref, r, state, phi_ref, vx_ref, kdoc_ref)
        state_low = state.astype(BF16)
        (query, phi_query, phi_valid, key, phi_key, exps, weight, attn, denominator, window, linear,
         valid) = block_forward(
            b, ends_ref, r, q_ref, kv_ref, phi_ref, phiq_ref, vx_ref, state_low, qdoc_ref, pdoc_ref
        )
        grads = []
        for h in range(0, heads, 2):
            g = g_ref[0, rows, HD * h : HD * h + 2 * HD].astype(F32)
            grads += [g, swap(g)]
        grad = jnp.concatenate(grads, axis=0)
        low = lower_lanes(grad)
        grad = jnp.where(low, grad, 0.0)
        g_denom = -jnp.sum(grad * attn, axis=1, keepdims=True)
        gx = (jnp.where(low, grad, g_denom * (1.0 / HD)) / denominator).astype(BF16)
        g_weight = dot(gx, vx_ref[pair], NT)
        part = lambda v, h: v[WIN * h : WIN * h + WIN]
        g_score = jnp.concatenate(
            [(exps[h] * part(g_weight, h)).astype(BF16) for h in range(heads)], axis=0
        )
        g_lin = jnp.concatenate(
            [jnp.where(linear, part(g_weight, h), 0.0).astype(BF16) for h in range(heads)], axis=0
        )
        g_query = dot(g_score, key) * scale
        gk_ref[pair] += dot(g_score, query, TN) * scale
        gv_ref[pair] += dot(weight, gx, TN)
        gphi_ref[0, 0, pair] += dot(g_lin, phi_query, TN)
        from_lin = dot(g_lin, phi_key)
        from_state = dot(gx, state_low, NT)
        gstate_ref[b] = dot(phi_valid, gx, TN)
        for h in range(heads):
            g_phi = part(from_lin, h) + jnp.where(valid, part(from_state, h), 0.0)
            g_logit = features_back(part(phi_query, h), g_phi)
            gphiq_ref[h, rows] = g_logit
        pieces = []
        for h in range(heads):
            g_logit = gphiq_ref[h, rows]
            pieces.append(part(g_query, h) + dot(g_logit, feat_ref[h][:, :HD], NT))
        gq_ref[0, rows] = jnp.concatenate(pieces, axis=1).astype(BF16)
    for h in range(0, heads, 2):
        gfeat_ref[0, h // 2] = jnp.concatenate(
            [dot(q_ref[0, i], gphiq_ref[i], TN) for i in (h, h + 1)], axis=1
        )
    later = gstate_ref[blocks - 1]
    for b in range(blocks - 1, 0, -1):
        rows = slice(WIN * (b - 1), WIN * b)
        low_state = later.astype(BF16)
        mask = kdoc_ref[0, rows] == ends_ref[r, b]
        gphi_ref[0, 0, rows] += jnp.where(mask, dot(vx_ref[rows], low_state, NT), 0.0)
        gv_ref[rows] += jnp.where(mask, dot(phi_ref[0, 0, rows], low_state), 0.0)
        keep = (ends_ref[r, b] == ends_ref[r, b - 1]).astype(F32)
        later = gstate_ref[b - 1] + keep * later
    gcarry_ref[0, 0] = later.astype(BF16)
    gv = gv_ref[...]
    gkv_ref[0, 0, :, :HD] = gk_ref[...]
    gkv_ref[0, 0, :, HD:] = gv[:, :HD]


def attend_back(ends, q, kv, phi, phiq, feat, carry, qdoc, kdoc, pdoc, g, after=()):
    slots, all_heads, length, _ = q.shape
    groups = kv.shape[1]
    heads = all_heads // groups
    ext = length + WIN
    sp = attention_specs(slots, groups, heads, length)
    return kernel_call(
        attend_back_kernel,
        [ends, q, kv, phi, phiq, feat, carry, qdoc, kdoc, pdoc, g],
        after,
        prefetch=1,
        grid=(slots, groups),
        in_specs=[
            sp[n]
            for n in ("q", "kv", "kv", "phiq", "feat", "state", "qdoc", "kdoc", "pdoc", "tokens")
        ],
        out_specs=[sp["tokens"], sp["fgrad"], sp["kv"], sp["kv"], sp["state"]],
        scratch=[
            pltpu.VMEM((ext, 2 * HD), BF16),
            pltpu.VMEM((length // WIN, 2 * HD, 2 * HD), F32),
            pltpu.VMEM((heads, length, HD), BF16),
            pltpu.VMEM((ext, HD), F32),
            pltpu.VMEM((ext, 2 * HD), F32),
        ],
        out_shape=[
            jax.ShapeDtypeStruct((slots, length, all_heads * HD), BF16),
            jax.ShapeDtypeStruct((slots, all_heads // 2, HD, 2 * HD), F32),
            jax.ShapeDtypeStruct((slots, groups, ext, 2 * HD), F32),
            jax.ShapeDtypeStruct((slots, groups, ext, 2 * HD), F32),
            jax.ShapeDtypeStruct((slots, groups, 2 * HD, 2 * HD), BF16),
        ],
        name="attend_back",
    )


def key_back_kernel(
    ends_ref, kv_ref, phi_ref, feat_ref, later_ref, kdoc_ref, gphi_ref, gkv_ref,
    gk_ref, gv_ref, gfeat_ref,
):
    r = pl.program_id(0)
    ext = kv_ref.shape[2]
    body = ext - WIN
    last = ends_ref[r, body // WIN]
    mask = kdoc_ref[0, :body] == last
    keys, vals, feats = [], [], []
    for i in range(2):
        kv, phi = kv_ref[0, i], phi_ref[0, i]
        later = later_ref[0, i].astype(BF16)
        more_phi = jnp.where(mask, dot(values_ones(kv[:body]), later, NT), 0.0)
        more_v = jnp.where(mask, dot(phi[:body], later), 0.0)
        tail = jnp.zeros((WIN, 2 * HD), F32)
        g_phi = gphi_ref[0, i] + jnp.concatenate([more_phi, tail], axis=0)
        g_logit = features_back(phi, g_phi)
        gkv = gkv_ref[0, i]
        keys.append(gkv[:, :HD] + dot(g_logit, feat_ref[i][:, :HD], NT))
        vals.append(gkv[:, HD:] + jnp.concatenate([more_v, tail], axis=0)[:, :HD])
        feats.append(dot(kv[:, :HD], g_logit, TN))
    gfeat_ref[0, 0] = jnp.concatenate(feats, axis=1)
    gk_ref[0] = jnp.concatenate(keys, axis=1)
    gv_ref[0] = jnp.concatenate(vals, axis=1)


def key_back(ends, kv, phi, feat, later, kdoc, gphi, gkv, after=()):
    slots, groups, ext, _ = kv.shape
    four = lambda r, s, *_: (r, s, 0, 0)
    wide = pl.BlockSpec((1, 2, ext, 2 * HD), four)
    out = pl.BlockSpec((1, ext, 2 * HD), lambda r, s, *_: (r, 0, s))
    flat = jax.ShapeDtypeStruct((slots, ext, groups * HD), F32)
    return kernel_call(
        key_back_kernel,
        [ends, kv, phi, feat, later, kdoc, gphi, gkv],
        after,
        prefetch=1,
        grid=(slots, groups // 2),
        in_specs=[
            wide,
            wide,
            pl.BlockSpec((2, HD, 2 * HD), lambda r, s, *_: (s, 0, 0)),
            pl.BlockSpec((1, 2, 2 * HD, 2 * HD), four),
            pl.BlockSpec((1, ext, 2 * HD), lambda r, s, *_: (r, 0, 0)),
            wide,
            wide,
        ],
        out_specs=[out, out, pl.BlockSpec((1, 1, HD, 2 * HD), four)],
        out_shape=[flat, flat, jax.ShapeDtypeStruct((slots, groups // 2, HD, 2 * HD), F32)],
        name="key_back",
    )


def project_kernel(sets, q_cols, k_cols, x_ref, w_ref, a_ref, b_ref, q_ref, kv_ref, small_ref):
    x = x_ref[0]
    width = q_cols + 2 * k_cols
    small = dot(x, a_ref[...]).astype(BF16)
    small_ref[0] = small
    heads, groups = q_cols // HD, k_cols // HD
    for s in range(sets):
        cols = slice(s * width, (s + 1) * width)
        full = dot(x, w_ref[s]) + ADAPTER_SCALE * dot(small, b_ref[:, cols])
        for h in range(heads):
            q_ref[0, s * heads + h] = full[:, h * HD : h * HD + HD].astype(BF16)
        for g in range(0, groups, 2):
            k = full[:, q_cols + g * HD : q_cols + g * HD + 2 * HD]
            start = q_cols + k_cols + g * HD
            v = full[:, start : start + 2 * HD]
            low = lower_lanes(k)
            kv_ref[0, s * groups + g] = jnp.where(low, k, swap(v)).astype(BF16)
            kv_ref[0, s * groups + g + 1] = jnp.where(low, swap(k), v).astype(BF16)


def project(x, w, a, b, q_cols, k_cols, after=()):
    slots, length, depth = x.shape
    sets = w.shape[0]
    heads, groups = sets * q_cols // HD, sets * k_cols // HD
    tile = min(256, length)
    ranks = a.shape[1]
    return kernel_call(
        functools.partial(project_kernel, sets, q_cols, k_cols),
        [x, w, a, b],
        after,
        grid=(slots, length // tile),
        in_specs=[
            pl.BlockSpec((1, tile, depth), lambda r, i: (r, i, 0)),
            pl.BlockSpec(w.shape, lambda r, i: (0, 0, 0)),
            pl.BlockSpec(a.shape, lambda r, i: (0, 0)),
            pl.BlockSpec(b.shape, lambda r, i: (0, 0)),
        ],
        out_specs=[
            pl.BlockSpec((1, heads, tile, HD), lambda r, i: (r, 0, i, 0)),
            pl.BlockSpec((1, groups, tile, 2 * HD), lambda r, i: (r, 0, i, 0)),
            pl.BlockSpec((1, tile, ranks), lambda r, i: (r, i, 0)),
        ],
        out_shape=[
            jax.ShapeDtypeStruct((slots, heads, length, HD), BF16),
            jax.ShapeDtypeStruct((slots, groups, length, 2 * HD), BF16),
            jax.ShapeDtypeStruct((slots, length, ranks), BF16),
        ],
        cost=pl.CostEstimate(
            flops=2 * slots * length * w.size,
            bytes_accessed=2 * (slots * length * depth + w.size),
            transcendentals=0,
        ),
        name="project",
    )


def local(
    hidden_in,
    grad_out,
    live_rows,
    doc_starts,
    norm_attn,
    norm_ffn,
    query_weight,
    key_weight,
    value_weight,
    out_weight,
    gate_weight,
    up_weight,
    down_weight,
    query_adapt_in,
    query_adapt_out,
    key_adapt_in,
    key_adapt_out,
    value_adapt_in,
    value_adapt_out,
    outproj_adapt_in,
    projection_adapter_second,
    query_feature,
    key_feature,
):
    rows, seqs, heads = lax.axis_size("row"), lax.axis_size("seq"), lax.axis_size("head")
    head = lax.axis_index("head")
    core = lax.rem(head, 2)
    x_count = heads // 2
    x_place = head // 2
    slots, share_len, model_dim = hidden_in.shape
    piece_len = 2 * share_len
    pieces = seqs * x_count
    piece = lax.axis_index("seq") * x_count + x_place
    blocks = piece_len // WIN
    ext_len = piece_len + WIN
    q_cols, k_cols = query_weight.shape[1], key_weight.shape[1]
    ff_cols = gate_weight.shape[1]

    def in_order(own, other):
        first = jnp.where(core == 0, own, other)
        second = jnp.where(core == 0, other, own)
        return jnp.concatenate([first, second], axis=1)

    def own_half(both):
        return lax.dynamic_slice_in_dim(both, core * share_len, share_len, 1)

    def other_half(both):
        return lax.dynamic_slice_in_dim(both, (1 - core) * share_len, share_len, 1)

    qkv_shard = jnp.concatenate([query_weight, key_weight, value_weight], axis=1)
    out_shard = out_weight.T
    down_shard = down_weight.T
    chunk = ff_cols // FF_CHUNKS
    ffn_shards = [
        jnp.concatenate(
            [w[:, j * chunk : (j + 1) * chunk] for w in (gate_weight, up_weight, down_shard)], axis=1
        )
        for j in range(FF_CHUNKS)
    ]
    ffn_later = [
        lax.all_gather(v, ("row", "seq"), axis=0, tiled=True) for v in ffn_shards[1:]
    ]
    half_chunk = ffn_shards[0].shape[1] // 2
    own_smalls = [
        query_feature, key_feature, query_adapt_out, key_adapt_out, value_adapt_out, outproj_adapt_in
    ]
    (qkv_mat, out_mat, first_mat), other_smalls, (hidden_other, cot_mine, cot_away) = gather(
        [qkv_shard, out_shard, ffn_shards[0]],
        [True, True, False],
        [
            (0, (0, qkv_shard.shape[1]), True, 0),
            (1, (0, out_shard.shape[1]), True, 0),
            (2, (0, half_chunk), True, rows * seqs),
            (2, (half_chunk, half_chunk), False, rows * seqs),
        ],
        own_smalls,
        hidden_in,
        grad_out,
    )
    ffn_mats = [first_mat] + ffn_later

    def both(i, axis):
        own, other = own_smalls[i], other_smalls[i]
        return jnp.concatenate(
            [jnp.where(x_place == 0, own, other), jnp.where(x_place == 0, other, own)], axis=axis
        )

    query_feat_all, key_feat_all = both(0, 0), both(1, 0)
    q_out, k_out, v_out = both(2, 1), both(3, 1), both(4, 1)
    o_in = both(5, 0)

    doc_ids = jnp.cumsum(doc_starts, axis=1)
    padded_docs = jnp.concatenate(
        [jnp.full((slots, WIN + 1), -1, jnp.int32), doc_ids], axis=1
    )
    piece_docs = padded_docs[:, ::piece_len][:, : pieces + 1]
    near_docs = lax.dynamic_slice_in_dim(padded_docs, piece * piece_len, ext_len + 1, 1)
    end_docs = near_docs[:, ::WIN][:, : blocks + 1]
    carry_doc = end_docs[:, 0]
    next_doc = end_docs[:, blocks]
    key_docs = near_docs[:, 1:]
    key_doc_lanes = jnp.broadcast_to(key_docs[:, :, None], (slots, ext_len, 2 * HD))
    query_doc_lanes = key_doc_lanes[:, WIN:]
    doc_blocks = key_docs.reshape(slots, blocks + 1, WIN)
    pair_docs = jnp.concatenate([doc_blocks[:, :-1], doc_blocks[:, 1:]], axis=2)

    def from_pieces(block):
        held = []
        for d, start in enumerate((block, flip_x(block))):
            for l in range(seqs):
                if l:
                    start = shift(start, "seq", 1)
                source = (
                    lax.rem(lax.axis_index("seq") - l + seqs, seqs) * x_count
                    + lax.rem(x_place + d, x_count)
                )
                held.append((source, start))
        return held[1:]

    gain_attn = norm_attn.astype(F32)
    gain_ffn = norm_ffn.astype(F32)
    slot_live = (jnp.arange(slots) < live_rows[0])[:, None, None]
    grad_low = jnp.where(slot_live, grad_out, jnp.zeros_like(grad_out))
    grad_share = grad_low.astype(F32)
    rows_float = hidden_in.astype(F32)
    normed_share = rms_scaled(rows_float, gain_attn).astype(BF16)
    normed_other = rms_scaled(tie(hidden_other, qkv_mat).astype(F32), gain_attn).astype(BF16)
    normed = in_order(normed_share, normed_other)

    flat = normed.reshape(slots * piece_len, model_dim)
    set_cols = q_cols + 2 * k_cols
    adapt_in_all = jnp.concatenate([query_adapt_in, key_adapt_in, value_adapt_in], axis=1)

    def by_sets(parts):
        return jnp.concatenate(
            [v[:, d * (v.shape[1] // 2) : (d + 1) * (v.shape[1] // 2)] for d in range(2) for v in parts],
            axis=1,
        )

    def diagonal(parts):
        rows = [
            [p if i == j else jnp.zeros((RANK, q.shape[1]), BF16) for j, q in enumerate(parts)]
            for i, p in enumerate(parts)
        ]
        return jnp.concatenate([by_sets(r) for r in rows], axis=0)

    adapt_out_all = diagonal([q_out, k_out, v_out])
    query, kv_own, small = project(
        normed, qkv_mat, adapt_in_all, adapt_out_all, q_cols, k_cols
    )

    def along_pieces(block, distance):
        route = []
        for p in range(pieces):
            to = p + distance
            if 0 <= to < pieces:
                for c in range(2):
                    route.append((2 * p + c, 2 * to + c))
        return lax.ppermute(block, ("seq", "head"), route)

    kv = jnp.concatenate([along_pieces(kv_own[:, :, -WIN:], 1), kv_own], axis=2)
    doubled = lambda feat: jnp.concatenate([feat, -feat], axis=2)
    query_feat, key_feat = doubled(query_feat_all), doubled(key_feat_all)
    phi_key, end_state = key_state(end_docs, kv, key_feat, key_doc_lanes)
    carry = jnp.zeros(end_state.shape, F32)
    for source, part in from_pieces(end_state):
        after = lax.dynamic_index_in_dim(piece_docs, source + 1, 1, keepdims=False)
        keep = (source < piece) & (after == carry_doc)
        carry = carry + jnp.where(keep[:, None, None, None], part.astype(F32), 0.0)
    attn, phi_query = attend(
        end_docs, query, kv, phi_key, query_feat, carry, query_doc_lanes, key_doc_lanes, pair_docs
    )
    attn = attn.reshape(slots * piece_len, -1)

    half_q = q_cols
    proj_part = dot(attn[:, :half_q], out_mat[0], NT) + dot(attn[:, half_q:], out_mat[1], NT)
    proj_part = proj_part.reshape(slots, piece_len, model_dim)
    low_part = dot(attn, o_in).reshape(slots, piece_len, RANK)
    proj_sum = own_half(proj_part) + flip_core(other_half(proj_part).astype(BF16)).astype(F32)
    low_mix = (own_half(low_part) + flip_core(other_half(low_part))).astype(BF16)
    mid_rows = (
        rows_float
        + proj_sum
        + ADAPTER_SCALE
        * dot(low_mix.reshape(-1, RANK), projection_adapter_second).reshape(rows_float.shape)
    )

    nmid = rms_scaled(mid_rows, gain_ffn).astype(BF16)
    nmid_x = flip_x(nmid)

    def chip_tokens(own):
        return own.reshape(-1, model_dim), flip_core(own).reshape(-1, model_dim)

    def sum_away(away):
        away = away.reshape(2, slots, share_len, model_dim)
        return (away[0].astype(F32) + flip_core(away[1]).astype(F32)).astype(BF16)

    def sum_mine(mine, back):
        mine = mine.reshape(2, slots, share_len, model_dim)
        return mine[0].astype(F32) + flip_core(mine[1]).astype(F32) + back.astype(F32)

    flat_tokens = lambda v: v.reshape(-1, model_dim)
    x_mine = chip_tokens(nmid)
    c_mine, c_away = flat_tokens(cot_mine), flat_tokens(cot_away)
    pre = lambda x, c, w, after: ffn_pre(x, c, w, live_rows, share_len, slots, after)
    acts_mine, acts_away, after = [], [], ()
    for w in ffn_mats[:-1]:
        acts_mine.append(pre(x_mine, c_mine, w, after))
        after = (acts_mine[-1][0],)
    x_away = chip_tokens(hold(nmid_x, (acts_mine[1][0],)))
    for w in ffn_mats:
        acts_away.append(pre(x_away, c_away, w, after))
        after = (acts_away[-1][0],)
    gn_away = ffn_post([v[1:] for v in acts_away], ffn_mats, 0, "ffn_gn")
    gn_there = sum_away(gn_away)
    gn_back = flip_x(gn_there)
    acts_mine.append(pre(x_mine, c_mine, ffn_mats[-1], (gn_there,)))
    gn_mine = ffn_post([v[1:] for v in acts_mine], ffn_mats, 0, "ffn_gn")
    y_away = ffn_post([v[:1] for v in acts_away], ffn_mats, 2, "ffn_y", (gn_mine,))
    y_there = sum_away(y_away)
    y_back = flip_x(y_there)
    grad_nmid = sum_mine(gn_mine, gn_back)
    grad_mid = grad_share + rms_back(mid_rows, gain_ffn, grad_nmid)

    branch_share = grad_mid.astype(BF16)
    branch = in_order(branch_share, flip_core(branch_share)).reshape(-1, model_dim)
    grad_low_mix = (
        ADAPTER_SCALE * dot(branch, projection_adapter_second, ((1,), (1,)))
    ).astype(BF16)
    sum_o_in = dot(grad_low_mix, attn, TN)
    sum_o_out = ADAPTER_SCALE * dot(
        low_mix.reshape(-1, RANK), branch_share.reshape(-1, model_dim), ((0,), (0,))
    )
    branch_out = jnp.concatenate([dot(branch, out_mat[0]), dot(branch, out_mat[1])], axis=1)
    grad_attn = (branch_out + dot(grad_low_mix, o_in, NT)).astype(BF16)

    grad_query, feat_query, gphi, gkv, grad_carry = attend_back(
        end_docs, query, kv, phi_key, phi_query, query_feat, carry, query_doc_lanes, key_doc_lanes,
        pair_docs, grad_attn.reshape(slots, piece_len, -1), (y_there,),
    )
    y_mine = ffn_post([v[:1] for v in acts_mine], ffn_mats, 2, "ffn_y", (grad_carry,))
    block_out = (mid_rows + sum_mine(y_mine, y_back)).astype(BF16)
    later = jnp.zeros(grad_carry.shape, F32)
    for source, part in from_pieces(grad_carry):
        start = lax.dynamic_index_in_dim(piece_docs, source, 1, keepdims=False)
        keep = (source > piece) & (start == next_doc)
        later = later + jnp.where(keep[:, None, None, None], part.astype(F32), 0.0)
    grad_key_ext, grad_value_ext, feat_key = key_back(
        end_docs, kv, phi_key, key_feat, later, key_doc_lanes, gphi, gkv, (y_mine,)
    )
    sum_q_feat = jnp.sum(feat_query, axis=0).reshape(2, -1, 2 * HD)
    sum_k_feat = jnp.sum(feat_key, axis=0).reshape(2, -1, 2 * HD)
    tail_pad = ((0, 0), (piece_len - WIN, 0), (0, 0))

    def fold_back(ext):
        back = along_pieces(ext[:, :WIN].astype(BF16), -1).astype(F32)
        return (ext[:, WIN:] + jnp.pad(back, tail_pad)).astype(BF16)

    grad_key_low = fold_back(grad_key_ext).reshape(slots * piece_len, -1)
    grad_value_low = fold_back(grad_value_ext).reshape(slots * piece_len, -1)
    grad_query_low = grad_query.reshape(slots * piece_len, -1)

    nt = ((1,), (1,))
    stacked = by_sets([grad_query_low, grad_key_low, grad_value_low])
    grad_normed_part = dot(stacked[:, :set_cols], qkv_mat[0], nt) + dot(
        stacked[:, set_cols:], qkv_mat[1], nt
    )
    small_part = ADAPTER_SCALE * dot(stacked, adapt_out_all, nt)
    small = small.reshape(slots * piece_len, 3 * RANK)
    outs = [
        ADAPTER_SCALE * dot(small[:, i * RANK : (i + 1) * RANK], g, ((0,), (0,)))
        for i, g in enumerate((grad_query_low, grad_key_low, grad_value_low))
    ]
    grad_normed_part = grad_normed_part.reshape(slots, piece_len, model_dim)
    small_part = small_part.reshape(slots, piece_len, 3 * RANK)
    grad_normed = own_half(grad_normed_part) + flip_core(
        other_half(grad_normed_part).astype(BF16)
    ).astype(F32)
    small_low = (own_half(small_part) + flip_core(other_half(small_part))).astype(BF16)
    small_low = small_low.reshape(-1, 3 * RANK)
    grad_normed = grad_normed + dot(small_low, adapt_in_all, nt).reshape(rows_float.shape)
    sum_in = dot(small_low, normed_share.reshape(-1, model_dim), ((0,), (0,)))
    grad_hidden = (grad_mid + rms_back(rows_float, gain_attn, grad_normed)).astype(BF16)

    by_rows = jnp.concatenate([sum_in, sum_o_out], axis=0)
    width = model_dim // (rows * seqs * heads)
    by_rows = by_rows.reshape(4 * RANK, rows, seqs, heads, width).transpose(3, 2, 1, 0, 4)
    for axis in ("head", "seq", "row"):
        by_rows = scatter_sum(by_rows, axis)
    in_parts = by_rows.reshape(4, RANK, width)

    def lanes_of(v):
        v = v.reshape(RANK, 2, -1, 2 * HD).transpose(1, 2, 0, 3)
        return v.reshape(2, -1, 2 * HD)

    packed = [lanes_of(v) for v in outs + [sum_o_in]] + [sum_q_feat, sum_k_feat]
    sizes = [v.shape[1] for v in packed]
    packed = jnp.concatenate(packed, axis=1)
    kept = lax.dynamic_index_in_dim(packed, x_place, 0, keepdims=False)
    sent = lax.dynamic_index_in_dim(packed, 1 - x_place, 0, keepdims=False)
    packed = kept + flip_x(sent.astype(BF16)).astype(F32)
    for axis in ("seq", "row"):
        packed = full_sum(packed, axis)
    cols, at = [], 0
    for size in sizes:
        cols.append(packed[at : at + size])
        at += size
    from_lanes = lambda v: v.reshape(-1, RANK, 2 * HD).transpose(1, 0, 2).reshape(RANK, -1)
    from_pairs = lambda v: v.reshape(-1, HD, 2, HD).transpose(0, 2, 1, 3).reshape(-1, HD, HD)
    cols = [from_lanes(v) for v in cols[:4]] + [from_pairs(v) for v in cols[4:]]
    cols[3] = cols[3].T

    return (
        block_out,
        grad_hidden,
        in_parts[0].T,
        cols[0],
        in_parts[1].T,
        cols[1],
        in_parts[2].T,
        cols[2],
        cols[3],
        in_parts[3],
        cols[4],
        cols[5],
    )


def solution(mesh):
    return jax.shard_map(
        local,
        mesh=mesh,
        in_specs=(
            P("row", ("seq", "head"), None),
            P("row", ("seq", "head"), None),
            P("row"),
            P("row", None),
            P(),
            P(),
            P(("row", "seq"), "head"),
            P(("row", "seq"), "head"),
            P(("row", "seq"), "head"),
            P("head", ("row", "seq")),
            P(("row", "seq"), "head"),
            P(("row", "seq"), "head"),
            P("head", ("row", "seq")),
            P(),
            P(None, "head"),
            P(),
            P(None, "head"),
            P(),
            P(None, "head"),
            P("head", None),
            P(),
            P("head", None, None),
            P("head", None, None),
        ),
        out_specs=(
            P("row", ("seq", "head"), None),
            P("row", ("seq", "head"), None),
            P(("row", "seq", "head"), None),
            P(None, "head"),
            P(("row", "seq", "head"), None),
            P(None, "head"),
            P(("row", "seq", "head"), None),
            P(None, "head"),
            P("head", None),
            P(None, ("row", "seq", "head")),
            P("head", None, None),
            P("head", None, None),
        ),
        check_vma=False,
    )
```

```python
import functools

import jax
import jax.numpy as jnp
from jax import lax
from jax.experimental import pallas as pl
from jax.experimental.pallas import tpu as pltpu
from jax.sharding import PartitionSpec as P

HD = 64
RANK = 8
WIN = 64
FF_CHUNKS = 4

NORM_EPS = 1e-05
ADAPTER_SCALE = 2.0
F32 = jnp.float32
NT = ((1,), (1,))
TN = ((0,), (0,))
BF16 = jnp.bfloat16


def shift(block, axis, distance):
    size = lax.axis_size(axis)
    return lax.ppermute(block, axis, [(i, (i + distance) % size) for i in range(size)])


def flip_core(block):
    return lax.ppermute(block, "head", [(i, i ^ 1) for i in range(lax.axis_size("head"))])


def flip_core_parts(block, parts):
    size = block.shape[0] // parts
    return jnp.concatenate(
        [flip_core(block[i * size : (i + 1) * size]) for i in range(parts)], axis=0
    )


def flip_x(block):
    return lax.ppermute(block, "head", [(i, i ^ 2) for i in range(lax.axis_size("head"))])


def kernel_call(
    kernel, args, after, *, grid, in_specs, out_specs, out_shape, name, prefetch=0, scratch=(), cost=None
):
    count = len(args)

    def body(*refs):
        kernel(*refs[:count], *refs[count + len(after) :])

    return pl.pallas_call(
        body,
        grid_spec=pltpu.PrefetchScalarGridSpec(
            num_scalar_prefetch=prefetch,
            grid=grid,
            in_specs=list(in_specs) + [pl.BlockSpec(memory_space=pl.ANY)] * len(after),
            out_specs=out_specs,
            scratch_shapes=list(scratch),
        ),
        out_shape=out_shape,
        compiler_params=pltpu.CompilerParams(vmem_limit_bytes=60 * 2**20),
        cost_estimate=cost and pl.CostEstimate(
            flops=cost.flops // 4, bytes_accessed=cost.bytes_accessed // 4, transcendentals=0
        ),
        name=name,
    )(*args, *after)


def copy_kernel(src_ref, dst_ref):
    dst_ref[...] = src_ref[...]


def hold(value, after):
    flat = value.reshape(-1, value.shape[-1])
    tile = min(256, flat.shape[0])
    block = pl.BlockSpec((tile, flat.shape[1]), lambda i: (i, 0))
    held = kernel_call(
        copy_kernel, [flat], after, grid=(flat.shape[0] // tile,), in_specs=[block], out_specs=block,
        out_shape=jax.ShapeDtypeStruct(flat.shape, flat.dtype), name="hold",
    )
    return held.reshape(value.shape)


def dot(a, b, dims=((1,), (0,))):
    return lax.dot_general(a, b, (dims, ((), ())), preferred_element_type=F32)


def tie(value, *after):
    return lax.optimization_barrier((value,) + after)[0]


def rms_scaled(values, gain_vec):
    return (
        values * lax.rsqrt(jnp.mean(values * values, axis=-1, keepdims=True) + NORM_EPS) * gain_vec
    )


def rms_back(values, gain_vec, grad_in):
    factor = lax.rsqrt(jnp.mean(values * values, axis=-1, keepdims=True) + NORM_EPS)
    scaled = gain_vec * grad_in
    return factor * scaled - values * factor**3 * jnp.mean(values * scaled, axis=-1, keepdims=True)


def scatter_sum(parts, axis):
    size, place = lax.axis_size(axis), lax.axis_index(axis)
    total = lax.dynamic_index_in_dim(parts, place, 0, keepdims=False)
    for k in range(1, size):
        away = lax.dynamic_index_in_dim(parts, lax.rem(place + k, size), 0, keepdims=False)
        total = total + shift(away, axis, k)
    return total


def full_sum(part, axis):
    size = lax.axis_size(axis)
    step = 1
    while step < size:
        sent = part.astype(BF16)
        got = lax.ppermute(sent, axis, [(i, i ^ step) for i in range(size)])
        part = sent.astype(F32) + got.astype(F32)
        step *= 2
    return part


def gather_plan(rows, seqs, weights):
    free = {"row": 0.0, "seq": 0.0, "x": 0.0}
    running = []
    plan = []

    def begin(now, starts):
        for t in starts:
            w, link = t[0], t[1]
            end = max(now, free[link]) + weights[w][0]
            free[link] = end
            running.append((end, len(plan), len(running), t))
        return starts

    def spread(w, k, l):
        starts = []
        row_first = weights[w][2]
        if (l == 0 or not row_first) and k + 1 < rows:
            starts.append((w, "row", k + 1, l))
        if (k == 0 or row_first) and l + 1 < seqs:
            starts.append((w, "seq", k, l + 1))
        if weights[w][1]:
            starts.append((w, "x", k, l))
        return starts

    first = [t for w in range(len(weights)) if weights[w][3] == 0 for t in spread(w, 0, 0)]
    plan.append((None, begin(0.0, first)))
    done = 0
    while running:
        event = min(running)
        running.remove(event)
        now, t = event[0], event[3]
        done += 1
        starts = [] if t[1] == "x" else spread(t[0], t[2], t[3])
        for w in range(len(weights)):
            if weights[w][3] == done:
                starts = starts + spread(w, 0, 0)
        plan.append((t, begin(now, starts)))
    return plan


def gather_kernel(plan, rows, seqs, parts, over_x, small_count, *refs):
    count = len(over_x)
    inputs, refs = refs[: count + small_count + 2], refs[count + small_count + 2 :]
    shards, smalls = inputs[:count], inputs[count : count + small_count]
    hidden, cot = inputs[count + small_count :]
    wholes, refs = refs[:count], refs[count:]
    small_outs, refs = refs[:small_count], refs[small_count:]
    hidden_out, cot_mine, cot_away = refs[:3]
    send_sem, recv_sem, copy_sem, more_send, more_recv = refs[3:]
    row, seq, head = lax.axis_index("row"), lax.axis_index("seq"), lax.axis_index("head")
    x_place = head // 2
    across = {"head": lax.rem(head + 2, 4)}
    partner = {"head": head + 1 - 2 * lax.rem(head, 2)}
    away = {
        "row": {"row": lax.rem(row + 1, rows)},
        "seq": {"seq": lax.rem(seq + 1, seqs)},
        "x": across,
    }
    barrier = pltpu.get_barrier_semaphore()
    sources = (
        {"row": lax.rem(row + rows - 1, rows)},
        {"seq": lax.rem(seq + seqs - 1, seqs)},
        across,
        partner,
    )
    for source in sources:
        pl.semaphore_signal(
            barrier, inc=1, device_id=source, device_id_type=pl.DeviceIdType.MESH
        )
    pl.semaphore_wait(barrier, len(sources))

    def slot(p, k, l):
        w, columns = parts[p][0], pl.ds(*parts[p][1])
        depth = shards[w].shape[0]
        place = lax.rem(row - k + rows, rows) * seqs + lax.rem(seq - l + seqs, seqs)
        at = pl.ds(pl.multiple_of(place * depth, depth), depth)
        return wholes[w].at[x_place, at, columns] if over_x[w] else wholes[w].at[at, columns]

    number = {}
    last_x = 0
    for i, (event, starts) in enumerate(plan):
        for t in starts:
            number[t] = len(number)
            if t[1] == "x":
                last_x = i

    def remote(src, dst, send, recv, device):
        return pltpu.make_async_remote_copy(
            src_ref=src, dst_ref=dst, send_sem=send, recv_sem=recv, device_id=device,
            device_id_type=pl.DeviceIdType.MESH,
        )

    def transfer(t):
        w, link, k, l = t
        source = {"row": (k - 1, l), "seq": (k, l - 1), "x": (k, l)}[link]
        dst = slot(w, *source)
        n = number[t]
        src = shards[parts[w][0]].at[:, pl.ds(*parts[w][1])] if source == (0, 0) else dst
        return remote(src, dst, send_sem.at[n], recv_sem.at[n], away[link])

    def more(i, src, dst, device):
        return remote(src, dst, more_send.at[i], more_recv.at[i], device)

    early = [more(i, a, b, across) for i, (a, b) in enumerate(zip(smalls, small_outs))]
    early.append(more(small_count, hidden, hidden_out, partner))
    early.append(more(small_count + 1, cot, cot_mine.at[1], partner))
    cot_x = more(small_count + 2, cot, cot_away.at[0], across)
    cot_last = more(small_count + 3, cot_away.at[0], cot_away.at[1], partner)
    own = [
        pltpu.make_async_copy(
            shards[w].at[:, pl.ds(*columns)], slot(p, 0, 0), copy_sem.at[p]
        )
        for p, (w, columns) in enumerate(parts)
    ] + [pltpu.make_async_copy(cot, cot_mine.at[0], copy_sem.at[len(parts)])]
    for i, (event, starts) in enumerate(plan):
        if event is not None:
            transfer(event).wait_recv()
        for t in starts:
            transfer(t).start()
        if event is None:
            for copy in early + own:
                copy.start()
        if i == last_x:
            cot_x.start()
    cot_x.wait()
    cot_last.start()
    for t in number:
        transfer(t).wait_send()
    for copy in early + own + [cot_last]:
        copy.wait()


def gather(shards, over_x, pieces, smalls, hidden, cot):
    rows, seqs = lax.axis_size("row"), lax.axis_size("seq")
    plan = gather_plan(
        rows,
        seqs,
        [(float(shards[w].shape[0] * c[1]), over_x[w], first, later) for w, c, first, later in pieces],
    )
    parts = [(w, c) for w, c, _, _ in pieces]
    total = sum(len(starts) for _, starts in plan)
    shapes = []
    for shard, x in zip(shards, over_x):
        depth, width = shard.shape
        whole = (rows * seqs * depth, width)
        shapes.append(jax.ShapeDtypeStruct(((2,) + whole) if x else whole, shard.dtype))
    same = lambda v: jax.ShapeDtypeStruct(v.shape, v.dtype)
    twice = jax.ShapeDtypeStruct((2,) + cot.shape, cot.dtype)
    shapes += [same(v) for v in smalls] + [same(hidden), twice, twice]
    more = len(smalls) + 4
    place = pl.BlockSpec(memory_space=pl.ANY)
    outs = pl.pallas_call(
        functools.partial(gather_kernel, plan, rows, seqs, parts, over_x, len(smalls)),
        out_shape=shapes,
        in_specs=[place] * (len(shards) + len(smalls) + 2),
        out_specs=[place] * len(shapes),
        scratch_shapes=[
            pltpu.SemaphoreType.DMA((total,)),
            pltpu.SemaphoreType.DMA((total,)),
            pltpu.SemaphoreType.DMA((len(parts) + 1,)),
            pltpu.SemaphoreType.DMA((more,)),
            pltpu.SemaphoreType.DMA((more,)),
        ],
        compiler_params=pltpu.CompilerParams(collective_id=0, has_side_effects=True),
        name="gather",
    )(*shards, *smalls, hidden, cot)
    n = len(shards)
    return outs[:n], outs[n : n + len(smalls)], outs[-3:]


def ffn_kernel(chunks, before, share_len, slots, live_ref, x_ref, more_ref, cot_ref, *refs):
    weights, refs = refs[:chunks], refs[chunks:]
    earlier, refs = refs[: 4 * before], refs[4 * before :]
    outs, (held, sem) = refs[:4], refs[4:]
    step = pl.program_id(0)
    tile = x_ref.shape[0]
    width = held.shape[2] // 3
    copies = [pltpu.make_async_copy(weights[c], held.at[c], sem.at[c]) for c in range(chunks)]

    @pl.when(step == 0)
    def _():
        for copy in copies:
            copy.start()

    first = step < pl.num_programs(0) // 2
    live = (lax.rem(step * tile // share_len, slots) < live_ref[0]).astype(F32)
    x, cot = jnp.where(first, x_ref[...], more_ref[...]), cot_ref[...]
    sums = [None, None]
    if before:
        sums = [jnp.where(first, earlier[i][...], earlier[i + 1][...]).astype(F32) for i in (0, 2)]
    for c in range(chunks):

        @pl.when(step == 0)
        def _():
            copies[c].wait()

        gate = dot(x, held[c, :, :width])
        up = dot(x, held[c, :, width : 2 * width])
        gm = dot(cot, held[c, :, 2 * width :]) * live
        sig = jax.nn.sigmoid(gate)
        silu = gate * sig
        mixed = (silu * up).astype(BF16)
        g_gate = (gm * up * (sig + silu * (1.0 - sig))).astype(BF16)
        g_up = (gm * silu).astype(BF16)
        parts = (
            dot(jnp.concatenate([g_gate, g_up], axis=1), held[c, :, : 2 * width], NT),
            dot(mixed, held[c, :, 2 * width :], NT),
        )
        sums = [p if t is None else t + p for t, p in zip(sums, parts)]

    @pl.when(first)
    def _():
        outs[0][...] = sums[0].astype(BF16)
        outs[2][...] = sums[1].astype(BF16)

    @pl.when(jnp.logical_not(first))
    def _():
        outs[1][...] = sums[0].astype(BF16)
        outs[3][...] = sums[1].astype(BF16)


def ffn(x, cot, weights, live_rows, share_len, slots, before=(), after=()):
    tokens, depth = cot.shape
    chunks = len(weights)
    width = weights[0].shape[1] // 3
    tile = min(256, share_len)
    half = tokens // tile // 2
    lower = pl.BlockSpec((tile, depth), lambda i, *_: (jnp.minimum(i, half - 1), 0))
    upper = pl.BlockSpec((tile, depth), lambda i, *_: (jnp.maximum(i - half, 0), 0))
    out = jax.ShapeDtypeStruct((tokens // 2, depth), BF16)
    return kernel_call(
        functools.partial(ffn_kernel, chunks, len(before) // 4, share_len, slots),
        [live_rows, x[0], x[1], cot, *weights, *before],
        after,
        prefetch=1,
        grid=(tokens // tile,),
        in_specs=[lower, upper, pl.BlockSpec((tile, depth), lambda i, *_: (i, 0))]
        + [pl.BlockSpec(memory_space=pl.ANY)] * chunks
        + [lower, upper] * (len(before) // 2),
        out_specs=[lower, upper, lower, upper],
        out_shape=[out] * 4,
        scratch=[
            pltpu.VMEM((chunks, depth, 3 * width), BF16),
            pltpu.SemaphoreType.DMA((chunks,)),
        ],
        cost=pl.CostEstimate(
            flops=12 * tokens * depth * width * chunks,
            bytes_accessed=8 * tokens * depth + 6 * depth * width * chunks,
            transcendentals=0,
        ),
        name="ffn",
    )


def lower_lanes(like):
    return lax.broadcasted_iota(jnp.int32, like.shape, 1) < HD


def half_ones():
    r = lax.broadcasted_iota(jnp.int32, (2 * HD, 2 * HD), 0) // HD
    c = lax.broadcasted_iota(jnp.int32, (2 * HD, 2 * HD), 1) // HD
    return (r == c).astype(F32).astype(BF16)


def swap(v):
    return pltpu.roll(v, HD, 1)


def features(x, feat):
    logit = dot(x, feat)
    low = lower_lanes(logit)
    top = jnp.max(jnp.where(low, logit, -jnp.inf), axis=1, keepdims=True)
    bottom = jnp.max(jnp.where(low, -jnp.inf, logit), axis=1, keepdims=True)
    e = jnp.exp(logit - jnp.where(low, top, bottom))
    return e / dot(e.astype(BF16), half_ones())


def features_back(phi, grad):
    p = phi.astype(F32)
    prod = p * grad
    low = lower_lanes(prod)
    first = jnp.sum(jnp.where(low, prod, 0.0), axis=1, keepdims=True)
    second = jnp.sum(jnp.where(low, 0.0, prod), axis=1, keepdims=True)
    g = prod - p * jnp.where(low, first, second)
    return (g - swap(g)).astype(BF16)[:, :HD]


def values_ones(kv):
    kv = kv.astype(F32)
    return jnp.where(lower_lanes(kv), swap(kv), 1.0).astype(BF16)


def key_state_kernel(ends_ref, kv_ref, feat_ref, kdoc_ref, phi_ref, state_ref):
    r = pl.program_id(0)
    kv = kv_ref[0, 0]
    body = kv.shape[0] - WIN
    phi = features(kv[:, :HD], feat_ref[0]).astype(BF16)
    phi_ref[0, 0] = phi
    last = ends_ref[r, body // WIN]
    held = jnp.where(kdoc_ref[0, :body] == last, phi[:body].astype(F32), 0.0).astype(BF16)
    state_ref[0, 0] = dot(held, values_ones(kv[:body]), TN).astype(BF16)


def key_state(ends, kv, feat, kdoc, after=()):
    slots, groups, ext, _ = kv.shape
    block = lambda r, g, *_: (r, g, 0, 0)
    return kernel_call(
        key_state_kernel,
        [ends, kv, feat, kdoc],
        after,
        prefetch=1,
        grid=(slots, groups),
        in_specs=[
            pl.BlockSpec((1, 1, ext, 2 * HD), block),
            pl.BlockSpec((1, HD, 2 * HD), lambda r, g, *_: (g, 0, 0)),
            pl.BlockSpec((1, ext, 2 * HD), lambda r, g, *_: (r, 0, 0)),
        ],
        out_specs=[
            pl.BlockSpec((1, 1, ext, 2 * HD), block),
            pl.BlockSpec((1, 1, 2 * HD, 2 * HD), block),
        ],
        out_shape=[
            jax.ShapeDtypeStruct((slots, groups, ext, 2 * HD), BF16),
            jax.ShapeDtypeStruct((slots, groups, 2 * HD, 2 * HD), BF16),
        ],
        name="key_state",
    )


def block_masks(b, qdoc_ref, pdoc_ref):
    rows = slice(WIN * b, WIN * b + WIN)
    same = qdoc_ref[0, rows] == pdoc_ref[0, b : b + 1]
    row = lax.broadcasted_iota(jnp.int32, (WIN, 2 * WIN), 0)
    col = lax.broadcasted_iota(jnp.int32, (WIN, 2 * WIN), 1)
    linear = same & (col <= row)
    window = same & (col > row) & (col <= row + WIN)
    return window, linear


def next_state(b, ends_ref, r, state, phi_ref, vx_ref, kdoc_ref):
    rows = slice(WIN * (b - 1), WIN * b)
    keep = (ends_ref[r, b] == ends_ref[r, b - 1]).astype(F32)
    held = jnp.where(
        kdoc_ref[0, rows] == ends_ref[r, b], phi_ref[0, 0, rows].astype(F32), 0.0
    ).astype(BF16)
    return state * keep + dot(held, vx_ref[rows], TN)


def block_forward(b, ends_ref, r, q_ref, kv_ref, phi_ref, phiq_ref, vx_ref, state_low, qdoc_ref, pdoc_ref):
    heads = q_ref.shape[1]
    rows, pair = slice(WIN * b, WIN * b + WIN), slice(WIN * b, WIN * b + 2 * WIN)
    window, linear = block_masks(b, qdoc_ref, pdoc_ref)
    valid = qdoc_ref[0, rows] == ends_ref[r, b]
    query = jnp.concatenate([q_ref[0, h, rows] for h in range(heads)], axis=0)
    phi_query = jnp.concatenate([phiq_ref[0, h, rows] for h in range(heads)], axis=0)
    key = kv_ref[0, 0, pair, :HD]
    phi_key = phi_ref[0, 0, pair]
    score = dot(query, key, NT) * (HD**-0.5)
    lin = dot(phi_query, phi_key, NT)
    part = lambda v, h: v[WIN * h : WIN * h + WIN]
    exps = [jnp.where(window, jnp.exp(part(score, h)), 0.0) for h in range(heads)]
    weight = jnp.concatenate(
        [jnp.where(linear, part(lin, h), exps[h]).astype(BF16) for h in range(heads)], axis=0
    )
    phi_valid = jnp.concatenate(
        [jnp.where(valid, part(phi_query, h).astype(F32), 0.0).astype(BF16) for h in range(heads)],
        axis=0,
    )
    both = dot(weight, vx_ref[pair]) + dot(phi_valid, state_low)
    denominator = jnp.where(lower_lanes(both), swap(both), both)
    return (query, phi_query, phi_valid, key, phi_key, exps, weight, both / denominator, denominator,
            window, linear, valid)


def attend_kernel(
    ends_ref, q_ref, kv_ref, phi_ref, feat_ref, carry_ref, qdoc_ref, kdoc_ref, pdoc_ref,
    attn_ref, phiq_ref, vx_ref,
):
    r = pl.program_id(0)
    heads, length = q_ref.shape[1], q_ref.shape[2]
    vx_ref[...] = values_ones(kv_ref[0, 0])
    for h in range(heads):
        phiq_ref[0, h] = features(q_ref[0, h], feat_ref[h]).astype(BF16)
    state = carry_ref[0, 0]
    for b in range(length // WIN):
        if b:
            state = next_state(b, ends_ref, r, state, phi_ref, vx_ref, kdoc_ref)
        out = block_forward(
            b, ends_ref, r, q_ref, kv_ref, phi_ref, phiq_ref, vx_ref, state.astype(BF16), qdoc_ref,
            pdoc_ref,
        )
        attn = out[7]
        low = lower_lanes(attn[:WIN])
        for h in range(0, heads, 2):
            first, second = attn[WIN * h : WIN * h + WIN], attn[WIN * h + WIN : WIN * h + 2 * WIN]
            attn_ref[0, WIN * b : WIN * b + WIN, HD * h : HD * h + 2 * HD] = jnp.where(
                low, first, swap(second)
            ).astype(BF16)


def attention_specs(slots, groups, heads, length):
    ext = length + WIN
    four = lambda r, g, *_: (r, g, 0, 0)
    docs = lambda r, g, *_: (r, 0, 0)
    return dict(
        q=pl.BlockSpec((1, heads, length, HD), four),
        kv=pl.BlockSpec((1, 1, ext, 2 * HD), four),
        phiq=pl.BlockSpec((1, heads, length, 2 * HD), four),
        feat=pl.BlockSpec((heads, HD, 2 * HD), lambda r, g, *_: (g, 0, 0)),
        state=pl.BlockSpec((1, 1, 2 * HD, 2 * HD), four),
        qdoc=pl.BlockSpec((1, length, 2 * HD), docs),
        kdoc=pl.BlockSpec((1, ext, 2 * HD), docs),
        pdoc=pl.BlockSpec((1, length // WIN, 2 * HD), docs),
        tokens=pl.BlockSpec((1, length, heads * HD), lambda r, g, *_: (r, 0, g)),
        fgrad=pl.BlockSpec((1, heads // 2, HD, 2 * HD), four),
    )


def attend(ends, q, kv, phi, feat, carry, qdoc, kdoc, pdoc, after=()):
    slots, all_heads, length, _ = q.shape
    groups = kv.shape[1]
    heads = all_heads // groups
    sp = attention_specs(slots, groups, heads, length)
    return kernel_call(
        attend_kernel,
        [ends, q, kv, phi, feat, carry, qdoc, kdoc, pdoc],
        after,
        prefetch=1,
        grid=(slots, groups),
        in_specs=[sp[n] for n in ("q", "kv", "kv", "feat", "state", "qdoc", "kdoc", "pdoc")],
        out_specs=[sp["tokens"], sp["phiq"]],
        scratch=[pltpu.VMEM((length + WIN, 2 * HD), BF16)],
        out_shape=[
            jax.ShapeDtypeStruct((slots, length, all_heads * HD), BF16),
            jax.ShapeDtypeStruct((slots, all_heads, length, 2 * HD), BF16),
        ],
        name="attend",
    )


def attend_back_kernel(
    ends_ref, q_ref, kv_ref, phi_ref, phiq_ref, feat_ref, carry_ref, qdoc_ref, kdoc_ref, pdoc_ref,
    g_ref, gq_ref, gfeat_ref, gphi_ref, gkv_ref, gcarry_ref, vx_ref, gstate_ref, gphiq_ref, gk_ref,
    gv_ref, gqs_ref, gl_ref,
):
    r = pl.program_id(0)
    heads, length = q_ref.shape[1], q_ref.shape[2]
    blocks = length // WIN
    vx_ref[...] = values_ones(kv_ref[0, 0])
    gphi_ref[...] = jnp.zeros_like(gphi_ref)
    gk_ref[...] = jnp.zeros_like(gk_ref)
    gv_ref[...] = jnp.zeros_like(gv_ref)
    scale = HD**-0.5
    state = carry_ref[0, 0]
    for b in range(blocks):
        rows, pair = slice(WIN * b, WIN * b + WIN), slice(WIN * b, WIN * b + 2 * WIN)
        if b:
            state = next_state(b, ends_ref, r, state, phi_ref, vx_ref, kdoc_ref)
        state_low = state.astype(BF16)
        (query, phi_query, phi_valid, key, phi_key, exps, weight, attn, denominator, window, linear,
         valid) = block_forward(
            b, ends_ref, r, q_ref, kv_ref, phi_ref, phiq_ref, vx_ref, state_low, qdoc_ref, pdoc_ref
        )
        grads = []
        for h in range(0, heads, 2):
            g = g_ref[0, rows, HD * h : HD * h + 2 * HD].astype(F32)
            grads += [g, swap(g)]
        grad = jnp.concatenate(grads, axis=0)
        low = lower_lanes(grad)
        grad = jnp.where(low, grad, 0.0)
        g_denom = -jnp.sum(grad * attn, axis=1, keepdims=True)
        gx = (jnp.where(low, grad, g_denom * (1.0 / HD)) / denominator).astype(BF16)
        g_weight = dot(gx, vx_ref[pair], NT)
        part = lambda v, h: v[WIN * h : WIN * h + WIN]
        g_score = jnp.concatenate(
            [(exps[h] * part(g_weight, h)).astype(BF16) for h in range(heads)], axis=0
        )
        g_lin = jnp.concatenate(
            [jnp.where(linear, part(g_weight, h), 0.0).astype(BF16) for h in range(heads)], axis=0
        )
        g_query = dot(g_score, key) * scale
        gk_ref[pair] += dot(g_score, query, TN) * scale
        gv_ref[pair] += dot(weight, gx, TN)
        gphi_ref[0, 0, pair] += dot(g_lin, phi_query, TN)
        from_lin = dot(g_lin, phi_key)
        from_state = dot(gx, state_low, NT)
        gstate_ref[b] = dot(phi_valid, gx, TN)
        for h in range(heads):
            gphiq_ref[h, rows] = part(from_lin, h) + jnp.where(valid, part(from_state, h), 0.0)
            gqs_ref[h, rows] = part(g_query, h)
    for h in range(heads):
        g_logit = features_back(phiq_ref[0, h], gphiq_ref[h])
        gl_ref[h] = g_logit
        gqs_ref[h] += dot(g_logit, feat_ref[h][:, :HD], NT)
    gq_ref[0] = jnp.concatenate([gqs_ref[h] for h in range(heads)], axis=1).astype(BF16)
    for h in range(0, heads, 2):
        gfeat_ref[0, h // 2] = jnp.concatenate(
            [dot(q_ref[0, i], gl_ref[i], TN) for i in (h, h + 1)], axis=1
        )
    later = gstate_ref[blocks - 1]
    for b in range(blocks - 1, 0, -1):
        rows = slice(WIN * (b - 1), WIN * b)
        low_state = later.astype(BF16)
        mask = kdoc_ref[0, rows] == ends_ref[r, b]
        gphi_ref[0, 0, rows] += jnp.where(mask, dot(vx_ref[rows], low_state, NT), 0.0)
        gv_ref[rows] += jnp.where(mask, dot(phi_ref[0, 0, rows], low_state), 0.0)
        keep = (ends_ref[r, b] == ends_ref[r, b - 1]).astype(F32)
        later = gstate_ref[b - 1] + keep * later
    gcarry_ref[0, 0] = later.astype(BF16)
    gv = gv_ref[...]
    gkv_ref[0, 0, :, :HD] = gk_ref[...]
    gkv_ref[0, 0, :, HD:] = gv[:, :HD]


def attend_back(ends, q, kv, phi, phiq, feat, carry, qdoc, kdoc, pdoc, g, after=()):
    slots, all_heads, length, _ = q.shape
    groups = kv.shape[1]
    heads = all_heads // groups
    ext = length + WIN
    sp = attention_specs(slots, groups, heads, length)
    return kernel_call(
        attend_back_kernel,
        [ends, q, kv, phi, phiq, feat, carry, qdoc, kdoc, pdoc, g],
        after,
        prefetch=1,
        grid=(slots, groups),
        in_specs=[
            sp[n]
            for n in ("q", "kv", "kv", "phiq", "feat", "state", "qdoc", "kdoc", "pdoc", "tokens")
        ],
        out_specs=[sp["tokens"], sp["fgrad"], sp["kv"], sp["kv"], sp["state"]],
        scratch=[
            pltpu.VMEM((ext, 2 * HD), BF16),
            pltpu.VMEM((length // WIN, 2 * HD, 2 * HD), F32),
            pltpu.VMEM((heads, length, 2 * HD), F32),
            pltpu.VMEM((ext, HD), F32),
            pltpu.VMEM((ext, 2 * HD), F32),
            pltpu.VMEM((heads, length, HD), F32),
            pltpu.VMEM((heads, length, HD), BF16),
        ],
        out_shape=[
            jax.ShapeDtypeStruct((slots, length, all_heads * HD), BF16),
            jax.ShapeDtypeStruct((slots, all_heads // 2, HD, 2 * HD), F32),
            jax.ShapeDtypeStruct((slots, groups, ext, 2 * HD), F32),
            jax.ShapeDtypeStruct((slots, groups, ext, 2 * HD), F32),
            jax.ShapeDtypeStruct((slots, groups, 2 * HD, 2 * HD), BF16),
        ],
        name="attend_back",
    )


def key_back_kernel(
    ends_ref, kv_ref, phi_ref, feat_ref, later_ref, kdoc_ref, gphi_ref, gkv_ref,
    body_ref, edge_ref, gfeat_ref,
):
    r = pl.program_id(0)
    ext = kv_ref.shape[2]
    body = ext - WIN
    last = ends_ref[r, body // WIN]
    mask = kdoc_ref[0, :body] == last
    keys, vals, feats = [], [], []
    for i in range(2):
        kv, phi = kv_ref[0, i], phi_ref[0, i]
        later = later_ref[0, i].astype(BF16)
        more_phi = jnp.where(mask, dot(values_ones(kv[:body]), later, NT), 0.0)
        more_v = jnp.where(mask, dot(phi[:body], later), 0.0)
        tail = jnp.zeros((WIN, 2 * HD), F32)
        g_phi = gphi_ref[0, i] + jnp.concatenate([more_phi, tail], axis=0)
        g_logit = features_back(phi, g_phi)
        gkv = gkv_ref[0, i]
        keys.append(gkv[:, :HD] + dot(g_logit, feat_ref[i][:, :HD], NT))
        vals.append(gkv[:, HD:] + jnp.concatenate([more_v, tail], axis=0)[:, :HD])
        feats.append(dot(kv[:, :HD], g_logit, TN))
    gfeat_ref[0, 0] = jnp.concatenate(feats, axis=1)
    both = jnp.concatenate(keys + vals, axis=1)
    body_ref[0, 0] = both[WIN:]
    edge_ref[0, 0] = both[:WIN].astype(BF16)


def key_back(ends, kv, phi, feat, later, kdoc, gphi, gkv, after=()):
    slots, groups, ext, _ = kv.shape
    four = lambda r, s, *_: (r, s, 0, 0)
    wide = pl.BlockSpec((1, 2, ext, 2 * HD), four)
    body = pl.BlockSpec((1, 1, ext - WIN, 4 * HD), four)
    edge = pl.BlockSpec((1, 1, WIN, 4 * HD), four)
    sets = groups // 2
    return kernel_call(
        key_back_kernel,
        [ends, kv, phi, feat, later, kdoc, gphi, gkv],
        after,
        prefetch=1,
        grid=(slots, groups // 2),
        in_specs=[
            wide,
            wide,
            pl.BlockSpec((2, HD, 2 * HD), lambda r, s, *_: (s, 0, 0)),
            pl.BlockSpec((1, 2, 2 * HD, 2 * HD), four),
            pl.BlockSpec((1, ext, 2 * HD), lambda r, s, *_: (r, 0, 0)),
            wide,
            wide,
        ],
        out_specs=[body, edge, pl.BlockSpec((1, 1, HD, 2 * HD), four)],
        out_shape=[
            jax.ShapeDtypeStruct((slots, sets, ext - WIN, 4 * HD), F32),
            jax.ShapeDtypeStruct((slots, sets, WIN, 4 * HD), BF16),
            jax.ShapeDtypeStruct((slots, sets, HD, 2 * HD), F32),
        ],
        name="key_back",
    )


LOW = 128


def normalize(values, gain):
    scale = lax.rsqrt(jnp.mean(values * values, axis=-1, keepdims=True) + NORM_EPS)
    return (values * scale * gain).astype(BF16)


def project_kernel(
    sets, q_cols, k_cols, shares, core_ref, own_ref, other_ref, gain_ref, w_ref, a_ref, b_ref, q_ref,
    kv_ref, small_ref
):
    own = pl.program_id(1) // shares == core_ref[0]
    x = normalize(jnp.where(own, own_ref[0], other_ref[0]).astype(F32), gain_ref[...])
    width = q_cols + 2 * k_cols
    small = dot(x, a_ref[...]).astype(BF16)
    small_ref[0] = small
    heads, groups = q_cols // HD, k_cols // HD
    for s in range(sets):
        cols = slice(s * width, (s + 1) * width)
        full = dot(x, w_ref[s]) + ADAPTER_SCALE * dot(small, b_ref[:, cols])
        for h in range(heads):
            q_ref[0, s * heads + h] = full[:, h * HD : h * HD + HD].astype(BF16)
        for g in range(0, groups, 2):
            k = full[:, q_cols + g * HD : q_cols + g * HD + 2 * HD]
            start = q_cols + k_cols + g * HD
            v = full[:, start : start + 2 * HD]
            low = lower_lanes(k)
            kv_ref[0, s * groups + g] = jnp.where(low, k, swap(v)).astype(BF16)
            kv_ref[0, s * groups + g + 1] = jnp.where(low, swap(k), v).astype(BF16)


def project(core, own, other, gain, w, a, b, q_cols, k_cols, after=()):
    slots, share, depth = own.shape
    length = 2 * share
    sets = w.shape[0]
    heads, groups = sets * q_cols // HD, sets * k_cols // HD
    tile = min(256, share)
    shares = share // tile
    token = pl.BlockSpec((1, tile, depth), lambda r, i, *_: (r, lax.rem(i, shares), 0))
    return kernel_call(
        functools.partial(project_kernel, sets, q_cols, k_cols, shares),
        [core, own, other, gain, w, a, b],
        after,
        prefetch=1,
        grid=(slots, length // tile),
        in_specs=[
            token,
            token,
            pl.BlockSpec(gain.shape, lambda r, i, *_: (0, 0)),
            pl.BlockSpec(w.shape, lambda r, i, *_: (0, 0, 0)),
            pl.BlockSpec(a.shape, lambda r, i, *_: (0, 0)),
            pl.BlockSpec(b.shape, lambda r, i, *_: (0, 0)),
        ],
        out_specs=[
            pl.BlockSpec((1, heads, tile, HD), lambda r, i, *_: (r, 0, i, 0)),
            pl.BlockSpec((1, groups, tile, 2 * HD), lambda r, i, *_: (r, 0, i, 0)),
            pl.BlockSpec((1, tile, LOW), lambda r, i, *_: (r, i, 0)),
        ],
        out_shape=[
            jax.ShapeDtypeStruct((slots, heads, length, HD), BF16),
            jax.ShapeDtypeStruct((slots, groups, length, 2 * HD), BF16),
            jax.ShapeDtypeStruct((slots, length, LOW), BF16),
        ],
        cost=pl.CostEstimate(
            flops=2 * slots * length * w.size,
            bytes_accessed=2 * (slots * length * depth + w.size),
            transcendentals=0,
        ),
        name="project",
    )


def halves(share, tile):
    shares = share // tile
    own = lambda r, i, core: (r, core[0] * shares + i, 0)
    other = lambda r, i, core: (r, (1 - core[0]) * shares + i, 0)
    return own, other


def out_project_kernel(core_ref, own_ref, other_ref, w_ref, low_ref, keep_ref, away_ref):
    depth = w_ref.shape[1]
    half = w_ref.shape[2]
    for src, dst in ((own_ref, keep_ref), (other_ref, away_ref)):
        attn = src[0]
        full = dot(attn[:, :half], w_ref[0], NT) + dot(attn[:, half:], w_ref[1], NT)
        dst[0, :, :depth] = full.astype(BF16)
        dst[0, :, depth:] = dot(attn, low_ref[...]).astype(BF16)


def out_project(core, attn, w, low, share):
    slots, length, width = attn.shape
    depth = w.shape[1]
    tile = min(256, share)
    own, other = halves(share, tile)
    out = pl.BlockSpec((1, tile, depth + LOW), lambda r, i, *_: (r, i, 0))
    shape = jax.ShapeDtypeStruct((slots, share, depth + LOW), BF16)
    return kernel_call(
        out_project_kernel,
        [core, attn, attn, w, low],
        (),
        prefetch=1,
        grid=(slots, share // tile),
        in_specs=[
            pl.BlockSpec((1, tile, width), own),
            pl.BlockSpec((1, tile, width), other),
            pl.BlockSpec(w.shape, lambda r, i, *_: (0, 0, 0)),
            pl.BlockSpec(low.shape, lambda r, i, *_: (0, 0)),
        ],
        out_specs=[out, out],
        out_shape=[shape, shape],
        name="out_project",
    )


def middle_kernel(hidden_ref, keep_ref, got_ref, second_ref, gain_ref, mid_ref, normed_ref, low_ref):
    depth = hidden_ref.shape[1]
    total = keep_ref[...].astype(F32) + got_ref[...].astype(F32)
    low = total[:, depth:].astype(BF16)
    low_ref[...] = low
    mid = hidden_ref[...].astype(F32) + total[:, :depth]
    mid = mid + ADAPTER_SCALE * dot(low, second_ref[...])
    mid_ref[...] = mid
    normed_ref[...] = normalize(mid, gain_ref[...])


def tokens_call(kernel, tiled, whole, outs, name, prefetch=(), sums=()):
    tokens = tiled[0].shape[0]
    tile = min(256, tokens)
    rows = lambda v: pl.BlockSpec((tile, v.shape[1]), lambda i, *_: (i, 0))
    full = lambda v: pl.BlockSpec(v.shape, lambda i, *_: (0, 0))
    shapes = [jax.ShapeDtypeStruct((tokens, width), kind) for width, kind in outs]
    totals = [jax.ShapeDtypeStruct(v, F32) for v in sums]
    return kernel_call(
        kernel,
        [*prefetch, *tiled, *whole],
        (),
        prefetch=len(prefetch),
        grid=(tokens // tile,),
        in_specs=[rows(v) for v in tiled] + [full(v) for v in whole],
        out_specs=[rows(v) for v in shapes] + [full(v) for v in totals],
        out_shape=shapes + totals,
        name=name,
    )


def norm_back(values, gain, grad):
    scale = lax.rsqrt(jnp.mean(values * values, axis=-1, keepdims=True) + NORM_EPS)
    scaled = gain * grad
    shared = scale * scale * scale * jnp.mean(values * scaled, axis=-1, keepdims=True)
    return scale, scale * scaled - values * shared


def sum_kernel(*refs):
    refs[-1][...] = sum(r[...].astype(F32) for r in refs[:-1]).astype(BF16)


def branch_kernel(slot_len, live_ref, mid_ref, a_ref, b_ref, c_ref, cot_ref, gain_ref, grad_ref, low_ref):
    grad = a_ref[...].astype(F32) + b_ref[...].astype(F32) + c_ref[...].astype(F32)
    tile = mid_ref.shape[0]
    token = pl.program_id(0) * tile + lax.broadcasted_iota(jnp.int32, (tile, 1), 0)
    live = token < live_ref[0] * slot_len
    cot = jnp.where(live, cot_ref[...].astype(F32), 0.0)
    total = cot + norm_back(mid_ref[...], gain_ref[...], grad)[1]
    grad_ref[...] = total
    low_ref[...] = total.astype(BF16)


def attn_grad_kernel(
    shares, core_ref, own_ref, other_ref, attn_ref, w_ref, second_ref, first_ref, grad_ref, sum_ref
):
    own = pl.program_id(1) // shares == core_ref[0]
    x = jnp.where(own, own_ref[0], other_ref[0])
    low = (ADAPTER_SCALE * dot(x, second_ref[...], NT)).astype(BF16)
    half = w_ref.shape[2]
    first = first_ref[...]
    for s in range(2):
        cols = slice(s * half, (s + 1) * half)
        grad_ref[0, :, cols] = (dot(x, w_ref[s]) + dot(low, first[cols], NT)).astype(BF16)

    @pl.when((pl.program_id(0) == 0) & (pl.program_id(1) == 0))
    def _():
        sum_ref[...] = jnp.zeros_like(sum_ref)

    sum_ref[...] += dot(low, attn_ref[0], TN)


def attn_grad(core, own, other, attn, w, second, first):
    slots, share, depth = own.shape
    length = 2 * share
    width = attn.shape[2]
    tile = min(256, share)
    shares = share // tile
    token = pl.BlockSpec((1, tile, depth), lambda r, i, *_: (r, lax.rem(i, shares), 0))
    wide = pl.BlockSpec((1, tile, width), lambda r, i, *_: (r, i, 0))
    full = lambda v: pl.BlockSpec(v.shape, lambda r, i, *_: (0,) * v.ndim)
    total = jax.ShapeDtypeStruct((LOW, width), F32)
    return kernel_call(
        functools.partial(attn_grad_kernel, shares),
        [core, own, other, attn, w, second, first],
        (),
        prefetch=1,
        grid=(slots, length // tile),
        in_specs=[token, token, wide, full(w), full(second), full(first)],
        out_specs=[wide, full(total)],
        out_shape=[jax.ShapeDtypeStruct(attn.shape, BF16), total],
        name="attn_grad",
    )


def normed_grad_kernel(
    q_cols, shares, core_ref, q_own_ref, q_other_ref, kv_own_ref, kv_other_ref, s_own_ref, s_other_ref,
    back_ref, w_ref, b_ref, keep_ref, away_ref, sum_ref
):
    depth, width = w_ref.shape[1:]
    core, step = core_ref[0], pl.program_id(1)

    @pl.when((pl.program_id(0) == 0) & (step == 0))
    def _():
        sum_ref[...] = jnp.zeros_like(sum_ref)

    sides = (
        (q_own_ref, kv_own_ref, s_own_ref, keep_ref, core),
        (q_other_ref, kv_other_ref, s_other_ref, away_ref, 1 - core),
    )
    for q_ref, kv_ref, s_ref, out_ref, share in sides:
        tile = q_ref.shape[1]
        last = (share * shares + step == 2 * shares - 1).astype(F32)
        full = low = None
        for s in range(2):
            kv = kv_ref[0, s]
            edge = back_ref[0, s].astype(F32) * last
            if tile > WIN:
                edge = jnp.concatenate([jnp.zeros((tile - WIN, kv.shape[1]), F32), edge], axis=0)
            kv = (kv + edge).astype(BF16)
            q = q_ref[0, :, s * q_cols : (s + 1) * q_cols]
            grads = jnp.concatenate([q, kv], axis=1)
            part = dot(grads, w_ref[s], NT)
            small = dot(grads, b_ref[:, s * width : (s + 1) * width], NT)
            full = part if full is None else full + part
            low = small if low is None else low + small
            sum_ref[s] += dot(s_ref[0], grads, TN)
        out_ref[0, :, :depth] = full.astype(BF16)
        out_ref[0, :, depth:] = (ADAPTER_SCALE * low).astype(BF16)


def normed_grad(core, q, kv, small, back, w, b, q_cols, share):
    slots, length, q_width = q.shape
    sets, depth, width = w.shape
    tile = min(256, share)
    shares = share // tile
    own, other = halves(share, tile)
    four = lambda f: (lambda r, i, core: (r, 0, f(r, i, core)[1], 0))
    out = pl.BlockSpec((1, tile, depth + LOW), lambda r, i, *_: (r, i, 0))
    shape = jax.ShapeDtypeStruct((slots, share, depth + LOW), BF16)
    total = jax.ShapeDtypeStruct((sets, LOW, width), F32)
    kv_block = (1, sets, tile, kv.shape[3])
    return kernel_call(
        functools.partial(normed_grad_kernel, q_cols, shares),
        [core, q, q, kv, kv, small, small, back, w, b],
        (),
        prefetch=1,
        grid=(slots, shares),
        in_specs=[
            pl.BlockSpec((1, tile, q_width), own),
            pl.BlockSpec((1, tile, q_width), other),
            pl.BlockSpec(kv_block, four(own)),
            pl.BlockSpec(kv_block, four(other)),
            pl.BlockSpec((1, tile, LOW), own),
            pl.BlockSpec((1, tile, LOW), other),
            pl.BlockSpec((1, sets, WIN, kv.shape[3]), lambda r, i, *_: (r, 0, 0, 0)),
            pl.BlockSpec(w.shape, lambda r, i, *_: (0, 0, 0)),
            pl.BlockSpec(b.shape, lambda r, i, *_: (0, 0)),
        ],
        out_specs=[out, out, pl.BlockSpec(total.shape, lambda r, i, *_: (0, 0, 0))],
        out_shape=[shape, shape, total],
        name="normed_grad",
    )


def finish_kernel(keep_ref, got_ref, hidden_ref, mid_ref, gain_ref, first_ref, out_ref, sum_ref):
    depth = hidden_ref.shape[1]
    total = keep_ref[...].astype(F32) + got_ref[...].astype(F32)
    low = total[:, depth:].astype(BF16)
    grad = total[:, :depth] + dot(low, first_ref[...])
    values, gain = hidden_ref[...].astype(F32), gain_ref[...]
    scale, back = norm_back(values, gain, grad)
    out_ref[...] = (mid_ref[...] + back).astype(BF16)

    @pl.when(pl.program_id(0) == 0)
    def _():
        sum_ref[...] = jnp.zeros_like(sum_ref)

    sum_ref[...] += dot(low, (values * scale * gain).astype(BF16), TN)


def local(
    hidden_in,
    grad_out,
    live_rows,
    doc_starts,
    norm_attn,
    norm_ffn,
    query_weight,
    key_weight,
    value_weight,
    out_weight,
    gate_weight,
    up_weight,
    down_weight,
    query_adapt_in,
    query_adapt_out,
    key_adapt_in,
    key_adapt_out,
    value_adapt_in,
    value_adapt_out,
    outproj_adapt_in,
    projection_adapter_second,
    query_feature,
    key_feature,
):
    rows, seqs, heads = lax.axis_size("row"), lax.axis_size("seq"), lax.axis_size("head")
    head = lax.axis_index("head")
    core = lax.rem(head, 2)
    x_count = heads // 2
    x_place = head // 2
    slots, share_len, model_dim = hidden_in.shape
    piece_len = 2 * share_len
    pieces = seqs * x_count
    piece = lax.axis_index("seq") * x_count + x_place
    blocks = piece_len // WIN
    ext_len = piece_len + WIN
    q_cols, k_cols = query_weight.shape[1], key_weight.shape[1]
    ff_cols = gate_weight.shape[1]

    def in_order(own, other):
        first = jnp.where(core == 0, own, other)
        second = jnp.where(core == 0, other, own)
        return jnp.concatenate([first, second], axis=1)

    def own_half(both):
        return lax.dynamic_slice_in_dim(both, core * share_len, share_len, 1)

    def other_half(both):
        return lax.dynamic_slice_in_dim(both, (1 - core) * share_len, share_len, 1)

    qkv_shard = jnp.concatenate([query_weight, key_weight, value_weight], axis=1)
    out_shard = out_weight.T
    down_shard = down_weight.T
    chunk = ff_cols // FF_CHUNKS
    ffn_shards = [
        jnp.concatenate(
            [w[:, j * chunk : (j + 1) * chunk] for w in (gate_weight, up_weight, down_shard)], axis=1
        )
        for j in range(FF_CHUNKS)
    ]
    ffn_later = [
        lax.all_gather(v, ("row", "seq"), axis=0, tiled=True) for v in ffn_shards[1:]
    ]
    own_smalls = [
        query_feature, key_feature, query_adapt_out, key_adapt_out, value_adapt_out, outproj_adapt_in
    ]
    (qkv_mat, out_mat, first_mat), other_smalls, (hidden_other, cot_mine, cot_away) = gather(
        [qkv_shard, out_shard, ffn_shards[0]],
        [True, True, False],
        [
            (0, (0, qkv_shard.shape[1]), True, 0),
            (1, (0, out_shard.shape[1]), True, 0),
            (2, (0, ffn_shards[0].shape[1]), True, rows * seqs),
        ],
        own_smalls,
        hidden_in,
        grad_out,
    )
    ffn_mats = [first_mat] + ffn_later

    def both(i, axis):
        own, other = own_smalls[i], other_smalls[i]
        return jnp.concatenate(
            [jnp.where(x_place == 0, own, other), jnp.where(x_place == 0, other, own)], axis=axis
        )

    query_feat_all, key_feat_all = both(0, 0), both(1, 0)
    q_out, k_out, v_out = both(2, 1), both(3, 1), both(4, 1)
    o_in = both(5, 0)

    doc_ids = jnp.cumsum(doc_starts, axis=1)
    padded_docs = jnp.concatenate(
        [jnp.full((slots, WIN + 1), -1, jnp.int32), doc_ids], axis=1
    )
    piece_docs = padded_docs[:, ::piece_len][:, : pieces + 1]
    near_docs = lax.dynamic_slice_in_dim(padded_docs, piece * piece_len, ext_len + 1, 1)
    end_docs = near_docs[:, ::WIN][:, : blocks + 1]
    carry_doc = end_docs[:, 0]
    next_doc = end_docs[:, blocks]
    key_docs = near_docs[:, 1:]
    key_doc_lanes = jnp.broadcast_to(key_docs[:, :, None], (slots, ext_len, 2 * HD))
    query_doc_lanes = key_doc_lanes[:, WIN:]
    doc_blocks = key_docs.reshape(slots, blocks + 1, WIN)
    pair_docs = jnp.concatenate([doc_blocks[:, :-1], doc_blocks[:, 1:]], axis=2)

    def from_pieces(block):
        held = []
        for d, start in enumerate((block, flip_x(block))):
            for l in range(seqs):
                if l:
                    start = shift(start, "seq", 1)
                source = (
                    lax.rem(lax.axis_index("seq") - l + seqs, seqs) * x_count
                    + lax.rem(x_place + d, x_count)
                )
                held.append((source, start))
        return held[1:]

    gain_attn = norm_attn.astype(F32)[None]
    gain_ffn = norm_ffn.astype(F32)[None]
    core_index = core.astype(jnp.int32).reshape(1)
    flat_tokens = lambda v: v.reshape(-1, v.shape[-1])

    set_cols = q_cols + 2 * k_cols
    adapt_in_all = jnp.concatenate([query_adapt_in, key_adapt_in, value_adapt_in], axis=1)

    def by_sets(parts):
        return jnp.concatenate(
            [v[:, d * (v.shape[1] // 2) : (d + 1) * (v.shape[1] // 2)] for d in range(2) for v in parts],
            axis=1,
        )

    def diagonal(parts):
        rows = [
            [p if i == j else jnp.zeros((RANK, q.shape[1]), BF16) for j, q in enumerate(parts)]
            for i, p in enumerate(parts)
        ]
        return jnp.concatenate([by_sets(r) for r in rows], axis=0)

    pad_rows = lambda v: jnp.pad(v, ((0, LOW - v.shape[0]), (0, 0)))
    pad_cols = lambda v: jnp.pad(v, ((0, 0), (0, LOW - v.shape[1])))
    adapt_in_all = pad_cols(adapt_in_all)
    adapt_out_all = pad_rows(diagonal([q_out, k_out, v_out]))
    second = pad_rows(projection_adapter_second)
    o_in = pad_cols(o_in)
    query, kv_own, small = project(
        core_index, hidden_in, hidden_other, gain_attn, qkv_mat, adapt_in_all, adapt_out_all, q_cols,
        k_cols,
    )

    def along_pieces(block, distance):
        route = []
        for p in range(pieces):
            to = p + distance
            if 0 <= to < pieces:
                for c in range(2):
                    route.append((2 * p + c, 2 * to + c))
        return lax.ppermute(block, ("seq", "head"), route)

    kv = jnp.concatenate([along_pieces(kv_own[:, :, -WIN:], 1), kv_own], axis=2)
    doubled = lambda feat: jnp.concatenate([feat, -feat], axis=2)
    query_feat, key_feat = doubled(query_feat_all), doubled(key_feat_all)
    phi_key, end_state = key_state(end_docs, kv, key_feat, key_doc_lanes)
    carry = jnp.zeros(end_state.shape, F32)
    for source, part in from_pieces(end_state):
        after = lax.dynamic_index_in_dim(piece_docs, source + 1, 1, keepdims=False)
        keep = (source < piece) & (after == carry_doc)
        carry = carry + jnp.where(keep[:, None, None, None], part.astype(F32), 0.0)
    attn, phi_query = attend(
        end_docs, query, kv, phi_key, query_feat, carry, query_doc_lanes, key_doc_lanes, pair_docs
    )

    keep, away = out_project(core_index, attn, out_mat, o_in, share_len)
    mid_rows, nmid, low_mix = tokens_call(
        middle_kernel,
        [flat_tokens(v) for v in (hidden_in, keep, flip_core(away))],
        [second, gain_ffn],
        [(model_dim, F32), (model_dim, BF16), (LOW, BF16)],
        "middle",
    )

    nmid_x = flip_x(nmid)

    def chip_tokens(own):
        return own, flip_core(own)

    def sum_away(own, other):
        return (own.astype(F32) + flip_core(other).astype(F32)).astype(BF16)

    x_mine = chip_tokens(nmid)
    c_mine, c_away = flat_tokens(cot_mine), flat_tokens(cot_away)
    run = lambda x, c, w, before=(), after=(): ffn(
        x, c, w, live_rows, share_len, slots, before, after
    )
    mine = run(x_mine, c_mine, ffn_mats[:-1])
    x_away = chip_tokens(hold(nmid_x, (mine[0],)))
    away = run(x_away, c_away, ffn_mats[:-1])
    away = run(x_away, c_away, ffn_mats[-1:], away)
    gn_there = sum_away(*away[:2])
    gn_back = flip_x(gn_there)
    gn_own, gn_other, y_own, y_other = run(
        x_mine, c_mine, ffn_mats[-1:], mine, (gn_there,)
    )
    y_there = sum_away(*away[2:])
    y_back = flip_x(y_there)
    grad_mid, branch = tokens_call(
        functools.partial(branch_kernel, share_len),
        [mid_rows, gn_own, flip_core_parts(gn_other, 4), gn_back, flat_tokens(grad_out)],
        [gain_ffn],
        [(model_dim, F32), (model_dim, BF16)],
        "branch",
        prefetch=[live_rows],
    )

    shaped = lambda v: v.reshape(slots, share_len, -1)
    grad_attn, sum_o_in = attn_grad(
        core_index, shaped(branch), shaped(flip_core(branch)), attn, out_mat, second, o_in
    )
    sum_o_in = sum_o_in[:RANK]
    sum_o_out = ADAPTER_SCALE * dot(low_mix, branch, TN)[:RANK]

    grad_query, feat_query, gphi, gkv, grad_carry = attend_back(
        end_docs, query, kv, phi_key, phi_query, query_feat, carry, query_doc_lanes, key_doc_lanes,
        pair_docs, grad_attn, (y_there,),
    )
    block_out = tokens_call(
        sum_kernel, [mid_rows, y_own, flip_core(y_other), y_back], [], [(model_dim, BF16)], "sum_y"
    )[0].reshape(hidden_in.shape)
    later = jnp.zeros(grad_carry.shape, F32)
    for source, part in from_pieces(grad_carry):
        start = lax.dynamic_index_in_dim(piece_docs, source, 1, keepdims=False)
        keep = (source > piece) & (start == next_doc)
        later = later + jnp.where(keep[:, None, None, None], part.astype(F32), 0.0)
    grad_body, grad_edge, feat_key = key_back(
        end_docs, kv, phi_key, key_feat, later, key_doc_lanes, gphi, gkv, (y_back,)
    )
    sum_q_feat = jnp.sum(feat_query, axis=0).reshape(2, -1, 2 * HD)
    sum_k_feat = jnp.sum(feat_key, axis=0).reshape(2, -1, 2 * HD)

    keep, away, outs = normed_grad(
        core_index, grad_query, grad_body, small, along_pieces(grad_edge, -1), qkv_mat, adapt_out_all,
        q_cols, share_len,
    )
    outs = ADAPTER_SCALE * outs
    outs = [
        outs[:, :RANK, :q_cols],
        outs[:, RANK : 2 * RANK, q_cols : q_cols + k_cols],
        outs[:, 2 * RANK : 3 * RANK, q_cols + k_cols :],
    ]
    grad_hidden, sum_in = tokens_call(
        finish_kernel,
        [flat_tokens(keep), flat_tokens(flip_core(away)), flat_tokens(hidden_in), grad_mid],
        [gain_attn, adapt_in_all.T],
        [(model_dim, BF16)],
        "finish",
        sums=[(LOW, model_dim)],
    )
    grad_hidden = grad_hidden.reshape(hidden_in.shape)
    sum_in = sum_in[: 3 * RANK]

    by_rows = jnp.concatenate([sum_in, sum_o_out], axis=0)
    width = model_dim // (rows * seqs * heads)
    by_rows = by_rows.reshape(4 * RANK, rows, seqs, heads, width).transpose(3, 2, 1, 0, 4)
    for axis in ("head", "seq", "row"):
        by_rows = scatter_sum(by_rows, axis)
    in_parts = by_rows.reshape(4, RANK, width)

    def lanes_of(v):
        v = v.reshape(2, RANK, -1, 2 * HD).transpose(0, 2, 1, 3)
        return v.reshape(2, -1, 2 * HD)

    o_sets = jnp.stack([sum_o_in[:, :q_cols], sum_o_in[:, q_cols:]])
    packed = [lanes_of(v) for v in outs + [o_sets]] + [sum_q_feat, sum_k_feat]
    sizes = [v.shape[1] for v in packed]
    packed = jnp.concatenate(packed, axis=1)
    kept = lax.dynamic_index_in_dim(packed, x_place, 0, keepdims=False)
    sent = lax.dynamic_index_in_dim(packed, 1 - x_place, 0, keepdims=False)
    packed = kept + flip_x(sent.astype(BF16)).astype(F32)
    for axis in ("seq", "row"):
        packed = full_sum(packed, axis)
    cols, at = [], 0
    for size in sizes:
        cols.append(packed[at : at + size])
        at += size
    from_lanes = lambda v: v.reshape(-1, RANK, 2 * HD).transpose(1, 0, 2).reshape(RANK, -1)
    from_pairs = lambda v: v.reshape(-1, HD, 2, HD).transpose(0, 2, 1, 3).reshape(-1, HD, HD)
    cols = [from_lanes(v) for v in cols[:4]] + [from_pairs(v) for v in cols[4:]]
    cols[3] = cols[3].T

    return (
        block_out,
        grad_hidden,
        in_parts[0].T,
        cols[0],
        in_parts[1].T,
        cols[1],
        in_parts[2].T,
        cols[2],
        cols[3],
        in_parts[3],
        cols[4],
        cols[5],
    )


def solution(mesh):
    return jax.shard_map(
        local,
        mesh=mesh,
        in_specs=(
            P("row", ("seq", "head"), None),
            P("row", ("seq", "head"), None),
            P("row"),
            P("row", None),
            P(),
            P(),
            P(("row", "seq"), "head"),
            P(("row", "seq"), "head"),
            P(("row", "seq"), "head"),
            P("head", ("row", "seq")),
            P(("row", "seq"), "head"),
            P(("row", "seq"), "head"),
            P("head", ("row", "seq")),
            P(),
            P(None, "head"),
            P(),
            P(None, "head"),
            P(),
            P(None, "head"),
            P("head", None),
            P(),
            P("head", None, None),
            P("head", None, None),
        ),
        out_specs=(
            P("row", ("seq", "head"), None),
            P("row", ("seq", "head"), None),
            P(("row", "seq", "head"), None),
            P(None, "head"),
            P(("row", "seq", "head"), None),
            P(None, "head"),
            P(("row", "seq", "head"), None),
            P(None, "head"),
            P("head", None),
            P(None, ("row", "seq", "head")),
            P("head", None, None),
            P("head", None, None),
        ),
        check_vma=False,
    )
```

```python
import functools

import jax
import jax.numpy as jnp
from jax import lax
from jax.experimental import pallas as pl
from jax.experimental.pallas import tpu as pltpu
from jax.sharding import PartitionSpec as P

HD = 64
RANK = 8
WIN = 64
FF_CHUNKS = (1, 2, 3, 2)

NORM_EPS = 1e-05
ADAPTER_SCALE = 2.0
F32 = jnp.float32
NT = ((1,), (1,))
TN = ((0,), (0,))
BF16 = jnp.bfloat16


def shift(block, axis, distance):
    size = lax.axis_size(axis)
    return lax.ppermute(block, axis, [(i, (i + distance) % size) for i in range(size)])


def flip_core(block):
    return lax.ppermute(block, "head", [(i, i ^ 1) for i in range(lax.axis_size("head"))])


def flip_core_parts(block, parts):
    size = block.shape[0] // parts
    return jnp.concatenate(
        [flip_core(block[i * size : (i + 1) * size]) for i in range(parts)], axis=0
    )


def flip_x(block):
    return lax.ppermute(block, "head", [(i, i ^ 2) for i in range(lax.axis_size("head"))])


def kernel_call(
    kernel, args, after, *, grid, in_specs, out_specs, out_shape, name, prefetch=0, scratch=(), cost=None
):
    count = len(args)

    def body(*refs):
        kernel(*refs[:count], *refs[count + len(after) :])

    return pl.pallas_call(
        body,
        grid_spec=pltpu.PrefetchScalarGridSpec(
            num_scalar_prefetch=prefetch,
            grid=grid,
            in_specs=list(in_specs) + [pl.BlockSpec(memory_space=pl.ANY)] * len(after),
            out_specs=out_specs,
            scratch_shapes=list(scratch),
        ),
        out_shape=out_shape,
        compiler_params=pltpu.CompilerParams(vmem_limit_bytes=60 * 2**20),
        cost_estimate=cost and pl.CostEstimate(
            flops=cost.flops // 4, bytes_accessed=cost.bytes_accessed // 4, transcendentals=0
        ),
        name=name,
    )(*args, *after)


def copy_kernel(src_ref, dst_ref):
    dst_ref[...] = src_ref[...]


def hold(value, after):
    flat = value.reshape(-1, value.shape[-1])
    tile = min(256, flat.shape[0])
    block = pl.BlockSpec((tile, flat.shape[1]), lambda i: (i, 0))
    held = kernel_call(
        copy_kernel, [flat], after, grid=(flat.shape[0] // tile,), in_specs=[block], out_specs=block,
        out_shape=jax.ShapeDtypeStruct(flat.shape, flat.dtype), name="hold",
    )
    return held.reshape(value.shape)


def dot(a, b, dims=((1,), (0,))):
    return lax.dot_general(a, b, (dims, ((), ())), preferred_element_type=F32)


def tie(value, *after):
    return lax.optimization_barrier((value,) + after)[0]


def rms_scaled(values, gain_vec):
    return (
        values * lax.rsqrt(jnp.mean(values * values, axis=-1, keepdims=True) + NORM_EPS) * gain_vec
    )


def rms_back(values, gain_vec, grad_in):
    factor = lax.rsqrt(jnp.mean(values * values, axis=-1, keepdims=True) + NORM_EPS)
    scaled = gain_vec * grad_in
    return factor * scaled - values * factor**3 * jnp.mean(values * scaled, axis=-1, keepdims=True)


def scatter_sum(parts, axis):
    size, place = lax.axis_size(axis), lax.axis_index(axis)
    total = lax.dynamic_index_in_dim(parts, place, 0, keepdims=False)
    for k in range(1, size):
        away = lax.dynamic_index_in_dim(parts, lax.rem(place + k, size), 0, keepdims=False)
        total = total + shift(away, axis, k)
    return total


def full_sum(part, axis):
    size = lax.axis_size(axis)
    step = 1
    while step < size:
        sent = part.astype(BF16)
        got = lax.ppermute(sent, axis, [(i, i ^ step) for i in range(size)])
        part = sent.astype(F32) + got.astype(F32)
        step *= 2
    return part


def gather_plan(rows, seqs, weights):
    free = {"row": 0.0, "seq": 0.0, "x": 0.0}
    running = []
    plan = []

    def begin(now, starts):
        for t in starts:
            w, link = t[0], t[1]
            end = max(now, free[link]) + weights[w][0]
            free[link] = end
            running.append((end, len(plan), len(running), t))
        return starts

    def spread(w, k, l):
        starts = []
        row_first = weights[w][2]
        if (l == 0 or not row_first) and k + 1 < rows:
            starts.append((w, "row", k + 1, l))
        if (k == 0 or row_first) and l + 1 < seqs:
            starts.append((w, "seq", k, l + 1))
        if weights[w][1]:
            starts.append((w, "x", k, l))
        return starts

    first = [t for w in range(len(weights)) if weights[w][3] == 0 for t in spread(w, 0, 0)]
    plan.append((None, begin(0.0, first)))
    done = 0
    while running:
        event = min(running)
        running.remove(event)
        now, t = event[0], event[3]
        done += 1
        starts = [] if t[1] == "x" else spread(t[0], t[2], t[3])
        for w in range(len(weights)):
            if weights[w][3] == done:
                starts = starts + spread(w, 0, 0)
        plan.append((t, begin(now, starts)))
    return plan


def gather_kernel(plan, rows, seqs, parts, over_x, small_count, *refs):
    count = len(over_x)
    inputs, refs = refs[: count + small_count + 2], refs[count + small_count + 2 :]
    shards, smalls = inputs[:count], inputs[count : count + small_count]
    hidden, cot = inputs[count + small_count :]
    wholes, refs = refs[:count], refs[count:]
    small_outs, refs = refs[:small_count], refs[small_count:]
    hidden_out, cot_mine, cot_away = refs[:3]
    send_sem, recv_sem, copy_sem, more_send, more_recv = refs[3:]
    row, seq, head = lax.axis_index("row"), lax.axis_index("seq"), lax.axis_index("head")
    x_place = head // 2
    across = {"head": lax.rem(head + 2, 4)}
    partner = {"head": head + 1 - 2 * lax.rem(head, 2)}
    away = {
        "row": {"row": lax.rem(row + 1, rows)},
        "seq": {"seq": lax.rem(seq + 1, seqs)},
        "x": across,
    }
    barrier = pltpu.get_barrier_semaphore()
    sources = (
        {"row": lax.rem(row + rows - 1, rows)},
        {"seq": lax.rem(seq + seqs - 1, seqs)},
        across,
        partner,
    )
    for source in sources:
        pl.semaphore_signal(
            barrier, inc=1, device_id=source, device_id_type=pl.DeviceIdType.MESH
        )
    pl.semaphore_wait(barrier, len(sources))

    def slot(p, k, l):
        w, columns = parts[p][0], pl.ds(*parts[p][1])
        depth = shards[w].shape[0]
        place = lax.rem(row - k + rows, rows) * seqs + lax.rem(seq - l + seqs, seqs)
        at = pl.ds(pl.multiple_of(place * depth, depth), depth)
        return wholes[w].at[x_place, at, columns] if over_x[w] else wholes[w].at[at, columns]

    number = {}
    last_x = 0
    for i, (event, starts) in enumerate(plan):
        for t in starts:
            number[t] = len(number)
            if t[1] == "x":
                last_x = i

    def remote(src, dst, send, recv, device):
        return pltpu.make_async_remote_copy(
            src_ref=src, dst_ref=dst, send_sem=send, recv_sem=recv, device_id=device,
            device_id_type=pl.DeviceIdType.MESH,
        )

    def transfer(t):
        w, link, k, l = t
        source = {"row": (k - 1, l), "seq": (k, l - 1), "x": (k, l)}[link]
        dst = slot(w, *source)
        n = number[t]
        src = shards[parts[w][0]].at[:, pl.ds(*parts[w][1])] if source == (0, 0) else dst
        return remote(src, dst, send_sem.at[n], recv_sem.at[n], away[link])

    def more(i, src, dst, device):
        return remote(src, dst, more_send.at[i], more_recv.at[i], device)

    early = [more(i, a, b, across) for i, (a, b) in enumerate(zip(smalls, small_outs))]
    early.append(more(small_count, hidden, hidden_out, partner))
    early.append(more(small_count + 1, cot, cot_mine.at[1], partner))
    cot_x = more(small_count + 2, cot, cot_away.at[0], across)
    cot_last = more(small_count + 3, cot_away.at[0], cot_away.at[1], partner)
    own = [
        pltpu.make_async_copy(
            shards[w].at[:, pl.ds(*columns)], slot(p, 0, 0), copy_sem.at[p]
        )
        for p, (w, columns) in enumerate(parts)
    ] + [pltpu.make_async_copy(cot, cot_mine.at[0], copy_sem.at[len(parts)])]
    for i, (event, starts) in enumerate(plan):
        if event is not None:
            transfer(event).wait_recv()
        for t in starts:
            transfer(t).start()
        if event is None:
            for copy in early + own:
                copy.start()
        if i == last_x:
            cot_x.start()
    cot_x.wait()
    cot_last.start()
    for t in number:
        transfer(t).wait_send()
    for copy in early + own + [cot_last]:
        copy.wait()


def gather(shards, over_x, pieces, smalls, hidden, cot):
    rows, seqs = lax.axis_size("row"), lax.axis_size("seq")
    plan = gather_plan(
        rows,
        seqs,
        [(float(shards[w].shape[0] * c[1]), over_x[w], first, later) for w, c, first, later in pieces],
    )
    parts = [(w, c) for w, c, _, _ in pieces]
    total = sum(len(starts) for _, starts in plan)
    shapes = []
    for shard, x in zip(shards, over_x):
        depth, width = shard.shape
        whole = (rows * seqs * depth, width)
        shapes.append(jax.ShapeDtypeStruct(((2,) + whole) if x else whole, shard.dtype))
    same = lambda v: jax.ShapeDtypeStruct(v.shape, v.dtype)
    twice = jax.ShapeDtypeStruct((2,) + cot.shape, cot.dtype)
    shapes += [same(v) for v in smalls] + [same(hidden), twice, twice]
    more = len(smalls) + 4
    place = pl.BlockSpec(memory_space=pl.ANY)
    outs = pl.pallas_call(
        functools.partial(gather_kernel, plan, rows, seqs, parts, over_x, len(smalls)),
        out_shape=shapes,
        in_specs=[place] * (len(shards) + len(smalls) + 2),
        out_specs=[place] * len(shapes),
        scratch_shapes=[
            pltpu.SemaphoreType.DMA((total,)),
            pltpu.SemaphoreType.DMA((total,)),
            pltpu.SemaphoreType.DMA((len(parts) + 1,)),
            pltpu.SemaphoreType.DMA((more,)),
            pltpu.SemaphoreType.DMA((more,)),
        ],
        compiler_params=pltpu.CompilerParams(collective_id=0, has_side_effects=True),
        name="gather",
    )(*shards, *smalls, hidden, cot)
    n = len(shards)
    return outs[:n], outs[n : n + len(smalls)], outs[-3:]


def ffn_kernel(chunks, before, share_len, slots, live_ref, x_ref, more_ref, cot_ref, *refs):
    weights, refs = refs[:chunks], refs[chunks:]
    earlier, refs = refs[: 4 * before], refs[4 * before :]
    outs, held, sem = refs[:4], refs[4:-1], refs[-1]
    step = pl.program_id(0)
    tile = x_ref.shape[0]
    copies = [pltpu.make_async_copy(weights[c], held[c], sem.at[c]) for c in range(chunks)]

    @pl.when(step == 0)
    def _():
        for copy in copies:
            copy.start()

    first = step < pl.num_programs(0) // 2
    live = (lax.rem(step * tile // share_len, slots) < live_ref[0]).astype(F32)
    x, cot = jnp.where(first, x_ref[...], more_ref[...]), cot_ref[...]
    sums = [None, None]
    if before:
        sums = [jnp.where(first, earlier[i][...], earlier[i + 1][...]).astype(F32) for i in (0, 2)]
    for c in range(chunks):

        @pl.when(step == 0)
        def _():
            copies[c].wait()

        w, width = held[c], held[c].shape[1] // 3
        gate = dot(x, w[:, :width])
        up = dot(x, w[:, width : 2 * width])
        gm = dot(cot, w[:, 2 * width :]) * live
        sig = jax.nn.sigmoid(gate)
        silu = gate * sig
        mixed = (silu * up).astype(BF16)
        g_gate = (gm * up * (sig + silu * (1.0 - sig))).astype(BF16)
        g_up = (gm * silu).astype(BF16)
        parts = (
            dot(jnp.concatenate([g_gate, g_up], axis=1), w[:, : 2 * width], NT),
            dot(mixed, w[:, 2 * width :], NT),
        )
        sums = [p if t is None else t + p for t, p in zip(sums, parts)]

    @pl.when(first)
    def _():
        outs[0][...] = sums[0].astype(BF16)
        outs[2][...] = sums[1].astype(BF16)

    @pl.when(jnp.logical_not(first))
    def _():
        outs[1][...] = sums[0].astype(BF16)
        outs[3][...] = sums[1].astype(BF16)


def ffn(x, cot, weights, live_rows, share_len, slots, before=(), after=()):
    tokens, depth = cot.shape
    chunks = len(weights)
    units = sum(w.shape[1] for w in weights) // 3
    tile = min(256, share_len)
    half = tokens // tile // 2
    lower = pl.BlockSpec((tile, depth), lambda i, *_: (jnp.minimum(i, half - 1), 0))
    upper = pl.BlockSpec((tile, depth), lambda i, *_: (jnp.maximum(i - half, 0), 0))
    out = jax.ShapeDtypeStruct((tokens // 2, depth), BF16)
    return kernel_call(
        functools.partial(ffn_kernel, chunks, len(before) // 4, share_len, slots),
        [live_rows, x[0], x[1], cot, *weights, *before],
        after,
        prefetch=1,
        grid=(tokens // tile,),
        in_specs=[lower, upper, pl.BlockSpec((tile, depth), lambda i, *_: (i, 0))]
        + [pl.BlockSpec(memory_space=pl.ANY)] * chunks
        + [lower, upper] * (len(before) // 2),
        out_specs=[lower, upper, lower, upper],
        out_shape=[out] * 4,
        scratch=[
            *[pltpu.VMEM(w.shape, BF16) for w in weights],
            pltpu.SemaphoreType.DMA((chunks,)),
        ],
        cost=pl.CostEstimate(
            flops=12 * tokens * depth * units,
            bytes_accessed=8 * tokens * depth + 6 * depth * units,
            transcendentals=0,
        ),
        name="ffn",
    )


def lower_lanes(like):
    return lax.broadcasted_iota(jnp.int32, like.shape, 1) < HD


def half_ones():
    r = lax.broadcasted_iota(jnp.int32, (2 * HD, 2 * HD), 0) // HD
    c = lax.broadcasted_iota(jnp.int32, (2 * HD, 2 * HD), 1) // HD
    return (r == c).astype(F32).astype(BF16)


def swap(v):
    return pltpu.roll(v, HD, 1)


def features(x, feat):
    logit = dot(x, feat)
    low = lower_lanes(logit)
    top = jnp.max(jnp.where(low, logit, -jnp.inf), axis=1, keepdims=True)
    bottom = jnp.max(jnp.where(low, -jnp.inf, logit), axis=1, keepdims=True)
    e = jnp.exp(logit - jnp.where(low, top, bottom))
    return e / dot(e.astype(BF16), half_ones())


def features_back(phi, grad):
    p = phi.astype(F32)
    prod = p * grad
    low = lower_lanes(prod)
    first = jnp.sum(jnp.where(low, prod, 0.0), axis=1, keepdims=True)
    second = jnp.sum(jnp.where(low, 0.0, prod), axis=1, keepdims=True)
    g = prod - p * jnp.where(low, first, second)
    return (g - swap(g)).astype(BF16)[:, :HD]


def values_ones(kv):
    kv = kv.astype(F32)
    return jnp.where(lower_lanes(kv), swap(kv), 1.0).astype(BF16)


def key_state_kernel(ends_ref, kv_ref, feat_ref, kdoc_ref, phi_ref, state_ref):
    r = pl.program_id(0)
    kv = kv_ref[0, 0]
    body = kv.shape[0] - WIN
    phi = features(kv[:, :HD], feat_ref[0]).astype(BF16)
    phi_ref[0, 0] = phi
    last = ends_ref[r, body // WIN]
    held = jnp.where(kdoc_ref[0, :body] == last, phi[:body].astype(F32), 0.0).astype(BF16)
    state_ref[0, 0] = dot(held, values_ones(kv[:body]), TN).astype(BF16)


def key_state(ends, kv, feat, kdoc, after=()):
    slots, groups, ext, _ = kv.shape
    block = lambda r, g, *_: (r, g, 0, 0)
    return kernel_call(
        key_state_kernel,
        [ends, kv, feat, kdoc],
        after,
        prefetch=1,
        grid=(slots, groups),
        in_specs=[
            pl.BlockSpec((1, 1, ext, 2 * HD), block),
            pl.BlockSpec((1, HD, 2 * HD), lambda r, g, *_: (g, 0, 0)),
            pl.BlockSpec((1, ext, 2 * HD), lambda r, g, *_: (r, 0, 0)),
        ],
        out_specs=[
            pl.BlockSpec((1, 1, ext, 2 * HD), block),
            pl.BlockSpec((1, 1, 2 * HD, 2 * HD), block),
        ],
        out_shape=[
            jax.ShapeDtypeStruct((slots, groups, ext, 2 * HD), BF16),
            jax.ShapeDtypeStruct((slots, groups, 2 * HD, 2 * HD), BF16),
        ],
        name="key_state",
    )


def block_masks(b, qdoc_ref, pdoc_ref):
    rows = slice(WIN * b, WIN * b + WIN)
    same = qdoc_ref[0, rows] == pdoc_ref[0, b : b + 1]
    row = lax.broadcasted_iota(jnp.int32, (WIN, 2 * WIN), 0)
    col = lax.broadcasted_iota(jnp.int32, (WIN, 2 * WIN), 1)
    linear = same & (col <= row)
    window = same & (col > row) & (col <= row + WIN)
    return window, linear


def next_state(b, ends_ref, r, state, phi_ref, vx_ref, kdoc_ref):
    rows = slice(WIN * (b - 1), WIN * b)
    keep = (ends_ref[r, b] == ends_ref[r, b - 1]).astype(F32)
    held = jnp.where(
        kdoc_ref[0, rows] == ends_ref[r, b], phi_ref[0, 0, rows].astype(F32), 0.0
    ).astype(BF16)
    return state * keep + dot(held, vx_ref[rows], TN)


def block_forward(b, ends_ref, r, q_ref, kv_ref, phi_ref, phiq_ref, vx_ref, state_low, qdoc_ref, pdoc_ref):
    heads = q_ref.shape[1]
    rows, pair = slice(WIN * b, WIN * b + WIN), slice(WIN * b, WIN * b + 2 * WIN)
    window, linear = block_masks(b, qdoc_ref, pdoc_ref)
    valid = qdoc_ref[0, rows] == ends_ref[r, b]
    query = jnp.concatenate([q_ref[0, h, rows] for h in range(heads)], axis=0)
    phi_query = jnp.concatenate([phiq_ref[0, h, rows] for h in range(heads)], axis=0)
    key = kv_ref[0, 0, pair, :HD]
    phi_key = phi_ref[0, 0, pair]
    score = dot(query, key, NT) * (HD**-0.5)
    lin = dot(phi_query, phi_key, NT)
    part = lambda v, h: v[WIN * h : WIN * h + WIN]
    exps = [jnp.where(window, jnp.exp(part(score, h)), 0.0) for h in range(heads)]
    weight = jnp.concatenate(
        [jnp.where(linear, part(lin, h), exps[h]).astype(BF16) for h in range(heads)], axis=0
    )
    phi_valid = jnp.concatenate(
        [jnp.where(valid, part(phi_query, h).astype(F32), 0.0).astype(BF16) for h in range(heads)],
        axis=0,
    )
    both = dot(weight, vx_ref[pair]) + dot(phi_valid, state_low)
    denominator = jnp.where(lower_lanes(both), swap(both), both)
    return (query, phi_query, phi_valid, key, phi_key, exps, weight, both / denominator, denominator,
            window, linear, valid)


def query_feature_kernel(q_ref, feat_ref, phi_ref):
    for h in range(q_ref.shape[1]):
        phi_ref[0, h] = features(q_ref[0, h], feat_ref[h]).astype(BF16)


def query_features(q, feat, groups):
    slots, all_heads, length, _ = q.shape
    sp = attention_specs(slots, groups, all_heads // groups, length)
    return kernel_call(
        query_feature_kernel,
        [q, feat],
        (),
        grid=(slots, groups),
        in_specs=[sp["q"], sp["feat"]],
        out_specs=sp["phiq"],
        out_shape=jax.ShapeDtypeStruct((slots, all_heads, length, 2 * HD), BF16),
        name="query_features",
    )


def attend_kernel(
    ends_ref, q_ref, kv_ref, phi_ref, phiq_ref, carry_ref, qdoc_ref, kdoc_ref, pdoc_ref,
    attn_ref, vx_ref,
):
    r = pl.program_id(0)
    heads, length = q_ref.shape[1], q_ref.shape[2]
    vx_ref[...] = values_ones(kv_ref[0, 0])
    state = carry_ref[0, 0]
    for b in range(length // WIN):
        if b:
            state = next_state(b, ends_ref, r, state, phi_ref, vx_ref, kdoc_ref)
        out = block_forward(
            b, ends_ref, r, q_ref, kv_ref, phi_ref, phiq_ref, vx_ref, state.astype(BF16), qdoc_ref,
            pdoc_ref,
        )
        attn = out[7]
        low = lower_lanes(attn[:WIN])
        for h in range(0, heads, 2):
            first, second = attn[WIN * h : WIN * h + WIN], attn[WIN * h + WIN : WIN * h + 2 * WIN]
            attn_ref[0, WIN * b : WIN * b + WIN, HD * h : HD * h + 2 * HD] = jnp.where(
                low, first, swap(second)
            ).astype(BF16)


def attention_specs(slots, groups, heads, length):
    ext = length + WIN
    four = lambda r, g, *_: (r, g, 0, 0)
    docs = lambda r, g, *_: (r, 0, 0)
    return dict(
        q=pl.BlockSpec((1, heads, length, HD), four),
        kv=pl.BlockSpec((1, 1, ext, 2 * HD), four),
        phiq=pl.BlockSpec((1, heads, length, 2 * HD), four),
        feat=pl.BlockSpec((heads, HD, 2 * HD), lambda r, g, *_: (g, 0, 0)),
        state=pl.BlockSpec((1, 1, 2 * HD, 2 * HD), four),
        qdoc=pl.BlockSpec((1, length, 2 * HD), docs),
        kdoc=pl.BlockSpec((1, ext, 2 * HD), docs),
        pdoc=pl.BlockSpec((1, length // WIN, 2 * HD), docs),
        tokens=pl.BlockSpec((1, length, heads * HD), lambda r, g, *_: (r, 0, g)),
        fgrad=pl.BlockSpec((1, heads // 2, HD, 2 * HD), four),
    )


def attend(ends, q, kv, phi, phiq, carry, qdoc, kdoc, pdoc, after=()):
    slots, all_heads, length, _ = q.shape
    groups = kv.shape[1]
    heads = all_heads // groups
    sp = attention_specs(slots, groups, heads, length)
    return kernel_call(
        attend_kernel,
        [ends, q, kv, phi, phiq, carry, qdoc, kdoc, pdoc],
        after,
        prefetch=1,
        grid=(slots, groups),
        in_specs=[sp[n] for n in ("q", "kv", "kv", "phiq", "state", "qdoc", "kdoc", "pdoc")],
        out_specs=sp["tokens"],
        scratch=[pltpu.VMEM((length + WIN, 2 * HD), BF16)],
        out_shape=jax.ShapeDtypeStruct((slots, length, all_heads * HD), BF16),
        name="attend",
    )


def attend_back_kernel(
    ends_ref, q_ref, kv_ref, phi_ref, phiq_ref, feat_ref, carry_ref, qdoc_ref, kdoc_ref, pdoc_ref,
    g_ref, gq_ref, gfeat_ref, gphi_ref, gkv_ref, gcarry_ref, vx_ref, gstate_ref, gphiq_ref, gk_ref,
    gv_ref, gqs_ref, gl_ref,
):
    r = pl.program_id(0)
    heads, length = q_ref.shape[1], q_ref.shape[2]
    blocks = length // WIN
    vx_ref[...] = values_ones(kv_ref[0, 0])
    gphi_ref[...] = jnp.zeros_like(gphi_ref)
    gk_ref[...] = jnp.zeros_like(gk_ref)
    gv_ref[...] = jnp.zeros_like(gv_ref)
    scale = HD**-0.5
    state = carry_ref[0, 0]
    for b in range(blocks):
        rows, pair = slice(WIN * b, WIN * b + WIN), slice(WIN * b, WIN * b + 2 * WIN)
        if b:
            state = next_state(b, ends_ref, r, state, phi_ref, vx_ref, kdoc_ref)
        state_low = state.astype(BF16)
        (query, phi_query, phi_valid, key, phi_key, exps, weight, attn, denominator, window, linear,
         valid) = block_forward(
            b, ends_ref, r, q_ref, kv_ref, phi_ref, phiq_ref, vx_ref, state_low, qdoc_ref, pdoc_ref
        )
        grads = []
        for h in range(0, heads, 2):
            g = g_ref[0, rows, HD * h : HD * h + 2 * HD].astype(F32)
            grads += [g, swap(g)]
        grad = jnp.concatenate(grads, axis=0)
        low = lower_lanes(grad)
        grad = jnp.where(low, grad, 0.0)
        g_denom = -jnp.sum(grad * attn, axis=1, keepdims=True)
        gx = (jnp.where(low, grad, g_denom * (1.0 / HD)) / denominator).astype(BF16)
        g_weight = dot(gx, vx_ref[pair], NT)
        part = lambda v, h: v[WIN * h : WIN * h + WIN]
        g_score = jnp.concatenate(
            [(exps[h] * part(g_weight, h)).astype(BF16) for h in range(heads)], axis=0
        )
        g_lin = jnp.concatenate(
            [jnp.where(linear, part(g_weight, h), 0.0).astype(BF16) for h in range(heads)], axis=0
        )
        g_query = dot(g_score, key) * scale
        gk_ref[pair] += dot(g_score, query, TN) * scale
        gv_ref[pair] += dot(weight, gx, TN)
        gphi_ref[0, 0, pair] += dot(g_lin, phi_query, TN)
        from_lin = dot(g_lin, phi_key)
        from_state = dot(gx, state_low, NT)
        gstate_ref[b] = dot(phi_valid, gx, TN)
        for h in range(heads):
            gphiq_ref[h, rows] = part(from_lin, h) + jnp.where(valid, part(from_state, h), 0.0)
            gqs_ref[h, rows] = part(g_query, h)
    for h in range(heads):
        g_logit = features_back(phiq_ref[0, h], gphiq_ref[h])
        gl_ref[h] = g_logit
        gqs_ref[h] += dot(g_logit, feat_ref[h][:, :HD], NT)
    gq_ref[0] = jnp.concatenate([gqs_ref[h] for h in range(heads)], axis=1).astype(BF16)
    for h in range(0, heads, 2):
        gfeat_ref[0, h // 2] = jnp.concatenate(
            [dot(q_ref[0, i], gl_ref[i], TN) for i in (h, h + 1)], axis=1
        )
    later = gstate_ref[blocks - 1]
    for b in range(blocks - 1, 0, -1):
        rows = slice(WIN * (b - 1), WIN * b)
        low_state = later.astype(BF16)
        mask = kdoc_ref[0, rows] == ends_ref[r, b]
        gphi_ref[0, 0, rows] += jnp.where(mask, dot(vx_ref[rows], low_state, NT), 0.0)
        gv_ref[rows] += jnp.where(mask, dot(phi_ref[0, 0, rows], low_state), 0.0)
        keep = (ends_ref[r, b] == ends_ref[r, b - 1]).astype(F32)
        later = gstate_ref[b - 1] + keep * later
    gcarry_ref[0, 0] = later.astype(BF16)
    gv = gv_ref[...]
    gkv_ref[0, 0, :, :HD] = gk_ref[...]
    gkv_ref[0, 0, :, HD:] = gv[:, :HD]


def attend_back(ends, q, kv, phi, phiq, feat, carry, qdoc, kdoc, pdoc, g, after=()):
    slots, all_heads, length, _ = q.shape
    groups = kv.shape[1]
    heads = all_heads // groups
    ext = length + WIN
    sp = attention_specs(slots, groups, heads, length)
    return kernel_call(
        attend_back_kernel,
        [ends, q, kv, phi, phiq, feat, carry, qdoc, kdoc, pdoc, g],
        after,
        prefetch=1,
        grid=(slots, groups),
        in_specs=[
            sp[n]
            for n in ("q", "kv", "kv", "phiq", "feat", "state", "qdoc", "kdoc", "pdoc", "tokens")
        ],
        out_specs=[sp["tokens"], sp["fgrad"], sp["kv"], sp["kv"], sp["state"]],
        scratch=[
            pltpu.VMEM((ext, 2 * HD), BF16),
            pltpu.VMEM((length // WIN, 2 * HD, 2 * HD), F32),
            pltpu.VMEM((heads, length, 2 * HD), F32),
            pltpu.VMEM((ext, HD), F32),
            pltpu.VMEM((ext, 2 * HD), F32),
            pltpu.VMEM((heads, length, HD), F32),
            pltpu.VMEM((heads, length, HD), BF16),
        ],
        out_shape=[
            jax.ShapeDtypeStruct((slots, length, all_heads * HD), BF16),
            jax.ShapeDtypeStruct((slots, all_heads // 2, HD, 2 * HD), F32),
            jax.ShapeDtypeStruct((slots, groups, ext, 2 * HD), F32),
            jax.ShapeDtypeStruct((slots, groups, ext, 2 * HD), F32),
            jax.ShapeDtypeStruct((slots, groups, 2 * HD, 2 * HD), BF16),
        ],
        name="attend_back",
    )


def key_back_kernel(
    ends_ref, kv_ref, phi_ref, feat_ref, later_ref, kdoc_ref, gphi_ref, gkv_ref,
    body_ref, edge_ref, gfeat_ref,
):
    r = pl.program_id(0)
    ext = kv_ref.shape[2]
    body = ext - WIN
    last = ends_ref[r, body // WIN]
    mask = kdoc_ref[0, :body] == last
    keys, vals, feats = [], [], []
    for i in range(2):
        kv, phi = kv_ref[0, i], phi_ref[0, i]
        later = later_ref[0, i].astype(BF16)
        more_phi = jnp.where(mask, dot(values_ones(kv[:body]), later, NT), 0.0)
        more_v = jnp.where(mask, dot(phi[:body], later), 0.0)
        tail = jnp.zeros((WIN, 2 * HD), F32)
        g_phi = gphi_ref[0, i] + jnp.concatenate([more_phi, tail], axis=0)
        g_logit = features_back(phi, g_phi)
        gkv = gkv_ref[0, i]
        keys.append(gkv[:, :HD] + dot(g_logit, feat_ref[i][:, :HD], NT))
        vals.append(gkv[:, HD:] + jnp.concatenate([more_v, tail], axis=0)[:, :HD])
        feats.append(dot(kv[:, :HD], g_logit, TN))
    gfeat_ref[0, 0] = jnp.concatenate(feats, axis=1)
    both = jnp.concatenate(keys + vals, axis=1)
    body_ref[0, 0] = both[WIN:]
    edge_ref[0, 0] = both[:WIN].astype(BF16)


def key_back(ends, kv, phi, feat, later, kdoc, gphi, gkv, after=()):
    slots, groups, ext, _ = kv.shape
    four = lambda r, s, *_: (r, s, 0, 0)
    wide = pl.BlockSpec((1, 2, ext, 2 * HD), four)
    body = pl.BlockSpec((1, 1, ext - WIN, 4 * HD), four)
    edge = pl.BlockSpec((1, 1, WIN, 4 * HD), four)
    sets = groups // 2
    return kernel_call(
        key_back_kernel,
        [ends, kv, phi, feat, later, kdoc, gphi, gkv],
        after,
        prefetch=1,
        grid=(slots, groups // 2),
        in_specs=[
            wide,
            wide,
            pl.BlockSpec((2, HD, 2 * HD), lambda r, s, *_: (s, 0, 0)),
            pl.BlockSpec((1, 2, 2 * HD, 2 * HD), four),
            pl.BlockSpec((1, ext, 2 * HD), lambda r, s, *_: (r, 0, 0)),
            wide,
            wide,
        ],
        out_specs=[body, edge, pl.BlockSpec((1, 1, HD, 2 * HD), four)],
        out_shape=[
            jax.ShapeDtypeStruct((slots, sets, ext - WIN, 4 * HD), F32),
            jax.ShapeDtypeStruct((slots, sets, WIN, 4 * HD), BF16),
            jax.ShapeDtypeStruct((slots, sets, HD, 2 * HD), F32),
        ],
        name="key_back",
    )


LOW = 128


def normalize(values, gain):
    scale = lax.rsqrt(jnp.mean(values * values, axis=-1, keepdims=True) + NORM_EPS)
    return (values * scale * gain).astype(BF16)


def project_kernel(
    sets, q_cols, k_cols, shares, core_ref, own_ref, other_ref, gain_ref, w_ref, a_ref, b_ref, q_ref,
    kv_ref, small_ref
):
    own = pl.program_id(1) // shares == core_ref[0]
    x = normalize(jnp.where(own, own_ref[0], other_ref[0]).astype(F32), gain_ref[...])
    width = q_cols + 2 * k_cols
    small = dot(x, a_ref[...]).astype(BF16)
    small_ref[0] = small
    heads, groups = q_cols // HD, k_cols // HD
    for s in range(sets):
        cols = slice(s * width, (s + 1) * width)
        full = dot(x, w_ref[s]) + ADAPTER_SCALE * dot(small, b_ref[:, cols])
        for h in range(heads):
            q_ref[0, s * heads + h] = full[:, h * HD : h * HD + HD].astype(BF16)
        for g in range(0, groups, 2):
            k = full[:, q_cols + g * HD : q_cols + g * HD + 2 * HD]
            start = q_cols + k_cols + g * HD
            v = full[:, start : start + 2 * HD]
            low = lower_lanes(k)
            kv_ref[0, s * groups + g] = jnp.where(low, k, swap(v)).astype(BF16)
            kv_ref[0, s * groups + g + 1] = jnp.where(low, swap(k), v).astype(BF16)


def project(core, own, other, gain, w, a, b, q_cols, k_cols, after=()):
    slots, share, depth = own.shape
    length = 2 * share
    sets = w.shape[0]
    heads, groups = sets * q_cols // HD, sets * k_cols // HD
    tile = min(256, share)
    shares = share // tile
    token = pl.BlockSpec((1, tile, depth), lambda r, i, *_: (r, lax.rem(i, shares), 0))
    return kernel_call(
        functools.partial(project_kernel, sets, q_cols, k_cols, shares),
        [core, own, other, gain, w, a, b],
        after,
        prefetch=1,
        grid=(slots, length // tile),
        in_specs=[
            token,
            token,
            pl.BlockSpec(gain.shape, lambda r, i, *_: (0, 0)),
            pl.BlockSpec(w.shape, lambda r, i, *_: (0, 0, 0)),
            pl.BlockSpec(a.shape, lambda r, i, *_: (0, 0)),
            pl.BlockSpec(b.shape, lambda r, i, *_: (0, 0)),
        ],
        out_specs=[
            pl.BlockSpec((1, heads, tile, HD), lambda r, i, *_: (r, 0, i, 0)),
            pl.BlockSpec((1, groups, tile, 2 * HD), lambda r, i, *_: (r, 0, i, 0)),
            pl.BlockSpec((1, tile, LOW), lambda r, i, *_: (r, i, 0)),
        ],
        out_shape=[
            jax.ShapeDtypeStruct((slots, heads, length, HD), BF16),
            jax.ShapeDtypeStruct((slots, groups, length, 2 * HD), BF16),
            jax.ShapeDtypeStruct((slots, length, LOW), BF16),
        ],
        cost=pl.CostEstimate(
            flops=2 * slots * length * w.size,
            bytes_accessed=2 * (slots * length * depth + w.size),
            transcendentals=0,
        ),
        name="project",
    )


def halves(share, tile):
    shares = share // tile
    own = lambda r, i, core: (r, core[0] * shares + i, 0)
    other = lambda r, i, core: (r, (1 - core[0]) * shares + i, 0)
    return own, other


def out_project_kernel(core_ref, own_ref, other_ref, w_ref, low_ref, keep_ref, away_ref):
    depth = w_ref.shape[1]
    half = w_ref.shape[2]
    for src, dst in ((own_ref, keep_ref), (other_ref, away_ref)):
        attn = src[0]
        full = dot(attn[:, :half], w_ref[0], NT) + dot(attn[:, half:], w_ref[1], NT)
        dst[0, :, :depth] = full.astype(BF16)
        dst[0, :, depth:] = dot(attn, low_ref[...]).astype(BF16)


def out_project(core, attn, w, low, share):
    slots, length, width = attn.shape
    depth = w.shape[1]
    tile = min(256, share)
    own, other = halves(share, tile)
    out = pl.BlockSpec((1, tile, depth + LOW), lambda r, i, *_: (r, i, 0))
    shape = jax.ShapeDtypeStruct((slots, share, depth + LOW), BF16)
    return kernel_call(
        out_project_kernel,
        [core, attn, attn, w, low],
        (),
        prefetch=1,
        grid=(slots, share // tile),
        in_specs=[
            pl.BlockSpec((1, tile, width), own),
            pl.BlockSpec((1, tile, width), other),
            pl.BlockSpec(w.shape, lambda r, i, *_: (0, 0, 0)),
            pl.BlockSpec(low.shape, lambda r, i, *_: (0, 0)),
        ],
        out_specs=[out, out],
        out_shape=[shape, shape],
        name="out_project",
    )


def middle_kernel(hidden_ref, keep_ref, got_ref, second_ref, gain_ref, mid_ref, normed_ref, low_ref):
    depth = hidden_ref.shape[1]
    total = keep_ref[...].astype(F32) + got_ref[...].astype(F32)
    low = total[:, depth:].astype(BF16)
    low_ref[...] = low
    mid = hidden_ref[...].astype(F32) + total[:, :depth]
    mid = mid + ADAPTER_SCALE * dot(low, second_ref[...])
    mid_ref[...] = mid
    normed_ref[...] = normalize(mid, gain_ref[...])


def tokens_call(kernel, tiled, whole, outs, name, prefetch=(), sums=(), tile=256, after=()):
    tokens = tiled[0].shape[0]
    tile = min(tile, tokens)
    rows = lambda v: pl.BlockSpec((tile, v.shape[1]), lambda i, *_: (i, 0))
    full = lambda v: pl.BlockSpec(v.shape, lambda i, *_: (0, 0))
    shapes = [jax.ShapeDtypeStruct((tokens, width), kind) for width, kind in outs]
    totals = [jax.ShapeDtypeStruct(v, F32) for v in sums]
    return kernel_call(
        kernel,
        [*prefetch, *tiled, *whole],
        after,
        prefetch=len(prefetch),
        grid=(tokens // tile,),
        in_specs=[rows(v) for v in tiled] + [full(v) for v in whole],
        out_specs=[rows(v) for v in shapes] + [full(v) for v in totals],
        out_shape=shapes + totals,
        name=name,
    )


def norm_back(values, gain, grad):
    scale = lax.rsqrt(jnp.mean(values * values, axis=-1, keepdims=True) + NORM_EPS)
    scaled = gain * grad
    shared = scale * scale * scale * jnp.mean(values * scaled, axis=-1, keepdims=True)
    return scale, scale * scaled - values * shared


def pair_kernel(a_ref, b_ref, out_ref):
    out_ref[...] = a_ref[...] + b_ref[...].astype(F32)


def sum_kernel(*refs):
    refs[-1][...] = sum(r[...].astype(F32) for r in refs[:-1]).astype(BF16)


def branch_kernel(slot_len, live_ref, mid_ref, a_ref, b_ref, c_ref, cot_ref, gain_ref, grad_ref, low_ref):
    grad = a_ref[...].astype(F32) + b_ref[...].astype(F32) + c_ref[...].astype(F32)
    tile = mid_ref.shape[0]
    token = pl.program_id(0) * tile + lax.broadcasted_iota(jnp.int32, (tile, 1), 0)
    live = token < live_ref[0] * slot_len
    cot = jnp.where(live, cot_ref[...].astype(F32), 0.0)
    total = cot + norm_back(mid_ref[...], gain_ref[...], grad)[1]
    grad_ref[...] = total
    low_ref[...] = total.astype(BF16)


def attn_grad_kernel(
    shares, core_ref, own_ref, other_ref, attn_ref, w_ref, second_ref, first_ref, grad_ref, sum_ref
):
    own = pl.program_id(1) // shares == core_ref[0]
    x = jnp.where(own, own_ref[0], other_ref[0])
    low = (ADAPTER_SCALE * dot(x, second_ref[...], NT)).astype(BF16)
    half = w_ref.shape[2]
    first = first_ref[...]
    for s in range(2):
        cols = slice(s * half, (s + 1) * half)
        grad_ref[0, :, cols] = (dot(x, w_ref[s]) + dot(low, first[cols], NT)).astype(BF16)

    @pl.when((pl.program_id(0) == 0) & (pl.program_id(1) == 0))
    def _():
        sum_ref[...] = jnp.zeros_like(sum_ref)

    sum_ref[...] += dot(low, attn_ref[0], TN)


def attn_grad(core, own, other, attn, w, second, first):
    slots, share, depth = own.shape
    length = 2 * share
    width = attn.shape[2]
    tile = min(256, share)
    shares = share // tile
    token = pl.BlockSpec((1, tile, depth), lambda r, i, *_: (r, lax.rem(i, shares), 0))
    wide = pl.BlockSpec((1, tile, width), lambda r, i, *_: (r, i, 0))
    full = lambda v: pl.BlockSpec(v.shape, lambda r, i, *_: (0,) * v.ndim)
    total = jax.ShapeDtypeStruct((LOW, width), F32)
    return kernel_call(
        functools.partial(attn_grad_kernel, shares),
        [core, own, other, attn, w, second, first],
        (),
        prefetch=1,
        grid=(slots, length // tile),
        in_specs=[token, token, wide, full(w), full(second), full(first)],
        out_specs=[wide, full(total)],
        out_shape=[jax.ShapeDtypeStruct(attn.shape, BF16), total],
        name="attn_grad",
    )


def normed_grad_kernel(
    q_cols, shares, core_ref, q_own_ref, q_other_ref, kv_own_ref, kv_other_ref, s_own_ref, s_other_ref,
    back_ref, w_ref, b_ref, keep_ref, away_ref, sum_ref
):
    depth, width = w_ref.shape[1:]
    core, step = core_ref[0], pl.program_id(1)

    @pl.when((pl.program_id(0) == 0) & (step == 0))
    def _():
        sum_ref[...] = jnp.zeros_like(sum_ref)

    sides = (
        (q_own_ref, kv_own_ref, s_own_ref, keep_ref, core),
        (q_other_ref, kv_other_ref, s_other_ref, away_ref, 1 - core),
    )
    for q_ref, kv_ref, s_ref, out_ref, share in sides:
        tile = q_ref.shape[1]
        last = (share * shares + step == 2 * shares - 1).astype(F32)
        full = low = None
        for s in range(2):
            kv = kv_ref[0, s]
            edge = back_ref[0, s].astype(F32) * last
            if tile > WIN:
                edge = jnp.concatenate([jnp.zeros((tile - WIN, kv.shape[1]), F32), edge], axis=0)
            kv = (kv + edge).astype(BF16)
            q = q_ref[0, :, s * q_cols : (s + 1) * q_cols]
            grads = jnp.concatenate([q, kv], axis=1)
            part = dot(grads, w_ref[s], NT)
            small = dot(grads, b_ref[:, s * width : (s + 1) * width], NT)
            full = part if full is None else full + part
            low = small if low is None else low + small
            sum_ref[s] += dot(s_ref[0], grads, TN)
        out_ref[0, :, :depth] = full.astype(BF16)
        out_ref[0, :, depth:] = (ADAPTER_SCALE * low).astype(BF16)


def normed_grad(core, q, kv, small, back, w, b, q_cols, share):
    slots, length, q_width = q.shape
    sets, depth, width = w.shape
    tile = min(256, share)
    shares = share // tile
    own, other = halves(share, tile)
    four = lambda f: (lambda r, i, core: (r, 0, f(r, i, core)[1], 0))
    out = pl.BlockSpec((1, tile, depth + LOW), lambda r, i, *_: (r, i, 0))
    shape = jax.ShapeDtypeStruct((slots, share, depth + LOW), BF16)
    total = jax.ShapeDtypeStruct((sets, LOW, width), F32)
    kv_block = (1, sets, tile, kv.shape[3])
    return kernel_call(
        functools.partial(normed_grad_kernel, q_cols, shares),
        [core, q, q, kv, kv, small, small, back, w, b],
        (),
        prefetch=1,
        grid=(slots, shares),
        in_specs=[
            pl.BlockSpec((1, tile, q_width), own),
            pl.BlockSpec((1, tile, q_width), other),
            pl.BlockSpec(kv_block, four(own)),
            pl.BlockSpec(kv_block, four(other)),
            pl.BlockSpec((1, tile, LOW), own),
            pl.BlockSpec((1, tile, LOW), other),
            pl.BlockSpec((1, sets, WIN, kv.shape[3]), lambda r, i, *_: (r, 0, 0, 0)),
            pl.BlockSpec(w.shape, lambda r, i, *_: (0, 0, 0)),
            pl.BlockSpec(b.shape, lambda r, i, *_: (0, 0)),
        ],
        out_specs=[out, out, pl.BlockSpec(total.shape, lambda r, i, *_: (0, 0, 0))],
        out_shape=[shape, shape, total],
        name="normed_grad",
    )


def finish_kernel(keep_ref, got_ref, hidden_ref, mid_ref, gain_ref, first_ref, out_ref, sum_ref):
    depth = hidden_ref.shape[1]
    total = keep_ref[...].astype(F32) + got_ref[...].astype(F32)
    low = total[:, depth:].astype(BF16)
    grad = total[:, :depth] + dot(low, first_ref[...])
    values, gain = hidden_ref[...].astype(F32), gain_ref[...]
    scale, back = norm_back(values, gain, grad)
    out_ref[...] = (mid_ref[...] + back).astype(BF16)

    @pl.when(pl.program_id(0) == 0)
    def _():
        sum_ref[...] = jnp.zeros_like(sum_ref)

    sum_ref[...] += dot(low, (values * scale * gain).astype(BF16), TN)


def sums_kernel(rows, seqs, heads, part_ref, pack_ref, out_ref, cols_ref, *scratch):
    a1, a2, a3, c2, c3, b1, b2, b3, e2, e3, send_sem, recv_sem = scratch
    place = {a: lax.axis_index(a) for a in ("row", "seq", "head")}
    counts = {"row": rows, "seq": seqs, "head": heads}
    x_place = place["head"] // 2
    peers = [
        (a, {a: lax.rem(place[a] + d, counts[a])}) for a in counts for d in range(1, counts[a])
    ]
    barrier = pltpu.get_barrier_semaphore()
    for _, peer in peers:
        pl.semaphore_signal(barrier, inc=1, device_id=peer, device_id_type=pl.DeviceIdType.MESH)
    pl.semaphore_wait(barrier, len(peers))
    used = [0]

    def remote(src, dst, device):
        n = used[0]
        used[0] += 1
        return pltpu.make_async_remote_copy(
            src_ref=src, dst_ref=dst, send_sem=send_sem.at[n], recv_sem=recv_sem.at[n],
            device_id=device, device_id_type=pl.DeviceIdType.MESH,
        )

    def exchange(axis, parts, slots, packs, pack_slots):
        me, size = place[axis], counts[axis]
        copies = []
        for d in range(1, size):
            to = lax.rem(me + d, size)
            copies.append(remote(parts.at[to], slots.at[me], {axis: to}))
            if pack_slots is not None:
                copies.append(remote(packs, pack_slots.at[me], {axis: to}))
        return copies

    def add_up(ref, size):
        total = ref[0].astype(F32)
        for i in range(1, size):
            total = total + ref[i].astype(F32)
        return total

    b1[0] = pack_ref[1 - x_place].astype(BF16)
    copies = exchange("head", part_ref, a1, None, None)
    copies.append(remote(b1.at[0], b1.at[1], {"head": lax.rem(place["head"] + 2, heads)}))
    for copy in copies:
        copy.start()
    a1[place["head"]] = part_ref[place["head"]]
    for copy in copies:
        copy.wait()
    stages = (
        ("seq", add_up(a1, heads), pack_ref[x_place] + b1[1].astype(F32), c2, a2, e2, b2),
        ("row", None, None, c3, a3, e3, b3),
    )
    for axis, part, pack, held, slots, pack_held, pack_slots in stages:
        if part is None:
            part, pack = add_up(a2, seqs), add_up(b2, seqs)
        held[...] = part
        pack_held[...] = pack.astype(BF16)
        copies = exchange(axis, held, slots, pack_held, pack_slots)
        for copy in copies:
            copy.start()
        slots[place[axis]] = held[place[axis]]
        pack_slots[place[axis]] = pack_held[...]
        for copy in copies:
            copy.wait()
    out_ref[...] = add_up(a3, rows)
    cols_ref[...] = add_up(b3, rows)


def final_sums(part, pack):
    rows, seqs, heads = (lax.axis_size(a) for a in ("row", "seq", "head"))
    low, width = part.shape[3:]
    count, lanes = pack.shape[1:]
    place = pl.BlockSpec(memory_space=pltpu.VMEM)
    copies = heads + 2 * (seqs - 1) + 2 * (rows - 1)
    return pl.pallas_call(
        functools.partial(sums_kernel, rows, seqs, heads),
        in_specs=[place, place],
        out_specs=[place, place],
        out_shape=[
            jax.ShapeDtypeStruct((low, width), F32),
            jax.ShapeDtypeStruct((count, lanes), F32),
        ],
        scratch_shapes=[
            pltpu.VMEM((heads, seqs, rows, low, width), F32),
            pltpu.VMEM((seqs, rows, low, width), F32),
            pltpu.VMEM((rows, low, width), F32),
            pltpu.VMEM((seqs, rows, low, width), F32),
            pltpu.VMEM((rows, low, width), F32),
            pltpu.VMEM((2, count, lanes), BF16),
            pltpu.VMEM((seqs, count, lanes), BF16),
            pltpu.VMEM((rows, count, lanes), BF16),
            pltpu.VMEM((count, lanes), BF16),
            pltpu.VMEM((count, lanes), BF16),
            pltpu.SemaphoreType.DMA((copies,)),
            pltpu.SemaphoreType.DMA((copies,)),
        ],
        compiler_params=pltpu.CompilerParams(
            collective_id=1, has_side_effects=True, vmem_limit_bytes=32 * 2**20
        ),
        name="final_sums",
    )(part, pack)


def local(
    hidden_in,
    grad_out,
    live_rows,
    doc_starts,
    norm_attn,
    norm_ffn,
    query_weight,
    key_weight,
    value_weight,
    out_weight,
    gate_weight,
    up_weight,
    down_weight,
    query_adapt_in,
    query_adapt_out,
    key_adapt_in,
    key_adapt_out,
    value_adapt_in,
    value_adapt_out,
    outproj_adapt_in,
    projection_adapter_second,
    query_feature,
    key_feature,
):
    rows, seqs, heads = lax.axis_size("row"), lax.axis_size("seq"), lax.axis_size("head")
    head = lax.axis_index("head")
    core = lax.rem(head, 2)
    x_count = heads // 2
    x_place = head // 2
    slots, share_len, model_dim = hidden_in.shape
    piece_len = 2 * share_len
    pieces = seqs * x_count
    piece = lax.axis_index("seq") * x_count + x_place
    blocks = piece_len // WIN
    ext_len = piece_len + WIN
    q_cols, k_cols = query_weight.shape[1], key_weight.shape[1]
    ff_cols = gate_weight.shape[1]

    def in_order(own, other):
        first = jnp.where(core == 0, own, other)
        second = jnp.where(core == 0, other, own)
        return jnp.concatenate([first, second], axis=1)

    def own_half(both):
        return lax.dynamic_slice_in_dim(both, core * share_len, share_len, 1)

    def other_half(both):
        return lax.dynamic_slice_in_dim(both, (1 - core) * share_len, share_len, 1)

    qkv_shard = jnp.concatenate([query_weight, key_weight, value_weight], axis=1)
    out_shard = out_weight.T
    down_shard = down_weight.T
    unit = ff_cols // sum(FF_CHUNKS)
    bounds = [unit * sum(FF_CHUNKS[:j]) for j in range(len(FF_CHUNKS) + 1)]
    ffn_shards = [
        jnp.concatenate([w[:, lo:hi] for w in (gate_weight, up_weight, down_shard)], axis=1)
        for lo, hi in zip(bounds[:-1], bounds[1:])
    ]
    ffn_later = [
        lax.all_gather(v, ("row", "seq"), axis=0, tiled=True) for v in ffn_shards[1:]
    ]
    own_smalls = [
        query_feature, key_feature, query_adapt_out, key_adapt_out, value_adapt_out, outproj_adapt_in
    ]
    (qkv_mat, out_mat, first_mat), other_smalls, (hidden_other, cot_mine, cot_away) = gather(
        [qkv_shard, out_shard, ffn_shards[0]],
        [True, True, False],
        [
            (0, (0, qkv_shard.shape[1]), True, 0),
            (1, (0, out_shard.shape[1]), True, 0),
            (2, (0, ffn_shards[0].shape[1]), True, rows * seqs),
        ],
        own_smalls,
        hidden_in,
        grad_out,
    )
    ffn_mats = [first_mat] + ffn_later

    def both(i, axis):
        own, other = own_smalls[i], other_smalls[i]
        return jnp.concatenate(
            [jnp.where(x_place == 0, own, other), jnp.where(x_place == 0, other, own)], axis=axis
        )

    query_feat_all, key_feat_all = both(0, 0), both(1, 0)
    q_out, k_out, v_out = both(2, 1), both(3, 1), both(4, 1)
    o_in = both(5, 0)

    doc_ids = jnp.cumsum(doc_starts, axis=1)
    padded_docs = jnp.concatenate(
        [jnp.full((slots, WIN + 1), -1, jnp.int32), doc_ids], axis=1
    )
    piece_docs = padded_docs[:, ::piece_len][:, : pieces + 1]
    near_docs = lax.dynamic_slice_in_dim(padded_docs, piece * piece_len, ext_len + 1, 1)
    end_docs = near_docs[:, ::WIN][:, : blocks + 1]
    carry_doc = end_docs[:, 0]
    next_doc = end_docs[:, blocks]
    key_docs = near_docs[:, 1:]
    key_doc_lanes = jnp.broadcast_to(key_docs[:, :, None], (slots, ext_len, 2 * HD))
    query_doc_lanes = key_doc_lanes[:, WIN:]
    doc_blocks = key_docs.reshape(slots, blocks + 1, WIN)
    pair_docs = jnp.concatenate([doc_blocks[:, :-1], doc_blocks[:, 1:]], axis=2)

    def from_pieces(block):
        held = []
        for d, start in enumerate((block, flip_x(block))):
            for l in range(seqs):
                if l:
                    start = shift(start, "seq", 1)
                source = (
                    lax.rem(lax.axis_index("seq") - l + seqs, seqs) * x_count
                    + lax.rem(x_place + d, x_count)
                )
                held.append((source, start))
        return held[1:]

    gain_attn = norm_attn.astype(F32)[None]
    gain_ffn = norm_ffn.astype(F32)[None]
    core_index = core.astype(jnp.int32).reshape(1)
    flat_tokens = lambda v: v.reshape(-1, v.shape[-1])

    set_cols = q_cols + 2 * k_cols
    adapt_in_all = jnp.concatenate([query_adapt_in, key_adapt_in, value_adapt_in], axis=1)

    def by_sets(parts):
        return jnp.concatenate(
            [v[:, d * (v.shape[1] // 2) : (d + 1) * (v.shape[1] // 2)] for d in range(2) for v in parts],
            axis=1,
        )

    def diagonal(parts):
        rows = [
            [p if i == j else jnp.zeros((RANK, q.shape[1]), BF16) for j, q in enumerate(parts)]
            for i, p in enumerate(parts)
        ]
        return jnp.concatenate([by_sets(r) for r in rows], axis=0)

    pad_rows = lambda v: jnp.pad(v, ((0, LOW - v.shape[0]), (0, 0)))
    pad_cols = lambda v: jnp.pad(v, ((0, 0), (0, LOW - v.shape[1])))
    adapt_in_all = pad_cols(adapt_in_all)
    adapt_out_all = pad_rows(diagonal([q_out, k_out, v_out]))
    second = pad_rows(projection_adapter_second)
    o_in = pad_cols(o_in)
    query, kv_own, small = project(
        core_index, hidden_in, hidden_other, gain_attn, qkv_mat, adapt_in_all, adapt_out_all, q_cols,
        k_cols,
    )

    def along_pieces(block, distance):
        route = []
        for p in range(pieces):
            to = p + distance
            if 0 <= to < pieces:
                for c in range(2):
                    route.append((2 * p + c, 2 * to + c))
        return lax.ppermute(block, ("seq", "head"), route)

    kv = jnp.concatenate([along_pieces(kv_own[:, :, -WIN:], 1), kv_own], axis=2)
    doubled = lambda feat: jnp.concatenate([feat, -feat], axis=2)
    query_feat, key_feat = doubled(query_feat_all), doubled(key_feat_all)
    phi_key, end_state = key_state(end_docs, kv, key_feat, key_doc_lanes)
    carry = jnp.zeros(end_state.shape, F32)
    for source, part in from_pieces(end_state):
        after = lax.dynamic_index_in_dim(piece_docs, source + 1, 1, keepdims=False)
        keep = (source < piece) & (after == carry_doc)
        carry = carry + jnp.where(keep[:, None, None, None], part.astype(F32), 0.0)
    phi_query = query_features(query, query_feat, kv.shape[1])
    attn = attend(
        end_docs, query, kv, phi_key, phi_query, carry, query_doc_lanes, key_doc_lanes, pair_docs
    )

    keep, away = out_project(core_index, attn, out_mat, o_in, share_len)
    mid_rows, nmid, low_mix = tokens_call(
        middle_kernel,
        [flat_tokens(v) for v in (hidden_in, keep, flip_core(away))],
        [second, gain_ffn],
        [(model_dim, F32), (model_dim, BF16), (LOW, BF16)],
        "middle",
    )

    nmid_x = flip_x(nmid)

    def chip_tokens(own):
        return own, flip_core(own)

    def sum_away(own, other):
        return (own.astype(F32) + flip_core(other).astype(F32)).astype(BF16)

    x_mine = chip_tokens(nmid)
    c_mine, c_away = flat_tokens(cot_mine), flat_tokens(cot_away)
    run = lambda x, c, w, before=(), after=(): ffn(
        x, c, w, live_rows, share_len, slots, before, after
    )
    mine = run(x_mine, c_mine, ffn_mats[:2])
    x_away = chip_tokens(hold(nmid_x, (mine[0],)))
    away = run(x_away, c_away, ffn_mats[:-1])
    away = run(x_away, c_away, ffn_mats[-1:], away)
    gn_there = sum_away(*away[:2])
    gn_back = flip_x(gn_there)
    gn_own, gn_other, y_own, y_other = run(
        x_mine, c_mine, ffn_mats[2:], mine, (gn_there,)
    )
    y_there = sum_away(*away[2:])
    y_back = flip_x(y_there)
    grad_mid, branch = tokens_call(
        functools.partial(branch_kernel, share_len),
        [mid_rows, gn_own, flip_core_parts(gn_other, 4), gn_back, flat_tokens(grad_out)],
        [gain_ffn],
        [(model_dim, F32), (model_dim, BF16)],
        "branch",
        prefetch=[live_rows],
    )

    shaped = lambda v: v.reshape(slots, share_len, -1)
    grad_attn, sum_o_in = attn_grad(
        core_index, shaped(branch), shaped(flip_core(branch)), attn, out_mat, second, o_in
    )
    sum_o_in = sum_o_in[:RANK]
    sum_o_out = ADAPTER_SCALE * dot(low_mix, branch, TN)[:RANK]

    grad_query, feat_query, gphi, gkv, grad_carry = attend_back(
        end_docs, query, kv, phi_key, phi_query, query_feat, carry, query_doc_lanes, key_doc_lanes,
        pair_docs, grad_attn, (y_there,),
    )
    block_out = tokens_call(
        sum_kernel, [mid_rows, y_own, flip_core(y_other), y_back], [], [(model_dim, BF16)], "sum_y",
        after=(grad_carry,),
    )[0]
    later = jnp.zeros(grad_carry.shape, F32)
    for source, part in from_pieces(grad_carry):
        start = lax.dynamic_index_in_dim(piece_docs, source, 1, keepdims=False)
        keep = (source > piece) & (start == next_doc)
        later = later + jnp.where(keep[:, None, None, None], part.astype(F32), 0.0)
    grad_body, grad_edge, feat_key = key_back(
        end_docs, kv, phi_key, key_feat, later, key_doc_lanes, gphi, gkv, (block_out,)
    )
    sum_q_feat = jnp.sum(feat_query, axis=0).reshape(2, -1, 2 * HD)
    sum_k_feat = jnp.sum(feat_key, axis=0).reshape(2, -1, 2 * HD)

    keep, away, outs = normed_grad(
        core_index, grad_query, grad_body, small, along_pieces(grad_edge, -1), qkv_mat, adapt_out_all,
        q_cols, share_len,
    )
    outs = ADAPTER_SCALE * outs
    outs = [
        outs[:, :RANK, :q_cols],
        outs[:, RANK : 2 * RANK, q_cols : q_cols + k_cols],
        outs[:, 2 * RANK : 3 * RANK, q_cols + k_cols :],
    ]
    grad_hidden, sum_in = tokens_call(
        finish_kernel,
        [flat_tokens(keep), flat_tokens(flip_core(away)), flat_tokens(hidden_in), grad_mid],
        [gain_attn, adapt_in_all.T],
        [(model_dim, BF16)],
        "finish",
        sums=[(LOW, model_dim)],
    )
    grad_hidden = grad_hidden.reshape(hidden_in.shape)
    sum_in = sum_in[: 3 * RANK]

    by_rows = jnp.concatenate([sum_in, sum_o_out], axis=0)
    width = model_dim // (rows * seqs * heads)
    by_rows = by_rows.reshape(4 * RANK, rows, seqs, heads, width).transpose(3, 2, 1, 0, 4)

    def lanes_of(v):
        v = v.reshape(2, RANK, -1, 2 * HD).transpose(0, 2, 1, 3)
        return v.reshape(2, -1, 2 * HD)

    o_sets = jnp.stack([sum_o_in[:, :q_cols], sum_o_in[:, q_cols:]])
    packed = [lanes_of(v) for v in outs + [o_sets]] + [sum_q_feat, sum_k_feat]
    sizes = [v.shape[1] for v in packed]
    packed = jnp.concatenate(packed, axis=1)
    in_parts, packed = final_sums(by_rows, packed)
    in_parts = in_parts.reshape(4, RANK, width)
    cols, at = [], 0
    for size in sizes:
        cols.append(packed[at : at + size])
        at += size
    from_lanes = lambda v: v.reshape(-1, RANK, 2 * HD).transpose(1, 0, 2).reshape(RANK, -1)
    from_pairs = lambda v: v.reshape(-1, HD, 2, HD).transpose(0, 2, 1, 3).reshape(-1, HD, HD)
    cols = [from_lanes(v) for v in cols[:4]] + [from_pairs(v) for v in cols[4:]]
    cols[3] = cols[3].T

    return (
        block_out.reshape(hidden_in.shape),
        grad_hidden,
        in_parts[0].T,
        cols[0],
        in_parts[1].T,
        cols[1],
        in_parts[2].T,
        cols[2],
        cols[3],
        in_parts[3],
        cols[4],
        cols[5],
    )


def solution(mesh):
    return jax.shard_map(
        local,
        mesh=mesh,
        in_specs=(
            P("row", ("seq", "head"), None),
            P("row", ("seq", "head"), None),
            P("row"),
            P("row", None),
            P(),
            P(),
            P(("row", "seq"), "head"),
            P(("row", "seq"), "head"),
            P(("row", "seq"), "head"),
            P("head", ("row", "seq")),
            P(("row", "seq"), "head"),
            P(("row", "seq"), "head"),
            P("head", ("row", "seq")),
            P(),
            P(None, "head"),
            P(),
            P(None, "head"),
            P(),
            P(None, "head"),
            P("head", None),
            P(),
            P("head", None, None),
            P("head", None, None),
        ),
        out_specs=(
            P("row", ("seq", "head"), None),
            P("row", ("seq", "head"), None),
            P(("row", "seq", "head"), None),
            P(None, "head"),
            P(("row", "seq", "head"), None),
            P(None, "head"),
            P(("row", "seq", "head"), None),
            P(None, "head"),
            P("head", None),
            P(None, ("row", "seq", "head")),
            P("head", None, None),
            P("head", None, None),
        ),
        check_vma=False,
    )
```

```python
import functools

import jax
import jax.numpy as jnp
from jax import lax
from jax.experimental import pallas as pl
from jax.experimental.pallas import tpu as pltpu
from jax.sharding import PartitionSpec as P

HD = 64
RANK = 8
WIN = 64
FF_CHUNKS = (3, 4, 6, 3)

NORM_EPS = 1e-05
ADAPTER_SCALE = 2.0
F32 = jnp.float32
NT = ((1,), (1,))
TN = ((0,), (0,))
BF16 = jnp.bfloat16


def shift(block, axis, distance):
    size = lax.axis_size(axis)
    return lax.ppermute(block, axis, [(i, (i + distance) % size) for i in range(size)])


def flip_core(block):
    return lax.ppermute(block, "head", [(i, i ^ 1) for i in range(lax.axis_size("head"))])


def flip_core_parts(block, parts):
    size = block.shape[0] // parts
    return jnp.concatenate(
        [flip_core(block[i * size : (i + 1) * size]) for i in range(parts)], axis=0
    )


def flip_x(block):
    return lax.ppermute(block, "head", [(i, i ^ 2) for i in range(lax.axis_size("head"))])


def kernel_call(
    kernel, args, after, *, grid, in_specs, out_specs, out_shape, name, prefetch=0, scratch=(), cost=None
):
    count = len(args)

    def body(*refs):
        kernel(*refs[:count], *refs[count + len(after) :])

    return pl.pallas_call(
        body,
        grid_spec=pltpu.PrefetchScalarGridSpec(
            num_scalar_prefetch=prefetch,
            grid=grid,
            in_specs=list(in_specs) + [pl.BlockSpec(memory_space=pl.ANY)] * len(after),
            out_specs=out_specs,
            scratch_shapes=list(scratch),
        ),
        out_shape=out_shape,
        compiler_params=pltpu.CompilerParams(vmem_limit_bytes=60 * 2**20),
        cost_estimate=cost and pl.CostEstimate(
            flops=cost.flops // 4, bytes_accessed=cost.bytes_accessed // 4, transcendentals=0
        ),
        name=name,
    )(*args, *after)


def copy_kernel(src_ref, dst_ref):
    dst_ref[...] = src_ref[...]


def hold(value, after):
    flat = value.reshape(-1, value.shape[-1])
    tile = min(256, flat.shape[0])
    block = pl.BlockSpec((tile, flat.shape[1]), lambda i: (i, 0))
    held = kernel_call(
        copy_kernel, [flat], after, grid=(flat.shape[0] // tile,), in_specs=[block], out_specs=block,
        out_shape=jax.ShapeDtypeStruct(flat.shape, flat.dtype), name="hold",
    )
    return held.reshape(value.shape)


def dot(a, b, dims=((1,), (0,))):
    return lax.dot_general(a, b, (dims, ((), ())), preferred_element_type=F32)


def tie(value, *after):
    return lax.optimization_barrier((value,) + after)[0]


def rms_scaled(values, gain_vec):
    return (
        values * lax.rsqrt(jnp.mean(values * values, axis=-1, keepdims=True) + NORM_EPS) * gain_vec
    )


def rms_back(values, gain_vec, grad_in):
    factor = lax.rsqrt(jnp.mean(values * values, axis=-1, keepdims=True) + NORM_EPS)
    scaled = gain_vec * grad_in
    return factor * scaled - values * factor**3 * jnp.mean(values * scaled, axis=-1, keepdims=True)


def scatter_sum(parts, axis):
    size, place = lax.axis_size(axis), lax.axis_index(axis)
    total = lax.dynamic_index_in_dim(parts, place, 0, keepdims=False)
    for k in range(1, size):
        away = lax.dynamic_index_in_dim(parts, lax.rem(place + k, size), 0, keepdims=False)
        total = total + shift(away, axis, k)
    return total


def full_sum(part, axis):
    size = lax.axis_size(axis)
    step = 1
    while step < size:
        sent = part.astype(BF16)
        got = lax.ppermute(sent, axis, [(i, i ^ step) for i in range(size)])
        part = sent.astype(F32) + got.astype(F32)
        step *= 2
    return part


def gather_plan(rows, seqs, weights):
    free = {"row": 0.0, "seq": 0.0, "x": 0.0}
    running = []
    plan = []

    def begin(now, starts):
        for t in starts:
            w, link = t[0], t[1]
            end = max(now, free[link]) + weights[w][0]
            free[link] = end
            running.append((end, len(plan), len(running), t))
        return starts

    def spread(w, k, l):
        starts = []
        row_first = weights[w][2]
        if (l == 0 or not row_first) and k + 1 < rows:
            starts.append((w, "row", k + 1, l))
        if (k == 0 or row_first) and l + 1 < seqs:
            starts.append((w, "seq", k, l + 1))
        if weights[w][1]:
            starts.append((w, "x", k, l))
        return starts

    first = [t for w in range(len(weights)) if weights[w][3] == 0 for t in spread(w, 0, 0)]
    plan.append((None, begin(0.0, first)))
    done = 0
    while running:
        event = min(running)
        running.remove(event)
        now, t = event[0], event[3]
        done += 1
        starts = [] if t[1] == "x" else spread(t[0], t[2], t[3])
        for w in range(len(weights)):
            if weights[w][3] == done:
                starts = starts + spread(w, 0, 0)
        plan.append((t, begin(now, starts)))
    return plan


def gather_kernel(plan, rows, seqs, parts, over_x, small_count, *refs):
    count = len(over_x)
    inputs, refs = refs[: count + small_count + 2], refs[count + small_count + 2 :]
    shards, smalls = inputs[:count], inputs[count : count + small_count]
    hidden, cot = inputs[count + small_count :]
    wholes, refs = refs[:count], refs[count:]
    small_outs, refs = refs[:small_count], refs[small_count:]
    hidden_out, cot_mine, cot_away = refs[:3]
    send_sem, recv_sem, copy_sem, more_send, more_recv = refs[3:]
    row, seq, head = lax.axis_index("row"), lax.axis_index("seq"), lax.axis_index("head")
    x_place = head // 2
    across = {"head": lax.rem(head + 2, 4)}
    partner = {"head": head + 1 - 2 * lax.rem(head, 2)}
    away = {
        "row": {"row": lax.rem(row + 1, rows)},
        "seq": {"seq": lax.rem(seq + 1, seqs)},
        "x": across,
    }
    barrier = pltpu.get_barrier_semaphore()
    sources = (
        {"row": lax.rem(row + rows - 1, rows)},
        {"seq": lax.rem(seq + seqs - 1, seqs)},
        across,
        partner,
    )
    for source in sources:
        pl.semaphore_signal(
            barrier, inc=1, device_id=source, device_id_type=pl.DeviceIdType.MESH
        )
    pl.semaphore_wait(barrier, len(sources))

    def slot(p, k, l):
        w, columns = parts[p][0], pl.ds(*parts[p][1])
        depth = shards[w].shape[0]
        place = lax.rem(row - k + rows, rows) * seqs + lax.rem(seq - l + seqs, seqs)
        at = pl.ds(pl.multiple_of(place * depth, depth), depth)
        return wholes[w].at[x_place, at, columns] if over_x[w] else wholes[w].at[at, columns]

    number = {}
    last_x = 0
    for i, (event, starts) in enumerate(plan):
        for t in starts:
            number[t] = len(number)
            if t[1] == "x":
                last_x = i

    def remote(src, dst, send, recv, device):
        return pltpu.make_async_remote_copy(
            src_ref=src, dst_ref=dst, send_sem=send, recv_sem=recv, device_id=device,
            device_id_type=pl.DeviceIdType.MESH,
        )

    def transfer(t):
        w, link, k, l = t
        source = {"row": (k - 1, l), "seq": (k, l - 1), "x": (k, l)}[link]
        dst = slot(w, *source)
        n = number[t]
        src = shards[parts[w][0]].at[:, pl.ds(*parts[w][1])] if source == (0, 0) else dst
        return remote(src, dst, send_sem.at[n], recv_sem.at[n], away[link])

    def more(i, src, dst, device):
        return remote(src, dst, more_send.at[i], more_recv.at[i], device)

    early = [more(i, a, b, across) for i, (a, b) in enumerate(zip(smalls, small_outs))]
    early.append(more(small_count, hidden, hidden_out, partner))
    early.append(more(small_count + 1, cot, cot_mine.at[1], partner))
    cot_x = more(small_count + 2, cot, cot_away.at[0], across)
    cot_last = more(small_count + 3, cot_away.at[0], cot_away.at[1], partner)
    own = [
        pltpu.make_async_copy(
            shards[w].at[:, pl.ds(*columns)], slot(p, 0, 0), copy_sem.at[p]
        )
        for p, (w, columns) in enumerate(parts)
    ] + [pltpu.make_async_copy(cot, cot_mine.at[0], copy_sem.at[len(parts)])]
    for i, (event, starts) in enumerate(plan):
        if event is not None:
            transfer(event).wait_recv()
        for t in starts:
            transfer(t).start()
        if event is None:
            for copy in [cot_x] + early + own:
                copy.start()
        if i == last_x:
            cot_x.wait()
            cot_last.start()
    for t in number:
        transfer(t).wait_send()
    for copy in early + own + [cot_last]:
        copy.wait()


def gather(shards, over_x, pieces, smalls, hidden, cot):
    rows, seqs = lax.axis_size("row"), lax.axis_size("seq")
    plan = gather_plan(
        rows,
        seqs,
        [(float(shards[w].shape[0] * c[1]), over_x[w], first, later) for w, c, first, later in pieces],
    )
    parts = [(w, c) for w, c, _, _ in pieces]
    total = sum(len(starts) for _, starts in plan)
    shapes = []
    for shard, x in zip(shards, over_x):
        depth, width = shard.shape
        whole = (rows * seqs * depth, width)
        shapes.append(jax.ShapeDtypeStruct(((2,) + whole) if x else whole, shard.dtype))
    same = lambda v: jax.ShapeDtypeStruct(v.shape, v.dtype)
    twice = jax.ShapeDtypeStruct((2,) + cot.shape, cot.dtype)
    shapes += [same(v) for v in smalls] + [same(hidden), twice, twice]
    more = len(smalls) + 4
    place = pl.BlockSpec(memory_space=pl.ANY)
    outs = pl.pallas_call(
        functools.partial(gather_kernel, plan, rows, seqs, parts, over_x, len(smalls)),
        out_shape=shapes,
        in_specs=[place] * (len(shards) + len(smalls) + 2),
        out_specs=[place] * len(shapes),
        scratch_shapes=[
            pltpu.SemaphoreType.DMA((total,)),
            pltpu.SemaphoreType.DMA((total,)),
            pltpu.SemaphoreType.DMA((len(parts) + 1,)),
            pltpu.SemaphoreType.DMA((more,)),
            pltpu.SemaphoreType.DMA((more,)),
        ],
        compiler_params=pltpu.CompilerParams(collective_id=0, has_side_effects=True),
        name="gather",
    )(*shards, *smalls, hidden, cot)
    n = len(shards)
    return outs[:n], outs[n : n + len(smalls)], outs[-3:]


def ffn_kernel(chunks, before, share_len, slots, live_ref, x_ref, more_ref, cot_ref, *refs):
    weights, refs = refs[:chunks], refs[chunks:]
    earlier, refs = refs[: 4 * before], refs[4 * before :]
    outs, held, sem = refs[:4], refs[4:-1], refs[-1]
    step = pl.program_id(0)
    tile = x_ref.shape[0]
    copies = [pltpu.make_async_copy(weights[c], held[c], sem.at[c]) for c in range(chunks)]

    @pl.when(step == 0)
    def _():
        for copy in copies:
            copy.start()

    first = step < pl.num_programs(0) // 2
    live = (lax.rem(step * tile // share_len, slots) < live_ref[0]).astype(F32)
    x, cot = jnp.where(first, x_ref[...], more_ref[...]), cot_ref[...]
    sums = [None, None]
    if before:
        sums = [jnp.where(first, earlier[i][...], earlier[i + 1][...]).astype(F32) for i in (0, 2)]
    for c in range(chunks):

        @pl.when(step == 0)
        def _():
            copies[c].wait()

        w, width = held[c], held[c].shape[1] // 3
        gate = dot(x, w[:, :width])
        up = dot(x, w[:, width : 2 * width])
        gm = dot(cot, w[:, 2 * width :]) * live
        sig = jax.nn.sigmoid(gate)
        silu = gate * sig
        mixed = (silu * up).astype(BF16)
        g_gate = (gm * up * (sig + silu * (1.0 - sig))).astype(BF16)
        g_up = (gm * silu).astype(BF16)
        parts = (
            dot(jnp.concatenate([g_gate, g_up], axis=1), w[:, : 2 * width], NT),
            dot(mixed, w[:, 2 * width :], NT),
        )
        sums = [p if t is None else t + p for t, p in zip(sums, parts)]

    @pl.when(first)
    def _():
        outs[0][...] = sums[0].astype(BF16)
        outs[2][...] = sums[1].astype(BF16)

    @pl.when(jnp.logical_not(first))
    def _():
        outs[1][...] = sums[0].astype(BF16)
        outs[3][...] = sums[1].astype(BF16)


def ffn(x, cot, weights, live_rows, share_len, slots, before=(), after=()):
    tokens, depth = cot.shape
    chunks = len(weights)
    units = sum(w.shape[1] for w in weights) // 3
    tile = min(256, share_len)
    half = tokens // tile // 2
    lower = pl.BlockSpec((tile, depth), lambda i, *_: (jnp.minimum(i, half - 1), 0))
    upper = pl.BlockSpec((tile, depth), lambda i, *_: (jnp.maximum(i - half, 0), 0))
    out = jax.ShapeDtypeStruct((tokens // 2, depth), BF16)
    return kernel_call(
        functools.partial(ffn_kernel, chunks, len(before) // 4, share_len, slots),
        [live_rows, x[0], x[1], cot, *weights, *before],
        after,
        prefetch=1,
        grid=(tokens // tile,),
        in_specs=[lower, upper, pl.BlockSpec((tile, depth), lambda i, *_: (i, 0))]
        + [pl.BlockSpec(memory_space=pl.ANY)] * chunks
        + [lower, upper] * (len(before) // 2),
        out_specs=[lower, upper, lower, upper],
        out_shape=[out] * 4,
        scratch=[
            *[pltpu.VMEM(w.shape, BF16) for w in weights],
            pltpu.SemaphoreType.DMA((chunks,)),
        ],
        cost=pl.CostEstimate(
            flops=12 * tokens * depth * units,
            bytes_accessed=8 * tokens * depth + 6 * depth * units,
            transcendentals=0,
        ),
        name="ffn",
    )


def lower_lanes(like):
    return lax.broadcasted_iota(jnp.int32, like.shape, 1) < HD


def half_ones():
    r = lax.broadcasted_iota(jnp.int32, (2 * HD, 2 * HD), 0) // HD
    c = lax.broadcasted_iota(jnp.int32, (2 * HD, 2 * HD), 1) // HD
    return (r == c).astype(F32).astype(BF16)


def swap(v):
    return pltpu.roll(v, HD, 1)


def features(x, feat):
    logit = dot(x, feat)
    low = lower_lanes(logit)
    top = jnp.max(jnp.where(low, logit, -jnp.inf), axis=1, keepdims=True)
    bottom = jnp.max(jnp.where(low, -jnp.inf, logit), axis=1, keepdims=True)
    e = jnp.exp(logit - jnp.where(low, top, bottom))
    return e / dot(e.astype(BF16), half_ones())


def features_back(phi, grad):
    p = phi.astype(F32)
    prod = p * grad
    low = lower_lanes(prod)
    first = jnp.sum(jnp.where(low, prod, 0.0), axis=1, keepdims=True)
    second = jnp.sum(jnp.where(low, 0.0, prod), axis=1, keepdims=True)
    g = prod - p * jnp.where(low, first, second)
    return (g - swap(g)).astype(BF16)[:, :HD]


def values_ones(kv):
    kv = kv.astype(F32)
    return jnp.where(lower_lanes(kv), swap(kv), 1.0).astype(BF16)


def key_state_kernel(ends_ref, kv_ref, feat_ref, kdoc_ref, phi_ref, state_ref):
    r = pl.program_id(0)
    kv = kv_ref[0, 0]
    body = kv.shape[0] - WIN
    phi = features(kv[:, :HD], feat_ref[0]).astype(BF16)
    phi_ref[0, 0] = phi
    last = ends_ref[r, body // WIN]
    held = jnp.where(kdoc_ref[0, :body] == last, phi[:body].astype(F32), 0.0).astype(BF16)
    state_ref[0, 0] = dot(held, values_ones(kv[:body]), TN).astype(BF16)


def key_state(ends, kv, feat, kdoc, after=()):
    slots, groups, ext, _ = kv.shape
    block = lambda r, g, *_: (r, g, 0, 0)
    return kernel_call(
        key_state_kernel,
        [ends, kv, feat, kdoc],
        after,
        prefetch=1,
        grid=(slots, groups),
        in_specs=[
            pl.BlockSpec((1, 1, ext, 2 * HD), block),
            pl.BlockSpec((1, HD, 2 * HD), lambda r, g, *_: (g, 0, 0)),
            pl.BlockSpec((1, ext, 2 * HD), lambda r, g, *_: (r, 0, 0)),
        ],
        out_specs=[
            pl.BlockSpec((1, 1, ext, 2 * HD), block),
            pl.BlockSpec((1, 1, 2 * HD, 2 * HD), block),
        ],
        out_shape=[
            jax.ShapeDtypeStruct((slots, groups, ext, 2 * HD), BF16),
            jax.ShapeDtypeStruct((slots, groups, 2 * HD, 2 * HD), BF16),
        ],
        name="key_state",
    )


def block_masks(b, qdoc_ref, pdoc_ref):
    rows = slice(WIN * b, WIN * b + WIN)
    same = qdoc_ref[0, rows] == pdoc_ref[0, b : b + 1]
    row = lax.broadcasted_iota(jnp.int32, (WIN, 2 * WIN), 0)
    col = lax.broadcasted_iota(jnp.int32, (WIN, 2 * WIN), 1)
    linear = same & (col <= row)
    window = same & (col > row) & (col <= row + WIN)
    return window, linear


def next_state(b, ends_ref, r, state, phi_ref, vx_ref, kdoc_ref):
    rows = slice(WIN * (b - 1), WIN * b)
    keep = (ends_ref[r, b] == ends_ref[r, b - 1]).astype(F32)
    held = jnp.where(
        kdoc_ref[0, rows] == ends_ref[r, b], phi_ref[0, 0, rows].astype(F32), 0.0
    ).astype(BF16)
    return state * keep + dot(held, vx_ref[rows], TN)


def block_forward(b, ends_ref, r, q_ref, kv_ref, phi_ref, phiq_ref, vx_ref, state_low, qdoc_ref, pdoc_ref):
    heads = q_ref.shape[1]
    rows, pair = slice(WIN * b, WIN * b + WIN), slice(WIN * b, WIN * b + 2 * WIN)
    window, linear = block_masks(b, qdoc_ref, pdoc_ref)
    valid = qdoc_ref[0, rows] == ends_ref[r, b]
    query = jnp.concatenate([q_ref[0, h, rows] for h in range(heads)], axis=0)
    phi_query = jnp.concatenate([phiq_ref[0, h, rows] for h in range(heads)], axis=0)
    key = kv_ref[0, 0, pair, :HD]
    phi_key = phi_ref[0, 0, pair]
    score = dot(query, key, NT) * (HD**-0.5)
    lin = dot(phi_query, phi_key, NT)
    part = lambda v, h: v[WIN * h : WIN * h + WIN]
    exps = [jnp.where(window, jnp.exp(part(score, h)), 0.0) for h in range(heads)]
    weight = jnp.concatenate(
        [jnp.where(linear, part(lin, h), exps[h]).astype(BF16) for h in range(heads)], axis=0
    )
    phi_valid = jnp.concatenate(
        [jnp.where(valid, part(phi_query, h).astype(F32), 0.0).astype(BF16) for h in range(heads)],
        axis=0,
    )
    both = dot(weight, vx_ref[pair]) + dot(phi_valid, state_low)
    denominator = jnp.where(lower_lanes(both), swap(both), both)
    return (query, phi_query, phi_valid, key, phi_key, exps, weight, both / denominator, denominator,
            window, linear, valid)


def query_feature_kernel(q_ref, feat_ref, phi_ref):
    for h in range(q_ref.shape[1]):
        phi_ref[0, h] = features(q_ref[0, h], feat_ref[h]).astype(BF16)


def query_features(q, feat, groups):
    slots, all_heads, length, _ = q.shape
    sp = attention_specs(slots, groups, all_heads // groups, length)
    return kernel_call(
        query_feature_kernel,
        [q, feat],
        (),
        grid=(slots, groups),
        in_specs=[sp["q"], sp["feat"]],
        out_specs=sp["phiq"],
        out_shape=jax.ShapeDtypeStruct((slots, all_heads, length, 2 * HD), BF16),
        name="query_features",
    )


def attend_kernel(
    ends_ref, q_ref, kv_ref, phi_ref, phiq_ref, carry_ref, qdoc_ref, kdoc_ref, pdoc_ref,
    attn_ref, vx_ref,
):
    r = pl.program_id(0)
    heads, length = q_ref.shape[1], q_ref.shape[2]
    vx_ref[...] = values_ones(kv_ref[0, 0])
    state = carry_ref[0, 0]
    for b in range(length // WIN):
        if b:
            state = next_state(b, ends_ref, r, state, phi_ref, vx_ref, kdoc_ref)
        out = block_forward(
            b, ends_ref, r, q_ref, kv_ref, phi_ref, phiq_ref, vx_ref, state.astype(BF16), qdoc_ref,
            pdoc_ref,
        )
        attn = out[7]
        low = lower_lanes(attn[:WIN])
        for h in range(0, heads, 2):
            first, second = attn[WIN * h : WIN * h + WIN], attn[WIN * h + WIN : WIN * h + 2 * WIN]
            attn_ref[0, WIN * b : WIN * b + WIN, HD * h : HD * h + 2 * HD] = jnp.where(
                low, first, swap(second)
            ).astype(BF16)


def attention_specs(slots, groups, heads, length):
    ext = length + WIN
    four = lambda r, g, *_: (r, g, 0, 0)
    docs = lambda r, g, *_: (r, 0, 0)
    return dict(
        q=pl.BlockSpec((1, heads, length, HD), four),
        kv=pl.BlockSpec((1, 1, ext, 2 * HD), four),
        phiq=pl.BlockSpec((1, heads, length, 2 * HD), four),
        feat=pl.BlockSpec((heads, HD, 2 * HD), lambda r, g, *_: (g, 0, 0)),
        state=pl.BlockSpec((1, 1, 2 * HD, 2 * HD), four),
        qdoc=pl.BlockSpec((1, length, 2 * HD), docs),
        kdoc=pl.BlockSpec((1, ext, 2 * HD), docs),
        pdoc=pl.BlockSpec((1, length // WIN, 2 * HD), docs),
        tokens=pl.BlockSpec((1, length, heads * HD), lambda r, g, *_: (r, 0, g)),
        fgrad=pl.BlockSpec((1, heads // 2, HD, 2 * HD), four),
    )


def attend(ends, q, kv, phi, phiq, carry, qdoc, kdoc, pdoc, after=()):
    slots, all_heads, length, _ = q.shape
    groups = kv.shape[1]
    heads = all_heads // groups
    sp = attention_specs(slots, groups, heads, length)
    return kernel_call(
        attend_kernel,
        [ends, q, kv, phi, phiq, carry, qdoc, kdoc, pdoc],
        after,
        prefetch=1,
        grid=(slots, groups),
        in_specs=[sp[n] for n in ("q", "kv", "kv", "phiq", "state", "qdoc", "kdoc", "pdoc")],
        out_specs=sp["tokens"],
        scratch=[pltpu.VMEM((length + WIN, 2 * HD), BF16)],
        out_shape=jax.ShapeDtypeStruct((slots, length, all_heads * HD), BF16),
        name="attend",
    )


def attend_back_kernel(
    ends_ref, q_ref, kv_ref, phi_ref, phiq_ref, feat_ref, carry_ref, qdoc_ref, kdoc_ref, pdoc_ref,
    g_ref, gq_ref, gfeat_ref, gphi_ref, gkv_ref, gcarry_ref, vx_ref, gstate_ref, gphiq_ref, gk_ref,
    gv_ref, gqs_ref, gl_ref,
):
    r = pl.program_id(0)
    heads, length = q_ref.shape[1], q_ref.shape[2]
    blocks = length // WIN
    vx_ref[...] = values_ones(kv_ref[0, 0])
    gphi_ref[...] = jnp.zeros_like(gphi_ref)
    gk_ref[...] = jnp.zeros_like(gk_ref)
    gv_ref[...] = jnp.zeros_like(gv_ref)
    scale = HD**-0.5
    state = carry_ref[0, 0]
    for b in range(blocks):
        rows, pair = slice(WIN * b, WIN * b + WIN), slice(WIN * b, WIN * b + 2 * WIN)
        if b:
            state = next_state(b, ends_ref, r, state, phi_ref, vx_ref, kdoc_ref)
        state_low = state.astype(BF16)
        (query, phi_query, phi_valid, key, phi_key, exps, weight, attn, denominator, window, linear,
         valid) = block_forward(
            b, ends_ref, r, q_ref, kv_ref, phi_ref, phiq_ref, vx_ref, state_low, qdoc_ref, pdoc_ref
        )
        grads = []
        for h in range(0, heads, 2):
            g = g_ref[0, rows, HD * h : HD * h + 2 * HD].astype(F32)
            grads += [g, swap(g)]
        grad = jnp.concatenate(grads, axis=0)
        low = lower_lanes(grad)
        grad = jnp.where(low, grad, 0.0)
        g_denom = -jnp.sum(grad * attn, axis=1, keepdims=True)
        gx = (jnp.where(low, grad, g_denom * (1.0 / HD)) / denominator).astype(BF16)
        g_weight = dot(gx, vx_ref[pair], NT)
        part = lambda v, h: v[WIN * h : WIN * h + WIN]
        g_score = jnp.concatenate(
            [(exps[h] * part(g_weight, h)).astype(BF16) for h in range(heads)], axis=0
        )
        g_lin = jnp.concatenate(
            [jnp.where(linear, part(g_weight, h), 0.0).astype(BF16) for h in range(heads)], axis=0
        )
        g_query = dot(g_score, key) * scale
        gk_ref[pair] += dot(g_score, query, TN) * scale
        gv_ref[pair] += dot(weight, gx, TN)
        gphi_ref[0, 0, pair] += dot(g_lin, phi_query, TN)
        from_lin = dot(g_lin, phi_key)
        from_state = dot(gx, state_low, NT)
        gstate_ref[b] = dot(phi_valid, gx, TN)
        for h in range(heads):
            gphiq_ref[h, rows] = part(from_lin, h) + jnp.where(valid, part(from_state, h), 0.0)
            gqs_ref[h, rows] = part(g_query, h)
    for h in range(heads):
        g_logit = features_back(phiq_ref[0, h], gphiq_ref[h])
        gl_ref[h] = g_logit
        gqs_ref[h] += dot(g_logit, feat_ref[h][:, :HD], NT)
    gq_ref[0] = jnp.concatenate([gqs_ref[h] for h in range(heads)], axis=1).astype(BF16)
    for h in range(0, heads, 2):
        gfeat_ref[0, h // 2] = jnp.concatenate(
            [dot(q_ref[0, i], gl_ref[i], TN) for i in (h, h + 1)], axis=1
        )
    later = gstate_ref[blocks - 1]
    for b in range(blocks - 1, 0, -1):
        rows = slice(WIN * (b - 1), WIN * b)
        low_state = later.astype(BF16)
        mask = kdoc_ref[0, rows] == ends_ref[r, b]
        gphi_ref[0, 0, rows] += jnp.where(mask, dot(vx_ref[rows], low_state, NT), 0.0)
        gv_ref[rows] += jnp.where(mask, dot(phi_ref[0, 0, rows], low_state), 0.0)
        keep = (ends_ref[r, b] == ends_ref[r, b - 1]).astype(F32)
        later = gstate_ref[b - 1] + keep * later
    gcarry_ref[0, 0] = later.astype(BF16)
    gv = gv_ref[...]
    gkv_ref[0, 0, :, :HD] = gk_ref[...]
    gkv_ref[0, 0, :, HD:] = gv[:, :HD]


def attend_back(ends, q, kv, phi, phiq, feat, carry, qdoc, kdoc, pdoc, g, after=()):
    slots, all_heads, length, _ = q.shape
    groups = kv.shape[1]
    heads = all_heads // groups
    ext = length + WIN
    sp = attention_specs(slots, groups, heads, length)
    return kernel_call(
        attend_back_kernel,
        [ends, q, kv, phi, phiq, feat, carry, qdoc, kdoc, pdoc, g],
        after,
        prefetch=1,
        grid=(slots, groups),
        in_specs=[
            sp[n]
            for n in ("q", "kv", "kv", "phiq", "feat", "state", "qdoc", "kdoc", "pdoc", "tokens")
        ],
        out_specs=[sp["tokens"], sp["fgrad"], sp["kv"], sp["kv"], sp["state"]],
        scratch=[
            pltpu.VMEM((ext, 2 * HD), BF16),
            pltpu.VMEM((length // WIN, 2 * HD, 2 * HD), F32),
            pltpu.VMEM((heads, length, 2 * HD), F32),
            pltpu.VMEM((ext, HD), F32),
            pltpu.VMEM((ext, 2 * HD), F32),
            pltpu.VMEM((heads, length, HD), F32),
            pltpu.VMEM((heads, length, HD), BF16),
        ],
        out_shape=[
            jax.ShapeDtypeStruct((slots, length, all_heads * HD), BF16),
            jax.ShapeDtypeStruct((slots, all_heads // 2, HD, 2 * HD), F32),
            jax.ShapeDtypeStruct((slots, groups, ext, 2 * HD), F32),
            jax.ShapeDtypeStruct((slots, groups, ext, 2 * HD), F32),
            jax.ShapeDtypeStruct((slots, groups, 2 * HD, 2 * HD), BF16),
        ],
        name="attend_back",
    )


def key_back_kernel(
    ends_ref, kv_ref, phi_ref, feat_ref, later_ref, kdoc_ref, gphi_ref, gkv_ref,
    body_ref, edge_ref, gfeat_ref,
):
    r = pl.program_id(0)
    ext = kv_ref.shape[2]
    body = ext - WIN
    last = ends_ref[r, body // WIN]
    mask = kdoc_ref[0, :body] == last
    keys, vals, feats = [], [], []
    for i in range(2):
        kv, phi = kv_ref[0, i], phi_ref[0, i]
        later = later_ref[0, i].astype(BF16)
        more_phi = jnp.where(mask, dot(values_ones(kv[:body]), later, NT), 0.0)
        more_v = jnp.where(mask, dot(phi[:body], later), 0.0)
        tail = jnp.zeros((WIN, 2 * HD), F32)
        g_phi = gphi_ref[0, i] + jnp.concatenate([more_phi, tail], axis=0)
        g_logit = features_back(phi, g_phi)
        gkv = gkv_ref[0, i]
        keys.append(gkv[:, :HD] + dot(g_logit, feat_ref[i][:, :HD], NT))
        vals.append(gkv[:, HD:] + jnp.concatenate([more_v, tail], axis=0)[:, :HD])
        feats.append(dot(kv[:, :HD], g_logit, TN))
    gfeat_ref[0, 0] = jnp.concatenate(feats, axis=1)
    both = jnp.concatenate(keys + vals, axis=1)
    body_ref[0, 0] = both[WIN:]
    edge_ref[0, 0] = both[:WIN].astype(BF16)


def key_back(ends, kv, phi, feat, later, kdoc, gphi, gkv, after=()):
    slots, groups, ext, _ = kv.shape
    four = lambda r, s, *_: (r, s, 0, 0)
    wide = pl.BlockSpec((1, 2, ext, 2 * HD), four)
    body = pl.BlockSpec((1, 1, ext - WIN, 4 * HD), four)
    edge = pl.BlockSpec((1, 1, WIN, 4 * HD), four)
    sets = groups // 2
    return kernel_call(
        key_back_kernel,
        [ends, kv, phi, feat, later, kdoc, gphi, gkv],
        after,
        prefetch=1,
        grid=(slots, groups // 2),
        in_specs=[
            wide,
            wide,
            pl.BlockSpec((2, HD, 2 * HD), lambda r, s, *_: (s, 0, 0)),
            pl.BlockSpec((1, 2, 2 * HD, 2 * HD), four),
            pl.BlockSpec((1, ext, 2 * HD), lambda r, s, *_: (r, 0, 0)),
            wide,
            wide,
        ],
        out_specs=[body, edge, pl.BlockSpec((1, 1, HD, 2 * HD), four)],
        out_shape=[
            jax.ShapeDtypeStruct((slots, sets, ext - WIN, 4 * HD), F32),
            jax.ShapeDtypeStruct((slots, sets, WIN, 4 * HD), BF16),
            jax.ShapeDtypeStruct((slots, sets, HD, 2 * HD), F32),
        ],
        name="key_back",
    )


LOW = 128


def normalize(values, gain):
    scale = lax.rsqrt(jnp.mean(values * values, axis=-1, keepdims=True) + NORM_EPS)
    return (values * scale * gain).astype(BF16)


def project_kernel(
    sets, q_cols, k_cols, shares, core_ref, own_ref, other_ref, gain_ref, w_ref, a_ref, b_ref, q_ref,
    kv_ref, small_ref
):
    own = pl.program_id(1) // shares == core_ref[0]
    x = normalize(jnp.where(own, own_ref[0], other_ref[0]).astype(F32), gain_ref[...])
    width = q_cols + 2 * k_cols
    small = dot(x, a_ref[...]).astype(BF16)
    small_ref[0] = small
    heads, groups = q_cols // HD, k_cols // HD
    for s in range(sets):
        cols = slice(s * width, (s + 1) * width)
        full = dot(x, w_ref[s]) + ADAPTER_SCALE * dot(small, b_ref[:, cols])
        for h in range(heads):
            q_ref[0, s * heads + h] = full[:, h * HD : h * HD + HD].astype(BF16)
        for g in range(0, groups, 2):
            k = full[:, q_cols + g * HD : q_cols + g * HD + 2 * HD]
            start = q_cols + k_cols + g * HD
            v = full[:, start : start + 2 * HD]
            low = lower_lanes(k)
            kv_ref[0, s * groups + g] = jnp.where(low, k, swap(v)).astype(BF16)
            kv_ref[0, s * groups + g + 1] = jnp.where(low, swap(k), v).astype(BF16)


def project(core, own, other, gain, w, a, b, q_cols, k_cols, after=()):
    slots, share, depth = own.shape
    length = 2 * share
    sets = w.shape[0]
    heads, groups = sets * q_cols // HD, sets * k_cols // HD
    tile = min(256, share)
    shares = share // tile
    token = pl.BlockSpec((1, tile, depth), lambda r, i, *_: (r, lax.rem(i, shares), 0))
    return kernel_call(
        functools.partial(project_kernel, sets, q_cols, k_cols, shares),
        [core, own, other, gain, w, a, b],
        after,
        prefetch=1,
        grid=(slots, length // tile),
        in_specs=[
            token,
            token,
            pl.BlockSpec(gain.shape, lambda r, i, *_: (0, 0)),
            pl.BlockSpec(w.shape, lambda r, i, *_: (0, 0, 0)),
            pl.BlockSpec(a.shape, lambda r, i, *_: (0, 0)),
            pl.BlockSpec(b.shape, lambda r, i, *_: (0, 0)),
        ],
        out_specs=[
            pl.BlockSpec((1, heads, tile, HD), lambda r, i, *_: (r, 0, i, 0)),
            pl.BlockSpec((1, groups, tile, 2 * HD), lambda r, i, *_: (r, 0, i, 0)),
            pl.BlockSpec((1, tile, LOW), lambda r, i, *_: (r, i, 0)),
        ],
        out_shape=[
            jax.ShapeDtypeStruct((slots, heads, length, HD), BF16),
            jax.ShapeDtypeStruct((slots, groups, length, 2 * HD), BF16),
            jax.ShapeDtypeStruct((slots, length, LOW), BF16),
        ],
        cost=pl.CostEstimate(
            flops=2 * slots * length * w.size,
            bytes_accessed=2 * (slots * length * depth + w.size),
            transcendentals=0,
        ),
        name="project",
    )


def halves(share, tile):
    shares = share // tile
    own = lambda r, i, core: (r, core[0] * shares + i, 0)
    other = lambda r, i, core: (r, (1 - core[0]) * shares + i, 0)
    return own, other


def out_project_kernel(core_ref, own_ref, other_ref, w_ref, low_ref, keep_ref, away_ref):
    depth = w_ref.shape[1]
    half = w_ref.shape[2]
    for src, dst in ((own_ref, keep_ref), (other_ref, away_ref)):
        attn = src[0]
        full = dot(attn[:, :half], w_ref[0], NT) + dot(attn[:, half:], w_ref[1], NT)
        dst[0, :, :depth] = full.astype(BF16)
        dst[0, :, depth:] = dot(attn, low_ref[...]).astype(BF16)


def out_project(core, attn, w, low, share):
    slots, length, width = attn.shape
    depth = w.shape[1]
    tile = min(256, share)
    own, other = halves(share, tile)
    out = pl.BlockSpec((1, tile, depth + LOW), lambda r, i, *_: (r, i, 0))
    shape = jax.ShapeDtypeStruct((slots, share, depth + LOW), BF16)
    return kernel_call(
        out_project_kernel,
        [core, attn, attn, w, low],
        (),
        prefetch=1,
        grid=(slots, share // tile),
        in_specs=[
            pl.BlockSpec((1, tile, width), own),
            pl.BlockSpec((1, tile, width), other),
            pl.BlockSpec(w.shape, lambda r, i, *_: (0, 0, 0)),
            pl.BlockSpec(low.shape, lambda r, i, *_: (0, 0)),
        ],
        out_specs=[out, out],
        out_shape=[shape, shape],
        name="out_project",
    )


def middle_kernel(hidden_ref, keep_ref, got_ref, second_ref, gain_ref, mid_ref, normed_ref, low_ref):
    depth = hidden_ref.shape[1]
    total = keep_ref[...].astype(F32) + got_ref[...].astype(F32)
    low = total[:, depth:].astype(BF16)
    low_ref[...] = low
    mid = hidden_ref[...].astype(F32) + total[:, :depth]
    mid = mid + ADAPTER_SCALE * dot(low, second_ref[...])
    mid_ref[...] = mid.astype(BF16)
    normed_ref[...] = normalize(mid, gain_ref[...])


def tokens_call(kernel, tiled, whole, outs, name, prefetch=(), sums=(), tile=256, after=()):
    tokens = tiled[0].shape[0]
    tile = min(tile, tokens)
    rows = lambda v: pl.BlockSpec((tile, v.shape[1]), lambda i, *_: (i, 0))
    full = lambda v: pl.BlockSpec(v.shape, lambda i, *_: (0, 0))
    shapes = [jax.ShapeDtypeStruct((tokens, width), kind) for width, kind in outs]
    totals = [jax.ShapeDtypeStruct(v, F32) for v in sums]
    return kernel_call(
        kernel,
        [*prefetch, *tiled, *whole],
        after,
        prefetch=len(prefetch),
        grid=(tokens // tile,),
        in_specs=[rows(v) for v in tiled] + [full(v) for v in whole],
        out_specs=[rows(v) for v in shapes] + [full(v) for v in totals],
        out_shape=shapes + totals,
        name=name,
    )


def norm_back(values, gain, grad):
    scale = lax.rsqrt(jnp.mean(values * values, axis=-1, keepdims=True) + NORM_EPS)
    scaled = gain * grad
    shared = scale * scale * scale * jnp.mean(values * scaled, axis=-1, keepdims=True)
    return scale, scale * scaled - values * shared


def pair_kernel(a_ref, b_ref, out_ref):
    out_ref[...] = a_ref[...] + b_ref[...].astype(F32)


def sum_kernel(*refs):
    refs[-1][...] = sum(r[...].astype(F32) for r in refs[:-1]).astype(BF16)


def branch_kernel(slot_len, slots, live_ref, mid_ref, a_ref, c_ref, cot_ref, *refs):
    parts, (gain_ref, grad_ref) = refs[:slots], refs[slots:]
    part = parts[0][...]
    for r in range(1, slots):
        part = jnp.where(pl.program_id(0) == r, parts[r][...], part)
    grad = a_ref[...].astype(F32) + part.astype(F32) + c_ref[...].astype(F32)
    tile = mid_ref.shape[0]
    token = pl.program_id(0) * tile + lax.broadcasted_iota(jnp.int32, (tile, 1), 0)
    live = token < live_ref[0] * slot_len
    cot = jnp.where(live, cot_ref[...].astype(F32), 0.0)
    mid = mid_ref[...].astype(F32)
    grad_ref[...] = (cot + norm_back(mid, gain_ref[...], grad)[1]).astype(BF16)


def attn_grad_kernel(
    shares, core_ref, own_ref, other_ref, attn_ref, w_ref, second_ref, first_ref, grad_ref, sum_ref
):
    own = pl.program_id(1) // shares == core_ref[0]
    x = jnp.where(own, own_ref[0], other_ref[0])
    low = (ADAPTER_SCALE * dot(x, second_ref[...], NT)).astype(BF16)
    half = w_ref.shape[2]
    first = first_ref[...]
    for s in range(2):
        cols = slice(s * half, (s + 1) * half)
        grad_ref[0, :, cols] = (dot(x, w_ref[s]) + dot(low, first[cols], NT)).astype(BF16)

    @pl.when((pl.program_id(0) == 0) & (pl.program_id(1) == 0))
    def _():
        sum_ref[...] = jnp.zeros_like(sum_ref)

    sum_ref[...] += dot(low, attn_ref[0], TN)


def attn_grad(core, own, other, attn, w, second, first):
    slots, share, depth = own.shape
    length = 2 * share
    width = attn.shape[2]
    tile = min(256, share)
    shares = share // tile
    token = pl.BlockSpec((1, tile, depth), lambda r, i, *_: (r, lax.rem(i, shares), 0))
    wide = pl.BlockSpec((1, tile, width), lambda r, i, *_: (r, i, 0))
    full = lambda v: pl.BlockSpec(v.shape, lambda r, i, *_: (0,) * v.ndim)
    total = jax.ShapeDtypeStruct((LOW, width), F32)
    return kernel_call(
        functools.partial(attn_grad_kernel, shares),
        [core, own, other, attn, w, second, first],
        (),
        prefetch=1,
        grid=(slots, length // tile),
        in_specs=[token, token, wide, full(w), full(second), full(first)],
        out_specs=[wide, full(total)],
        out_shape=[jax.ShapeDtypeStruct(attn.shape, BF16), total],
        name="attn_grad",
    )


def normed_grad_kernel(
    q_cols, shares, core_ref, q_own_ref, q_other_ref, kv_own_ref, kv_other_ref, s_own_ref, s_other_ref,
    back_ref, w_ref, b_ref, keep_ref, away_ref, sum_ref
):
    depth, width = w_ref.shape[1:]
    core, step = core_ref[0], pl.program_id(1)

    @pl.when((pl.program_id(0) == 0) & (step == 0))
    def _():
        sum_ref[...] = jnp.zeros_like(sum_ref)

    sides = (
        (q_own_ref, kv_own_ref, s_own_ref, keep_ref, core),
        (q_other_ref, kv_other_ref, s_other_ref, away_ref, 1 - core),
    )
    for q_ref, kv_ref, s_ref, out_ref, share in sides:
        tile = q_ref.shape[1]
        last = (share * shares + step == 2 * shares - 1).astype(F32)
        full = low = None
        for s in range(2):
            kv = kv_ref[0, s]
            edge = back_ref[0, s].astype(F32) * last
            if tile > WIN:
                edge = jnp.concatenate([jnp.zeros((tile - WIN, kv.shape[1]), F32), edge], axis=0)
            kv = (kv + edge).astype(BF16)
            q = q_ref[0, :, s * q_cols : (s + 1) * q_cols]
            grads = jnp.concatenate([q, kv], axis=1)
            part = dot(grads, w_ref[s], NT)
            small = dot(grads, b_ref[:, s * width : (s + 1) * width], NT)
            full = part if full is None else full + part
            low = small if low is None else low + small
            sum_ref[s] += dot(s_ref[0], grads, TN)
        out_ref[0, :, :depth] = full.astype(BF16)
        out_ref[0, :, depth:] = (ADAPTER_SCALE * low).astype(BF16)


def normed_grad(core, q, kv, small, back, w, b, q_cols, share):
    slots, length, q_width = q.shape
    sets, depth, width = w.shape
    tile = min(256, share)
    shares = share // tile
    own, other = halves(share, tile)
    four = lambda f: (lambda r, i, core: (r, 0, f(r, i, core)[1], 0))
    out = pl.BlockSpec((1, tile, depth + LOW), lambda r, i, *_: (r, i, 0))
    shape = jax.ShapeDtypeStruct((slots, share, depth + LOW), BF16)
    total = jax.ShapeDtypeStruct((sets, LOW, width), F32)
    kv_block = (1, sets, tile, kv.shape[3])
    return kernel_call(
        functools.partial(normed_grad_kernel, q_cols, shares),
        [core, q, q, kv, kv, small, small, back, w, b],
        (),
        prefetch=1,
        grid=(slots, shares),
        in_specs=[
            pl.BlockSpec((1, tile, q_width), own),
            pl.BlockSpec((1, tile, q_width), other),
            pl.BlockSpec(kv_block, four(own)),
            pl.BlockSpec(kv_block, four(other)),
            pl.BlockSpec((1, tile, LOW), own),
            pl.BlockSpec((1, tile, LOW), other),
            pl.BlockSpec((1, sets, WIN, kv.shape[3]), lambda r, i, *_: (r, 0, 0, 0)),
            pl.BlockSpec(w.shape, lambda r, i, *_: (0, 0, 0)),
            pl.BlockSpec(b.shape, lambda r, i, *_: (0, 0)),
        ],
        out_specs=[out, out, pl.BlockSpec(total.shape, lambda r, i, *_: (0, 0, 0))],
        out_shape=[shape, shape, total],
        name="normed_grad",
    )


def finish_kernel(keep_ref, got_ref, hidden_ref, mid_ref, gain_ref, first_ref, out_ref, sum_ref):
    depth = hidden_ref.shape[1]
    total = keep_ref[...].astype(F32) + got_ref[...].astype(F32)
    low = total[:, depth:].astype(BF16)
    grad = total[:, :depth] + dot(low, first_ref[...])
    values, gain = hidden_ref[...].astype(F32), gain_ref[...]
    scale, back = norm_back(values, gain, grad)
    out_ref[...] = (mid_ref[...].astype(F32) + back).astype(BF16)

    @pl.when(pl.program_id(0) == 0)
    def _():
        sum_ref[...] = jnp.zeros_like(sum_ref)

    sum_ref[...] += dot(low, (values * scale * gain).astype(BF16), TN)


def sums_kernel(rows, seqs, heads, part_ref, pack_ref, out_ref, cols_ref, *scratch):
    a1, a2, a3, c2, c3, b1, b2, b3, e2, e3, send_sem, recv_sem = scratch
    place = {a: lax.axis_index(a) for a in ("row", "seq", "head")}
    counts = {"row": rows, "seq": seqs, "head": heads}
    x_place = place["head"] // 2
    peers = [
        (a, {a: lax.rem(place[a] + d, counts[a])}) for a in counts for d in range(1, counts[a])
    ]
    barrier = pltpu.get_barrier_semaphore()
    for _, peer in peers:
        pl.semaphore_signal(barrier, inc=1, device_id=peer, device_id_type=pl.DeviceIdType.MESH)
    pl.semaphore_wait(barrier, len(peers))
    used = [0]

    def remote(src, dst, device):
        n = used[0]
        used[0] += 1
        return pltpu.make_async_remote_copy(
            src_ref=src, dst_ref=dst, send_sem=send_sem.at[n], recv_sem=recv_sem.at[n],
            device_id=device, device_id_type=pl.DeviceIdType.MESH,
        )

    def exchange(axis, parts, slots, packs, pack_slots):
        me, size = place[axis], counts[axis]
        copies = []
        for d in range(1, size):
            to = lax.rem(me + d, size)
            copies.append(remote(parts.at[to], slots.at[me], {axis: to}))
            if pack_slots is not None:
                copies.append(remote(packs, pack_slots.at[me], {axis: to}))
        return copies

    def add_up(ref, size):
        total = ref[0].astype(F32)
        for i in range(1, size):
            total = total + ref[i].astype(F32)
        return total

    b1[0] = pack_ref[1 - x_place].astype(BF16)
    copies = exchange("head", part_ref, a1, None, None)
    copies.append(remote(b1.at[0], b1.at[1], {"head": lax.rem(place["head"] + 2, heads)}))
    for copy in copies:
        copy.start()
    a1[place["head"]] = part_ref[place["head"]]
    for copy in copies:
        copy.wait()
    stages = (
        ("seq", add_up(a1, heads), pack_ref[x_place] + b1[1].astype(F32), c2, a2, e2, b2),
        ("row", None, None, c3, a3, e3, b3),
    )
    for axis, part, pack, held, slots, pack_held, pack_slots in stages:
        if part is None:
            part, pack = add_up(a2, seqs), add_up(b2, seqs)
        held[...] = part
        pack_held[...] = pack.astype(BF16)
        copies = exchange(axis, held, slots, pack_held, pack_slots)
        for copy in copies:
            copy.start()
        slots[place[axis]] = held[place[axis]]
        pack_slots[place[axis]] = pack_held[...]
        for copy in copies:
            copy.wait()
    out_ref[...] = add_up(a3, rows)
    cols_ref[...] = add_up(b3, rows)


def final_sums(part, pack):
    rows, seqs, heads = (lax.axis_size(a) for a in ("row", "seq", "head"))
    low, width = part.shape[3:]
    count, lanes = pack.shape[1:]
    place = pl.BlockSpec(memory_space=pltpu.VMEM)
    copies = heads + 2 * (seqs - 1) + 2 * (rows - 1)
    return pl.pallas_call(
        functools.partial(sums_kernel, rows, seqs, heads),
        in_specs=[place, place],
        out_specs=[place, place],
        out_shape=[
            jax.ShapeDtypeStruct((low, width), F32),
            jax.ShapeDtypeStruct((count, lanes), F32),
        ],
        scratch_shapes=[
            pltpu.VMEM((heads, seqs, rows, low, width), F32),
            pltpu.VMEM((seqs, rows, low, width), F32),
            pltpu.VMEM((rows, low, width), F32),
            pltpu.VMEM((seqs, rows, low, width), F32),
            pltpu.VMEM((rows, low, width), F32),
            pltpu.VMEM((2, count, lanes), BF16),
            pltpu.VMEM((seqs, count, lanes), BF16),
            pltpu.VMEM((rows, count, lanes), BF16),
            pltpu.VMEM((count, lanes), BF16),
            pltpu.VMEM((count, lanes), BF16),
            pltpu.SemaphoreType.DMA((copies,)),
            pltpu.SemaphoreType.DMA((copies,)),
        ],
        compiler_params=pltpu.CompilerParams(
            collective_id=1, has_side_effects=True, vmem_limit_bytes=32 * 2**20
        ),
        name="final_sums",
    )(part, pack)


def local(
    hidden_in,
    grad_out,
    live_rows,
    doc_starts,
    norm_attn,
    norm_ffn,
    query_weight,
    key_weight,
    value_weight,
    out_weight,
    gate_weight,
    up_weight,
    down_weight,
    query_adapt_in,
    query_adapt_out,
    key_adapt_in,
    key_adapt_out,
    value_adapt_in,
    value_adapt_out,
    outproj_adapt_in,
    projection_adapter_second,
    query_feature,
    key_feature,
):
    rows, seqs, heads = lax.axis_size("row"), lax.axis_size("seq"), lax.axis_size("head")
    head = lax.axis_index("head")
    core = lax.rem(head, 2)
    x_count = heads // 2
    x_place = head // 2
    slots, share_len, model_dim = hidden_in.shape
    piece_len = 2 * share_len
    pieces = seqs * x_count
    piece = lax.axis_index("seq") * x_count + x_place
    blocks = piece_len // WIN
    ext_len = piece_len + WIN
    q_cols, k_cols = query_weight.shape[1], key_weight.shape[1]
    ff_cols = gate_weight.shape[1]

    def in_order(own, other):
        first = jnp.where(core == 0, own, other)
        second = jnp.where(core == 0, other, own)
        return jnp.concatenate([first, second], axis=1)

    def own_half(both):
        return lax.dynamic_slice_in_dim(both, core * share_len, share_len, 1)

    def other_half(both):
        return lax.dynamic_slice_in_dim(both, (1 - core) * share_len, share_len, 1)

    qkv_shard = jnp.concatenate([query_weight, key_weight, value_weight], axis=1)
    out_shard = out_weight.T
    down_shard = down_weight.T
    unit = ff_cols // sum(FF_CHUNKS)
    bounds = [unit * sum(FF_CHUNKS[:j]) for j in range(len(FF_CHUNKS) + 1)]
    ffn_shards = [
        jnp.concatenate([w[:, lo:hi] for w in (gate_weight, up_weight, down_shard)], axis=1)
        for lo, hi in zip(bounds[:-1], bounds[1:])
    ]
    ffn_later = [
        lax.all_gather(v, ("row", "seq"), axis=0, tiled=True) for v in ffn_shards[1:]
    ]
    own_smalls = [
        query_feature, key_feature, query_adapt_out, key_adapt_out, value_adapt_out, outproj_adapt_in
    ]
    (qkv_mat, out_mat, first_mat), other_smalls, (hidden_other, cot_mine, cot_away) = gather(
        [qkv_shard, out_shard, ffn_shards[0]],
        [True, True, False],
        [
            (0, (0, qkv_shard.shape[1]), True, 0),
            (1, (0, out_shard.shape[1]), True, 0),
            (2, (0, ffn_shards[0].shape[1]), True, rows * seqs),
        ],
        own_smalls,
        hidden_in,
        grad_out,
    )
    ffn_mats = [first_mat] + ffn_later

    def both(i, axis):
        own, other = own_smalls[i], other_smalls[i]
        return jnp.concatenate(
            [jnp.where(x_place == 0, own, other), jnp.where(x_place == 0, other, own)], axis=axis
        )

    query_feat_all, key_feat_all = both(0, 0), both(1, 0)
    q_out, k_out, v_out = both(2, 1), both(3, 1), both(4, 1)
    o_in = both(5, 0)

    doc_ids = jnp.cumsum(doc_starts, axis=1)
    padded_docs = jnp.concatenate(
        [jnp.full((slots, WIN + 1), -1, jnp.int32), doc_ids], axis=1
    )
    piece_docs = padded_docs[:, ::piece_len][:, : pieces + 1]
    near_docs = lax.dynamic_slice_in_dim(padded_docs, piece * piece_len, ext_len + 1, 1)
    end_docs = near_docs[:, ::WIN][:, : blocks + 1]
    carry_doc = end_docs[:, 0]
    next_doc = end_docs[:, blocks]
    key_docs = near_docs[:, 1:]
    key_doc_lanes = jnp.broadcast_to(key_docs[:, :, None], (slots, ext_len, 2 * HD))
    query_doc_lanes = key_doc_lanes[:, WIN:]
    doc_blocks = key_docs.reshape(slots, blocks + 1, WIN)
    pair_docs = jnp.concatenate([doc_blocks[:, :-1], doc_blocks[:, 1:]], axis=2)

    def from_pieces(block):
        held = []
        for d, start in enumerate((block, flip_x(block))):
            for l in range(seqs):
                if l:
                    start = shift(start, "seq", 1)
                source = (
                    lax.rem(lax.axis_index("seq") - l + seqs, seqs) * x_count
                    + lax.rem(x_place + d, x_count)
                )
                held.append((source, start))
        return held[1:]

    gain_attn = norm_attn.astype(F32)[None]
    gain_ffn = norm_ffn.astype(F32)[None]
    core_index = core.astype(jnp.int32).reshape(1)
    flat_tokens = lambda v: v.reshape(-1, v.shape[-1])

    set_cols = q_cols + 2 * k_cols
    adapt_in_all = jnp.concatenate([query_adapt_in, key_adapt_in, value_adapt_in], axis=1)

    def by_sets(parts):
        return jnp.concatenate(
            [v[:, d * (v.shape[1] // 2) : (d + 1) * (v.shape[1] // 2)] for d in range(2) for v in parts],
            axis=1,
        )

    def diagonal(parts):
        rows = [
            [p if i == j else jnp.zeros((RANK, q.shape[1]), BF16) for j, q in enumerate(parts)]
            for i, p in enumerate(parts)
        ]
        return jnp.concatenate([by_sets(r) for r in rows], axis=0)

    pad_rows = lambda v: jnp.pad(v, ((0, LOW - v.shape[0]), (0, 0)))
    pad_cols = lambda v: jnp.pad(v, ((0, 0), (0, LOW - v.shape[1])))
    adapt_in_all = pad_cols(adapt_in_all)
    adapt_out_all = pad_rows(diagonal([q_out, k_out, v_out]))
    second = pad_rows(projection_adapter_second)
    o_in = pad_cols(o_in)
    query, kv_own, small = project(
        core_index, hidden_in, hidden_other, gain_attn, qkv_mat, adapt_in_all, adapt_out_all, q_cols,
        k_cols,
    )

    def along_pieces(block, distance):
        route = []
        for p in range(pieces):
            to = p + distance
            if 0 <= to < pieces:
                for c in range(2):
                    route.append((2 * p + c, 2 * to + c))
        return lax.ppermute(block, ("seq", "head"), route)

    kv = jnp.concatenate([along_pieces(kv_own[:, :, -WIN:], 1), kv_own], axis=2)
    doubled = lambda feat: jnp.concatenate([feat, -feat], axis=2)
    query_feat, key_feat = doubled(query_feat_all), doubled(key_feat_all)
    phi_key, end_state = key_state(end_docs, kv, key_feat, key_doc_lanes)
    carry = jnp.zeros(end_state.shape, F32)
    for source, part in from_pieces(end_state):
        after = lax.dynamic_index_in_dim(piece_docs, source + 1, 1, keepdims=False)
        keep = (source < piece) & (after == carry_doc)
        carry = carry + jnp.where(keep[:, None, None, None], part.astype(F32), 0.0)
    phi_query = query_features(query, query_feat, kv.shape[1])
    attn = attend(
        end_docs, query, kv, phi_key, phi_query, carry, query_doc_lanes, key_doc_lanes, pair_docs
    )

    keep, away = out_project(core_index, attn, out_mat, o_in, share_len)
    mid_rows, nmid, low_mix = tokens_call(
        middle_kernel,
        [flat_tokens(v) for v in (hidden_in, keep, flip_core(away))],
        [second, gain_ffn],
        [(model_dim, BF16), (model_dim, BF16), (LOW, BF16)],
        "middle",
    )

    nmid_x = flip_x(nmid)

    def chip_tokens(own):
        return own, flip_core(own)

    def sum_away(own, other):
        return (own.astype(F32) + flip_core(other).astype(F32)).astype(BF16)

    x_mine = chip_tokens(nmid)
    c_mine, c_away = flat_tokens(cot_mine), flat_tokens(cot_away)
    run = lambda x, c, w, before=(), after=(): ffn(
        x, c, w, live_rows, share_len, slots, before, after
    )
    mine = run(x_mine, c_mine, ffn_mats[:2])
    x_away = chip_tokens(hold(nmid_x, (mine[0],)))
    away = run(x_away, c_away, ffn_mats[:-1])
    away = run(x_away, c_away, ffn_mats[-1:], away)
    gn_there = sum_away(*away[:2])
    gn_back = flip_x(gn_there)
    gn_own, gn_other, y_own, y_other = run(
        x_mine, c_mine, ffn_mats[2:], mine, (gn_there,)
    )
    y_there = sum_away(*away[2:])
    y_back = flip_x(y_there)
    branch, = tokens_call(
        functools.partial(branch_kernel, share_len, slots),
        [mid_rows, gn_own, gn_back, flat_tokens(grad_out)],
        [flip_core(gn_other[r * share_len : (r + 1) * share_len]) for r in range(slots)] + [gain_ffn],
        [(model_dim, BF16)],
        "branch",
        prefetch=[live_rows],
        tile=share_len,
    )

    shaped = lambda v: v.reshape(slots, share_len, -1)
    grad_attn, sum_o_in = attn_grad(
        core_index, shaped(branch), shaped(flip_core(branch)), attn, out_mat, second, o_in
    )
    sum_o_in = sum_o_in[:RANK]
    sum_o_out = ADAPTER_SCALE * dot(low_mix, branch, TN)[:RANK]

    grad_query, feat_query, gphi, gkv, grad_carry = attend_back(
        end_docs, query, kv, phi_key, phi_query, query_feat, carry, query_doc_lanes, key_doc_lanes,
        pair_docs, grad_attn, (y_there,),
    )
    block_out = tokens_call(
        sum_kernel, [mid_rows, y_own, flip_core(y_other), y_back], [], [(model_dim, BF16)], "sum_y",
        after=(grad_carry,),
    )[0]
    later = jnp.zeros(grad_carry.shape, F32)
    for source, part in from_pieces(grad_carry):
        start = lax.dynamic_index_in_dim(piece_docs, source, 1, keepdims=False)
        keep = (source > piece) & (start == next_doc)
        later = later + jnp.where(keep[:, None, None, None], part.astype(F32), 0.0)
    grad_body, grad_edge, feat_key = key_back(
        end_docs, kv, phi_key, key_feat, later, key_doc_lanes, gphi, gkv, (block_out,)
    )
    sum_q_feat = jnp.sum(feat_query, axis=0).reshape(2, -1, 2 * HD)
    sum_k_feat = jnp.sum(feat_key, axis=0).reshape(2, -1, 2 * HD)

    keep, away, outs = normed_grad(
        core_index, grad_query, grad_body, small, along_pieces(grad_edge, -1), qkv_mat, adapt_out_all,
        q_cols, share_len,
    )
    outs = ADAPTER_SCALE * outs
    outs = [
        outs[:, :RANK, :q_cols],
        outs[:, RANK : 2 * RANK, q_cols : q_cols + k_cols],
        outs[:, 2 * RANK : 3 * RANK, q_cols + k_cols :],
    ]
    grad_hidden, sum_in = tokens_call(
        finish_kernel,
        [flat_tokens(keep), flat_tokens(flip_core(away)), flat_tokens(hidden_in), branch],
        [gain_attn, adapt_in_all.T],
        [(model_dim, BF16)],
        "finish",
        sums=[(LOW, model_dim)],
    )
    grad_hidden = grad_hidden.reshape(hidden_in.shape)
    sum_in = sum_in[: 3 * RANK]

    by_rows = jnp.concatenate([sum_in, sum_o_out], axis=0)
    width = model_dim // (rows * seqs * heads)
    by_rows = by_rows.reshape(4 * RANK, rows, seqs, heads, width).transpose(3, 2, 1, 0, 4)

    def lanes_of(v):
        v = v.reshape(2, RANK, -1, 2 * HD).transpose(0, 2, 1, 3)
        return v.reshape(2, -1, 2 * HD)

    o_sets = jnp.stack([sum_o_in[:, :q_cols], sum_o_in[:, q_cols:]])
    packed = [lanes_of(v) for v in outs + [o_sets]] + [sum_q_feat, sum_k_feat]
    sizes = [v.shape[1] for v in packed]
    packed = jnp.concatenate(packed, axis=1)
    in_parts, packed = final_sums(by_rows, packed)
    in_parts = in_parts.reshape(4, RANK, width)
    cols, at = [], 0
    for size in sizes:
        cols.append(packed[at : at + size])
        at += size
    from_lanes = lambda v: v.reshape(-1, RANK, 2 * HD).transpose(1, 0, 2).reshape(RANK, -1)
    from_pairs = lambda v: v.reshape(-1, HD, 2, HD).transpose(0, 2, 1, 3).reshape(-1, HD, HD)
    cols = [from_lanes(v) for v in cols[:4]] + [from_pairs(v) for v in cols[4:]]
    cols[3] = cols[3].T

    return (
        block_out.reshape(hidden_in.shape),
        grad_hidden,
        in_parts[0].T,
        cols[0],
        in_parts[1].T,
        cols[1],
        in_parts[2].T,
        cols[2],
        cols[3],
        in_parts[3],
        cols[4],
        cols[5],
    )


def solution(mesh):
    return jax.shard_map(
        local,
        mesh=mesh,
        in_specs=(
            P("row", ("seq", "head"), None),
            P("row", ("seq", "head"), None),
            P("row"),
            P("row", None),
            P(),
            P(),
            P(("row", "seq"), "head"),
            P(("row", "seq"), "head"),
            P(("row", "seq"), "head"),
            P("head", ("row", "seq")),
            P(("row", "seq"), "head"),
            P(("row", "seq"), "head"),
            P("head", ("row", "seq")),
            P(),
            P(None, "head"),
            P(),
            P(None, "head"),
            P(),
            P(None, "head"),
            P("head", None),
            P(),
            P("head", None, None),
            P("head", None, None),
        ),
        out_specs=(
            P("row", ("seq", "head"), None),
            P("row", ("seq", "head"), None),
            P(("row", "seq", "head"), None),
            P(None, "head"),
            P(("row", "seq", "head"), None),
            P(None, "head"),
            P(("row", "seq", "head"), None),
            P(None, "head"),
            P("head", None),
            P(None, ("row", "seq", "head")),
            P("head", None, None),
            P("head", None, None),
        ),
        check_vma=False,
    )
```

```python
import functools

import jax
import jax.numpy as jnp
from jax import lax
from jax.experimental import pallas as pl
from jax.experimental.pallas import tpu as pltpu
from jax.sharding import PartitionSpec as P

HD = 64
RANK = 8
WIN = 64
FF_CHUNKS = (3, 4, 6, 3)

NORM_EPS = 1e-05
ADAPTER_SCALE = 2.0
F32 = jnp.float32
NT = ((1,), (1,))
TN = ((0,), (0,))
BF16 = jnp.bfloat16


def shift(block, axis, distance):
    size = lax.axis_size(axis)
    return lax.ppermute(block, axis, [(i, (i + distance) % size) for i in range(size)])


def flip_core(block):
    return lax.ppermute(block, "head", [(i, i ^ 1) for i in range(lax.axis_size("head"))])


def flip_core_parts(block, parts):
    size = block.shape[0] // parts
    return jnp.concatenate(
        [flip_core(block[i * size : (i + 1) * size]) for i in range(parts)], axis=0
    )


def flip_x(block):
    return lax.ppermute(block, "head", [(i, i ^ 2) for i in range(lax.axis_size("head"))])


def kernel_call(
    kernel, args, after, *, grid, in_specs, out_specs, out_shape, name, prefetch=0, scratch=(), cost=None
):
    count = len(args)

    def body(*refs):
        kernel(*refs[:count], *refs[count + len(after) :])

    return pl.pallas_call(
        body,
        grid_spec=pltpu.PrefetchScalarGridSpec(
            num_scalar_prefetch=prefetch,
            grid=grid,
            in_specs=list(in_specs) + [pl.BlockSpec(memory_space=pl.ANY)] * len(after),
            out_specs=out_specs,
            scratch_shapes=list(scratch),
        ),
        out_shape=out_shape,
        compiler_params=pltpu.CompilerParams(vmem_limit_bytes=60 * 2**20),
        cost_estimate=cost and pl.CostEstimate(
            flops=cost.flops // 4, bytes_accessed=cost.bytes_accessed // 4, transcendentals=0
        ),
        name=name,
    )(*args, *after)


def copy_kernel(src_ref, dst_ref):
    dst_ref[...] = src_ref[...]


def hold(value, after):
    flat = value.reshape(-1, value.shape[-1])
    tile = min(256, flat.shape[0])
    block = pl.BlockSpec((tile, flat.shape[1]), lambda i: (i, 0))
    held = kernel_call(
        copy_kernel, [flat], after, grid=(flat.shape[0] // tile,), in_specs=[block], out_specs=block,
        out_shape=jax.ShapeDtypeStruct(flat.shape, flat.dtype), name="hold",
    )
    return held.reshape(value.shape)


def dot(a, b, dims=((1,), (0,))):
    return lax.dot_general(a, b, (dims, ((), ())), preferred_element_type=F32)


def tie(value, *after):
    return lax.optimization_barrier((value,) + after)[0]


def rms_scaled(values, gain_vec):
    return (
        values * lax.rsqrt(jnp.mean(values * values, axis=-1, keepdims=True) + NORM_EPS) * gain_vec
    )


def rms_back(values, gain_vec, grad_in):
    factor = lax.rsqrt(jnp.mean(values * values, axis=-1, keepdims=True) + NORM_EPS)
    scaled = gain_vec * grad_in
    return factor * scaled - values * factor**3 * jnp.mean(values * scaled, axis=-1, keepdims=True)


def scatter_sum(parts, axis):
    size, place = lax.axis_size(axis), lax.axis_index(axis)
    total = lax.dynamic_index_in_dim(parts, place, 0, keepdims=False)
    for k in range(1, size):
        away = lax.dynamic_index_in_dim(parts, lax.rem(place + k, size), 0, keepdims=False)
        total = total + shift(away, axis, k)
    return total


def full_sum(part, axis):
    size = lax.axis_size(axis)
    step = 1
    while step < size:
        sent = part.astype(BF16)
        got = lax.ppermute(sent, axis, [(i, i ^ step) for i in range(size)])
        part = sent.astype(F32) + got.astype(F32)
        step *= 2
    return part


def gather_plan(rows, seqs, weights):
    free = {"row": 0.0, "seq": 0.0, "x": 0.0}
    running = []
    plan = []

    def begin(now, starts):
        for t in starts:
            w, link = t[0], t[1]
            end = max(now, free[link]) + weights[w][0]
            free[link] = end
            running.append((end, len(plan), len(running), t))
        return starts

    def spread(w, k, l):
        starts = []
        row_first = weights[w][2]
        if (l == 0 or not row_first) and k + 1 < rows:
            starts.append((w, "row", k + 1, l))
        if (k == 0 or row_first) and l + 1 < seqs:
            starts.append((w, "seq", k, l + 1))
        if weights[w][1]:
            starts.append((w, "x", k, l))
        return starts

    first = [t for w in range(len(weights)) if weights[w][3] == 0 for t in spread(w, 0, 0)]
    plan.append((None, begin(0.0, first)))
    done = 0
    while running:
        event = min(running)
        running.remove(event)
        now, t = event[0], event[3]
        done += 1
        starts = [] if t[1] == "x" else spread(t[0], t[2], t[3])
        for w in range(len(weights)):
            if weights[w][3] == done:
                starts = starts + spread(w, 0, 0)
        plan.append((t, begin(now, starts)))
    return plan


def gather_kernel(plan, rows, seqs, parts, over_x, small_count, *refs):
    count = len(over_x)
    inputs, refs = refs[: count + small_count + 2], refs[count + small_count + 2 :]
    shards, smalls = inputs[:count], inputs[count : count + small_count]
    hidden, cot = inputs[count + small_count :]
    wholes, refs = refs[:count], refs[count:]
    small_outs, refs = refs[:small_count], refs[small_count:]
    hidden_out, cot_mine, cot_away = refs[:3]
    send_sem, recv_sem, copy_sem, more_send, more_recv = refs[3:]
    row, seq, head = lax.axis_index("row"), lax.axis_index("seq"), lax.axis_index("head")
    x_place = head // 2
    across = {"head": lax.rem(head + 2, 4)}
    partner = {"head": head + 1 - 2 * lax.rem(head, 2)}
    away = {
        "row": {"row": lax.rem(row + 1, rows)},
        "seq": {"seq": lax.rem(seq + 1, seqs)},
        "x": across,
    }
    barrier = pltpu.get_barrier_semaphore()
    sources = (
        {"row": lax.rem(row + rows - 1, rows)},
        {"seq": lax.rem(seq + seqs - 1, seqs)},
        across,
        partner,
    )
    for source in sources:
        pl.semaphore_signal(
            barrier, inc=1, device_id=source, device_id_type=pl.DeviceIdType.MESH
        )
    pl.semaphore_wait(barrier, len(sources))

    def slot(p, k, l):
        w, columns = parts[p][0], pl.ds(*parts[p][1])
        depth = shards[w].shape[0]
        place = lax.rem(row - k + rows, rows) * seqs + lax.rem(seq - l + seqs, seqs)
        at = pl.ds(pl.multiple_of(place * depth, depth), depth)
        return wholes[w].at[x_place, at, columns] if over_x[w] else wholes[w].at[at, columns]

    number = {}
    last_x = 0
    for i, (event, starts) in enumerate(plan):
        for t in starts:
            number[t] = len(number)
            if t[1] == "x":
                last_x = i

    def remote(src, dst, send, recv, device):
        return pltpu.make_async_remote_copy(
            src_ref=src, dst_ref=dst, send_sem=send, recv_sem=recv, device_id=device,
            device_id_type=pl.DeviceIdType.MESH,
        )

    def transfer(t):
        w, link, k, l = t
        source = {"row": (k - 1, l), "seq": (k, l - 1), "x": (k, l)}[link]
        dst = slot(w, *source)
        n = number[t]
        src = shards[parts[w][0]].at[:, pl.ds(*parts[w][1])] if source == (0, 0) else dst
        return remote(src, dst, send_sem.at[n], recv_sem.at[n], away[link])

    def more(i, src, dst, device):
        return remote(src, dst, more_send.at[i], more_recv.at[i], device)

    early = [more(i, a, b, across) for i, (a, b) in enumerate(zip(smalls, small_outs))]
    early.append(more(small_count, hidden, hidden_out, partner))
    early.append(more(small_count + 1, cot, cot_mine.at[1], partner))
    cot_x = more(small_count + 2, cot, cot_away.at[0], across)
    cot_last = more(small_count + 3, cot_away.at[0], cot_away.at[1], partner)
    own = [
        pltpu.make_async_copy(
            shards[w].at[:, pl.ds(*columns)], slot(p, 0, 0), copy_sem.at[p]
        )
        for p, (w, columns) in enumerate(parts)
    ] + [pltpu.make_async_copy(cot, cot_mine.at[0], copy_sem.at[len(parts)])]
    for i, (event, starts) in enumerate(plan):
        if event is not None:
            transfer(event).wait_recv()
        for t in starts:
            transfer(t).start()
        if event is None:
            for copy in [cot_x] + early + own:
                copy.start()
        if i == last_x:
            cot_x.wait()
            cot_last.start()
    for t in number:
        transfer(t).wait_send()
    for copy in early + own + [cot_last]:
        copy.wait()


def gather(shards, over_x, pieces, smalls, hidden, cot):
    rows, seqs = lax.axis_size("row"), lax.axis_size("seq")
    plan = gather_plan(
        rows,
        seqs,
        [(float(shards[w].shape[0] * c[1]), over_x[w], first, later) for w, c, first, later in pieces],
    )
    parts = [(w, c) for w, c, _, _ in pieces]
    total = sum(len(starts) for _, starts in plan)
    shapes = []
    for shard, x in zip(shards, over_x):
        depth, width = shard.shape
        whole = (rows * seqs * depth, width)
        shapes.append(jax.ShapeDtypeStruct(((2,) + whole) if x else whole, shard.dtype))
    same = lambda v: jax.ShapeDtypeStruct(v.shape, v.dtype)
    twice = jax.ShapeDtypeStruct((2,) + cot.shape, cot.dtype)
    shapes += [same(v) for v in smalls] + [same(hidden), twice, twice]
    more = len(smalls) + 4
    place = pl.BlockSpec(memory_space=pl.ANY)
    outs = pl.pallas_call(
        functools.partial(gather_kernel, plan, rows, seqs, parts, over_x, len(smalls)),
        out_shape=shapes,
        in_specs=[place] * (len(shards) + len(smalls) + 2),
        out_specs=[place] * len(shapes),
        scratch_shapes=[
            pltpu.SemaphoreType.DMA((total,)),
            pltpu.SemaphoreType.DMA((total,)),
            pltpu.SemaphoreType.DMA((len(parts) + 1,)),
            pltpu.SemaphoreType.DMA((more,)),
            pltpu.SemaphoreType.DMA((more,)),
        ],
        compiler_params=pltpu.CompilerParams(collective_id=0, has_side_effects=True),
        name="gather",
    )(*shards, *smalls, hidden, cot)
    n = len(shards)
    return outs[:n], outs[n : n + len(smalls)], outs[-3:]


def ffn_kernel(chunks, before, share_len, slots, live_ref, x_ref, more_ref, cot_ref, *refs):
    weights, refs = refs[:chunks], refs[chunks:]
    earlier, refs = refs[: 4 * before], refs[4 * before :]
    outs, held, sem = refs[:4], refs[4:-1], refs[-1]
    step = pl.program_id(0)
    tile = x_ref.shape[0]
    copies = [pltpu.make_async_copy(weights[c], held[c], sem.at[c]) for c in range(chunks)]

    @pl.when(step == 0)
    def _():
        for copy in copies:
            copy.start()

    first = step < pl.num_programs(0) // 2
    live = (lax.rem(step * tile // share_len, slots) < live_ref[0]).astype(F32)
    x, cot = jnp.where(first, x_ref[...], more_ref[...]), cot_ref[...]
    sums = [None, None]
    if before:
        sums = [jnp.where(first, earlier[i][...], earlier[i + 1][...]).astype(F32) for i in (0, 2)]
    for c in range(chunks):

        @pl.when(step == 0)
        def _():
            copies[c].wait()

        w, width = held[c], held[c].shape[1] // 3
        gate = dot(x, w[:, :width])
        up = dot(x, w[:, width : 2 * width])
        gm = dot(cot, w[:, 2 * width :]) * live
        sig = jax.nn.sigmoid(gate)
        silu = gate * sig
        mixed = (silu * up).astype(BF16)
        g_gate = (gm * up * (sig + silu * (1.0 - sig))).astype(BF16)
        g_up = (gm * silu).astype(BF16)
        parts = (
            dot(jnp.concatenate([g_gate, g_up], axis=1), w[:, : 2 * width], NT),
            dot(mixed, w[:, 2 * width :], NT),
        )
        sums = [p if t is None else t + p for t, p in zip(sums, parts)]

    @pl.when(first)
    def _():
        outs[0][...] = sums[0].astype(BF16)
        outs[2][...] = sums[1].astype(BF16)

    @pl.when(jnp.logical_not(first))
    def _():
        outs[1][...] = sums[0].astype(BF16)
        outs[3][...] = sums[1].astype(BF16)


def ffn(x, cot, weights, live_rows, share_len, slots, before=(), after=()):
    tokens, depth = cot.shape
    chunks = len(weights)
    units = sum(w.shape[1] for w in weights) // 3
    tile = min(256, share_len)
    half = tokens // tile // 2
    lower = pl.BlockSpec((tile, depth), lambda i, *_: (jnp.minimum(i, half - 1), 0))
    upper = pl.BlockSpec((tile, depth), lambda i, *_: (jnp.maximum(i - half, 0), 0))
    out = jax.ShapeDtypeStruct((tokens // 2, depth), BF16)
    return kernel_call(
        functools.partial(ffn_kernel, chunks, len(before) // 4, share_len, slots),
        [live_rows, x[0], x[1], cot, *weights, *before],
        after,
        prefetch=1,
        grid=(tokens // tile,),
        in_specs=[lower, upper, pl.BlockSpec((tile, depth), lambda i, *_: (i, 0))]
        + [pl.BlockSpec(memory_space=pl.ANY)] * chunks
        + [lower, upper] * (len(before) // 2),
        out_specs=[lower, upper, lower, upper],
        out_shape=[out] * 4,
        scratch=[
            *[pltpu.VMEM(w.shape, BF16) for w in weights],
            pltpu.SemaphoreType.DMA((chunks,)),
        ],
        cost=pl.CostEstimate(
            flops=12 * tokens * depth * units,
            bytes_accessed=8 * tokens * depth + 6 * depth * units,
            transcendentals=0,
        ),
        name="ffn",
    )


def lower_lanes(like):
    return lax.broadcasted_iota(jnp.int32, like.shape, 1) < HD


def half_ones():
    r = lax.broadcasted_iota(jnp.int32, (2 * HD, 2 * HD), 0) // HD
    c = lax.broadcasted_iota(jnp.int32, (2 * HD, 2 * HD), 1) // HD
    return (r == c).astype(F32).astype(BF16)


def swap(v):
    return pltpu.roll(v, HD, 1)


def features(x, feat):
    logit = dot(x, feat)
    low = lower_lanes(logit)
    top = jnp.max(jnp.where(low, logit, -jnp.inf), axis=1, keepdims=True)
    bottom = jnp.max(jnp.where(low, -jnp.inf, logit), axis=1, keepdims=True)
    e = jnp.exp(logit - jnp.where(low, top, bottom))
    return e / dot(e.astype(BF16), half_ones())


def features_back(phi, grad):
    p = phi.astype(F32)
    prod = p * grad
    low = lower_lanes(prod)
    first = jnp.sum(jnp.where(low, prod, 0.0), axis=1, keepdims=True)
    second = jnp.sum(jnp.where(low, 0.0, prod), axis=1, keepdims=True)
    g = prod - p * jnp.where(low, first, second)
    return (g - swap(g)).astype(BF16)[:, :HD]


def values_ones(kv):
    kv = kv.astype(F32)
    return jnp.where(lower_lanes(kv), swap(kv), 1.0).astype(BF16)


def key_state_kernel(ends_ref, kv_ref, feat_ref, kdoc_ref, phi_ref, state_ref):
    r = pl.program_id(0)
    kv = kv_ref[0, 0]
    body = kv.shape[0] - WIN
    phi = features(kv[:, :HD], feat_ref[0]).astype(BF16)
    phi_ref[0, 0] = phi
    last = ends_ref[r, body // WIN]
    held = jnp.where(kdoc_ref[0, :body] == last, phi[:body].astype(F32), 0.0).astype(BF16)
    state_ref[0, 0] = dot(held, values_ones(kv[:body]), TN).astype(BF16)


def key_state(ends, kv, feat, kdoc, after=()):
    slots, groups, ext, _ = kv.shape
    block = lambda r, g, *_: (r, g, 0, 0)
    return kernel_call(
        key_state_kernel,
        [ends, kv, feat, kdoc],
        after,
        prefetch=1,
        grid=(slots, groups),
        in_specs=[
            pl.BlockSpec((1, 1, ext, 2 * HD), block),
            pl.BlockSpec((1, HD, 2 * HD), lambda r, g, *_: (g, 0, 0)),
            pl.BlockSpec((1, ext, 2 * HD), lambda r, g, *_: (r, 0, 0)),
        ],
        out_specs=[
            pl.BlockSpec((1, 1, ext, 2 * HD), block),
            pl.BlockSpec((1, 1, 2 * HD, 2 * HD), block),
        ],
        out_shape=[
            jax.ShapeDtypeStruct((slots, groups, ext, 2 * HD), BF16),
            jax.ShapeDtypeStruct((slots, groups, 2 * HD, 2 * HD), BF16),
        ],
        name="key_state",
    )


def block_masks(b, qdoc_ref, pdoc_ref):
    rows = slice(WIN * b, WIN * b + WIN)
    same = qdoc_ref[0, rows] == pdoc_ref[0, b : b + 1]
    row = lax.broadcasted_iota(jnp.int32, (WIN, 2 * WIN), 0)
    col = lax.broadcasted_iota(jnp.int32, (WIN, 2 * WIN), 1)
    linear = same & (col <= row)
    window = same & (col > row) & (col <= row + WIN)
    return window, linear


def next_state(b, ends_ref, r, state, phi_ref, vx_ref, kdoc_ref):
    rows = slice(WIN * (b - 1), WIN * b)
    keep = (ends_ref[r, b] == ends_ref[r, b - 1]).astype(F32)
    held = jnp.where(
        kdoc_ref[0, rows] == ends_ref[r, b], phi_ref[0, 0, rows].astype(F32), 0.0
    ).astype(BF16)
    return state * keep + dot(held, vx_ref[rows], TN)


def block_forward(b, ends_ref, r, q_ref, kv_ref, phi_ref, phiq_ref, vx_ref, state_low, qdoc_ref, pdoc_ref):
    heads = q_ref.shape[1]
    rows, pair = slice(WIN * b, WIN * b + WIN), slice(WIN * b, WIN * b + 2 * WIN)
    window, linear = block_masks(b, qdoc_ref, pdoc_ref)
    valid = qdoc_ref[0, rows] == ends_ref[r, b]
    query = jnp.concatenate([q_ref[0, h, rows] for h in range(heads)], axis=0)
    phi_query = jnp.concatenate([phiq_ref[0, h, rows] for h in range(heads)], axis=0)
    key = kv_ref[0, 0, pair, :HD]
    phi_key = phi_ref[0, 0, pair]
    score = dot(query, key, NT) * (HD**-0.5)
    lin = dot(phi_query, phi_key, NT)
    part = lambda v, h: v[WIN * h : WIN * h + WIN]
    exps = [jnp.where(window, jnp.exp(part(score, h)), 0.0) for h in range(heads)]
    weight = jnp.concatenate(
        [jnp.where(linear, part(lin, h), exps[h]).astype(BF16) for h in range(heads)], axis=0
    )
    phi_valid = jnp.concatenate(
        [jnp.where(valid, part(phi_query, h).astype(F32), 0.0).astype(BF16) for h in range(heads)],
        axis=0,
    )
    both = dot(weight, vx_ref[pair]) + dot(phi_valid, state_low)
    denominator = jnp.where(lower_lanes(both), swap(both), both)
    return (query, phi_query, phi_valid, key, phi_key, exps, weight, both / denominator, denominator,
            window, linear, valid)


def query_feature_kernel(q_ref, feat_ref, phi_ref):
    for h in range(q_ref.shape[1]):
        phi_ref[0, h] = features(q_ref[0, h], feat_ref[h]).astype(BF16)


def query_features(q, feat, groups):
    slots, all_heads, length, _ = q.shape
    sp = attention_specs(slots, groups, all_heads // groups, length)
    return kernel_call(
        query_feature_kernel,
        [q, feat],
        (),
        grid=(slots, groups),
        in_specs=[sp["q"], sp["feat"]],
        out_specs=sp["phiq"],
        out_shape=jax.ShapeDtypeStruct((slots, all_heads, length, 2 * HD), BF16),
        name="query_features",
    )


def attend_kernel(
    ends_ref, q_ref, kv_ref, phi_ref, phiq_ref, carry_ref, qdoc_ref, kdoc_ref, pdoc_ref,
    attn_ref, vx_ref,
):
    r = pl.program_id(0)
    heads, length = q_ref.shape[1], q_ref.shape[2]
    vx_ref[...] = values_ones(kv_ref[0, 0])
    state = carry_ref[0, 0]
    for b in range(length // WIN):
        if b:
            state = next_state(b, ends_ref, r, state, phi_ref, vx_ref, kdoc_ref)
        out = block_forward(
            b, ends_ref, r, q_ref, kv_ref, phi_ref, phiq_ref, vx_ref, state.astype(BF16), qdoc_ref,
            pdoc_ref,
        )
        attn = out[7]
        low = lower_lanes(attn[:WIN])
        for h in range(0, heads, 2):
            first, second = attn[WIN * h : WIN * h + WIN], attn[WIN * h + WIN : WIN * h + 2 * WIN]
            attn_ref[0, WIN * b : WIN * b + WIN, HD * h : HD * h + 2 * HD] = jnp.where(
                low, first, swap(second)
            ).astype(BF16)


def attention_specs(slots, groups, heads, length):
    ext = length + WIN
    four = lambda r, g, *_: (r, g, 0, 0)
    docs = lambda r, g, *_: (r, 0, 0)
    return dict(
        q=pl.BlockSpec((1, heads, length, HD), four),
        kv=pl.BlockSpec((1, 1, ext, 2 * HD), four),
        phiq=pl.BlockSpec((1, heads, length, 2 * HD), four),
        feat=pl.BlockSpec((heads, HD, 2 * HD), lambda r, g, *_: (g, 0, 0)),
        state=pl.BlockSpec((1, 1, 2 * HD, 2 * HD), four),
        qdoc=pl.BlockSpec((1, length, 2 * HD), docs),
        kdoc=pl.BlockSpec((1, ext, 2 * HD), docs),
        pdoc=pl.BlockSpec((1, length // WIN, 2 * HD), docs),
        tokens=pl.BlockSpec((1, length, heads * HD), lambda r, g, *_: (r, 0, g)),
        fgrad=pl.BlockSpec((1, heads // 2, HD, 2 * HD), four),
    )


def attend(ends, q, kv, phi, phiq, carry, qdoc, kdoc, pdoc, after=()):
    slots, all_heads, length, _ = q.shape
    groups = kv.shape[1]
    heads = all_heads // groups
    sp = attention_specs(slots, groups, heads, length)
    return kernel_call(
        attend_kernel,
        [ends, q, kv, phi, phiq, carry, qdoc, kdoc, pdoc],
        after,
        prefetch=1,
        grid=(slots, groups),
        in_specs=[sp[n] for n in ("q", "kv", "kv", "phiq", "state", "qdoc", "kdoc", "pdoc")],
        out_specs=sp["tokens"],
        scratch=[pltpu.VMEM((length + WIN, 2 * HD), BF16)],
        out_shape=jax.ShapeDtypeStruct((slots, length, all_heads * HD), BF16),
        name="attend",
    )


def attend_back_kernel(
    ends_ref, q_ref, kv_ref, phi_ref, phiq_ref, feat_ref, carry_ref, qdoc_ref, kdoc_ref, pdoc_ref,
    g_ref, gq_ref, gfeat_ref, gphi_ref, gkv_ref, gcarry_ref, vx_ref, gstate_ref, gphiq_ref, gk_ref,
    gv_ref, gqs_ref, gl_ref,
):
    r = pl.program_id(0)
    heads, length = q_ref.shape[1], q_ref.shape[2]
    blocks = length // WIN
    vx_ref[...] = values_ones(kv_ref[0, 0])
    gphi_ref[...] = jnp.zeros_like(gphi_ref)
    gk_ref[...] = jnp.zeros_like(gk_ref)
    gv_ref[...] = jnp.zeros_like(gv_ref)
    scale = HD**-0.5
    state = carry_ref[0, 0]
    for b in range(blocks):
        rows, pair = slice(WIN * b, WIN * b + WIN), slice(WIN * b, WIN * b + 2 * WIN)
        if b:
            state = next_state(b, ends_ref, r, state, phi_ref, vx_ref, kdoc_ref)
        state_low = state.astype(BF16)
        (query, phi_query, phi_valid, key, phi_key, exps, weight, attn, denominator, window, linear,
         valid) = block_forward(
            b, ends_ref, r, q_ref, kv_ref, phi_ref, phiq_ref, vx_ref, state_low, qdoc_ref, pdoc_ref
        )
        grads = []
        for h in range(0, heads, 2):
            g = g_ref[0, rows, HD * h : HD * h + 2 * HD].astype(F32)
            grads += [g, swap(g)]
        grad = jnp.concatenate(grads, axis=0)
        low = lower_lanes(grad)
        grad = jnp.where(low, grad, 0.0)
        g_denom = -jnp.sum(grad * attn, axis=1, keepdims=True)
        gx = (jnp.where(low, grad, g_denom * (1.0 / HD)) / denominator).astype(BF16)
        g_weight = dot(gx, vx_ref[pair], NT)
        part = lambda v, h: v[WIN * h : WIN * h + WIN]
        g_score = jnp.concatenate(
            [(exps[h] * part(g_weight, h)).astype(BF16) for h in range(heads)], axis=0
        )
        g_lin = jnp.concatenate(
            [jnp.where(linear, part(g_weight, h), 0.0).astype(BF16) for h in range(heads)], axis=0
        )
        g_query = dot(g_score, key) * scale
        gk_ref[pair] += dot(g_score, query, TN) * scale
        gv_ref[pair] += dot(weight, gx, TN)
        gphi_ref[0, 0, pair] += dot(g_lin, phi_query, TN)
        from_lin = dot(g_lin, phi_key)
        from_state = dot(gx, state_low, NT)
        gstate_ref[b] = dot(phi_valid, gx, TN)
        for h in range(heads):
            gphiq_ref[h, rows] = part(from_lin, h) + jnp.where(valid, part(from_state, h), 0.0)
            gqs_ref[h, rows] = part(g_query, h)
    for h in range(heads):
        g_logit = features_back(phiq_ref[0, h], gphiq_ref[h])
        gl_ref[h] = g_logit
        gqs_ref[h] += dot(g_logit, feat_ref[h][:, :HD], NT)
    gq_ref[0] = jnp.concatenate([gqs_ref[h] for h in range(heads)], axis=1).astype(BF16)
    for h in range(0, heads, 2):
        gfeat_ref[0, h // 2] = jnp.concatenate(
            [dot(q_ref[0, i], gl_ref[i], TN) for i in (h, h + 1)], axis=1
        )
    later = gstate_ref[blocks - 1]
    for b in range(blocks - 1, 0, -1):
        rows = slice(WIN * (b - 1), WIN * b)
        low_state = later.astype(BF16)
        mask = kdoc_ref[0, rows] == ends_ref[r, b]
        gphi_ref[0, 0, rows] += jnp.where(mask, dot(vx_ref[rows], low_state, NT), 0.0)
        gv_ref[rows] += jnp.where(mask, dot(phi_ref[0, 0, rows], low_state), 0.0)
        keep = (ends_ref[r, b] == ends_ref[r, b - 1]).astype(F32)
        later = gstate_ref[b - 1] + keep * later
    gcarry_ref[0, 0] = later.astype(BF16)
    gv = gv_ref[...]
    gkv_ref[0, 0, :, :HD] = gk_ref[...]
    gkv_ref[0, 0, :, HD:] = gv[:, :HD]


def attend_back(ends, q, kv, phi, phiq, feat, carry, qdoc, kdoc, pdoc, g, after=()):
    slots, all_heads, length, _ = q.shape
    groups = kv.shape[1]
    heads = all_heads // groups
    ext = length + WIN
    sp = attention_specs(slots, groups, heads, length)
    return kernel_call(
        attend_back_kernel,
        [ends, q, kv, phi, phiq, feat, carry, qdoc, kdoc, pdoc, g],
        after,
        prefetch=1,
        grid=(slots, groups),
        in_specs=[
            sp[n]
            for n in ("q", "kv", "kv", "phiq", "feat", "state", "qdoc", "kdoc", "pdoc", "tokens")
        ],
        out_specs=[sp["tokens"], sp["fgrad"], sp["kv"], sp["kv"], sp["state"]],
        scratch=[
            pltpu.VMEM((ext, 2 * HD), BF16),
            pltpu.VMEM((length // WIN, 2 * HD, 2 * HD), F32),
            pltpu.VMEM((heads, length, 2 * HD), F32),
            pltpu.VMEM((ext, HD), F32),
            pltpu.VMEM((ext, 2 * HD), F32),
            pltpu.VMEM((heads, length, HD), F32),
            pltpu.VMEM((heads, length, HD), BF16),
        ],
        out_shape=[
            jax.ShapeDtypeStruct((slots, length, all_heads * HD), BF16),
            jax.ShapeDtypeStruct((slots, all_heads // 2, HD, 2 * HD), F32),
            jax.ShapeDtypeStruct((slots, groups, ext, 2 * HD), F32),
            jax.ShapeDtypeStruct((slots, groups, ext, 2 * HD), F32),
            jax.ShapeDtypeStruct((slots, groups, 2 * HD, 2 * HD), BF16),
        ],
        name="attend_back",
    )


def key_back_kernel(
    ends_ref, kv_ref, phi_ref, feat_ref, later_ref, kdoc_ref, gphi_ref, gkv_ref,
    body_ref, edge_ref, gfeat_ref,
):
    r = pl.program_id(0)
    ext = kv_ref.shape[2]
    body = ext - WIN
    last = ends_ref[r, body // WIN]
    mask = kdoc_ref[0, :body] == last
    keys, vals, feats = [], [], []
    for i in range(2):
        kv, phi = kv_ref[0, i], phi_ref[0, i]
        later = later_ref[0, i].astype(BF16)
        more_phi = jnp.where(mask, dot(values_ones(kv[:body]), later, NT), 0.0)
        more_v = jnp.where(mask, dot(phi[:body], later), 0.0)
        tail = jnp.zeros((WIN, 2 * HD), F32)
        g_phi = gphi_ref[0, i] + jnp.concatenate([more_phi, tail], axis=0)
        g_logit = features_back(phi, g_phi)
        gkv = gkv_ref[0, i]
        keys.append(gkv[:, :HD] + dot(g_logit, feat_ref[i][:, :HD], NT))
        vals.append(gkv[:, HD:] + jnp.concatenate([more_v, tail], axis=0)[:, :HD])
        feats.append(dot(kv[:, :HD], g_logit, TN))
    gfeat_ref[0, 0] = jnp.concatenate(feats, axis=1)
    both = jnp.concatenate(keys + vals, axis=1)
    body_ref[0, 0] = both[WIN:]
    edge_ref[0, 0] = both[:WIN].astype(BF16)


def key_back(ends, kv, phi, feat, later, kdoc, gphi, gkv, after=()):
    slots, groups, ext, _ = kv.shape
    four = lambda r, s, *_: (r, s, 0, 0)
    wide = pl.BlockSpec((1, 2, ext, 2 * HD), four)
    body = pl.BlockSpec((1, 1, ext - WIN, 4 * HD), four)
    edge = pl.BlockSpec((1, 1, WIN, 4 * HD), four)
    sets = groups // 2
    return kernel_call(
        key_back_kernel,
        [ends, kv, phi, feat, later, kdoc, gphi, gkv],
        after,
        prefetch=1,
        grid=(slots, groups // 2),
        in_specs=[
            wide,
            wide,
            pl.BlockSpec((2, HD, 2 * HD), lambda r, s, *_: (s, 0, 0)),
            pl.BlockSpec((1, 2, 2 * HD, 2 * HD), four),
            pl.BlockSpec((1, ext, 2 * HD), lambda r, s, *_: (r, 0, 0)),
            wide,
            wide,
        ],
        out_specs=[body, edge, pl.BlockSpec((1, 1, HD, 2 * HD), four)],
        out_shape=[
            jax.ShapeDtypeStruct((slots, sets, ext - WIN, 4 * HD), F32),
            jax.ShapeDtypeStruct((slots, sets, WIN, 4 * HD), BF16),
            jax.ShapeDtypeStruct((slots, sets, HD, 2 * HD), F32),
        ],
        name="key_back",
    )


LOW = 128


def normalize(values, gain):
    scale = lax.rsqrt(jnp.mean(values * values, axis=-1, keepdims=True) + NORM_EPS)
    return (values * scale * gain).astype(BF16)


def project_kernel(
    sets, q_cols, k_cols, shares, core_ref, own_ref, other_ref, gain_ref, w_ref, a_ref, b_ref, q_ref,
    kv_ref, small_ref
):
    own = pl.program_id(1) // shares == core_ref[0]
    x = normalize(jnp.where(own, own_ref[0], other_ref[0]).astype(F32), gain_ref[...])
    width = q_cols + 2 * k_cols
    small = dot(x, a_ref[...]).astype(BF16)
    small_ref[0] = small
    heads, groups = q_cols // HD, k_cols // HD
    for s in range(sets):
        cols = slice(s * width, (s + 1) * width)
        full = dot(x, w_ref[s]) + ADAPTER_SCALE * dot(small, b_ref[:, cols])
        for h in range(heads):
            q_ref[0, s * heads + h] = full[:, h * HD : h * HD + HD].astype(BF16)
        for g in range(0, groups, 2):
            k = full[:, q_cols + g * HD : q_cols + g * HD + 2 * HD]
            start = q_cols + k_cols + g * HD
            v = full[:, start : start + 2 * HD]
            low = lower_lanes(k)
            kv_ref[0, s * groups + g] = jnp.where(low, k, swap(v)).astype(BF16)
            kv_ref[0, s * groups + g + 1] = jnp.where(low, swap(k), v).astype(BF16)


def project(core, own, other, gain, w, a, b, q_cols, k_cols, after=()):
    slots, share, depth = own.shape
    length = 2 * share
    sets = w.shape[0]
    heads, groups = sets * q_cols // HD, sets * k_cols // HD
    tile = min(256, share)
    shares = share // tile
    token = pl.BlockSpec((1, tile, depth), lambda r, i, *_: (r, lax.rem(i, shares), 0))
    return kernel_call(
        functools.partial(project_kernel, sets, q_cols, k_cols, shares),
        [core, own, other, gain, w, a, b],
        after,
        prefetch=1,
        grid=(slots, length // tile),
        in_specs=[
            token,
            token,
            pl.BlockSpec(gain.shape, lambda r, i, *_: (0, 0)),
            pl.BlockSpec(w.shape, lambda r, i, *_: (0, 0, 0)),
            pl.BlockSpec(a.shape, lambda r, i, *_: (0, 0)),
            pl.BlockSpec(b.shape, lambda r, i, *_: (0, 0)),
        ],
        out_specs=[
            pl.BlockSpec((1, heads, tile, HD), lambda r, i, *_: (r, 0, i, 0)),
            pl.BlockSpec((1, groups, tile, 2 * HD), lambda r, i, *_: (r, 0, i, 0)),
            pl.BlockSpec((1, tile, LOW), lambda r, i, *_: (r, i, 0)),
        ],
        out_shape=[
            jax.ShapeDtypeStruct((slots, heads, length, HD), BF16),
            jax.ShapeDtypeStruct((slots, groups, length, 2 * HD), BF16),
            jax.ShapeDtypeStruct((slots, length, LOW), BF16),
        ],
        cost=pl.CostEstimate(
            flops=2 * slots * length * w.size,
            bytes_accessed=2 * (slots * length * depth + w.size),
            transcendentals=0,
        ),
        name="project",
    )


def halves(share, tile):
    shares = share // tile
    own = lambda r, i, core: (r, core[0] * shares + i, 0)
    other = lambda r, i, core: (r, (1 - core[0]) * shares + i, 0)
    return own, other


def out_project_kernel(core_ref, own_ref, other_ref, w_ref, low_ref, keep_ref, away_ref):
    depth = w_ref.shape[1]
    half = w_ref.shape[2]
    for src, dst in ((own_ref, keep_ref), (other_ref, away_ref)):
        attn = src[0]
        full = dot(attn[:, :half], w_ref[0], NT) + dot(attn[:, half:], w_ref[1], NT)
        dst[0, :, :depth] = full.astype(BF16)
        dst[0, :, depth:] = dot(attn, low_ref[...]).astype(BF16)


def out_project(core, attn, w, low, share):
    slots, length, width = attn.shape
    depth = w.shape[1]
    tile = min(256, share)
    own, other = halves(share, tile)
    out = pl.BlockSpec((1, tile, depth + LOW), lambda r, i, *_: (r, i, 0))
    shape = jax.ShapeDtypeStruct((slots, share, depth + LOW), BF16)
    return kernel_call(
        out_project_kernel,
        [core, attn, attn, w, low],
        (),
        prefetch=1,
        grid=(slots, share // tile),
        in_specs=[
            pl.BlockSpec((1, tile, width), own),
            pl.BlockSpec((1, tile, width), other),
            pl.BlockSpec(w.shape, lambda r, i, *_: (0, 0, 0)),
            pl.BlockSpec(low.shape, lambda r, i, *_: (0, 0)),
        ],
        out_specs=[out, out],
        out_shape=[shape, shape],
        name="out_project",
    )


def middle_kernel(hidden_ref, keep_ref, got_ref, second_ref, gain_ref, mid_ref, normed_ref, low_ref):
    depth = hidden_ref.shape[1]
    total = keep_ref[...].astype(F32) + got_ref[...].astype(F32)
    low = total[:, depth:].astype(BF16)
    low_ref[...] = low
    mid = hidden_ref[...].astype(F32) + total[:, :depth]
    mid = mid + ADAPTER_SCALE * dot(low, second_ref[...])
    mid_ref[...] = mid.astype(BF16)
    normed_ref[...] = normalize(mid, gain_ref[...])


def tokens_call(kernel, tiled, whole, outs, name, prefetch=(), sums=(), tile=256, after=()):
    tokens = tiled[0].shape[0]
    tile = min(tile, tokens)
    rows = lambda v: pl.BlockSpec((tile, v.shape[1]), lambda i, *_: (i, 0))
    full = lambda v: pl.BlockSpec(v.shape, lambda i, *_: (0, 0))
    shapes = [jax.ShapeDtypeStruct((tokens, width), kind) for width, kind in outs]
    totals = [jax.ShapeDtypeStruct(v, F32) for v in sums]
    return kernel_call(
        kernel,
        [*prefetch, *tiled, *whole],
        after,
        prefetch=len(prefetch),
        grid=(tokens // tile,),
        in_specs=[rows(v) for v in tiled] + [full(v) for v in whole],
        out_specs=[rows(v) for v in shapes] + [full(v) for v in totals],
        out_shape=shapes + totals,
        name=name,
    )


def norm_back(values, gain, grad):
    scale = lax.rsqrt(jnp.mean(values * values, axis=-1, keepdims=True) + NORM_EPS)
    scaled = gain * grad
    shared = scale * scale * scale * jnp.mean(values * scaled, axis=-1, keepdims=True)
    return scale, scale * scaled - values * shared


def pair_kernel(a_ref, b_ref, out_ref):
    out_ref[...] = a_ref[...] + b_ref[...].astype(F32)


def sum_kernel(*refs):
    refs[-1][...] = sum(r[...].astype(F32) for r in refs[:-1]).astype(BF16)


def branch_kernel(slot_len, slots, live_ref, mid_ref, a_ref, c_ref, cot_ref, *refs):
    parts, (gain_ref, grad_ref) = refs[:slots], refs[slots:]
    part = parts[0][...]
    for r in range(1, slots):
        part = jnp.where(pl.program_id(0) == r, parts[r][...], part)
    grad = a_ref[...].astype(F32) + part.astype(F32) + c_ref[...].astype(F32)
    tile = mid_ref.shape[0]
    token = pl.program_id(0) * tile + lax.broadcasted_iota(jnp.int32, (tile, 1), 0)
    live = token < live_ref[0] * slot_len
    cot = jnp.where(live, cot_ref[...].astype(F32), 0.0)
    mid = mid_ref[...].astype(F32)
    grad_ref[...] = (cot + norm_back(mid, gain_ref[...], grad)[1]).astype(BF16)


def attn_grad_kernel(
    shares, core_ref, own_ref, other_ref, attn_ref, w_ref, second_ref, first_ref, grad_ref, sum_ref
):
    own = pl.program_id(1) // shares == core_ref[0]
    x = jnp.where(own, own_ref[0], other_ref[0])
    low = (ADAPTER_SCALE * dot(x, second_ref[...], NT)).astype(BF16)
    half = w_ref.shape[2]
    first = first_ref[...]
    for s in range(2):
        cols = slice(s * half, (s + 1) * half)
        grad_ref[0, :, cols] = (dot(x, w_ref[s]) + dot(low, first[cols], NT)).astype(BF16)

    @pl.when((pl.program_id(0) == 0) & (pl.program_id(1) == 0))
    def _():
        sum_ref[...] = jnp.zeros_like(sum_ref)

    sum_ref[...] += dot(low, attn_ref[0], TN)


def attn_grad(core, own, other, attn, w, second, first):
    slots, share, depth = own.shape
    length = 2 * share
    width = attn.shape[2]
    tile = min(256, share)
    shares = share // tile
    token = pl.BlockSpec((1, tile, depth), lambda r, i, *_: (r, lax.rem(i, shares), 0))
    wide = pl.BlockSpec((1, tile, width), lambda r, i, *_: (r, i, 0))
    full = lambda v: pl.BlockSpec(v.shape, lambda r, i, *_: (0,) * v.ndim)
    total = jax.ShapeDtypeStruct((LOW, width), F32)
    return kernel_call(
        functools.partial(attn_grad_kernel, shares),
        [core, own, other, attn, w, second, first],
        (),
        prefetch=1,
        grid=(slots, length // tile),
        in_specs=[token, token, wide, full(w), full(second), full(first)],
        out_specs=[wide, full(total)],
        out_shape=[jax.ShapeDtypeStruct(attn.shape, BF16), total],
        name="attn_grad",
    )


def normed_grad_kernel(
    q_cols, shares, core_ref, q_own_ref, q_other_ref, kv_own_ref, kv_other_ref, s_own_ref, s_other_ref,
    back_ref, w_ref, b_ref, keep_ref, away_ref, sum_ref
):
    depth, width = w_ref.shape[1:]
    core, step = core_ref[0], pl.program_id(1)

    @pl.when((pl.program_id(0) == 0) & (step == 0))
    def _():
        sum_ref[...] = jnp.zeros_like(sum_ref)

    sides = (
        (q_own_ref, kv_own_ref, s_own_ref, keep_ref, core),
        (q_other_ref, kv_other_ref, s_other_ref, away_ref, 1 - core),
    )
    for q_ref, kv_ref, s_ref, out_ref, share in sides:
        tile = q_ref.shape[1]
        last = (share * shares + step == 2 * shares - 1).astype(F32)
        full = low = None
        for s in range(2):
            kv = kv_ref[0, s]
            edge = back_ref[0, s].astype(F32) * last
            if tile > WIN:
                edge = jnp.concatenate([jnp.zeros((tile - WIN, kv.shape[1]), F32), edge], axis=0)
            kv = (kv + edge).astype(BF16)
            q = q_ref[0, :, s * q_cols : (s + 1) * q_cols]
            grads = jnp.concatenate([q, kv], axis=1)
            part = dot(grads, w_ref[s], NT)
            small = dot(grads, b_ref[:, s * width : (s + 1) * width], NT)
            full = part if full is None else full + part
            low = small if low is None else low + small
            sum_ref[s] += dot(s_ref[0], grads, TN)
        out_ref[0, :, :depth] = full.astype(BF16)
        out_ref[0, :, depth:] = (ADAPTER_SCALE * low).astype(BF16)


def normed_grad(core, q, kv, small, back, w, b, q_cols, share):
    slots, length, q_width = q.shape
    sets, depth, width = w.shape
    tile = min(256, share)
    shares = share // tile
    own, other = halves(share, tile)
    four = lambda f: (lambda r, i, core: (r, 0, f(r, i, core)[1], 0))
    out = pl.BlockSpec((1, tile, depth + LOW), lambda r, i, *_: (r, i, 0))
    shape = jax.ShapeDtypeStruct((slots, share, depth + LOW), BF16)
    total = jax.ShapeDtypeStruct((sets, LOW, width), F32)
    kv_block = (1, sets, tile, kv.shape[3])
    return kernel_call(
        functools.partial(normed_grad_kernel, q_cols, shares),
        [core, q, q, kv, kv, small, small, back, w, b],
        (),
        prefetch=1,
        grid=(slots, shares),
        in_specs=[
            pl.BlockSpec((1, tile, q_width), own),
            pl.BlockSpec((1, tile, q_width), other),
            pl.BlockSpec(kv_block, four(own)),
            pl.BlockSpec(kv_block, four(other)),
            pl.BlockSpec((1, tile, LOW), own),
            pl.BlockSpec((1, tile, LOW), other),
            pl.BlockSpec((1, sets, WIN, kv.shape[3]), lambda r, i, *_: (r, 0, 0, 0)),
            pl.BlockSpec(w.shape, lambda r, i, *_: (0, 0, 0)),
            pl.BlockSpec(b.shape, lambda r, i, *_: (0, 0)),
        ],
        out_specs=[out, out, pl.BlockSpec(total.shape, lambda r, i, *_: (0, 0, 0))],
        out_shape=[shape, shape, total],
        name="normed_grad",
    )


def finish_kernel(keep_ref, got_ref, hidden_ref, mid_ref, gain_ref, first_ref, out_ref, sum_ref):
    depth = hidden_ref.shape[1]
    total = keep_ref[...].astype(F32) + got_ref[...].astype(F32)
    low = total[:, depth:].astype(BF16)
    grad = total[:, :depth] + dot(low, first_ref[...])
    values, gain = hidden_ref[...].astype(F32), gain_ref[...]
    scale, back = norm_back(values, gain, grad)
    out_ref[...] = (mid_ref[...].astype(F32) + back).astype(BF16)

    @pl.when(pl.program_id(0) == 0)
    def _():
        sum_ref[...] = jnp.zeros_like(sum_ref)

    sum_ref[...] += dot(low, (values * scale * gain).astype(BF16), TN)


def sums_kernel(rows, seqs, heads, part_ref, pack_ref, out_ref, cols_ref, *scratch):
    a1, a2, a3, c2, c3, b1, b2, b3, e2, e3, send_sem, recv_sem = scratch
    place = {a: lax.axis_index(a) for a in ("row", "seq", "head")}
    counts = {"row": rows, "seq": seqs, "head": heads}
    x_place = place["head"] // 2
    peers = [
        (a, {a: lax.rem(place[a] + d, counts[a])}) for a in counts for d in range(1, counts[a])
    ]
    barrier = pltpu.get_barrier_semaphore()
    for _, peer in peers:
        pl.semaphore_signal(barrier, inc=1, device_id=peer, device_id_type=pl.DeviceIdType.MESH)
    pl.semaphore_wait(barrier, len(peers))
    used = [0]

    def remote(src, dst, device):
        n = used[0]
        used[0] += 1
        return pltpu.make_async_remote_copy(
            src_ref=src, dst_ref=dst, send_sem=send_sem.at[n], recv_sem=recv_sem.at[n],
            device_id=device, device_id_type=pl.DeviceIdType.MESH,
        )

    def exchange(axis, parts, slots, packs, pack_slots):
        me, size = place[axis], counts[axis]
        copies = []
        for d in range(1, size):
            to = lax.rem(me + d, size)
            copies.append(remote(parts.at[to], slots.at[me], {axis: to}))
            if pack_slots is not None:
                copies.append(remote(packs, pack_slots.at[me], {axis: to}))
        return copies

    def add_up(ref, size):
        total = ref[0].astype(F32)
        for i in range(1, size):
            total = total + ref[i].astype(F32)
        return total

    b1[0] = pack_ref[1 - x_place].astype(BF16)
    copies = exchange("head", part_ref, a1, None, None)
    copies.append(remote(b1.at[0], b1.at[1], {"head": lax.rem(place["head"] + 2, heads)}))
    for copy in copies:
        copy.start()
    a1[place["head"]] = part_ref[place["head"]]
    for copy in copies:
        copy.wait()
    stages = (
        ("seq", add_up(a1, heads), pack_ref[x_place] + b1[1].astype(F32), c2, a2, e2, b2),
        ("row", None, None, c3, a3, e3, b3),
    )
    for axis, part, pack, held, slots, pack_held, pack_slots in stages:
        if part is None:
            part, pack = add_up(a2, seqs), add_up(b2, seqs)
        held[...] = part
        pack_held[...] = pack.astype(BF16)
        copies = exchange(axis, held, slots, pack_held, pack_slots)
        for copy in copies:
            copy.start()
        slots[place[axis]] = held[place[axis]]
        pack_slots[place[axis]] = pack_held[...]
        for copy in copies:
            copy.wait()
    out_ref[...] = add_up(a3, rows)
    cols_ref[...] = add_up(b3, rows)


def final_sums(part, pack):
    rows, seqs, heads = (lax.axis_size(a) for a in ("row", "seq", "head"))
    low, width = part.shape[3:]
    count, lanes = pack.shape[1:]
    place = pl.BlockSpec(memory_space=pltpu.VMEM)
    copies = heads + 2 * (seqs - 1) + 2 * (rows - 1)
    return pl.pallas_call(
        functools.partial(sums_kernel, rows, seqs, heads),
        in_specs=[place, place],
        out_specs=[place, place],
        out_shape=[
            jax.ShapeDtypeStruct((low, width), F32),
            jax.ShapeDtypeStruct((count, lanes), F32),
        ],
        scratch_shapes=[
            pltpu.VMEM((heads, seqs, rows, low, width), F32),
            pltpu.VMEM((seqs, rows, low, width), F32),
            pltpu.VMEM((rows, low, width), F32),
            pltpu.VMEM((seqs, rows, low, width), F32),
            pltpu.VMEM((rows, low, width), F32),
            pltpu.VMEM((2, count, lanes), BF16),
            pltpu.VMEM((seqs, count, lanes), BF16),
            pltpu.VMEM((rows, count, lanes), BF16),
            pltpu.VMEM((count, lanes), BF16),
            pltpu.VMEM((count, lanes), BF16),
            pltpu.SemaphoreType.DMA((copies,)),
            pltpu.SemaphoreType.DMA((copies,)),
        ],
        compiler_params=pltpu.CompilerParams(
            collective_id=1, has_side_effects=True, vmem_limit_bytes=32 * 2**20
        ),
        name="final_sums",
    )(part, pack)


def local(
    hidden_in,
    grad_out,
    live_rows,
    doc_starts,
    norm_attn,
    norm_ffn,
    query_weight,
    key_weight,
    value_weight,
    out_weight,
    gate_weight,
    up_weight,
    down_weight,
    query_adapt_in,
    query_adapt_out,
    key_adapt_in,
    key_adapt_out,
    value_adapt_in,
    value_adapt_out,
    outproj_adapt_in,
    projection_adapter_second,
    query_feature,
    key_feature,
):
    rows, seqs, heads = lax.axis_size("row"), lax.axis_size("seq"), lax.axis_size("head")
    head = lax.axis_index("head")
    core = lax.rem(head, 2)
    x_count = heads // 2
    x_place = head // 2
    slots, share_len, model_dim = hidden_in.shape
    piece_len = 2 * share_len
    pieces = seqs * x_count
    piece = lax.axis_index("seq") * x_count + x_place
    blocks = piece_len // WIN
    ext_len = piece_len + WIN
    q_cols, k_cols = query_weight.shape[1], key_weight.shape[1]
    ff_cols = gate_weight.shape[1]

    def in_order(own, other):
        first = jnp.where(core == 0, own, other)
        second = jnp.where(core == 0, other, own)
        return jnp.concatenate([first, second], axis=1)

    def own_half(both):
        return lax.dynamic_slice_in_dim(both, core * share_len, share_len, 1)

    def other_half(both):
        return lax.dynamic_slice_in_dim(both, (1 - core) * share_len, share_len, 1)

    qkv_shard = jnp.concatenate([query_weight, key_weight, value_weight], axis=1)
    out_shard = out_weight.T
    down_shard = down_weight.T
    unit = ff_cols // sum(FF_CHUNKS)
    bounds = [unit * sum(FF_CHUNKS[:j]) for j in range(len(FF_CHUNKS) + 1)]
    ffn_shards = [
        jnp.concatenate([w[:, lo:hi] for w in (gate_weight, up_weight, down_shard)], axis=1)
        for lo, hi in zip(bounds[:-1], bounds[1:])
    ]
    ffn_later = [
        lax.all_gather(v, ("row", "seq"), axis=0, tiled=True) for v in ffn_shards[1:]
    ]
    own_smalls = [
        query_feature, key_feature, query_adapt_out, key_adapt_out, value_adapt_out, outproj_adapt_in
    ]
    (qkv_mat, out_mat, first_mat), other_smalls, (hidden_other, cot_mine, cot_away) = gather(
        [qkv_shard, out_shard, ffn_shards[0]],
        [True, True, False],
        [
            (0, (0, qkv_shard.shape[1]), True, 0),
            (1, (0, out_shard.shape[1]), True, 0),
            (2, (0, ffn_shards[0].shape[1]), True, rows * seqs),
        ],
        own_smalls,
        hidden_in,
        grad_out,
    )
    ffn_mats = [first_mat] + ffn_later

    def both(i, axis):
        own, other = own_smalls[i], other_smalls[i]
        return jnp.concatenate(
            [jnp.where(x_place == 0, own, other), jnp.where(x_place == 0, other, own)], axis=axis
        )

    query_feat_all, key_feat_all = both(0, 0), both(1, 0)
    q_out, k_out, v_out = both(2, 1), both(3, 1), both(4, 1)
    o_in = both(5, 0)

    doc_ids = jnp.cumsum(doc_starts, axis=1)
    padded_docs = jnp.concatenate(
        [jnp.full((slots, WIN + 1), -1, jnp.int32), doc_ids], axis=1
    )
    piece_docs = padded_docs[:, ::piece_len][:, : pieces + 1]
    near_docs = lax.dynamic_slice_in_dim(padded_docs, piece * piece_len, ext_len + 1, 1)
    end_docs = near_docs[:, ::WIN][:, : blocks + 1]
    carry_doc = end_docs[:, 0]
    next_doc = end_docs[:, blocks]
    key_docs = near_docs[:, 1:]
    key_doc_lanes = jnp.broadcast_to(key_docs[:, :, None], (slots, ext_len, 2 * HD))
    query_doc_lanes = key_doc_lanes[:, WIN:]
    doc_blocks = key_docs.reshape(slots, blocks + 1, WIN)
    pair_docs = jnp.concatenate([doc_blocks[:, :-1], doc_blocks[:, 1:]], axis=2)

    def from_pieces(block):
        held = []
        for d, start in enumerate((block, flip_x(block))):
            for l in range(seqs):
                if l:
                    start = shift(start, "seq", 1)
                source = (
                    lax.rem(lax.axis_index("seq") - l + seqs, seqs) * x_count
                    + lax.rem(x_place + d, x_count)
                )
                held.append((source, start))
        return held[1:]

    gain_attn = norm_attn.astype(F32)[None]
    gain_ffn = norm_ffn.astype(F32)[None]
    core_index = core.astype(jnp.int32).reshape(1)
    flat_tokens = lambda v: v.reshape(-1, v.shape[-1])

    set_cols = q_cols + 2 * k_cols
    adapt_in_all = jnp.concatenate([query_adapt_in, key_adapt_in, value_adapt_in], axis=1)

    def by_sets(parts):
        return jnp.concatenate(
            [v[:, d * (v.shape[1] // 2) : (d + 1) * (v.shape[1] // 2)] for d in range(2) for v in parts],
            axis=1,
        )

    def diagonal(parts):
        rows = [
            [p if i == j else jnp.zeros((RANK, q.shape[1]), BF16) for j, q in enumerate(parts)]
            for i, p in enumerate(parts)
        ]
        return jnp.concatenate([by_sets(r) for r in rows], axis=0)

    pad_rows = lambda v: jnp.pad(v, ((0, LOW - v.shape[0]), (0, 0)))
    pad_cols = lambda v: jnp.pad(v, ((0, 0), (0, LOW - v.shape[1])))
    adapt_in_all = pad_cols(adapt_in_all)
    adapt_out_all = pad_rows(diagonal([q_out, k_out, v_out]))
    second = pad_rows(projection_adapter_second)
    o_in = pad_cols(o_in)
    query, kv_own, small = project(
        core_index, hidden_in, hidden_other, gain_attn, qkv_mat, adapt_in_all, adapt_out_all, q_cols,
        k_cols,
    )

    def along_pieces(block, distance):
        route = []
        for p in range(pieces):
            to = p + distance
            if 0 <= to < pieces:
                for c in range(2):
                    route.append((2 * p + c, 2 * to + c))
        return lax.ppermute(block, ("seq", "head"), route)

    kv = jnp.concatenate([along_pieces(kv_own[:, :, -WIN:], 1), kv_own], axis=2)
    doubled = lambda feat: jnp.concatenate([feat, -feat], axis=2)
    query_feat, key_feat = doubled(query_feat_all), doubled(key_feat_all)
    phi_key, end_state = key_state(end_docs, kv, key_feat, key_doc_lanes)
    carry = jnp.zeros(end_state.shape, F32)
    for source, part in from_pieces(end_state):
        after = lax.dynamic_index_in_dim(piece_docs, source + 1, 1, keepdims=False)
        keep = (source < piece) & (after == carry_doc)
        carry = carry + jnp.where(keep[:, None, None, None], part.astype(F32), 0.0)
    phi_query = query_features(query, query_feat, kv.shape[1])
    attn = attend(
        end_docs, query, kv, phi_key, phi_query, carry, query_doc_lanes, key_doc_lanes, pair_docs
    )

    keep, away = out_project(core_index, attn, out_mat, o_in, share_len)
    mid_rows, nmid, low_mix = tokens_call(
        middle_kernel,
        [flat_tokens(v) for v in (hidden_in, keep, flip_core(away))],
        [second, gain_ffn],
        [(model_dim, BF16), (model_dim, BF16), (LOW, BF16)],
        "middle",
    )

    nmid_x = flip_x(nmid)

    def chip_tokens(own):
        return own, flip_core(own)

    def sum_away(own, other):
        return (own.astype(F32) + flip_core(other).astype(F32)).astype(BF16)

    x_mine = chip_tokens(nmid)
    c_mine, c_away = flat_tokens(cot_mine), flat_tokens(cot_away)
    run = lambda x, c, w, before=(), after=(): ffn(
        x, c, w, live_rows, share_len, slots, before, after
    )
    mine = run(x_mine, c_mine, ffn_mats[:2])
    x_away = chip_tokens(hold(nmid_x, (mine[0],)))
    away = run(x_away, c_away, ffn_mats[:-1])
    away = run(x_away, c_away, ffn_mats[-1:], away)
    gn_there = sum_away(*away[:2])
    gn_back = flip_x(gn_there)
    gn_own, gn_other, y_own, y_other = run(
        x_mine, c_mine, ffn_mats[2:], mine, (gn_there,)
    )
    y_there = sum_away(*away[2:])
    y_back = flip_x(y_there)
    branch, = tokens_call(
        functools.partial(branch_kernel, share_len, slots),
        [mid_rows, gn_own, gn_back, flat_tokens(grad_out)],
        [flip_core(gn_other[r * share_len : (r + 1) * share_len]) for r in range(slots)] + [gain_ffn],
        [(model_dim, BF16)],
        "branch",
        prefetch=[live_rows],
        tile=share_len,
    )

    shaped = lambda v: v.reshape(slots, share_len, -1)
    grad_attn, sum_o_in = attn_grad(
        core_index, shaped(branch), shaped(flip_core(branch)), attn, out_mat, second, o_in
    )
    sum_o_in = sum_o_in[:RANK]
    sum_o_out = ADAPTER_SCALE * dot(low_mix, branch, TN)[:RANK]

    grad_query, feat_query, gphi, gkv, grad_carry = attend_back(
        end_docs, query, kv, phi_key, phi_query, query_feat, carry, query_doc_lanes, key_doc_lanes,
        pair_docs, grad_attn, (y_there,),
    )
    block_out = tokens_call(
        sum_kernel, [mid_rows, y_own, flip_core(y_other), y_back], [], [(model_dim, BF16)], "sum_y",
        after=(grad_carry,),
    )[0]
    later = jnp.zeros(grad_carry.shape, F32)
    for source, part in from_pieces(grad_carry):
        start = lax.dynamic_index_in_dim(piece_docs, source, 1, keepdims=False)
        keep = (source > piece) & (start == next_doc)
        later = later + jnp.where(keep[:, None, None, None], part.astype(F32), 0.0)
    grad_body, grad_edge, feat_key = key_back(
        end_docs, kv, phi_key, key_feat, later, key_doc_lanes, gphi, gkv, (block_out,)
    )
    sum_q_feat = jnp.sum(feat_query, axis=0).reshape(2, -1, 2 * HD)
    sum_k_feat = jnp.sum(feat_key, axis=0).reshape(2, -1, 2 * HD)

    keep, away, outs = normed_grad(
        core_index, grad_query, grad_body, small, along_pieces(grad_edge, -1), qkv_mat, adapt_out_all,
        q_cols, share_len,
    )
    outs = ADAPTER_SCALE * outs
    outs = [
        outs[:, :RANK, :q_cols],
        outs[:, RANK : 2 * RANK, q_cols : q_cols + k_cols],
        outs[:, 2 * RANK : 3 * RANK, q_cols + k_cols :],
    ]
    grad_hidden, sum_in = tokens_call(
        finish_kernel,
        [flat_tokens(keep), flat_tokens(flip_core(away)), flat_tokens(hidden_in), branch],
        [gain_attn, adapt_in_all.T],
        [(model_dim, BF16)],
        "finish",
        sums=[(LOW, model_dim)],
    )
    grad_hidden = grad_hidden.reshape(hidden_in.shape)
    sum_in = sum_in[: 3 * RANK]

    by_rows = jnp.concatenate([sum_in, sum_o_out], axis=0)
    width = model_dim // (rows * seqs * heads)
    by_rows = by_rows.reshape(4 * RANK, rows, seqs, heads, width).transpose(3, 2, 1, 0, 4)
    by_rows = by_rows.reshape(heads, seqs, rows, -1, 2 * HD)

    def lanes_of(v):
        v = v.reshape(2, RANK, -1, 2 * HD).transpose(0, 2, 1, 3)
        return v.reshape(2, -1, 2 * HD)

    o_sets = jnp.stack([sum_o_in[:, :q_cols], sum_o_in[:, q_cols:]])
    packed = [lanes_of(v) for v in outs + [o_sets]] + [sum_q_feat, sum_k_feat]
    sizes = [v.shape[1] for v in packed]
    packed = jnp.concatenate(packed, axis=1)
    in_parts, packed = final_sums(by_rows, packed)
    in_parts = in_parts.reshape(4, RANK, width)
    cols, at = [], 0
    for size in sizes:
        cols.append(packed[at : at + size])
        at += size
    from_lanes = lambda v: v.reshape(-1, RANK, 2 * HD).transpose(1, 0, 2).reshape(RANK, -1)
    from_pairs = lambda v: v.reshape(-1, HD, 2, HD).transpose(0, 2, 1, 3).reshape(-1, HD, HD)
    cols = [from_lanes(v) for v in cols[:4]] + [from_pairs(v) for v in cols[4:]]
    cols[3] = cols[3].T

    return (
        block_out.reshape(hidden_in.shape),
        grad_hidden,
        in_parts[0].T,
        cols[0],
        in_parts[1].T,
        cols[1],
        in_parts[2].T,
        cols[2],
        cols[3],
        in_parts[3],
        cols[4],
        cols[5],
    )


def solution(mesh):
    return jax.shard_map(
        local,
        mesh=mesh,
        in_specs=(
            P("row", ("seq", "head"), None),
            P("row", ("seq", "head"), None),
            P("row"),
            P("row", None),
            P(),
            P(),
            P(("row", "seq"), "head"),
            P(("row", "seq"), "head"),
            P(("row", "seq"), "head"),
            P("head", ("row", "seq")),
            P(("row", "seq"), "head"),
            P(("row", "seq"), "head"),
            P("head", ("row", "seq")),
            P(),
            P(None, "head"),
            P(),
            P(None, "head"),
            P(),
            P(None, "head"),
            P("head", None),
            P(),
            P("head", None, None),
            P("head", None, None),
        ),
        out_specs=(
            P("row", ("seq", "head"), None),
            P("row", ("seq", "head"), None),
            P(("row", "seq", "head"), None),
            P(None, "head"),
            P(("row", "seq", "head"), None),
            P(None, "head"),
            P(("row", "seq", "head"), None),
            P(None, "head"),
            P("head", None),
            P(None, ("row", "seq", "head")),
            P("head", None, None),
            P("head", None, None),
        ),
        check_vma=False,
    )
```

```python
import functools

import jax
import jax.numpy as jnp
from jax import lax
from jax.experimental import pallas as pl
from jax.experimental.pallas import tpu as pltpu
from jax.sharding import PartitionSpec as P

HD = 64
RANK = 8
WIN = 64
FF_CHUNKS = (3, 4, 6, 3)

NORM_EPS = 1e-05
ADAPTER_SCALE = 2.0
F32 = jnp.float32
NT = ((1,), (1,))
TN = ((0,), (0,))
BF16 = jnp.bfloat16


def shift(block, axis, distance):
    size = lax.axis_size(axis)
    return lax.ppermute(block, axis, [(i, (i + distance) % size) for i in range(size)])


def flip_core(block):
    return lax.ppermute(block, "head", [(i, i ^ 1) for i in range(lax.axis_size("head"))])


def flip_core_parts(block, parts):
    size = block.shape[0] // parts
    return jnp.concatenate(
        [flip_core(block[i * size : (i + 1) * size]) for i in range(parts)], axis=0
    )


def flip_x(block):
    return lax.ppermute(block, "head", [(i, i ^ 2) for i in range(lax.axis_size("head"))])


def kernel_call(
    kernel, args, after, *, grid, in_specs, out_specs, out_shape, name, prefetch=0, scratch=(), cost=None
):
    count = len(args)

    def body(*refs):
        kernel(*refs[:count], *refs[count + len(after) :])

    return pl.pallas_call(
        body,
        grid_spec=pltpu.PrefetchScalarGridSpec(
            num_scalar_prefetch=prefetch,
            grid=grid,
            in_specs=list(in_specs) + [pl.BlockSpec(memory_space=pl.ANY)] * len(after),
            out_specs=out_specs,
            scratch_shapes=list(scratch),
        ),
        out_shape=out_shape,
        compiler_params=pltpu.CompilerParams(vmem_limit_bytes=60 * 2**20),
        cost_estimate=cost and pl.CostEstimate(
            flops=cost.flops // 4, bytes_accessed=cost.bytes_accessed // 4, transcendentals=0
        ),
        name=name,
    )(*args, *after)


def copy_kernel(src_ref, dst_ref):
    dst_ref[...] = src_ref[...]


def hold(value, after):
    flat = value.reshape(-1, value.shape[-1])
    tile = min(256, flat.shape[0])
    block = pl.BlockSpec((tile, flat.shape[1]), lambda i: (i, 0))
    held = kernel_call(
        copy_kernel, [flat], after, grid=(flat.shape[0] // tile,), in_specs=[block], out_specs=block,
        out_shape=jax.ShapeDtypeStruct(flat.shape, flat.dtype), name="hold",
    )
    return held.reshape(value.shape)


def dot(a, b, dims=((1,), (0,))):
    return lax.dot_general(a, b, (dims, ((), ())), preferred_element_type=F32)


def tie(value, *after):
    return lax.optimization_barrier((value,) + after)[0]


def rms_scaled(values, gain_vec):
    return (
        values * lax.rsqrt(jnp.mean(values * values, axis=-1, keepdims=True) + NORM_EPS) * gain_vec
    )


def rms_back(values, gain_vec, grad_in):
    factor = lax.rsqrt(jnp.mean(values * values, axis=-1, keepdims=True) + NORM_EPS)
    scaled = gain_vec * grad_in
    return factor * scaled - values * factor**3 * jnp.mean(values * scaled, axis=-1, keepdims=True)


def scatter_sum(parts, axis):
    size, place = lax.axis_size(axis), lax.axis_index(axis)
    total = lax.dynamic_index_in_dim(parts, place, 0, keepdims=False)
    for k in range(1, size):
        away = lax.dynamic_index_in_dim(parts, lax.rem(place + k, size), 0, keepdims=False)
        total = total + shift(away, axis, k)
    return total


def full_sum(part, axis):
    size = lax.axis_size(axis)
    step = 1
    while step < size:
        sent = part.astype(BF16)
        got = lax.ppermute(sent, axis, [(i, i ^ step) for i in range(size)])
        part = sent.astype(F32) + got.astype(F32)
        step *= 2
    return part


def gather_plan(rows, seqs, weights):
    free = {"row": 0.0, "seq": 0.0, "x": 0.0}
    running = []
    plan = []

    def begin(now, starts):
        for t in starts:
            w, link = t[0], t[1]
            end = max(now, free[link]) + weights[w][0]
            free[link] = end
            running.append((end, len(plan), len(running), t))
        return starts

    def spread(w, k, l):
        starts = []
        row_first = weights[w][2]
        if (l == 0 or not row_first) and k + 1 < rows:
            starts.append((w, "row", k + 1, l))
        if (k == 0 or row_first) and l + 1 < seqs:
            starts.append((w, "seq", k, l + 1))
        if weights[w][1]:
            starts.append((w, "x", k, l))
        return starts

    first = [t for w in range(len(weights)) if weights[w][3] == 0 for t in spread(w, 0, 0)]
    plan.append((None, begin(0.0, first)))
    done = 0
    while running:
        event = min(running)
        running.remove(event)
        now, t = event[0], event[3]
        done += 1
        starts = [] if t[1] == "x" else spread(t[0], t[2], t[3])
        for w in range(len(weights)):
            if weights[w][3] == done:
                starts = starts + spread(w, 0, 0)
        plan.append((t, begin(now, starts)))
    return plan


def gather_kernel(plan, rows, seqs, parts, over_x, small_count, *refs):
    count = len(over_x)
    inputs, refs = refs[: count + small_count + 2], refs[count + small_count + 2 :]
    shards, smalls = inputs[:count], inputs[count : count + small_count]
    hidden, cot = inputs[count + small_count :]
    wholes, refs = refs[:count], refs[count:]
    small_outs, refs = refs[:small_count], refs[small_count:]
    hidden_out, cot_mine, cot_away = refs[:3]
    send_sem, recv_sem, copy_sem, more_send, more_recv = refs[3:]
    row, seq, head = lax.axis_index("row"), lax.axis_index("seq"), lax.axis_index("head")
    x_place = head // 2
    across = {"head": lax.rem(head + 2, 4)}
    partner = {"head": head + 1 - 2 * lax.rem(head, 2)}
    away = {
        "row": {"row": lax.rem(row + 1, rows)},
        "seq": {"seq": lax.rem(seq + 1, seqs)},
        "x": across,
    }
    barrier = pltpu.get_barrier_semaphore()
    sources = (
        {"row": lax.rem(row + rows - 1, rows)},
        {"seq": lax.rem(seq + seqs - 1, seqs)},
        across,
        partner,
    )
    for source in sources:
        pl.semaphore_signal(
            barrier, inc=1, device_id=source, device_id_type=pl.DeviceIdType.MESH
        )
    pl.semaphore_wait(barrier, len(sources))

    def slot(p, k, l):
        w, columns = parts[p][0], pl.ds(*parts[p][1])
        depth = shards[w].shape[0]
        place = lax.rem(row - k + rows, rows) * seqs + lax.rem(seq - l + seqs, seqs)
        at = pl.ds(pl.multiple_of(place * depth, depth), depth)
        return wholes[w].at[x_place, at, columns] if over_x[w] else wholes[w].at[at, columns]

    number = {}
    last_x = 0
    for i, (event, starts) in enumerate(plan):
        for t in starts:
            number[t] = len(number)
            if t[1] == "x":
                last_x = i

    def remote(src, dst, send, recv, device):
        return pltpu.make_async_remote_copy(
            src_ref=src, dst_ref=dst, send_sem=send, recv_sem=recv, device_id=device,
            device_id_type=pl.DeviceIdType.MESH,
        )

    def transfer(t):
        w, link, k, l = t
        source = {"row": (k - 1, l), "seq": (k, l - 1), "x": (k, l)}[link]
        dst = slot(w, *source)
        n = number[t]
        src = shards[parts[w][0]].at[:, pl.ds(*parts[w][1])] if source == (0, 0) else dst
        return remote(src, dst, send_sem.at[n], recv_sem.at[n], away[link])

    def more(i, src, dst, device):
        return remote(src, dst, more_send.at[i], more_recv.at[i], device)

    early = [more(i, a, b, across) for i, (a, b) in enumerate(zip(smalls, small_outs))]
    early.append(more(small_count, hidden, hidden_out, partner))
    early.append(more(small_count + 1, cot, cot_mine.at[1], partner))
    cot_x = more(small_count + 2, cot, cot_away.at[0], across)
    cot_last = more(small_count + 3, cot_away.at[0], cot_away.at[1], partner)
    own = [
        pltpu.make_async_copy(
            shards[w].at[:, pl.ds(*columns)], slot(p, 0, 0), copy_sem.at[p]
        )
        for p, (w, columns) in enumerate(parts)
    ] + [pltpu.make_async_copy(cot, cot_mine.at[0], copy_sem.at[len(parts)])]
    for i, (event, starts) in enumerate(plan):
        if event is not None:
            transfer(event).wait_recv()
        for t in starts:
            transfer(t).start()
        if event is None:
            for copy in [cot_x] + early + own:
                copy.start()
        if i == last_x:
            cot_x.wait()
            cot_last.start()
    for t in number:
        transfer(t).wait_send()
    for copy in early + own + [cot_last]:
        copy.wait()


def gather(shards, over_x, pieces, smalls, hidden, cot):
    rows, seqs = lax.axis_size("row"), lax.axis_size("seq")
    plan = gather_plan(
        rows,
        seqs,
        [(float(shards[w].shape[0] * c[1]), over_x[w], first, later) for w, c, first, later in pieces],
    )
    parts = [(w, c) for w, c, _, _ in pieces]
    total = sum(len(starts) for _, starts in plan)
    shapes = []
    for shard, x in zip(shards, over_x):
        depth, width = shard.shape
        whole = (rows * seqs * depth, width)
        shapes.append(jax.ShapeDtypeStruct(((2,) + whole) if x else whole, shard.dtype))
    same = lambda v: jax.ShapeDtypeStruct(v.shape, v.dtype)
    twice = jax.ShapeDtypeStruct((2,) + cot.shape, cot.dtype)
    shapes += [same(v) for v in smalls] + [same(hidden), twice, twice]
    more = len(smalls) + 4
    place = pl.BlockSpec(memory_space=pl.ANY)
    outs = pl.pallas_call(
        functools.partial(gather_kernel, plan, rows, seqs, parts, over_x, len(smalls)),
        out_shape=shapes,
        in_specs=[place] * (len(shards) + len(smalls) + 2),
        out_specs=[place] * len(shapes),
        scratch_shapes=[
            pltpu.SemaphoreType.DMA((total,)),
            pltpu.SemaphoreType.DMA((total,)),
            pltpu.SemaphoreType.DMA((len(parts) + 1,)),
            pltpu.SemaphoreType.DMA((more,)),
            pltpu.SemaphoreType.DMA((more,)),
        ],
        compiler_params=pltpu.CompilerParams(collective_id=0, has_side_effects=True),
        name="gather",
    )(*shards, *smalls, hidden, cot)
    n = len(shards)
    return outs[:n], outs[n : n + len(smalls)], outs[-3:]


def ffn_kernel(chunks, before, share_len, slots, live_ref, x_ref, more_ref, cot_ref, *refs):
    weights, refs = refs[:chunks], refs[chunks:]
    earlier, refs = refs[: 4 * before], refs[4 * before :]
    outs, held, sem = refs[:4], refs[4:-1], refs[-1]
    step = pl.program_id(0)
    tile = x_ref.shape[0]
    copies = [pltpu.make_async_copy(weights[c], held[c], sem.at[c]) for c in range(chunks)]

    @pl.when(step == 0)
    def _():
        for copy in copies:
            copy.start()

    first = step < pl.num_programs(0) // 2
    live = (lax.rem(step * tile // share_len, slots) < live_ref[0]).astype(F32)
    x, cot = jnp.where(first, x_ref[...], more_ref[...]), cot_ref[...]
    sums = [None, None]
    if before:
        sums = [jnp.where(first, earlier[i][...], earlier[i + 1][...]).astype(F32) for i in (0, 2)]
    for c in range(chunks):

        @pl.when(step == 0)
        def _():
            copies[c].wait()

        w, width = held[c], held[c].shape[1] // 3
        gate = dot(x, w[:, :width])
        up = dot(x, w[:, width : 2 * width])
        gm = dot(cot, w[:, 2 * width :]) * live
        sig = jax.nn.sigmoid(gate)
        silu = gate * sig
        mixed = (silu * up).astype(BF16)
        g_gate = (gm * up * (sig + silu * (1.0 - sig))).astype(BF16)
        g_up = (gm * silu).astype(BF16)
        parts = (
            dot(jnp.concatenate([g_gate, g_up], axis=1), w[:, : 2 * width], NT),
            dot(mixed, w[:, 2 * width :], NT),
        )
        sums = [p if t is None else t + p for t, p in zip(sums, parts)]

    @pl.when(first)
    def _():
        outs[0][...] = sums[0].astype(BF16)
        outs[2][...] = sums[1].astype(BF16)

    @pl.when(jnp.logical_not(first))
    def _():
        outs[1][...] = sums[0].astype(BF16)
        outs[3][...] = sums[1].astype(BF16)


def ffn(x, cot, weights, live_rows, share_len, slots, before=(), after=()):
    tokens, depth = cot.shape
    chunks = len(weights)
    units = sum(w.shape[1] for w in weights) // 3
    tile = min(256, share_len)
    half = tokens // tile // 2
    lower = pl.BlockSpec((tile, depth), lambda i, *_: (jnp.minimum(i, half - 1), 0))
    upper = pl.BlockSpec((tile, depth), lambda i, *_: (jnp.maximum(i - half, 0), 0))
    out = jax.ShapeDtypeStruct((tokens // 2, depth), BF16)
    return kernel_call(
        functools.partial(ffn_kernel, chunks, len(before) // 4, share_len, slots),
        [live_rows, x[0], x[1], cot, *weights, *before],
        after,
        prefetch=1,
        grid=(tokens // tile,),
        in_specs=[lower, upper, pl.BlockSpec((tile, depth), lambda i, *_: (i, 0))]
        + [pl.BlockSpec(memory_space=pl.ANY)] * chunks
        + [lower, upper] * (len(before) // 2),
        out_specs=[lower, upper, lower, upper],
        out_shape=[out] * 4,
        scratch=[
            *[pltpu.VMEM(w.shape, BF16) for w in weights],
            pltpu.SemaphoreType.DMA((chunks,)),
        ],
        cost=pl.CostEstimate(
            flops=12 * tokens * depth * units,
            bytes_accessed=8 * tokens * depth + 6 * depth * units,
            transcendentals=0,
        ),
        name="ffn",
    )


def lower_lanes(like):
    return lax.broadcasted_iota(jnp.int32, like.shape, 1) < HD


def half_ones():
    r = lax.broadcasted_iota(jnp.int32, (2 * HD, 2 * HD), 0) // HD
    c = lax.broadcasted_iota(jnp.int32, (2 * HD, 2 * HD), 1) // HD
    return (r == c).astype(F32).astype(BF16)


def swap(v):
    return pltpu.roll(v, HD, 1)


def features(x, feat):
    logit = dot(x, feat)
    low = lower_lanes(logit)
    top = jnp.max(jnp.where(low, logit, -jnp.inf), axis=1, keepdims=True)
    bottom = jnp.max(jnp.where(low, -jnp.inf, logit), axis=1, keepdims=True)
    e = jnp.exp(logit - jnp.where(low, top, bottom))
    return e / dot(e.astype(BF16), half_ones())


def features_back(phi, grad):
    p = phi.astype(F32)
    prod = p * grad
    low = lower_lanes(prod)
    first = jnp.sum(jnp.where(low, prod, 0.0), axis=1, keepdims=True)
    second = jnp.sum(jnp.where(low, 0.0, prod), axis=1, keepdims=True)
    g = prod - p * jnp.where(low, first, second)
    return (g - swap(g)).astype(BF16)[:, :HD]


def values_ones(kv):
    kv = kv.astype(F32)
    return jnp.where(lower_lanes(kv), swap(kv), 1.0).astype(BF16)


def key_state_kernel(ends_ref, kv_ref, feat_ref, kdoc_ref, phi_ref, state_ref):
    r = pl.program_id(0)
    kv = kv_ref[0, 0]
    body = kv.shape[0] - WIN
    phi = features(kv[:, :HD], feat_ref[0]).astype(BF16)
    phi_ref[0, 0] = phi
    last = ends_ref[r, body // WIN]
    held = jnp.where(kdoc_ref[0, :body] == last, phi[:body].astype(F32), 0.0).astype(BF16)
    state_ref[0, 0] = dot(held, values_ones(kv[:body]), TN).astype(BF16)


def key_state(ends, kv, feat, kdoc, after=()):
    slots, groups, ext, _ = kv.shape
    block = lambda r, g, *_: (r, g, 0, 0)
    return kernel_call(
        key_state_kernel,
        [ends, kv, feat, kdoc],
        after,
        prefetch=1,
        grid=(slots, groups),
        in_specs=[
            pl.BlockSpec((1, 1, ext, 2 * HD), block),
            pl.BlockSpec((1, HD, 2 * HD), lambda r, g, *_: (g, 0, 0)),
            pl.BlockSpec((1, ext, 2 * HD), lambda r, g, *_: (r, 0, 0)),
        ],
        out_specs=[
            pl.BlockSpec((1, 1, ext, 2 * HD), block),
            pl.BlockSpec((1, 1, 2 * HD, 2 * HD), block),
        ],
        out_shape=[
            jax.ShapeDtypeStruct((slots, groups, ext, 2 * HD), BF16),
            jax.ShapeDtypeStruct((slots, groups, 2 * HD, 2 * HD), BF16),
        ],
        name="key_state",
    )


def block_masks(b, qdoc_ref, pdoc_ref):
    rows = slice(WIN * b, WIN * b + WIN)
    same = qdoc_ref[0, rows] == pdoc_ref[0, b : b + 1]
    row = lax.broadcasted_iota(jnp.int32, (WIN, 2 * WIN), 0)
    col = lax.broadcasted_iota(jnp.int32, (WIN, 2 * WIN), 1)
    linear = same & (col <= row)
    window = same & (col > row) & (col <= row + WIN)
    return window, linear


def next_state(b, ends_ref, r, state, phi_ref, vx_ref, kdoc_ref):
    rows = slice(WIN * (b - 1), WIN * b)
    keep = (ends_ref[r, b] == ends_ref[r, b - 1]).astype(F32)
    held = jnp.where(
        kdoc_ref[0, rows] == ends_ref[r, b], phi_ref[0, 0, rows].astype(F32), 0.0
    ).astype(BF16)
    return state * keep + dot(held, vx_ref[rows], TN)


def block_forward(b, ends_ref, r, q_ref, kv_ref, phi_ref, phiq_ref, vx_ref, state_low, qdoc_ref, pdoc_ref):
    heads = q_ref.shape[1]
    rows, pair = slice(WIN * b, WIN * b + WIN), slice(WIN * b, WIN * b + 2 * WIN)
    window, linear = block_masks(b, qdoc_ref, pdoc_ref)
    valid = qdoc_ref[0, rows] == ends_ref[r, b]
    query = jnp.concatenate([q_ref[0, h, rows] for h in range(heads)], axis=0)
    phi_query = jnp.concatenate([phiq_ref[0, h, rows] for h in range(heads)], axis=0)
    key = kv_ref[0, 0, pair, :HD]
    phi_key = phi_ref[0, 0, pair]
    score = dot(query, key, NT) * (HD**-0.5)
    lin = dot(phi_query, phi_key, NT)
    part = lambda v, h: v[WIN * h : WIN * h + WIN]
    exps = [jnp.where(window, jnp.exp(part(score, h)), 0.0) for h in range(heads)]
    weight = jnp.concatenate(
        [jnp.where(linear, part(lin, h), exps[h]).astype(BF16) for h in range(heads)], axis=0
    )
    phi_valid = jnp.concatenate(
        [jnp.where(valid, part(phi_query, h).astype(F32), 0.0).astype(BF16) for h in range(heads)],
        axis=0,
    )
    both = dot(weight, vx_ref[pair]) + dot(phi_valid, state_low)
    denominator = jnp.where(lower_lanes(both), swap(both), both)
    return (query, phi_query, phi_valid, key, phi_key, exps, weight, both / denominator, denominator,
            window, linear, valid)


def query_feature_kernel(q_ref, feat_ref, phi_ref):
    for h in range(q_ref.shape[1]):
        phi_ref[0, h] = features(q_ref[0, h], feat_ref[h]).astype(BF16)


def query_features(q, feat, groups):
    slots, all_heads, length, _ = q.shape
    sp = attention_specs(slots, groups, all_heads // groups, length)
    return kernel_call(
        query_feature_kernel,
        [q, feat],
        (),
        grid=(slots, groups),
        in_specs=[sp["q"], sp["feat"]],
        out_specs=sp["phiq"],
        out_shape=jax.ShapeDtypeStruct((slots, all_heads, length, 2 * HD), BF16),
        name="query_features",
    )


def attend_kernel(
    ends_ref, q_ref, kv_ref, phi_ref, phiq_ref, carry_ref, qdoc_ref, kdoc_ref, pdoc_ref,
    attn_ref, vx_ref,
):
    r = pl.program_id(0)
    heads, length = q_ref.shape[1], q_ref.shape[2]
    vx_ref[...] = values_ones(kv_ref[0, 0])
    state = carry_ref[0, 0]
    for b in range(length // WIN):
        if b:
            state = next_state(b, ends_ref, r, state, phi_ref, vx_ref, kdoc_ref)
        out = block_forward(
            b, ends_ref, r, q_ref, kv_ref, phi_ref, phiq_ref, vx_ref, state.astype(BF16), qdoc_ref,
            pdoc_ref,
        )
        attn = out[7]
        low = lower_lanes(attn[:WIN])
        for h in range(0, heads, 2):
            first, second = attn[WIN * h : WIN * h + WIN], attn[WIN * h + WIN : WIN * h + 2 * WIN]
            attn_ref[0, WIN * b : WIN * b + WIN, HD * h : HD * h + 2 * HD] = jnp.where(
                low, first, swap(second)
            ).astype(BF16)


def attention_specs(slots, groups, heads, length):
    ext = length + WIN
    four = lambda r, g, *_: (r, g, 0, 0)
    docs = lambda r, g, *_: (r, 0, 0)
    return dict(
        q=pl.BlockSpec((1, heads, length, HD), four),
        kv=pl.BlockSpec((1, 1, ext, 2 * HD), four),
        phiq=pl.BlockSpec((1, heads, length, 2 * HD), four),
        feat=pl.BlockSpec((heads, HD, 2 * HD), lambda r, g, *_: (g, 0, 0)),
        state=pl.BlockSpec((1, 1, 2 * HD, 2 * HD), four),
        qdoc=pl.BlockSpec((1, length, 2 * HD), docs),
        kdoc=pl.BlockSpec((1, ext, 2 * HD), docs),
        pdoc=pl.BlockSpec((1, length // WIN, 2 * HD), docs),
        tokens=pl.BlockSpec((1, length, heads * HD), lambda r, g, *_: (r, 0, g)),
        fgrad=pl.BlockSpec((1, heads // 2, HD, 2 * HD), four),
    )


def attend(ends, q, kv, phi, phiq, carry, qdoc, kdoc, pdoc, after=()):
    slots, all_heads, length, _ = q.shape
    groups = kv.shape[1]
    heads = all_heads // groups
    sp = attention_specs(slots, groups, heads, length)
    return kernel_call(
        attend_kernel,
        [ends, q, kv, phi, phiq, carry, qdoc, kdoc, pdoc],
        after,
        prefetch=1,
        grid=(slots, groups),
        in_specs=[sp[n] for n in ("q", "kv", "kv", "phiq", "state", "qdoc", "kdoc", "pdoc")],
        out_specs=sp["tokens"],
        scratch=[pltpu.VMEM((length + WIN, 2 * HD), BF16)],
        out_shape=jax.ShapeDtypeStruct((slots, length, all_heads * HD), BF16),
        name="attend",
    )


def attend_back_kernel(
    ends_ref, q_ref, kv_ref, phi_ref, phiq_ref, feat_ref, carry_ref, qdoc_ref, kdoc_ref, pdoc_ref,
    g_ref, gq_ref, gfeat_ref, gphi_ref, gkv_ref, gcarry_ref, vx_ref, gstate_ref, gphiq_ref, gk_ref,
    gv_ref, gqs_ref, gl_ref,
):
    r = pl.program_id(0)
    heads, length = q_ref.shape[1], q_ref.shape[2]
    blocks = length // WIN
    vx_ref[...] = values_ones(kv_ref[0, 0])
    gphi_ref[...] = jnp.zeros_like(gphi_ref)
    gk_ref[...] = jnp.zeros_like(gk_ref)
    gv_ref[...] = jnp.zeros_like(gv_ref)
    scale = HD**-0.5
    state = carry_ref[0, 0]
    for b in range(blocks):
        rows, pair = slice(WIN * b, WIN * b + WIN), slice(WIN * b, WIN * b + 2 * WIN)
        if b:
            state = next_state(b, ends_ref, r, state, phi_ref, vx_ref, kdoc_ref)
        state_low = state.astype(BF16)
        (query, phi_query, phi_valid, key, phi_key, exps, weight, attn, denominator, window, linear,
         valid) = block_forward(
            b, ends_ref, r, q_ref, kv_ref, phi_ref, phiq_ref, vx_ref, state_low, qdoc_ref, pdoc_ref
        )
        grads = []
        for h in range(0, heads, 2):
            g = g_ref[0, rows, HD * h : HD * h + 2 * HD].astype(F32)
            grads += [g, swap(g)]
        grad = jnp.concatenate(grads, axis=0)
        low = lower_lanes(grad)
        grad = jnp.where(low, grad, 0.0)
        g_denom = -jnp.sum(grad * attn, axis=1, keepdims=True)
        gx = (jnp.where(low, grad, g_denom * (1.0 / HD)) / denominator).astype(BF16)
        g_weight = dot(gx, vx_ref[pair], NT)
        part = lambda v, h: v[WIN * h : WIN * h + WIN]
        g_score = jnp.concatenate(
            [(exps[h] * part(g_weight, h)).astype(BF16) for h in range(heads)], axis=0
        )
        g_lin = jnp.concatenate(
            [jnp.where(linear, part(g_weight, h), 0.0).astype(BF16) for h in range(heads)], axis=0
        )
        g_query = dot(g_score, key) * scale
        gk_ref[pair] += dot(g_score, query, TN) * scale
        gv_ref[pair] += dot(weight, gx, TN)
        gphi_ref[0, 0, pair] += dot(g_lin, phi_query, TN)
        from_lin = dot(g_lin, phi_key)
        from_state = dot(gx, state_low, NT)
        gstate_ref[b] = dot(phi_valid, gx, TN)
        for h in range(heads):
            gphiq_ref[h, rows] = part(from_lin, h) + jnp.where(valid, part(from_state, h), 0.0)
            gqs_ref[h, rows] = part(g_query, h)
    for h in range(heads):
        g_logit = features_back(phiq_ref[0, h], gphiq_ref[h])
        gl_ref[h] = g_logit
        gqs_ref[h] += dot(g_logit, feat_ref[h][:, :HD], NT)
    gq_ref[0] = jnp.concatenate([gqs_ref[h] for h in range(heads)], axis=1).astype(BF16)
    for h in range(0, heads, 2):
        gfeat_ref[0, h // 2] = jnp.concatenate(
            [dot(q_ref[0, i], gl_ref[i], TN) for i in (h, h + 1)], axis=1
        )
    later = gstate_ref[blocks - 1]
    for b in range(blocks - 1, 0, -1):
        rows = slice(WIN * (b - 1), WIN * b)
        low_state = later.astype(BF16)
        mask = kdoc_ref[0, rows] == ends_ref[r, b]
        gphi_ref[0, 0, rows] += jnp.where(mask, dot(vx_ref[rows], low_state, NT), 0.0)
        gv_ref[rows] += jnp.where(mask, dot(phi_ref[0, 0, rows], low_state), 0.0)
        keep = (ends_ref[r, b] == ends_ref[r, b - 1]).astype(F32)
        later = gstate_ref[b - 1] + keep * later
    gcarry_ref[0, 0] = later.astype(BF16)
    gv = gv_ref[...]
    gkv_ref[0, 0, :, :HD] = gk_ref[...]
    gkv_ref[0, 0, :, HD:] = gv[:, :HD]


def attend_back(ends, q, kv, phi, phiq, feat, carry, qdoc, kdoc, pdoc, g, after=()):
    slots, all_heads, length, _ = q.shape
    groups = kv.shape[1]
    heads = all_heads // groups
    ext = length + WIN
    sp = attention_specs(slots, groups, heads, length)
    return kernel_call(
        attend_back_kernel,
        [ends, q, kv, phi, phiq, feat, carry, qdoc, kdoc, pdoc, g],
        after,
        prefetch=1,
        grid=(slots, groups),
        in_specs=[
            sp[n]
            for n in ("q", "kv", "kv", "phiq", "feat", "state", "qdoc", "kdoc", "pdoc", "tokens")
        ],
        out_specs=[sp["tokens"], sp["fgrad"], sp["kv"], sp["kv"], sp["state"]],
        scratch=[
            pltpu.VMEM((ext, 2 * HD), BF16),
            pltpu.VMEM((length // WIN, 2 * HD, 2 * HD), F32),
            pltpu.VMEM((heads, length, 2 * HD), F32),
            pltpu.VMEM((ext, HD), F32),
            pltpu.VMEM((ext, 2 * HD), F32),
            pltpu.VMEM((heads, length, HD), F32),
            pltpu.VMEM((heads, length, HD), BF16),
        ],
        out_shape=[
            jax.ShapeDtypeStruct((slots, length, all_heads * HD), BF16),
            jax.ShapeDtypeStruct((slots, all_heads // 2, HD, 2 * HD), F32),
            jax.ShapeDtypeStruct((slots, groups, ext, 2 * HD), F32),
            jax.ShapeDtypeStruct((slots, groups, ext, 2 * HD), F32),
            jax.ShapeDtypeStruct((slots, groups, 2 * HD, 2 * HD), BF16),
        ],
        name="attend_back",
    )


def key_back_kernel(
    ends_ref, kv_ref, phi_ref, feat_ref, later_ref, kdoc_ref, gphi_ref, gkv_ref,
    body_ref, edge_ref, gfeat_ref,
):
    r = pl.program_id(0)
    ext = kv_ref.shape[2]
    body = ext - WIN
    last = ends_ref[r, body // WIN]
    mask = kdoc_ref[0, :body] == last
    keys, vals, feats = [], [], []
    for i in range(2):
        kv, phi = kv_ref[0, i], phi_ref[0, i]
        later = later_ref[0, i].astype(BF16)
        more_phi = jnp.where(mask, dot(values_ones(kv[:body]), later, NT), 0.0)
        more_v = jnp.where(mask, dot(phi[:body], later), 0.0)
        tail = jnp.zeros((WIN, 2 * HD), F32)
        g_phi = gphi_ref[0, i] + jnp.concatenate([more_phi, tail], axis=0)
        g_logit = features_back(phi, g_phi)
        gkv = gkv_ref[0, i]
        keys.append(gkv[:, :HD] + dot(g_logit, feat_ref[i][:, :HD], NT))
        vals.append(gkv[:, HD:] + jnp.concatenate([more_v, tail], axis=0)[:, :HD])
        feats.append(dot(kv[:, :HD], g_logit, TN))
    gfeat_ref[0, 0] = jnp.concatenate(feats, axis=1)
    both = jnp.concatenate(keys + vals, axis=1)
    body_ref[0, 0] = both[WIN:]
    edge_ref[0, 0] = both[:WIN].astype(BF16)


def key_back(ends, kv, phi, feat, later, kdoc, gphi, gkv, after=()):
    slots, groups, ext, _ = kv.shape
    four = lambda r, s, *_: (r, s, 0, 0)
    wide = pl.BlockSpec((1, 2, ext, 2 * HD), four)
    body = pl.BlockSpec((1, 1, ext - WIN, 4 * HD), four)
    edge = pl.BlockSpec((1, 1, WIN, 4 * HD), four)
    sets = groups // 2
    return kernel_call(
        key_back_kernel,
        [ends, kv, phi, feat, later, kdoc, gphi, gkv],
        after,
        prefetch=1,
        grid=(slots, groups // 2),
        in_specs=[
            wide,
            wide,
            pl.BlockSpec((2, HD, 2 * HD), lambda r, s, *_: (s, 0, 0)),
            pl.BlockSpec((1, 2, 2 * HD, 2 * HD), four),
            pl.BlockSpec((1, ext, 2 * HD), lambda r, s, *_: (r, 0, 0)),
            wide,
            wide,
        ],
        out_specs=[body, edge, pl.BlockSpec((1, 1, HD, 2 * HD), four)],
        out_shape=[
            jax.ShapeDtypeStruct((slots, sets, ext - WIN, 4 * HD), F32),
            jax.ShapeDtypeStruct((slots, sets, WIN, 4 * HD), BF16),
            jax.ShapeDtypeStruct((slots, sets, HD, 2 * HD), F32),
        ],
        name="key_back",
    )


LOW = 128


def normalize(values, gain):
    scale = lax.rsqrt(jnp.mean(values * values, axis=-1, keepdims=True) + NORM_EPS)
    return (values * scale * gain).astype(BF16)


def project_kernel(
    sets, q_cols, k_cols, shares, core_ref, own_ref, other_ref, gain_ref, w_ref, a_ref, b_ref, q_ref,
    kv_ref, small_ref
):
    own = pl.program_id(1) // shares == core_ref[0]
    x = normalize(jnp.where(own, own_ref[0], other_ref[0]).astype(F32), gain_ref[...])
    width = q_cols + 2 * k_cols
    small = dot(x, a_ref[...]).astype(BF16)
    small_ref[0] = small
    heads, groups = q_cols // HD, k_cols // HD
    for s in range(sets):
        cols = slice(s * width, (s + 1) * width)
        full = dot(x, w_ref[s]) + ADAPTER_SCALE * dot(small, b_ref[:, cols])
        for h in range(heads):
            q_ref[0, s * heads + h] = full[:, h * HD : h * HD + HD].astype(BF16)
        for g in range(0, groups, 2):
            k = full[:, q_cols + g * HD : q_cols + g * HD + 2 * HD]
            start = q_cols + k_cols + g * HD
            v = full[:, start : start + 2 * HD]
            low = lower_lanes(k)
            kv_ref[0, s * groups + g] = jnp.where(low, k, swap(v)).astype(BF16)
            kv_ref[0, s * groups + g + 1] = jnp.where(low, swap(k), v).astype(BF16)


def project(core, own, other, gain, w, a, b, q_cols, k_cols, after=()):
    slots, share, depth = own.shape
    length = 2 * share
    sets = w.shape[0]
    heads, groups = sets * q_cols // HD, sets * k_cols // HD
    tile = min(256, share)
    shares = share // tile
    token = pl.BlockSpec((1, tile, depth), lambda r, i, *_: (r, lax.rem(i, shares), 0))
    return kernel_call(
        functools.partial(project_kernel, sets, q_cols, k_cols, shares),
        [core, own, other, gain, w, a, b],
        after,
        prefetch=1,
        grid=(slots, length // tile),
        in_specs=[
            token,
            token,
            pl.BlockSpec(gain.shape, lambda r, i, *_: (0, 0)),
            pl.BlockSpec(w.shape, lambda r, i, *_: (0, 0, 0)),
            pl.BlockSpec(a.shape, lambda r, i, *_: (0, 0)),
            pl.BlockSpec(b.shape, lambda r, i, *_: (0, 0)),
        ],
        out_specs=[
            pl.BlockSpec((1, heads, tile, HD), lambda r, i, *_: (r, 0, i, 0)),
            pl.BlockSpec((1, groups, tile, 2 * HD), lambda r, i, *_: (r, 0, i, 0)),
            pl.BlockSpec((1, tile, LOW), lambda r, i, *_: (r, i, 0)),
        ],
        out_shape=[
            jax.ShapeDtypeStruct((slots, heads, length, HD), BF16),
            jax.ShapeDtypeStruct((slots, groups, length, 2 * HD), BF16),
            jax.ShapeDtypeStruct((slots, length, LOW), BF16),
        ],
        cost=pl.CostEstimate(
            flops=2 * slots * length * w.size,
            bytes_accessed=2 * (slots * length * depth + w.size),
            transcendentals=0,
        ),
        name="project",
    )


def halves(share, tile):
    shares = share // tile
    own = lambda r, i, core: (r, core[0] * shares + i, 0)
    other = lambda r, i, core: (r, (1 - core[0]) * shares + i, 0)
    return own, other


def out_project_kernel(core_ref, own_ref, other_ref, w_ref, low_ref, keep_ref, away_ref):
    depth = w_ref.shape[1]
    half = w_ref.shape[2]
    for src, dst in ((own_ref, keep_ref), (other_ref, away_ref)):
        attn = src[0]
        full = dot(attn[:, :half], w_ref[0], NT) + dot(attn[:, half:], w_ref[1], NT)
        dst[0, :, :depth] = full.astype(BF16)
        dst[0, :, depth:] = dot(attn, low_ref[...]).astype(BF16)


def out_project(core, attn, w, low, share):
    slots, length, width = attn.shape
    depth = w.shape[1]
    tile = min(256, share)
    own, other = halves(share, tile)
    out = pl.BlockSpec((1, tile, depth + LOW), lambda r, i, *_: (r, i, 0))
    shape = jax.ShapeDtypeStruct((slots, share, depth + LOW), BF16)
    return kernel_call(
        out_project_kernel,
        [core, attn, attn, w, low],
        (),
        prefetch=1,
        grid=(slots, share // tile),
        in_specs=[
            pl.BlockSpec((1, tile, width), own),
            pl.BlockSpec((1, tile, width), other),
            pl.BlockSpec(w.shape, lambda r, i, *_: (0, 0, 0)),
            pl.BlockSpec(low.shape, lambda r, i, *_: (0, 0)),
        ],
        out_specs=[out, out],
        out_shape=[shape, shape],
        name="out_project",
    )


def middle_kernel(hidden_ref, keep_ref, got_ref, second_ref, gain_ref, mid_ref, normed_ref, low_ref):
    depth = hidden_ref.shape[1]
    total = keep_ref[...].astype(F32) + got_ref[...].astype(F32)
    low = total[:, depth:].astype(BF16)
    low_ref[...] = low
    mid = hidden_ref[...].astype(F32) + total[:, :depth]
    mid = mid + ADAPTER_SCALE * dot(low, second_ref[...])
    mid_ref[...] = mid.astype(BF16)
    normed_ref[...] = normalize(mid, gain_ref[...])


def tokens_call(kernel, tiled, whole, outs, name, prefetch=(), sums=(), tile=128, after=()):
    tokens = tiled[0].shape[0]
    tile = min(tile, tokens)
    rows = lambda v: pl.BlockSpec((tile, v.shape[1]), lambda i, *_: (i, 0))
    full = lambda v: pl.BlockSpec(v.shape, lambda i, *_: (0, 0))
    shapes = [jax.ShapeDtypeStruct((tokens, width), kind) for width, kind in outs]
    totals = [jax.ShapeDtypeStruct(v, F32) for v in sums]
    return kernel_call(
        kernel,
        [*prefetch, *tiled, *whole],
        after,
        prefetch=len(prefetch),
        grid=(tokens // tile,),
        in_specs=[rows(v) for v in tiled] + [full(v) for v in whole],
        out_specs=[rows(v) for v in shapes] + [full(v) for v in totals],
        out_shape=shapes + totals,
        name=name,
    )


def norm_back(values, gain, grad):
    scale = lax.rsqrt(jnp.mean(values * values, axis=-1, keepdims=True) + NORM_EPS)
    scaled = gain * grad
    shared = scale * scale * scale * jnp.mean(values * scaled, axis=-1, keepdims=True)
    return scale, scale * scaled - values * shared


def pair_kernel(a_ref, b_ref, out_ref):
    out_ref[...] = a_ref[...] + b_ref[...].astype(F32)


def sum_kernel(*refs):
    refs[-1][...] = sum(r[...].astype(F32) for r in refs[:-1]).astype(BF16)


def branch_kernel(slot_len, slots, live_ref, mid_ref, a_ref, c_ref, cot_ref, *refs):
    parts, (gain_ref, grad_ref) = refs[:slots], refs[slots:]
    part = parts[0][...]
    for r in range(1, slots):
        part = jnp.where(pl.program_id(0) == r, parts[r][...], part)
    grad = a_ref[...].astype(F32) + part.astype(F32) + c_ref[...].astype(F32)
    tile = mid_ref.shape[0]
    token = pl.program_id(0) * tile + lax.broadcasted_iota(jnp.int32, (tile, 1), 0)
    live = token < live_ref[0] * slot_len
    cot = jnp.where(live, cot_ref[...].astype(F32), 0.0)
    mid = mid_ref[...].astype(F32)
    grad_ref[...] = (cot + norm_back(mid, gain_ref[...], grad)[1]).astype(BF16)


def attn_grad_kernel(
    shares, core_ref, own_ref, other_ref, attn_ref, w_ref, second_ref, first_ref, grad_ref, sum_ref
):
    own = pl.program_id(1) // shares == core_ref[0]
    x = jnp.where(own, own_ref[0], other_ref[0])
    low = (ADAPTER_SCALE * dot(x, second_ref[...], NT)).astype(BF16)
    half = w_ref.shape[2]
    first = first_ref[...]
    for s in range(2):
        cols = slice(s * half, (s + 1) * half)
        grad_ref[0, :, cols] = (dot(x, w_ref[s]) + dot(low, first[cols], NT)).astype(BF16)

    @pl.when((pl.program_id(0) == 0) & (pl.program_id(1) == 0))
    def _():
        sum_ref[...] = jnp.zeros_like(sum_ref)

    sum_ref[...] += dot(low, attn_ref[0], TN)


def attn_grad(core, own, other, attn, w, second, first):
    slots, share, depth = own.shape
    length = 2 * share
    width = attn.shape[2]
    tile = min(256, share)
    shares = share // tile
    token = pl.BlockSpec((1, tile, depth), lambda r, i, *_: (r, lax.rem(i, shares), 0))
    wide = pl.BlockSpec((1, tile, width), lambda r, i, *_: (r, i, 0))
    full = lambda v: pl.BlockSpec(v.shape, lambda r, i, *_: (0,) * v.ndim)
    total = jax.ShapeDtypeStruct((LOW, width), F32)
    return kernel_call(
        functools.partial(attn_grad_kernel, shares),
        [core, own, other, attn, w, second, first],
        (),
        prefetch=1,
        grid=(slots, length // tile),
        in_specs=[token, token, wide, full(w), full(second), full(first)],
        out_specs=[wide, full(total)],
        out_shape=[jax.ShapeDtypeStruct(attn.shape, BF16), total],
        name="attn_grad",
    )


def normed_grad_kernel(
    q_cols, shares, core_ref, q_own_ref, q_other_ref, kv_own_ref, kv_other_ref, s_own_ref, s_other_ref,
    back_ref, w_ref, b_ref, keep_ref, away_ref, sum_ref
):
    depth, width = w_ref.shape[1:]
    core, step = core_ref[0], pl.program_id(1)

    @pl.when((pl.program_id(0) == 0) & (step == 0))
    def _():
        sum_ref[...] = jnp.zeros_like(sum_ref)

    sides = (
        (q_own_ref, kv_own_ref, s_own_ref, keep_ref, core),
        (q_other_ref, kv_other_ref, s_other_ref, away_ref, 1 - core),
    )
    for q_ref, kv_ref, s_ref, out_ref, share in sides:
        tile = q_ref.shape[1]
        last = (share * shares + step == 2 * shares - 1).astype(F32)
        full = low = None
        for s in range(2):
            kv = kv_ref[0, s]
            edge = back_ref[0, s].astype(F32) * last
            if tile > WIN:
                edge = jnp.concatenate([jnp.zeros((tile - WIN, kv.shape[1]), F32), edge], axis=0)
            kv = (kv + edge).astype(BF16)
            q = q_ref[0, :, s * q_cols : (s + 1) * q_cols]
            grads = jnp.concatenate([q, kv], axis=1)
            part = dot(grads, w_ref[s], NT)
            small = dot(grads, b_ref[:, s * width : (s + 1) * width], NT)
            full = part if full is None else full + part
            low = small if low is None else low + small
            sum_ref[s] += dot(s_ref[0], grads, TN)
        out_ref[0, :, :depth] = full.astype(BF16)
        out_ref[0, :, depth:] = (ADAPTER_SCALE * low).astype(BF16)


def normed_grad(core, q, kv, small, back, w, b, q_cols, share):
    slots, length, q_width = q.shape
    sets, depth, width = w.shape
    tile = min(256, share)
    shares = share // tile
    own, other = halves(share, tile)
    four = lambda f: (lambda r, i, core: (r, 0, f(r, i, core)[1], 0))
    out = pl.BlockSpec((1, tile, depth + LOW), lambda r, i, *_: (r, i, 0))
    shape = jax.ShapeDtypeStruct((slots, share, depth + LOW), BF16)
    total = jax.ShapeDtypeStruct((sets, LOW, width), F32)
    kv_block = (1, sets, tile, kv.shape[3])
    return kernel_call(
        functools.partial(normed_grad_kernel, q_cols, shares),
        [core, q, q, kv, kv, small, small, back, w, b],
        (),
        prefetch=1,
        grid=(slots, shares),
        in_specs=[
            pl.BlockSpec((1, tile, q_width), own),
            pl.BlockSpec((1, tile, q_width), other),
            pl.BlockSpec(kv_block, four(own)),
            pl.BlockSpec(kv_block, four(other)),
            pl.BlockSpec((1, tile, LOW), own),
            pl.BlockSpec((1, tile, LOW), other),
            pl.BlockSpec((1, sets, WIN, kv.shape[3]), lambda r, i, *_: (r, 0, 0, 0)),
            pl.BlockSpec(w.shape, lambda r, i, *_: (0, 0, 0)),
            pl.BlockSpec(b.shape, lambda r, i, *_: (0, 0)),
        ],
        out_specs=[out, out, pl.BlockSpec(total.shape, lambda r, i, *_: (0, 0, 0))],
        out_shape=[shape, shape, total],
        name="normed_grad",
    )


def finish_kernel(keep_ref, got_ref, hidden_ref, mid_ref, gain_ref, first_ref, out_ref, sum_ref):
    depth = hidden_ref.shape[1]
    total = keep_ref[...].astype(F32) + got_ref[...].astype(F32)
    low = total[:, depth:].astype(BF16)
    grad = total[:, :depth] + dot(low, first_ref[...])
    values, gain = hidden_ref[...].astype(F32), gain_ref[...]
    scale, back = norm_back(values, gain, grad)
    out_ref[...] = (mid_ref[...].astype(F32) + back).astype(BF16)

    @pl.when(pl.program_id(0) == 0)
    def _():
        sum_ref[...] = jnp.zeros_like(sum_ref)

    sum_ref[...] += dot(low, (values * scale * gain).astype(BF16), TN)


def sums_kernel(rows, seqs, heads, part_ref, pack_ref, out_ref, cols_ref, *scratch):
    a1, a2, a3, c2, c3, b1, b2, b3, e2, e3, send_sem, recv_sem = scratch
    place = {a: lax.axis_index(a) for a in ("row", "seq", "head")}
    counts = {"row": rows, "seq": seqs, "head": heads}
    x_place = place["head"] // 2
    peers = [
        (a, {a: lax.rem(place[a] + d, counts[a])}) for a in counts for d in range(1, counts[a])
    ]
    barrier = pltpu.get_barrier_semaphore()
    for _, peer in peers:
        pl.semaphore_signal(barrier, inc=1, device_id=peer, device_id_type=pl.DeviceIdType.MESH)
    pl.semaphore_wait(barrier, len(peers))
    used = [0]

    def remote(src, dst, device):
        n = used[0]
        used[0] += 1
        return pltpu.make_async_remote_copy(
            src_ref=src, dst_ref=dst, send_sem=send_sem.at[n], recv_sem=recv_sem.at[n],
            device_id=device, device_id_type=pl.DeviceIdType.MESH,
        )

    def exchange(axis, parts, slots, packs, pack_slots):
        me, size = place[axis], counts[axis]
        copies = []
        for d in range(1, size):
            to = lax.rem(me + d, size)
            copies.append(remote(parts.at[to], slots.at[me], {axis: to}))
            if pack_slots is not None:
                copies.append(remote(packs, pack_slots.at[me], {axis: to}))
        return copies

    def add_up(ref, size):
        total = ref[0].astype(F32)
        for i in range(1, size):
            total = total + ref[i].astype(F32)
        return total

    b1[0] = pack_ref[1 - x_place].astype(BF16)
    copies = exchange("head", part_ref, a1, None, None)
    copies.append(remote(b1.at[0], b1.at[1], {"head": lax.rem(place["head"] + 2, heads)}))
    for copy in copies:
        copy.start()
    a1[place["head"]] = part_ref[place["head"]]
    for copy in copies:
        copy.wait()
    stages = (
        ("seq", add_up(a1, heads), pack_ref[x_place] + b1[1].astype(F32), c2, a2, e2, b2),
        ("row", None, None, c3, a3, e3, b3),
    )
    for axis, part, pack, held, slots, pack_held, pack_slots in stages:
        if part is None:
            part, pack = add_up(a2, seqs), add_up(b2, seqs)
        held[...] = part
        pack_held[...] = pack.astype(BF16)
        copies = exchange(axis, held, slots, pack_held, pack_slots)
        for copy in copies:
            copy.start()
        slots[place[axis]] = held[place[axis]]
        pack_slots[place[axis]] = pack_held[...]
        for copy in copies:
            copy.wait()
    out_ref[...] = add_up(a3, rows)
    cols_ref[...] = add_up(b3, rows)


def final_sums(part, pack):
    rows, seqs, heads = (lax.axis_size(a) for a in ("row", "seq", "head"))
    low, width = part.shape[3:]
    count, lanes = pack.shape[1:]
    place = pl.BlockSpec(memory_space=pltpu.VMEM)
    copies = heads + 2 * (seqs - 1) + 2 * (rows - 1)
    return pl.pallas_call(
        functools.partial(sums_kernel, rows, seqs, heads),
        in_specs=[place, place],
        out_specs=[place, place],
        out_shape=[
            jax.ShapeDtypeStruct((low, width), F32),
            jax.ShapeDtypeStruct((count, lanes), F32),
        ],
        scratch_shapes=[
            pltpu.VMEM((heads, seqs, rows, low, width), F32),
            pltpu.VMEM((seqs, rows, low, width), F32),
            pltpu.VMEM((rows, low, width), F32),
            pltpu.VMEM((seqs, rows, low, width), F32),
            pltpu.VMEM((rows, low, width), F32),
            pltpu.VMEM((2, count, lanes), BF16),
            pltpu.VMEM((seqs, count, lanes), BF16),
            pltpu.VMEM((rows, count, lanes), BF16),
            pltpu.VMEM((count, lanes), BF16),
            pltpu.VMEM((count, lanes), BF16),
            pltpu.SemaphoreType.DMA((copies,)),
            pltpu.SemaphoreType.DMA((copies,)),
        ],
        compiler_params=pltpu.CompilerParams(
            collective_id=1, has_side_effects=True, vmem_limit_bytes=32 * 2**20
        ),
        name="final_sums",
    )(part, pack)


def local(
    hidden_in,
    grad_out,
    live_rows,
    doc_starts,
    norm_attn,
    norm_ffn,
    query_weight,
    key_weight,
    value_weight,
    out_weight,
    gate_weight,
    up_weight,
    down_weight,
    query_adapt_in,
    query_adapt_out,
    key_adapt_in,
    key_adapt_out,
    value_adapt_in,
    value_adapt_out,
    outproj_adapt_in,
    projection_adapter_second,
    query_feature,
    key_feature,
):
    rows, seqs, heads = lax.axis_size("row"), lax.axis_size("seq"), lax.axis_size("head")
    head = lax.axis_index("head")
    core = lax.rem(head, 2)
    x_count = heads // 2
    x_place = head // 2
    slots, share_len, model_dim = hidden_in.shape
    piece_len = 2 * share_len
    pieces = seqs * x_count
    piece = lax.axis_index("seq") * x_count + x_place
    blocks = piece_len // WIN
    ext_len = piece_len + WIN
    q_cols, k_cols = query_weight.shape[1], key_weight.shape[1]
    ff_cols = gate_weight.shape[1]

    def in_order(own, other):
        first = jnp.where(core == 0, own, other)
        second = jnp.where(core == 0, other, own)
        return jnp.concatenate([first, second], axis=1)

    def own_half(both):
        return lax.dynamic_slice_in_dim(both, core * share_len, share_len, 1)

    def other_half(both):
        return lax.dynamic_slice_in_dim(both, (1 - core) * share_len, share_len, 1)

    qkv_shard = jnp.concatenate([query_weight, key_weight, value_weight], axis=1)
    out_shard = out_weight.T
    down_shard = down_weight.T
    unit = ff_cols // sum(FF_CHUNKS)
    bounds = [unit * sum(FF_CHUNKS[:j]) for j in range(len(FF_CHUNKS) + 1)]
    ffn_shards = [
        jnp.concatenate([w[:, lo:hi] for w in (gate_weight, up_weight, down_shard)], axis=1)
        for lo, hi in zip(bounds[:-1], bounds[1:])
    ]
    ffn_later = [
        lax.all_gather(v, ("row", "seq"), axis=0, tiled=True) for v in ffn_shards[1:]
    ]
    own_smalls = [
        query_feature, key_feature, query_adapt_out, key_adapt_out, value_adapt_out, outproj_adapt_in
    ]
    (qkv_mat, out_mat, first_mat), other_smalls, (hidden_other, cot_mine, cot_away) = gather(
        [qkv_shard, out_shard, ffn_shards[0]],
        [True, True, False],
        [
            (0, (0, qkv_shard.shape[1]), True, 0),
            (1, (0, out_shard.shape[1]), True, 0),
            (2, (0, ffn_shards[0].shape[1]), True, rows * seqs),
        ],
        own_smalls,
        hidden_in,
        grad_out,
    )
    ffn_mats = [first_mat] + ffn_later

    def both(i, axis):
        own, other = own_smalls[i], other_smalls[i]
        return jnp.concatenate(
            [jnp.where(x_place == 0, own, other), jnp.where(x_place == 0, other, own)], axis=axis
        )

    query_feat_all, key_feat_all = both(0, 0), both(1, 0)
    q_out, k_out, v_out = both(2, 1), both(3, 1), both(4, 1)
    o_in = both(5, 0)

    doc_ids = jnp.cumsum(doc_starts, axis=1)
    padded_docs = jnp.concatenate(
        [jnp.full((slots, WIN + 1), -1, jnp.int32), doc_ids], axis=1
    )
    piece_docs = padded_docs[:, ::piece_len][:, : pieces + 1]
    near_docs = lax.dynamic_slice_in_dim(padded_docs, piece * piece_len, ext_len + 1, 1)
    end_docs = near_docs[:, ::WIN][:, : blocks + 1]
    carry_doc = end_docs[:, 0]
    next_doc = end_docs[:, blocks]
    key_docs = near_docs[:, 1:]
    key_doc_lanes = jnp.broadcast_to(key_docs[:, :, None], (slots, ext_len, 2 * HD))
    query_doc_lanes = key_doc_lanes[:, WIN:]
    doc_blocks = key_docs.reshape(slots, blocks + 1, WIN)
    pair_docs = jnp.concatenate([doc_blocks[:, :-1], doc_blocks[:, 1:]], axis=2)

    def from_pieces(block):
        held = []
        for d, start in enumerate((block, flip_x(block))):
            for l in range(seqs):
                if l:
                    start = shift(start, "seq", 1)
                source = (
                    lax.rem(lax.axis_index("seq") - l + seqs, seqs) * x_count
                    + lax.rem(x_place + d, x_count)
                )
                held.append((source, start))
        return held[1:]

    gain_attn = norm_attn.astype(F32)[None]
    gain_ffn = norm_ffn.astype(F32)[None]
    core_index = core.astype(jnp.int32).reshape(1)
    flat_tokens = lambda v: v.reshape(-1, v.shape[-1])

    set_cols = q_cols + 2 * k_cols
    adapt_in_all = jnp.concatenate([query_adapt_in, key_adapt_in, value_adapt_in], axis=1)

    def by_sets(parts):
        return jnp.concatenate(
            [v[:, d * (v.shape[1] // 2) : (d + 1) * (v.shape[1] // 2)] for d in range(2) for v in parts],
            axis=1,
        )

    def diagonal(parts):
        rows = [
            [p if i == j else jnp.zeros((RANK, q.shape[1]), BF16) for j, q in enumerate(parts)]
            for i, p in enumerate(parts)
        ]
        return jnp.concatenate([by_sets(r) for r in rows], axis=0)

    pad_rows = lambda v: jnp.pad(v, ((0, LOW - v.shape[0]), (0, 0)))
    pad_cols = lambda v: jnp.pad(v, ((0, 0), (0, LOW - v.shape[1])))
    adapt_in_all = pad_cols(adapt_in_all)
    adapt_out_all = pad_rows(diagonal([q_out, k_out, v_out]))
    second = pad_rows(projection_adapter_second)
    o_in = pad_cols(o_in)
    query, kv_own, small = project(
        core_index, hidden_in, hidden_other, gain_attn, qkv_mat, adapt_in_all, adapt_out_all, q_cols,
        k_cols,
    )

    def along_pieces(block, distance):
        route = []
        for p in range(pieces):
            to = p + distance
            if 0 <= to < pieces:
                for c in range(2):
                    route.append((2 * p + c, 2 * to + c))
        return lax.ppermute(block, ("seq", "head"), route)

    kv = jnp.concatenate([along_pieces(kv_own[:, :, -WIN:], 1), kv_own], axis=2)
    doubled = lambda feat: jnp.concatenate([feat, -feat], axis=2)
    query_feat, key_feat = doubled(query_feat_all), doubled(key_feat_all)
    phi_key, end_state = key_state(end_docs, kv, key_feat, key_doc_lanes)
    carry = jnp.zeros(end_state.shape, F32)
    for source, part in from_pieces(end_state):
        after = lax.dynamic_index_in_dim(piece_docs, source + 1, 1, keepdims=False)
        keep = (source < piece) & (after == carry_doc)
        carry = carry + jnp.where(keep[:, None, None, None], part.astype(F32), 0.0)
    phi_query = query_features(query, query_feat, kv.shape[1])
    attn = attend(
        end_docs, query, kv, phi_key, phi_query, carry, query_doc_lanes, key_doc_lanes, pair_docs
    )

    keep, away = out_project(core_index, attn, out_mat, o_in, share_len)
    mid_rows, nmid, low_mix = tokens_call(
        middle_kernel,
        [flat_tokens(v) for v in (hidden_in, keep, flip_core(away))],
        [second, gain_ffn],
        [(model_dim, BF16), (model_dim, BF16), (LOW, BF16)],
        "middle",
    )

    nmid_x = flip_x(nmid)

    def chip_tokens(own):
        return own, flip_core(own)

    def sum_away(own, other):
        return (own.astype(F32) + flip_core(other).astype(F32)).astype(BF16)

    x_mine = chip_tokens(nmid)
    c_mine, c_away = flat_tokens(cot_mine), flat_tokens(cot_away)
    run = lambda x, c, w, before=(), after=(): ffn(
        x, c, w, live_rows, share_len, slots, before, after
    )
    mine = run(x_mine, c_mine, ffn_mats[:2])
    x_away = chip_tokens(hold(nmid_x, (mine[0],)))
    away = run(x_away, c_away, ffn_mats[:-1])
    away = run(x_away, c_away, ffn_mats[-1:], away)
    gn_there = sum_away(*away[:2])
    gn_back = flip_x(gn_there)
    gn_own, gn_other, y_own, y_other = run(
        x_mine, c_mine, ffn_mats[2:], mine, (gn_there,)
    )
    y_there = sum_away(*away[2:])
    y_back = flip_x(y_there)
    branch, = tokens_call(
        functools.partial(branch_kernel, share_len, slots),
        [mid_rows, gn_own, gn_back, flat_tokens(grad_out)],
        [flip_core(gn_other[r * share_len : (r + 1) * share_len]) for r in range(slots)] + [gain_ffn],
        [(model_dim, BF16)],
        "branch",
        prefetch=[live_rows],
        tile=share_len,
    )

    shaped = lambda v: v.reshape(slots, share_len, -1)
    grad_attn, sum_o_in = attn_grad(
        core_index, shaped(branch), shaped(flip_core(branch)), attn, out_mat, second, o_in
    )
    sum_o_in = sum_o_in[:RANK]
    sum_o_out = ADAPTER_SCALE * dot(low_mix, branch, TN)[:RANK]

    grad_query, feat_query, gphi, gkv, grad_carry = attend_back(
        end_docs, query, kv, phi_key, phi_query, query_feat, carry, query_doc_lanes, key_doc_lanes,
        pair_docs, grad_attn, (y_there,),
    )
    block_out = tokens_call(
        sum_kernel, [mid_rows, y_own, flip_core(y_other), y_back], [], [(model_dim, BF16)], "sum_y",
        after=(grad_carry,),
    )[0]
    later = jnp.zeros(grad_carry.shape, F32)
    for source, part in from_pieces(grad_carry):
        start = lax.dynamic_index_in_dim(piece_docs, source, 1, keepdims=False)
        keep = (source > piece) & (start == next_doc)
        later = later + jnp.where(keep[:, None, None, None], part.astype(F32), 0.0)
    grad_body, grad_edge, feat_key = key_back(
        end_docs, kv, phi_key, key_feat, later, key_doc_lanes, gphi, gkv, (block_out,)
    )
    sum_q_feat = jnp.sum(feat_query, axis=0).reshape(2, -1, 2 * HD)
    sum_k_feat = jnp.sum(feat_key, axis=0).reshape(2, -1, 2 * HD)

    keep, away, outs = normed_grad(
        core_index, grad_query, grad_body, small, along_pieces(grad_edge, -1), qkv_mat, adapt_out_all,
        q_cols, share_len,
    )
    outs = ADAPTER_SCALE * outs
    outs = [
        outs[:, :RANK, :q_cols],
        outs[:, RANK : 2 * RANK, q_cols : q_cols + k_cols],
        outs[:, 2 * RANK : 3 * RANK, q_cols + k_cols :],
    ]
    grad_hidden, sum_in = tokens_call(
        finish_kernel,
        [flat_tokens(keep), flat_tokens(flip_core(away)), flat_tokens(hidden_in), branch],
        [gain_attn, adapt_in_all.T],
        [(model_dim, BF16)],
        "finish",
        sums=[(LOW, model_dim)],
    )
    grad_hidden = grad_hidden.reshape(hidden_in.shape)
    sum_in = sum_in[: 3 * RANK]

    by_rows = jnp.concatenate([sum_in, sum_o_out], axis=0)
    width = model_dim // (rows * seqs * heads)
    by_rows = by_rows.reshape(4 * RANK, rows, seqs, heads, width).transpose(3, 2, 1, 0, 4)
    by_rows = by_rows.reshape(heads, seqs, rows, -1, 2 * HD)

    def lanes_of(v):
        v = v.reshape(2, RANK, -1, 2 * HD).transpose(0, 2, 1, 3)
        return v.reshape(2, -1, 2 * HD)

    o_sets = jnp.stack([sum_o_in[:, :q_cols], sum_o_in[:, q_cols:]])
    packed = [lanes_of(v) for v in outs + [o_sets]] + [sum_q_feat, sum_k_feat]
    sizes = [v.shape[1] for v in packed]
    packed = jnp.concatenate(packed, axis=1)
    in_parts, packed = final_sums(by_rows, packed)
    in_parts = in_parts.reshape(4, RANK, width)
    cols, at = [], 0
    for size in sizes:
        cols.append(packed[at : at + size])
        at += size
    from_lanes = lambda v: v.reshape(-1, RANK, 2 * HD).transpose(1, 0, 2).reshape(RANK, -1)
    from_pairs = lambda v: v.reshape(-1, HD, 2, HD).transpose(0, 2, 1, 3).reshape(-1, HD, HD)
    cols = [from_lanes(v) for v in cols[:4]] + [from_pairs(v) for v in cols[4:]]
    cols[3] = cols[3].T

    return (
        block_out.reshape(hidden_in.shape),
        grad_hidden,
        in_parts[0].T,
        cols[0],
        in_parts[1].T,
        cols[1],
        in_parts[2].T,
        cols[2],
        cols[3],
        in_parts[3],
        cols[4],
        cols[5],
    )


def solution(mesh):
    return jax.shard_map(
        local,
        mesh=mesh,
        in_specs=(
            P("row", ("seq", "head"), None),
            P("row", ("seq", "head"), None),
            P("row"),
            P("row", None),
            P(),
            P(),
            P(("row", "seq"), "head"),
            P(("row", "seq"), "head"),
            P(("row", "seq"), "head"),
            P("head", ("row", "seq")),
            P(("row", "seq"), "head"),
            P(("row", "seq"), "head"),
            P("head", ("row", "seq")),
            P(),
            P(None, "head"),
            P(),
            P(None, "head"),
            P(),
            P(None, "head"),
            P("head", None),
            P(),
            P("head", None, None),
            P("head", None, None),
        ),
        out_specs=(
            P("row", ("seq", "head"), None),
            P("row", ("seq", "head"), None),
            P(("row", "seq", "head"), None),
            P(None, "head"),
            P(("row", "seq", "head"), None),
            P(None, "head"),
            P(("row", "seq", "head"), None),
            P(None, "head"),
            P("head", None),
            P(None, ("row", "seq", "head")),
            P("head", None, None),
            P("head", None, None),
        ),
        check_vma=False,
    )
```
